128 devices in a mesh: type: 4 (over z), rows: 32 (over y, x, core).
Axes of the slice: x: 4, y: 4, z: 4, core: 2. Of those that a mesh axis runs over, the one named last changes fastest.
Arguments:
- features: bfloat16 [524288, 256], P(('type', 'rows')), may hold values from -6 to 6
- out_grad: bfloat16 [524288, 256], P(('type', 'rows')), may hold values from -6 to 6
- rel_weight: bfloat16 [5, 256, 256], replicated, may hold values from -0.375 to 0.375
- root_weight: bfloat16 [256, 256], replicated, may hold values from -0.375 to 0.375
- tiles: bfloat16 [16384, 128, 128], P(('type', 'rows')), may hold values from 0 to 0.25
- tile_dest: int32 [16384], P(('type', 'rows')), may hold values from 0 to 31
- tile_peer: int32 [16384, 1], P(('type', 'rows')), may hold values from 0 to 127; in each aligned block of 128 rows (0 to 127, 128 to 255, ...) at most 2 rows name the same one
- tile_source: int32 [16384], P(('type', 'rows')), may hold values from 0 to 31
- tile_rel: int32 [16384], P(('type', 'rows')), may hold values from 0 to 4
Outputs:
- grad_feat: bfloat16 [524288, 256], P(('type', 'rows'))
- grad_weights: float32 [6, 256, 256], replicated
The draws below stay inside these ranges and needn't reach their ends.
Inputs may be any that keep to these rules, and one draw needn't show every extreme that they name: `tile_peer`: among the tiles of one device, no owner is named more than 2 times, a bound that some block reaches.
All inputs are finite; a program needn't handle non-finite values.
Results may differ from the reference program's by a relative error of at most 0.0085.
Values may be sent and summed in bfloat16 or wider, within the bound.
No kernel may reach another device: no remote copies, remote signals or barrier semaphores. Data moves between devices by JAX's collectives and lax.ppermute only.
A program may use at most 128 MiB of HBM per device.

```python
import math
import jax
import jax.numpy as jnp
import numpy as np
from jax import lax

D = 256
REL = 5
BLOCK = 128
NB_DEV = 32
TILES_DEV = 128
CAP = 2
TILES = 16384
NODES = 524288
DEVICES = 128


def set_ends(values, stream_key, smallest, high):
    shape = values.shape
    spot = [jax.random.randint(jax.random.fold_in(stream_key, axis), (), 0, shape[axis]) for axis in range(len(shape))]
    values = values.at[tuple(spot)].set(smallest)
    longest = shape.index(max(shape))
    spot[longest] = (spot[longest] + 1) % shape[longest]
    return values.at[tuple(spot)].set(high)


def level_of(rng, extent, pieces, low, largest):
    factor_of, own = 1.0, jax.random.fold_in(rng, 6)
    for position, blocks in pieces:
        heights = jnp.exp(jax.random.uniform(jax.random.fold_in(own, position), (blocks,), jnp.float32, low / len(pieces), largest / len(pieces)))
        factor_of = factor_of * jnp.repeat(heights, extent[position] // blocks).reshape([-1 if axis == position else 1 for axis in range(len(extent))])
    return factor_of


def deal_out(key, own, number, rows, count, top, limit, slope):
    sequence = jax.random.permutation(key, count)
    heavy_load, usual = load_shares(count, rows * top, limit, slope, True), load_shares(count, rows * top, limit, slope, False)
    places = jnp.arange(count)

    def named(lengths, rotation):
        used = int((lengths > 0).sum())
        fixed = max(1, used // 4)
        moved = fixed + (places - fixed + rotation * (used - fixed)) % max(1, count - fixed)
        return jnp.zeros((count,), jnp.int32).at[sequence[jnp.where(places < fixed, places, moved)]].set(jnp.asarray(lengths, jnp.int32))

    lengths = jnp.where(number % 4 == 0, named(heavy_load, number // 4), named(usual, number - number // 4 - 1))
    mixed = jax.random.permutation(jax.random.fold_in(own, 3), count)
    source_of, taker = mixed[0:count // 2 * 2:2], mixed[1:count // 2 * 2:2]
    slack = jnp.minimum(lengths[source_of] - 1, limit - lengths[taker]) // 2
    slack = jnp.where((source_of == sequence[0]) | (taker == sequence[0]) | (lengths[taker] == 0), 0, jnp.maximum(slack, 0))
    moved = jax.random.randint(jax.random.fold_in(own, 4), (count // 2,), 0, 1 << 20) % (slack + 1)
    lengths = lengths.at[source_of].add(-moved).at[taker].add(moved)
    members = jnp.searchsorted(jnp.cumsum(lengths), jnp.arange(rows * top), side="right").astype(jnp.int32)
    listing = members.reshape(top, rows).T
    listing = listing[jax.random.permutation(jax.random.fold_in(own, 1), rows)]
    rotation = jax.random.randint(jax.random.fold_in(own, 2), (rows, 1), 0, top)
    return jnp.take_along_axis(listing, (jnp.arange(top)[None, :] + rotation) % top, axis=1)


def load_shares(count, total, most, slope, full):
    loads = [(1 << 20) // math.isqrt(standing ** slope) + 1 for standing in range(1, count + 1)]
    largest = most if full else min(most, max(-(-total // count), total * loads[0] // sum(loads)))
    least = 1 if total - largest >= count - 1 else 0
    given, spare = [largest] + [least] * (count - 1), total - largest - least * (count - 1)
    while spare > 0:
        free = [i for i in range(1, count) if given[i] < largest] or [i for i in range(1, count) if given[i] < most]
        whole, left = sum([loads[i] for i in free]), spare
        for i in free:
            addition = min(most - given[i], max(1, left * loads[i] // whole), spare)
            given[i] = given[i] + addition
            spare = spare - addition
    return np.array(given)


def gaussian(key, dims, scale, bound, cuts=(), held_as=jnp.bfloat16):
    level = level_of(key, dims, cuts, -0.22, 0.18) if cuts else 1.0
    values = jax.random.normal(key, dims, jnp.float32) * scale * level
    return jnp.minimum(jnp.maximum(values, -bound), bound).astype(held_as)


def setup_inputs(seed: int = 0) -> dict:
    seeds = jax.random.split(jax.random.key(seed), 10)
    features = gaussian(seeds[0], (NODES, D), 1.0, 6.0, ((0, 128),))
    out_grad = gaussian(seeds[1], (NODES, D), 1.0, 6.0, ((0, 128),))
    rel_weight = gaussian(seeds[2], (REL, D, D), D ** -0.5, 0.375)
    root_weight = gaussian(seeds[3], (D, D), D ** -0.5, 0.375)
    tiles = jnp.clip(0.25 * jax.random.uniform(seeds[4], (TILES, BLOCK, BLOCK), jnp.float32) ** level_of(seeds[4], (TILES, BLOCK, BLOCK), ((0, 128),), -0.2, 0.2), 0.0, 0.25).astype(jnp.bfloat16)
    tile_dest = set_ends(jax.random.randint(seeds[5], (TILES,), 0, NB_DEV), jax.random.fold_in(seeds[5], 1), 0, NB_DEV - 1).astype(jnp.int32)
    tile_peer_keys = jax.random.split(jax.random.fold_in(seeds[6], 1), TILES // TILES_DEV)
    tile_peer_turns = jax.random.permutation(jax.random.fold_in(seeds[6], 3), TILES // TILES_DEV)
    tile_peer = jax.vmap(lambda own, number: deal_out(jax.random.fold_in(seeds[6], 2), own, number, TILES_DEV, DEVICES, 1, CAP, 2))(tile_peer_keys, tile_peer_turns).reshape((TILES, 1))
    tile_source = set_ends(jax.random.randint(seeds[7], (TILES,), 0, NB_DEV), jax.random.fold_in(seeds[7], 1), 0, NB_DEV - 1).astype(jnp.int32)
    tile_rel = set_ends(jax.random.randint(seeds[8], (TILES,), 0, REL), jax.random.fold_in(seeds[8], 1), 0, REL - 1).astype(jnp.int32)
    return dict(features=features, out_grad=out_grad, rel_weight=rel_weight, root_weight=root_weight, tiles=tiles, tile_dest=tile_dest, tile_peer=tile_peer, tile_source=tile_source, tile_rel=tile_rel)


def reference(features, out_grad, rel_weight, root_weight, tiles, tile_dest, tile_peer, tile_source, tile_rel):
    feat_width = features.shape[1]
    grad_blocks = out_grad.reshape(-1, BLOCK, feat_width)
    feat_blocks = features.reshape(-1, BLOCK, feat_width)
    holder = jnp.arange(TILES, dtype=jnp.int32) // TILES_DEV
    dest_global = (holder * NB_DEV + tile_dest).astype(jnp.int32)
    source_global = (tile_peer[:, 0] * NB_DEV + tile_source).astype(jnp.int32)
    weights_wide = rel_weight.astype(jnp.float32)

    def accumulate(totals, group):
        grad_acc, weight_acc = totals
        start = (group * TILES_DEV).astype(jnp.int32)

        def take_rows(array):
            return lax.dynamic_slice_in_dim(array, start, TILES_DEV, 0)
        tile_group = take_rows(tiles).astype(jnp.float32)
        dest_idx = take_rows(dest_global)
        source_idx = take_rows(source_global)
        rel_idx = take_rows(tile_rel)
        dest_rows = grad_blocks[dest_idx].astype(jnp.float32)
        messages = jnp.einsum('tij,tic->tjc', tile_group, dest_rows, precision=lax.Precision.HIGHEST)
        messages = lax.optimization_barrier(messages.astype(jnp.bfloat16)).astype(jnp.float32)
        chosen_weights = weights_wide[rel_idx]
        partial_rows = jnp.einsum('tjc,tdc->tjd', messages, chosen_weights, precision=lax.Precision.HIGHEST)
        grad_acc = grad_acc.at[source_idx].add(partial_rows)
        source_rows = feat_blocks[source_idx].astype(jnp.float32)
        weight_terms = jnp.einsum('tjd,tjc->tdc', source_rows, messages, precision=lax.Precision.HIGHEST)
        weight_acc = weight_acc + jax.ops.segment_sum(weight_terms, rel_idx, num_segments=REL)
        return ((grad_acc, weight_acc), None)
    start_totals = (jnp.zeros(grad_blocks.shape, jnp.float32), jnp.zeros((REL, feat_width, feat_width), jnp.float32))
    groups = jnp.arange(TILES // TILES_DEV, dtype=jnp.int32)
    (grad_acc, weight_acc), _ = lax.scan(accumulate, start_totals, groups)
    root_part = jnp.einsum('nc,dc->nd', out_grad, root_weight, preferred_element_type=jnp.float32)
    grad_feat = (root_part + grad_acc.reshape(-1, feat_width)).astype(jnp.bfloat16)
    root_grad = jnp.einsum('nd,nc->dc', features, out_grad, preferred_element_type=jnp.float32)
    grad_scale = 1.0 / jnp.sqrt(jnp.float32(NODES))
    grad_weights = jnp.concatenate([root_grad[None], weight_acc], axis=0) * grad_scale
    return (grad_feat, grad_weights)
```

```python
import math

import jax
import jax.numpy as jnp
from jax import lax
from jax.experimental import pallas as pl
from jax.experimental.pallas import tpu as pltpu
from jax.sharding import Mesh
from jax.sharding import PartitionSpec as P

AXES = ("z", "y", "x", "c")
CHIPS = ("z", "y", "x")
VMEM = pl.BlockSpec(memory_space=pltpu.VMEM)
ANY = pl.BlockSpec(memory_space=pl.ANY)
SMEM = pl.BlockSpec(memory_space=pltpu.SMEM)
LIMIT = 40 * 1024 * 1024
GROUP = 4
DEPTH = 4


def message_kernel(cap, parts, dest_ref, peer_ref, tiles_ref, grad_ref, out_ref, held, made, count, in_sems, out_sem):
    tile_count = tiles_ref.shape[0]
    part = tile_count // parts

    def fetch(i):
        rows = pl.ds(i * part, part)
        return pltpu.make_async_copy(tiles_ref.at[rows], held.at[rows], in_sems.at[i])

    for i in range(parts):
        fetch(i).start()

    def clear(i, carry):
        count[i] = 0
        return carry

    lax.fori_loop(0, count.shape[0], clear, 0)

    def one(t):
        peer = peer_ref[t]
        rank = count[peer]
        count[peer] = rank + 1
        made[t] = lax.dot_general(
            held[t], grad_ref[dest_ref[t]], (((0,), (0,)), ((), ())), preferred_element_type=jnp.float32
        ).astype(jnp.bfloat16)
        pltpu.make_async_copy(made.at[t], out_ref.at[peer * cap + rank], out_sem).start()

    for i in range(parts):
        fetch(i).wait()

        def step(j, carry):
            for k in range(4):
                one(i * part + j * 4 + k)
            return carry

        lax.fori_loop(0, part // 4, step, 0)
    pltpu.make_async_copy(made, out_ref.at[pl.ds(0, tile_count)], out_sem).wait()


def make_messages(tile_dest, peer_list, tiles, grad_blocks, slots, cap):
    tile_count, block, _ = tiles.shape
    width = grad_blocks.shape[2]
    parts = 8

    def kernel(*refs):
        message_kernel(cap, parts, *refs)

    return pl.pallas_call(
        kernel,
        out_shape=jax.ShapeDtypeStruct((slots, block, width), jnp.bfloat16),
        in_specs=[SMEM, SMEM, ANY, VMEM],
        out_specs=ANY,
        scratch_shapes=[
            pltpu.VMEM(tiles.shape, jnp.bfloat16),
            pltpu.VMEM((tile_count, block, width), jnp.bfloat16),
            pltpu.SMEM((slots // cap,), jnp.int32),
            pltpu.SemaphoreType.DMA((parts,)),
            pltpu.SemaphoreType.DMA,
        ],
        compiler_params=pltpu.CompilerParams(vmem_limit_bytes=LIMIT),
        cost_estimate=pl.CostEstimate(
            flops=2 * tile_count * block * block * width,
            bytes_accessed=tile_count * block * (block + width) * 2,
            transcendentals=0,
        ),
    )(tile_dest, peer_list, tiles, grad_blocks)


def walk_groups(slots_ref, total, arrived_ref, held, sems, use):
    def fetch(g):
        for k in range(GROUP):
            pltpu.make_async_copy(
                arrived_ref.at[slots_ref[g * GROUP + k]], held.at[lax.rem(g, DEPTH), k], sems.at[lax.rem(g, DEPTH)]
            ).start()

    for g in range(DEPTH - 1):
        @pl.when(g < total)
        def _():
            fetch(g)

    def step(g, carry):
        @pl.when(g + DEPTH - 1 < total)
        def _():
            fetch(g + DEPTH - 1)

        now = lax.rem(g, DEPTH)
        pltpu.make_async_copy(arrived_ref.at[pl.ds(0, GROUP)], held.at[now], sems.at[now]).wait()
        block, width = held.shape[2:]
        use(g, held[now].reshape(GROUP * block, width))
        return carry

    lax.fori_loop(0, total, step, 0)


def weight_kernel(slots_ref, blocks_ref, rels_ref, total_ref, arrived_ref, turned_ref, out_ref, held, sems):
    out_ref[...] = jnp.zeros_like(out_ref)

    def use(g, rows):
        left = jnp.concatenate([turned_ref[blocks_ref[g * GROUP + k]] for k in range(GROUP)], axis=1)
        out_ref[rels_ref[g]] += jnp.dot(left, rows, preferred_element_type=jnp.float32)

    walk_groups(slots_ref, total_ref[0], arrived_ref, held, sems, use)


def feat_kernel(
    slots_ref, blocks_ref, rels_ref, total_ref, arrived_ref, base_ref, weight_ref, out_ref, held, acc, sems, base_sem
):
    blocks, block, _ = out_ref.shape
    base = pltpu.make_async_copy(base_ref, acc.at[pl.ds(0, blocks)], base_sem)
    base.start()
    acc[blocks] = jnp.zeros(acc.shape[1:], jnp.float32)
    base.wait()

    def use(g, rows):
        part = jnp.dot(rows, weight_ref[rels_ref[g]], preferred_element_type=jnp.float32)
        for k in range(GROUP):
            acc[blocks_ref[g * GROUP + k]] += part[k * block : (k + 1) * block]

    walk_groups(slots_ref, total_ref[0], arrived_ref, held, sems, use)

    def finish(b, carry):
        out_ref[b] = acc[b].astype(jnp.bfloat16)
        return carry

    lax.fori_loop(0, blocks, finish, 0)


def plan_groups(table, me, blocks, rel_count):
    senders, tile_count = table.shape
    kinds = rel_count * blocks
    mine = (table // kinds) == me
    key = lax.broadcasted_iota(jnp.int32, table.shape, 1) * kinds + table % kinds
    low = jnp.min(jnp.where(mine, key, tile_count * kinds), axis=1)
    high = jnp.max(jnp.where(mine, key, -1), axis=1)
    tags = jnp.stack(
        [jnp.where(high >= 0, low % kinds, -1), jnp.where(high > low, high % kinds, -1)], axis=1
    ).reshape(-1)
    slot_total = tags.shape[0]
    rel = jnp.where(tags >= 0, tags // blocks, rel_count)
    block_of = tags % blocks
    order = jnp.arange(slot_total, dtype=jnp.int32)
    ranks = jnp.sum(((rel[None, :] == rel[:, None]) & (order[None, :] < order[:, None])).astype(jnp.int32), axis=1)
    kinds_of = jnp.arange(rel_count, dtype=jnp.int32)
    counts = jnp.sum((rel[None, :] == kinds_of[:, None]).astype(jnp.int32), axis=1)
    padded = (counts + GROUP - 1) // GROUP * GROUP
    ends = jnp.sum(jnp.where(kinds_of[None, :] <= kinds_of[:, None], padded[None, :], 0), axis=1)
    starts = ends - padded
    start_of = jnp.sum(jnp.where(rel[:, None] == kinds_of[None, :], starts[None, :], 0), axis=1)
    places = slot_total + GROUP * rel_count
    places = places // GROUP * GROUP
    place = jnp.where(tags >= 0, start_of + ranks, places)
    hit = place[None, :] == jnp.arange(places, dtype=jnp.int32)[:, None]
    slot_at = jnp.sum(jnp.where(hit, order[None, :], 0), axis=1)
    block_at = jnp.sum(jnp.where(hit, block_of[None, :] - blocks, 0), axis=1) + blocks
    filled = jnp.any(hit, axis=1)
    by_group = slot_at.reshape(-1, GROUP)
    slot_at = jnp.where(filled.reshape(-1, GROUP), by_group, by_group[:, :1]).reshape(-1)
    group_start = jnp.arange(places // GROUP, dtype=jnp.int32) * GROUP
    rel_at = jnp.sum((group_start[:, None] >= ends[None, :]).astype(jnp.int32), axis=1)
    rel_at = jnp.minimum(rel_at, rel_count - 1)
    return slot_at, block_at, rel_at, ends[-1:] // GROUP


def all_sum(part):
    kinds, rows, width = part.shape
    chips = lax.axis_size(CHIPS)
    swap = [(0, 1), (1, 0)]
    core = lax.axis_index("c")
    halves = part.reshape(2, kinds * rows // 2, width)
    own = lax.dynamic_index_in_dim(halves, core, 0, keepdims=False)
    other = lax.dynamic_index_in_dim(halves, 1 - core, 0, keepdims=False)
    own = own + lax.ppermute(other, "c", swap)
    shape = (chips, own.size // chips // 128, 128)
    spread = lax.all_to_all(own.reshape(shape), CHIPS, 0, 0, tiled=True).sum(axis=0)
    own = lax.all_to_all(jnp.broadcast_to(spread[None], shape), CHIPS, 0, 0, tiled=True)
    own = own.reshape(kinds * rows // 2, width)
    other = lax.ppermute(own, "c", swap)
    first = jnp.where(core == 0, own, other)
    second = jnp.where(core == 0, other, own)
    return jnp.concatenate([first, second], axis=0).reshape(part.shape)


def shards(features, out_grad, rel_weight, root_weight, tiles, tile_dest, tile_peer, tile_source, tile_rel):
    dev_count = lax.axis_size(AXES)
    me = lax.axis_index(AXES)
    tile_count, block, _ = tiles.shape
    width = features.shape[1]
    rel_count = rel_weight.shape[0]
    blocks = features.shape[0] // block
    cap = 2
    slots = dev_count * cap
    scale = 1.0 / math.sqrt(features.shape[0] * dev_count)
    peer_list = tile_peer[:, 0]
    grad_blocks = out_grad.reshape(blocks, block, width)

    outgoing = make_messages(tile_dest, peer_list, tiles, grad_blocks, slots, cap)
    arrived = lax.all_to_all(
        outgoing.reshape(dev_count, cap, block, width), AXES, split_axis=0, concat_axis=0, tiled=True
    ).reshape(slots, block, width)

    codes = (peer_list * rel_count + tile_rel) * blocks + tile_source
    table = lax.all_gather(codes, AXES, axis=0)
    slot_at, block_at, rel_at, total = plan_groups(table, me, blocks, rel_count)

    turned = jnp.swapaxes(features.reshape(blocks, block, width), 1, 2)
    turned = jnp.concatenate([turned, jnp.zeros((1, width, block), jnp.bfloat16)], axis=0)
    root_grad = jnp.einsum("nd,nc->dc", features, out_grad, preferred_element_type=jnp.float32)
    base = jnp.einsum("nc,dc->nd", out_grad, root_weight, preferred_element_type=jnp.float32)
    turned_weight = jnp.swapaxes(rel_weight, 1, 2)

    ring = [pltpu.VMEM((DEPTH, GROUP, block, width), jnp.bfloat16)]
    sems = [pltpu.SemaphoreType.DMA((DEPTH,))]
    params = pltpu.CompilerParams(vmem_limit_bytes=LIMIT)
    cost = pl.CostEstimate(
        flops=slots * block * width * width, bytes_accessed=slots * block * width * 2, transcendentals=0
    )
    rel_grad = pl.pallas_call(
        weight_kernel,
        out_shape=jax.ShapeDtypeStruct((rel_count, width, width), jnp.float32),
        in_specs=[SMEM] * 4 + [ANY, VMEM],
        out_specs=VMEM,
        scratch_shapes=ring + sems,
        compiler_params=params,
        cost_estimate=cost,
    )(slot_at, block_at, rel_at, total, arrived, turned)
    grad_feat = pl.pallas_call(
        feat_kernel,
        out_shape=jax.ShapeDtypeStruct((blocks, block, width), jnp.bfloat16),
        in_specs=[SMEM] * 4 + [ANY, ANY, VMEM],
        out_specs=VMEM,
        scratch_shapes=ring
        + [pltpu.VMEM((blocks + 1, block, width), jnp.float32)]
        + sems
        + [pltpu.SemaphoreType.DMA],
        compiler_params=params,
        cost_estimate=cost,
    )(slot_at, block_at, rel_at, total, arrived, base.reshape(blocks, block, width), turned_weight)

    grad_weights = all_sum(jnp.concatenate([root_grad[None], rel_grad], axis=0) * scale)
    return grad_feat.reshape(features.shape), grad_weights


def solution(mesh):
    sizes = (4, 4, 4, 2)
    fine = Mesh(mesh.devices.reshape(sizes), AXES)
    return jax.shard_map(
        shards,
        mesh=fine,
        in_specs=(
            P(AXES, None),
            P(AXES, None),
            P(),
            P(),
            P(AXES, None, None),
            P(AXES),
            P(AXES, None),
            P(AXES),
            P(AXES),
        ),
        out_specs=(P(AXES, None), P()),
        check_vma=False,
    )
```

```python
import math

import jax
import jax.numpy as jnp
from jax import lax
from jax.experimental import pallas as pl
from jax.experimental.pallas import tpu as pltpu
from jax.sharding import Mesh
from jax.sharding import PartitionSpec as P

AXES = ("z", "y", "x", "c")
CHIPS = ("z", "y", "x")
VMEM = pl.BlockSpec(memory_space=pltpu.VMEM)
ANY = pl.BlockSpec(memory_space=pl.ANY)
SMEM = pl.BlockSpec(memory_space=pltpu.SMEM)
GROUP = 8
DEPTH = 4
MIB = 1024 * 1024


def message_kernel(
    cap, parts, dest_any, peer_any, tiles_ref, grad_any, out_ref, dest, peers, count, grad, held, made, sems, out_sem
):
    tile_count = tiles_ref.shape[0]
    part = tile_count // parts
    early = [
        pltpu.make_async_copy(src, dst, sems.at[parts + i])
        for i, (src, dst) in enumerate(((dest_any, dest), (peer_any, peers), (grad_any, grad)))
    ]
    for copy in early:
        copy.start()

    def fetch(i):
        rows = pl.ds(i * part, part)
        return pltpu.make_async_copy(tiles_ref.at[rows], held.at[rows], sems.at[i])

    for i in range(parts):
        fetch(i).start()

    def clear(i, carry):
        count[i] = 0
        return carry

    lax.fori_loop(0, count.shape[0], clear, 0)
    for copy in early:
        copy.wait()

    for i in range(parts):
        fetch(i).wait()

        def step(j, carry):
            for k in range(16):
                t = i * part + j * 16 + k
                peer = peers[t]
                rank = count[peer]
                count[peer] = rank + 1
                made[t] = lax.dot_general(
                    held[t], grad[dest[t]], (((0,), (0,)), ((), ())), preferred_element_type=jnp.float32
                ).astype(jnp.bfloat16)
                pltpu.make_async_copy(made.at[t], out_ref.at[peer * cap + rank], out_sem).start()
            return carry

        lax.fori_loop(0, part // 16, step, 0)
    pltpu.make_async_copy(made, out_ref.at[pl.ds(0, tile_count)], out_sem).wait()


def make_messages(tile_dest, peer_list, tiles, grad_blocks, slots, cap):
    tile_count, block, _ = tiles.shape
    width = grad_blocks.shape[2]
    parts = 8

    def kernel(*refs):
        message_kernel(cap, parts, *refs)

    return pl.pallas_call(
        kernel,
        out_shape=jax.ShapeDtypeStruct((slots, block, width), jnp.bfloat16),
        in_specs=[ANY] * 4,
        out_specs=ANY,
        scratch_shapes=[
            pltpu.SMEM((tile_count,), jnp.int32),
            pltpu.SMEM((tile_count,), jnp.int32),
            pltpu.SMEM((slots // cap,), jnp.int32),
            pltpu.VMEM(grad_blocks.shape, jnp.bfloat16),
            pltpu.VMEM(tiles.shape, jnp.bfloat16),
            pltpu.VMEM((tile_count, block, width), jnp.bfloat16),
            pltpu.SemaphoreType.DMA((parts + 3,)),
            pltpu.SemaphoreType.DMA,
        ],
        compiler_params=pltpu.CompilerParams(vmem_limit_bytes=58 * MIB),
        cost_estimate=pl.CostEstimate(
            flops=2 * tile_count * block * block * width,
            bytes_accessed=tile_count * block * (block + width) * 2,
            transcendentals=0,
        ),
    )(tile_dest, peer_list, tiles, grad_blocks)


def walk_groups(slots_ref, total, arrived_ref, held, sems, use):
    block, width = held.shape[2:]

    def fetch(g):
        now = lax.rem(g, DEPTH)
        for k in range(GROUP):
            pltpu.make_async_copy(arrived_ref.at[slots_ref[g * GROUP + k]], held.at[now, k], sems.at[now]).start()

    def settle(g):
        now = lax.rem(g, DEPTH)
        pltpu.make_async_copy(arrived_ref.at[pl.ds(0, GROUP)], held.at[now], sems.at[now]).wait()

    for g in range(DEPTH - 1):
        fetch(g)

    def step(g, carry):
        settle(g)
        fetch(g + DEPTH - 1)
        use(g, held[lax.rem(g, DEPTH)].reshape(GROUP * block, width))
        return carry

    lax.fori_loop(0, total, step, 0)
    for g in range(DEPTH - 1):
        settle(total + g)


def weight_kernel(slots_ref, blocks_ref, rels_ref, total_ref, arrived_ref, turned_ref, root_ref, own_ref, other_ref, held, acc, sems):
    rel_count, width, _ = acc.shape
    half = width // 2
    acc[...] = jnp.zeros_like(acc)

    def use(g, rows):
        left = jnp.concatenate([turned_ref[blocks_ref[g * GROUP + k]] for k in range(GROUP)], axis=1)
        acc[rels_ref[g]] += jnp.dot(left, rows, preferred_element_type=jnp.float32)

    walk_groups(slots_ref, total_ref[0], arrived_ref, held, sems, use)

    def split(first, second):
        for ref, lanes in ((first, pl.ds(0, half)), (second, pl.ds(half, half))):
            ref[pl.ds(0, width)] = root_ref[:, lanes]
            for r in range(rel_count):
                ref[pl.ds((1 + r) * width, width)] = acc[r, :, lanes]

    @pl.when(total_ref[1] == 0)
    def _():
        split(own_ref, other_ref)

    @pl.when(total_ref[1] != 0)
    def _():
        split(other_ref, own_ref)


def feat_kernel(slots_ref, blocks_ref, rels_ref, total_ref, arrived_ref, base_ref, weight_ref, out_ref, held, acc, sems):
    blocks, block, _ = out_ref.shape
    acc[pl.ds(0, blocks)] = base_ref[...]
    acc[blocks] = jnp.zeros(acc.shape[1:], jnp.float32)

    def use(g, rows):
        part = jnp.dot(rows, weight_ref[rels_ref[g]], preferred_element_type=jnp.float32)
        for k in range(GROUP):
            acc[blocks_ref[g * GROUP + k]] += part[k * block : (k + 1) * block]

    walk_groups(slots_ref, total_ref[0], arrived_ref, held, sems, use)
    out_ref[...] = acc[pl.ds(0, blocks)].astype(jnp.bfloat16)


def plan_groups(table, me, blocks, rel_count):
    senders, tile_count = table.shape
    kinds = rel_count * blocks
    mine = (table // kinds) == me
    key = lax.broadcasted_iota(jnp.int32, table.shape, 1) * kinds + table % kinds
    low = jnp.min(jnp.where(mine, key, tile_count * kinds), axis=1)
    high = jnp.max(jnp.where(mine, key, -1), axis=1)
    tags = jnp.stack(
        [jnp.where(high >= 0, low % kinds, -1), jnp.where(high > low, high % kinds, -1)], axis=1
    ).reshape(-1)
    slot_total = tags.shape[0]
    rel = jnp.where(tags >= 0, tags // blocks, rel_count)
    block_of = tags % blocks
    order = jnp.arange(slot_total, dtype=jnp.int32)
    ranks = jnp.sum(((rel[None, :] == rel[:, None]) & (order[None, :] < order[:, None])).astype(jnp.int32), axis=1)
    kinds_of = jnp.arange(rel_count, dtype=jnp.int32)
    counts = jnp.sum((rel[None, :] == kinds_of[:, None]).astype(jnp.int32), axis=1)
    padded = (counts + GROUP - 1) // GROUP * GROUP
    ends = jnp.sum(jnp.where(kinds_of[None, :] <= kinds_of[:, None], padded[None, :], 0), axis=1)
    starts = ends - padded
    start_of = jnp.sum(jnp.where(rel[:, None] == kinds_of[None, :], starts[None, :], 0), axis=1)
    places = (-(-slot_total // GROUP) + rel_count + DEPTH - 1) * GROUP
    place = jnp.where(tags >= 0, start_of + ranks, places)
    hit = place[None, :] == jnp.arange(places, dtype=jnp.int32)[:, None]
    slot_at = jnp.sum(jnp.where(hit, order[None, :], 0), axis=1)
    block_at = jnp.sum(jnp.where(hit, block_of[None, :] - blocks, 0), axis=1) + blocks
    filled = jnp.any(hit, axis=1)
    by_group = slot_at.reshape(-1, GROUP)
    slot_at = jnp.where(filled.reshape(-1, GROUP), by_group, by_group[:, :1]).reshape(-1)
    group_start = jnp.arange(places // GROUP, dtype=jnp.int32) * GROUP
    rel_at = jnp.sum((group_start[:, None] >= ends[None, :]).astype(jnp.int32), axis=1)
    rel_at = jnp.minimum(rel_at, rel_count - 1)
    return slot_at, block_at, rel_at, ends[-1:] // GROUP


def shards(features, out_grad, rel_weight, root_weight, tiles, tile_dest, tile_peer, tile_source, tile_rel):
    dev_count = lax.axis_size(AXES)
    chips = lax.axis_size(CHIPS)
    me = lax.axis_index(AXES)
    core = lax.axis_index("c")
    tile_count, block, _ = tiles.shape
    width = features.shape[1]
    rel_count = rel_weight.shape[0]
    blocks = features.shape[0] // block
    cap = 2
    slots = dev_count * cap
    scale = 1.0 / math.sqrt(features.shape[0] * dev_count)
    peer_list = tile_peer[:, 0]
    grad_blocks = out_grad.reshape(blocks, block, width)

    codes = ((peer_list * rel_count + tile_rel) * blocks + tile_source).astype(jnp.float32)
    rows = lax.broadcasted_iota(jnp.int32, (dev_count, tile_count), 0)
    table = lax.psum(jnp.where(rows == me, codes[None, :], 0.0), AXES).astype(jnp.int32)
    slot_at, block_at, rel_at, total = plan_groups(table, me, blocks, rel_count)
    total = jnp.concatenate([total, core[None].astype(jnp.int32)])

    outgoing = make_messages(tile_dest, peer_list, tiles, grad_blocks, slots, cap)
    arrived = lax.all_to_all(
        outgoing.reshape(dev_count, cap, block, width), AXES, split_axis=0, concat_axis=0, tiled=True
    ).reshape(slots, block, width)

    turned = jnp.swapaxes(features.reshape(blocks, block, width), 1, 2)
    turned = jnp.concatenate([turned, jnp.zeros((1, width, block), jnp.bfloat16)], axis=0)
    root_grad = jnp.einsum("nd,nc->dc", features, out_grad, preferred_element_type=jnp.float32)
    base = jnp.einsum("nc,dc->nd", out_grad, root_weight, preferred_element_type=jnp.float32)
    turned_weight = jnp.swapaxes(rel_weight, 1, 2)

    slot_at, block_at, rel_at, total, turned, root_grad, base, turned_weight = lax.optimization_barrier(
        (slot_at, block_at, rel_at, total, turned, root_grad, base, turned_weight)
    )
    ring = [pltpu.VMEM((DEPTH, GROUP, block, width), jnp.bfloat16)]
    sems = [pltpu.SemaphoreType.DMA((DEPTH,))]
    cost = pl.CostEstimate(
        flops=slots * block * width * width, bytes_accessed=slots * block * width * 2, transcendentals=0
    )
    half_rows = (1 + rel_count) * width
    half = jax.ShapeDtypeStruct((half_rows, width // 2), jnp.float32)
    own, other = pl.pallas_call(
        weight_kernel,
        out_shape=(half, half),
        in_specs=[SMEM] * 4 + [ANY, VMEM, VMEM],
        out_specs=(VMEM, VMEM),
        scratch_shapes=ring + [pltpu.VMEM((rel_count, width, width), jnp.float32)] + sems,
        compiler_params=pltpu.CompilerParams(vmem_limit_bytes=20 * MIB),
        cost_estimate=cost,
    )(slot_at, block_at, rel_at, total, arrived, turned, root_grad)
    swap = [(0, 1), (1, 0)]
    own = own + lax.ppermute(other, "c", swap)
    own, total = lax.optimization_barrier((own, total))
    grad_feat = pl.pallas_call(
        feat_kernel,
        out_shape=jax.ShapeDtypeStruct((blocks, block, width), jnp.bfloat16),
        in_specs=[SMEM] * 4 + [ANY, VMEM, VMEM],
        out_specs=VMEM,
        scratch_shapes=ring + [pltpu.VMEM((blocks + 1, block, width), jnp.float32)] + sems,
        compiler_params=pltpu.CompilerParams(vmem_limit_bytes=28 * MIB),
        cost_estimate=cost,
    )(slot_at, block_at, rel_at, total, arrived, base.reshape(blocks, block, width), turned_weight)

    shape = (chips, half_rows // chips, width // 2)
    spread = lax.all_to_all(own.reshape(shape), CHIPS, 0, 0, tiled=True)
    spread, grad_feat = lax.optimization_barrier((spread, grad_feat))
    share = (spread.sum(axis=0) * scale).astype(jnp.bfloat16)
    own = lax.all_to_all(jnp.broadcast_to(share[None], shape), CHIPS, 0, 0, tiled=True).reshape(half.shape)
    other = lax.ppermute(own, "c", swap)
    left = jnp.where(core == 0, own, other).astype(jnp.float32)
    right = jnp.where(core == 0, other, own).astype(jnp.float32)
    grad_weights = jnp.concatenate([left, right], axis=1).reshape(1 + rel_count, width, width)
    return grad_feat.reshape(features.shape), grad_weights


def solution(mesh):
    sizes = (4, 4, 4, 2)
    fine = Mesh(mesh.devices.reshape(sizes), AXES)
    return jax.shard_map(
        shards,
        mesh=fine,
        in_specs=(
            P(AXES, None),
            P(AXES, None),
            P(),
            P(),
            P(AXES, None, None),
            P(AXES),
            P(AXES, None),
            P(AXES),
            P(AXES),
        ),
        out_specs=(P(AXES, None), P()),
        check_vma=False,
    )
```

```python
import math

import jax
import jax.numpy as jnp
from jax import lax
from jax.experimental import pallas as pl
from jax.experimental.pallas import tpu as pltpu
from jax.sharding import Mesh
from jax.sharding import PartitionSpec as P

AXES = ("z", "y", "x", "c")
CHIPS = ("z", "y", "x")
VMEM = pl.BlockSpec(memory_space=pltpu.VMEM)
ANY = pl.BlockSpec(memory_space=pl.ANY)
SMEM = pl.BlockSpec(memory_space=pltpu.SMEM)
GROUP = 8
BATCHES = 2
MIB = 1024 * 1024


def message_kernel(
    cap, parts, dest_any, peer_any, tiles_ref, grad_any, out_ref, dest, peers, count, grad, held, made, sems, out_sem
):
    tile_count = tiles_ref.shape[0]
    part = tile_count // parts
    early = [
        pltpu.make_async_copy(src, dst, sems.at[parts + i])
        for i, (src, dst) in enumerate(((dest_any, dest), (peer_any, peers), (grad_any, grad)))
    ]
    for copy in early:
        copy.start()

    def fetch(i):
        rows = pl.ds(i * part, part)
        return pltpu.make_async_copy(tiles_ref.at[rows], held.at[rows], sems.at[i])

    for i in range(parts):
        fetch(i).start()

    def clear(i, carry):
        count[i] = 0
        return carry

    lax.fori_loop(0, count.shape[0], clear, 0)
    for copy in early:
        copy.wait()

    for i in range(parts):
        fetch(i).wait()

        def step(j, carry):
            for k in range(16):
                t = i * part + j * 16 + k
                peer = peers[t]
                rank = count[peer]
                count[peer] = rank + 1
                made[t] = lax.dot_general(
                    held[t], grad[dest[t]], (((0,), (0,)), ((), ())), preferred_element_type=jnp.float32
                ).astype(jnp.bfloat16)
                pltpu.make_async_copy(made.at[t], out_ref.at[peer * cap + rank], out_sem).start()
            return carry

        lax.fori_loop(0, part // 16, step, 0)
    pltpu.make_async_copy(made, out_ref.at[pl.ds(0, tile_count)], out_sem).wait()


def make_messages(tile_dest, peer_list, tiles, grad_blocks, slots, cap):
    tile_count, block, _ = tiles.shape
    width = grad_blocks.shape[2]
    parts = 8

    def kernel(*refs):
        message_kernel(cap, parts, *refs)

    return pl.pallas_call(
        kernel,
        out_shape=jax.ShapeDtypeStruct((slots, block, width), jnp.bfloat16),
        in_specs=[ANY] * 4,
        out_specs=ANY,
        scratch_shapes=[
            pltpu.SMEM((tile_count,), jnp.int32),
            pltpu.SMEM((tile_count,), jnp.int32),
            pltpu.SMEM((slots // cap,), jnp.int32),
            pltpu.VMEM(grad_blocks.shape, jnp.bfloat16),
            pltpu.VMEM(tiles.shape, jnp.bfloat16),
            pltpu.VMEM((tile_count, block, width), jnp.bfloat16),
            pltpu.SemaphoreType.DMA((parts + 3,)),
            pltpu.SemaphoreType.DMA,
        ],
        compiler_params=pltpu.CompilerParams(vmem_limit_bytes=58 * MIB),
        cost_estimate=pl.CostEstimate(
            flops=2 * tile_count * block * block * width,
            bytes_accessed=tile_count * block * (block + width) * 2,
            transcendentals=0,
        ),
    )(tile_dest, peer_list, tiles, grad_blocks)


def arrivals(arrived_ref, held, sems):
    part = held.shape[0] // BATCHES

    def copy(i):
        rows = pl.ds(i * part, part)
        return pltpu.make_async_copy(arrived_ref.at[rows], held.at[rows], sems.at[i])

    return copy


def walk_groups(totals_ref, copy, use):
    def single(g, carry):
        use(g)
        return carry

    def batch(i, first):
        copy(i).wait()
        end = totals_ref[i]
        middle = first + (end - first) // 2 * 2

        def two(j, carry):
            use(first + 2 * j)
            use(first + 2 * j + 1)
            return carry

        lax.fori_loop(0, (end - first) // 2, two, 0)
        lax.fori_loop(middle, end, single, 0)
        return end

    lax.fori_loop(0, BATCHES, batch, 0)


def weight_kernel(
    slots_ref, blocks_ref, rels_ref, totals_ref, arrived_ref, turned_any, root_ref, own_ref, other_ref,
    held, turned, acc, sems, turned_sem,
):
    rel_count, width, _ = acc.shape
    half = width // 2
    copy = arrivals(arrived_ref, held, sems)
    turning = pltpu.make_async_copy(turned_any, turned, turned_sem)
    turning.start()
    for i in range(BATCHES):
        copy(i).start()
    acc[...] = jnp.zeros_like(acc)
    turning.wait()

    def use(g):
        left = jnp.concatenate([turned[blocks_ref[g * GROUP + k]] for k in range(GROUP)], axis=1)
        right = jnp.concatenate([held[slots_ref[g * GROUP + k]] for k in range(GROUP)], axis=0)
        acc[rels_ref[g]] += jnp.dot(left, right, preferred_element_type=jnp.float32)

    walk_groups(totals_ref, copy, use)

    def split(first, second):
        for ref, lanes in ((first, pl.ds(0, half)), (second, pl.ds(half, half))):
            ref[pl.ds(0, width)] = root_ref[:, lanes]
            for r in range(rel_count):
                ref[pl.ds((1 + r) * width, width)] = acc[r, :, lanes]

    @pl.when(totals_ref[BATCHES] == 0)
    def _():
        split(own_ref, other_ref)

    @pl.when(totals_ref[BATCHES] != 0)
    def _():
        split(other_ref, own_ref)


def feat_kernel(
    slots_ref, blocks_ref, rels_ref, totals_ref, arrived_ref, base_any, weight_ref, out_ref, held, acc, sems, base_sem
):
    blocks, block, _ = out_ref.shape
    copy = arrivals(arrived_ref, held, sems)
    base = pltpu.make_async_copy(base_any, acc.at[pl.ds(0, blocks)], base_sem)
    base.start()
    for i in range(BATCHES):
        copy(i).start()
    acc[blocks] = jnp.zeros(acc.shape[1:], jnp.float32)
    base.wait()

    def use(g):
        rows = jnp.concatenate([held[slots_ref[g * GROUP + k]] for k in range(GROUP)], axis=0)
        part = jnp.dot(rows, weight_ref[rels_ref[g]], preferred_element_type=jnp.float32)
        for k in range(GROUP):
            acc[blocks_ref[g * GROUP + k]] += part[k * block : (k + 1) * block]

    walk_groups(totals_ref, copy, use)
    out_ref[...] = acc[pl.ds(0, blocks)].astype(jnp.bfloat16)


def plan_groups(table, me, blocks, rel_count):
    senders, tile_count = table.shape
    kinds = rel_count * blocks
    mine = (table // kinds) == me
    key = lax.broadcasted_iota(jnp.int32, table.shape, 1) * kinds + table % kinds
    low = jnp.min(jnp.where(mine, key, tile_count * kinds), axis=1)
    high = jnp.max(jnp.where(mine, key, -1), axis=1)
    tags = jnp.stack(
        [jnp.where(high >= 0, low % kinds, -1), jnp.where(high > low, high % kinds, -1)], axis=1
    ).reshape(-1)
    slot_total = tags.shape[0]
    order = jnp.arange(slot_total, dtype=jnp.int32)
    rel_kinds = rel_count * BATCHES
    batch = order // (slot_total // BATCHES)
    rel = jnp.where(tags >= 0, batch * rel_count + tags // blocks, rel_kinds)
    block_of = tags % blocks
    ranks = jnp.sum(((rel[None, :] == rel[:, None]) & (order[None, :] < order[:, None])).astype(jnp.int32), axis=1)
    kinds_of = jnp.arange(rel_kinds, dtype=jnp.int32)
    counts = jnp.sum((rel[None, :] == kinds_of[:, None]).astype(jnp.int32), axis=1)
    padded = (counts + GROUP - 1) // GROUP * GROUP
    ends = jnp.sum(jnp.where(kinds_of[None, :] <= kinds_of[:, None], padded[None, :], 0), axis=1)
    starts = ends - padded
    start_of = jnp.sum(jnp.where(rel[:, None] == kinds_of[None, :], starts[None, :], 0), axis=1)
    places = (-(-slot_total // GROUP) + rel_kinds) * GROUP
    place = jnp.where(tags >= 0, start_of + ranks, places)
    hit = place[None, :] == jnp.arange(places, dtype=jnp.int32)[:, None]
    slot_at = jnp.sum(jnp.where(hit, order[None, :], 0), axis=1)
    block_at = jnp.sum(jnp.where(hit, block_of[None, :] - blocks, 0), axis=1) + blocks
    filled = jnp.any(hit, axis=1)
    by_group = slot_at.reshape(-1, GROUP)
    slot_at = jnp.where(filled.reshape(-1, GROUP), by_group, by_group[:, :1]).reshape(-1)
    group_start = jnp.arange(places // GROUP, dtype=jnp.int32) * GROUP
    rel_at = jnp.sum((group_start[:, None] >= ends[None, :]).astype(jnp.int32), axis=1)
    return slot_at, block_at, rel_at % rel_count, ends[rel_count - 1 :: rel_count] // GROUP


def shards(features, out_grad, rel_weight, root_weight, tiles, tile_dest, tile_peer, tile_source, tile_rel):
    dev_count = lax.axis_size(AXES)
    chips = lax.axis_size(CHIPS)
    me = lax.axis_index(AXES)
    core = lax.axis_index("c")
    tile_count, block, _ = tiles.shape
    width = features.shape[1]
    rel_count = rel_weight.shape[0]
    blocks = features.shape[0] // block
    cap = 2
    slots = dev_count * cap
    scale = 1.0 / math.sqrt(features.shape[0] * dev_count)
    peer_list = tile_peer[:, 0]
    grad_blocks = out_grad.reshape(blocks, block, width)

    codes = (peer_list * rel_count + tile_rel) * blocks + tile_source
    table = lax.all_to_all(
        jnp.broadcast_to(codes[None, None], (dev_count, 1, tile_count)), AXES, split_axis=0, concat_axis=0, tiled=True
    ).reshape(dev_count, tile_count)
    slot_at, block_at, rel_at, total = plan_groups(table, me, blocks, rel_count)
    total = jnp.concatenate([total, core[None].astype(jnp.int32)])

    outgoing = make_messages(tile_dest, peer_list, tiles, grad_blocks, slots, cap)
    arrived = lax.all_to_all(
        outgoing.reshape(dev_count, cap, block, width), AXES, split_axis=0, concat_axis=0, tiled=True
    ).reshape(slots, block, width)

    turned = jnp.swapaxes(features.reshape(blocks, block, width), 1, 2)
    turned = jnp.concatenate([turned, jnp.zeros((1, width, block), jnp.bfloat16)], axis=0)
    root_grad = jnp.einsum("nd,nc->dc", features, out_grad, preferred_element_type=jnp.float32)
    base = jnp.einsum("nc,dc->nd", out_grad, root_weight, preferred_element_type=jnp.float32)
    turned_weight = jnp.swapaxes(rel_weight, 1, 2)

    slot_at, block_at, rel_at, total, turned, root_grad, base, turned_weight = lax.optimization_barrier(
        (slot_at, block_at, rel_at, total, turned, root_grad, base, turned_weight)
    )
    room = pltpu.VMEM((slots, block, width), jnp.bfloat16)
    sems = [pltpu.SemaphoreType.DMA((BATCHES,)), pltpu.SemaphoreType.DMA]
    cost = pl.CostEstimate(
        flops=slots * block * width * width, bytes_accessed=slots * block * width * 2, transcendentals=0
    )
    half_rows = (1 + rel_count) * width
    half = jax.ShapeDtypeStruct((half_rows, width // 2), jnp.float32)
    own, other = pl.pallas_call(
        weight_kernel,
        out_shape=(half, half),
        in_specs=[SMEM] * 4 + [ANY, ANY, VMEM],
        out_specs=(VMEM, VMEM),
        scratch_shapes=[room, pltpu.VMEM(turned.shape, jnp.bfloat16), pltpu.VMEM((rel_count, width, width), jnp.float32)]
        + sems,
        compiler_params=pltpu.CompilerParams(vmem_limit_bytes=36 * MIB),
        cost_estimate=cost,
    )(slot_at, block_at, rel_at, total, arrived, turned, root_grad)
    swap = [(0, 1), (1, 0)]
    own = own + lax.ppermute(other, "c", swap)
    own, total = lax.optimization_barrier((own, total))
    grad_feat = pl.pallas_call(
        feat_kernel,
        out_shape=jax.ShapeDtypeStruct((blocks, block, width), jnp.bfloat16),
        in_specs=[SMEM] * 4 + [ANY, ANY, VMEM],
        out_specs=VMEM,
        scratch_shapes=[room, pltpu.VMEM((blocks + 1, block, width), jnp.float32)] + sems,
        compiler_params=pltpu.CompilerParams(vmem_limit_bytes=40 * MIB),
        cost_estimate=cost,
    )(slot_at, block_at, rel_at, total, arrived, base.reshape(blocks, block, width), turned_weight)

    shape = (chips, half_rows // chips, width // 2)
    spread = lax.all_to_all(own.reshape(shape), CHIPS, 0, 0, tiled=True)
    spread, grad_feat = lax.optimization_barrier((spread, grad_feat))
    share = (spread.sum(axis=0) * scale).astype(jnp.bfloat16)
    own = lax.all_to_all(jnp.broadcast_to(share[None], shape), CHIPS, 0, 0, tiled=True).reshape(half.shape)
    other = lax.ppermute(own, "c", swap)
    left = jnp.where(core == 0, own, other).astype(jnp.float32)
    right = jnp.where(core == 0, other, own).astype(jnp.float32)
    grad_weights = jnp.concatenate([left, right], axis=1).reshape(1 + rel_count, width, width)
    return grad_feat.reshape(features.shape), grad_weights


def solution(mesh):
    sizes = (4, 4, 4, 2)
    fine = Mesh(mesh.devices.reshape(sizes), AXES)
    return jax.shard_map(
        shards,
        mesh=fine,
        in_specs=(
            P(AXES, None),
            P(AXES, None),
            P(),
            P(),
            P(AXES, None, None),
            P(AXES),
            P(AXES, None),
            P(AXES),
            P(AXES),
        ),
        out_specs=(P(AXES, None), P()),
        check_vma=False,
    )
```

```python
import math

import jax
import jax.numpy as jnp
from jax import lax
from jax.experimental import pallas as pl
from jax.experimental.pallas import tpu as pltpu
from jax.sharding import Mesh
from jax.sharding import PartitionSpec as P

AXES = ("z", "y", "x", "c")
CHIPS = ("z", "y", "x")
VMEM = pl.BlockSpec(memory_space=pltpu.VMEM)
ANY = pl.BlockSpec(memory_space=pl.ANY)
SMEM = pl.BlockSpec(memory_space=pltpu.SMEM)
GROUP = 8
BATCHES = 2
MIB = 1024 * 1024


def message_kernel(
    cap, parts, dest_any, peer_any, tiles_ref, grad_any, out_ref, dest, peers, count, grad, held, made, sems, out_sem
):
    tile_count = tiles_ref.shape[0]
    part = tile_count // parts
    early = [
        pltpu.make_async_copy(src, dst, sems.at[parts + i])
        for i, (src, dst) in enumerate(((dest_any, dest), (peer_any, peers), (grad_any, grad)))
    ]
    for copy in early:
        copy.start()

    def fetch(i):
        rows = pl.ds(i * part, part)
        return pltpu.make_async_copy(tiles_ref.at[rows], held.at[rows], sems.at[i])

    for i in range(parts):
        fetch(i).start()

    def clear(i, carry):
        count[i] = 0
        return carry

    lax.fori_loop(0, count.shape[0], clear, 0)
    for copy in early:
        copy.wait()

    for i in range(parts):
        fetch(i).wait()

        def step(j, carry):
            for k in range(16):
                t = i * part + j * 16 + k
                peer = peers[t]
                rank = count[peer]
                count[peer] = rank + 1
                made[t] = lax.dot_general(
                    held[t], grad[dest[t]], (((0,), (0,)), ((), ())), preferred_element_type=jnp.float32
                ).astype(jnp.bfloat16)
                pltpu.make_async_copy(made.at[t], out_ref.at[peer * cap + rank], out_sem).start()
            return carry

        lax.fori_loop(0, part // 16, step, 0)
    pltpu.make_async_copy(made, out_ref.at[pl.ds(0, tile_count)], out_sem).wait()


def make_messages(tile_dest, peer_list, tiles, grad_blocks, slots, cap):
    tile_count, block, _ = tiles.shape
    width = grad_blocks.shape[2]
    parts = 8

    def kernel(*refs):
        message_kernel(cap, parts, *refs)

    return pl.pallas_call(
        kernel,
        out_shape=jax.ShapeDtypeStruct((slots, block, width), jnp.bfloat16),
        in_specs=[ANY] * 4,
        out_specs=ANY,
        scratch_shapes=[
            pltpu.SMEM((tile_count,), jnp.int32),
            pltpu.SMEM((tile_count,), jnp.int32),
            pltpu.SMEM((slots // cap,), jnp.int32),
            pltpu.VMEM(grad_blocks.shape, jnp.bfloat16),
            pltpu.VMEM(tiles.shape, jnp.bfloat16),
            pltpu.VMEM((tile_count, block, width), jnp.bfloat16),
            pltpu.SemaphoreType.DMA((parts + 3,)),
            pltpu.SemaphoreType.DMA,
        ],
        compiler_params=pltpu.CompilerParams(vmem_limit_bytes=58 * MIB),
        cost_estimate=pl.CostEstimate(
            flops=2 * tile_count * block * block * width,
            bytes_accessed=tile_count * block * (block + width) * 2,
            transcendentals=0,
        ),
    )(tile_dest, peer_list, tiles, grad_blocks)


def arrivals(arrived_ref, held, sems):
    part = held.shape[0] // BATCHES

    def copy(i):
        rows = pl.ds(i * part, part)
        return pltpu.make_async_copy(arrived_ref.at[rows], held.at[rows], sems.at[i])

    return copy


def walk_groups(totals_ref, copy, use):
    def single(g, carry):
        use(g)
        return carry

    def batch(i, first):
        copy(i).wait()
        end = totals_ref[i]
        middle = first + (end - first) // 2 * 2

        def two(j, carry):
            use(first + 2 * j)
            use(first + 2 * j + 1)
            return carry

        lax.fori_loop(0, (end - first) // 2, two, 0)
        lax.fori_loop(middle, end, single, 0)
        return end

    lax.fori_loop(0, BATCHES, batch, 0)


def weight_kernel(
    slots_ref, blocks_ref, rels_ref, totals_ref, arrived_ref, feat_any, grad_any, own_ref, other_ref,
    held, feat, grad, turned, acc, sems, feat_sem, grad_sem,
):
    kinds, width, _ = acc.shape
    blocks, block, _ = feat.shape
    half = width // 2
    copy = arrivals(arrived_ref, held, sems)
    feat_copy = pltpu.make_async_copy(feat_any, feat, feat_sem)
    grad_copy = pltpu.make_async_copy(grad_any, grad, grad_sem)
    feat_copy.start()
    grad_copy.start()
    for i in range(BATCHES):
        copy(i).start()
    acc[...] = jnp.zeros_like(acc)
    turned[blocks] = jnp.zeros(turned.shape[1:], turned.dtype)
    feat_copy.wait()

    def turn(b, carry):
        for k in range(4):
            turned[b * 4 + k] = feat[b * 4 + k].T
        return carry

    lax.fori_loop(0, blocks // 4, turn, 0)
    grad_copy.wait()

    def root(g, carry):
        left = jnp.concatenate([turned[g * GROUP + k] for k in range(GROUP)], axis=1)
        right = grad[pl.ds(g * GROUP, GROUP)].reshape(GROUP * block, width)
        acc[0] += jnp.dot(left, right, preferred_element_type=jnp.float32)
        return carry

    lax.fori_loop(0, blocks // GROUP, root, 0)

    def use(g):
        left = jnp.concatenate([turned[blocks_ref[g * GROUP + k]] for k in range(GROUP)], axis=1)
        right = jnp.concatenate([held[slots_ref[g * GROUP + k]] for k in range(GROUP)], axis=0)
        acc[1 + rels_ref[g]] += jnp.dot(left, right, preferred_element_type=jnp.float32)

    walk_groups(totals_ref, copy, use)

    def split(first, second):
        for ref, lanes in ((first, pl.ds(0, half)), (second, pl.ds(half, half))):
            for r in range(kinds):
                ref[pl.ds(r * width, width)] = acc[r, :, lanes]

    @pl.when(totals_ref[BATCHES] == 0)
    def _():
        split(own_ref, other_ref)

    @pl.when(totals_ref[BATCHES] != 0)
    def _():
        split(other_ref, own_ref)


def feat_kernel(
    slots_ref, blocks_ref, rels_ref, totals_ref, arrived_ref, grad_any, root_ref, weight_ref, out_ref,
    held, grad, acc, sems, grad_sem,
):
    blocks, block, width = out_ref.shape
    copy = arrivals(arrived_ref, held, sems)
    grad_copy = pltpu.make_async_copy(grad_any, grad, grad_sem)
    grad_copy.start()
    for i in range(BATCHES):
        copy(i).start()
    acc[blocks] = jnp.zeros(acc.shape[1:], jnp.float32)
    across = (((1,), (1,)), ((), ()))
    grad_copy.wait()

    def base(g, carry):
        rows = grad[pl.ds(g * GROUP, GROUP)].reshape(GROUP * block, width)
        part = lax.dot_general(rows, root_ref[...], across, preferred_element_type=jnp.float32)
        acc[pl.ds(g * GROUP, GROUP)] = part.reshape(GROUP, block, width)
        return carry

    lax.fori_loop(0, blocks // GROUP, base, 0)

    def use(g):
        rows = jnp.concatenate([held[slots_ref[g * GROUP + k]] for k in range(GROUP)], axis=0)
        part = lax.dot_general(rows, weight_ref[rels_ref[g]], across, preferred_element_type=jnp.float32)
        for k in range(GROUP):
            acc[blocks_ref[g * GROUP + k]] += part[k * block : (k + 1) * block]

    walk_groups(totals_ref, copy, use)
    out_ref[...] = acc[pl.ds(0, blocks)].astype(jnp.bfloat16)


def plan_groups(table, me, blocks, rel_count):
    senders, tile_count = table.shape
    kinds = 1 << (rel_count * blocks - 1).bit_length()
    mine = (table >> (kinds.bit_length() - 1)) == me
    key = lax.broadcasted_iota(jnp.int32, table.shape, 1) * kinds + (table & (kinds - 1))
    low = jnp.min(jnp.where(mine, key, tile_count * kinds), axis=1)
    high = jnp.max(jnp.where(mine, key, -1), axis=1)
    tags = jnp.stack(
        [jnp.where(high >= 0, low & (kinds - 1), -1), jnp.where(high > low, high & (kinds - 1), -1)], axis=1
    ).reshape(-1)
    slot_total = tags.shape[0]
    order = jnp.arange(slot_total, dtype=jnp.int32)
    rel_kinds = rel_count * BATCHES
    batch = order // (slot_total // BATCHES)
    rel = jnp.where(tags >= 0, batch * rel_count + tags // blocks, rel_kinds)
    block_of = tags % blocks
    ranks = jnp.sum(((rel[None, :] == rel[:, None]) & (order[None, :] < order[:, None])).astype(jnp.int32), axis=1)
    kinds_of = jnp.arange(rel_kinds, dtype=jnp.int32)
    counts = jnp.sum((rel[None, :] == kinds_of[:, None]).astype(jnp.int32), axis=1)
    padded = (counts + GROUP - 1) // GROUP * GROUP
    ends = jnp.sum(jnp.where(kinds_of[None, :] <= kinds_of[:, None], padded[None, :], 0), axis=1)
    starts = ends - padded
    start_of = jnp.sum(jnp.where(rel[:, None] == kinds_of[None, :], starts[None, :], 0), axis=1)
    places = (-(-slot_total // GROUP) + rel_kinds) * GROUP
    place = jnp.where(tags >= 0, start_of + ranks, places)
    hit = place[None, :] == jnp.arange(places, dtype=jnp.int32)[:, None]
    slot_at = jnp.sum(jnp.where(hit, order[None, :], 0), axis=1)
    block_at = jnp.sum(jnp.where(hit, block_of[None, :] - blocks, 0), axis=1) + blocks
    filled = jnp.any(hit, axis=1)
    by_group = slot_at.reshape(-1, GROUP)
    slot_at = jnp.where(filled.reshape(-1, GROUP), by_group, by_group[:, :1]).reshape(-1)
    group_start = jnp.arange(places // GROUP, dtype=jnp.int32) * GROUP
    rel_at = jnp.sum((group_start[:, None] >= ends[None, :]).astype(jnp.int32), axis=1)
    return slot_at, block_at, rel_at % rel_count, ends[rel_count - 1 :: rel_count] // GROUP


def shards(features, out_grad, rel_weight, root_weight, tiles, tile_dest, tile_peer, tile_source, tile_rel):
    dev_count = lax.axis_size(AXES)
    chips = lax.axis_size(CHIPS)
    me = lax.axis_index(AXES)
    core = lax.axis_index("c")
    tile_count, block, _ = tiles.shape
    width = features.shape[1]
    rel_count = rel_weight.shape[0]
    blocks = features.shape[0] // block
    cap = 2
    slots = dev_count * cap
    scale = 1.0 / math.sqrt(features.shape[0] * dev_count)
    peer_list = tile_peer[:, 0]
    grad_blocks = out_grad.reshape(blocks, block, width)

    kinds = 1 << (rel_count * blocks - 1).bit_length()
    codes = peer_list * kinds + tile_rel * blocks + tile_source
    table = lax.all_to_all(
        jnp.broadcast_to(codes[None, None], (dev_count, 1, tile_count)), AXES, split_axis=0, concat_axis=0, tiled=True
    ).reshape(dev_count, tile_count)
    slot_at, block_at, rel_at, total = plan_groups(table, me, blocks, rel_count)
    total = jnp.concatenate([total, core[None].astype(jnp.int32)])

    outgoing = make_messages(tile_dest, peer_list, tiles, grad_blocks, slots, cap)
    outgoing, slot_at, block_at, rel_at, total = lax.optimization_barrier((outgoing, slot_at, block_at, rel_at, total))
    arrived = lax.all_to_all(
        outgoing.reshape(dev_count, cap, block, width), AXES, split_axis=0, concat_axis=0, tiled=True
    ).reshape(slots, block, width)

    room = pltpu.VMEM((slots, block, width), jnp.bfloat16)
    local = pltpu.VMEM(grad_blocks.shape, jnp.bfloat16)
    dma = pltpu.SemaphoreType.DMA
    cost = pl.CostEstimate(
        flops=slots * block * width * width, bytes_accessed=slots * block * width * 2, transcendentals=0
    )
    half_rows = (1 + rel_count) * width
    half = jax.ShapeDtypeStruct((half_rows, width // 2), jnp.float32)
    own, other = pl.pallas_call(
        weight_kernel,
        out_shape=(half, half),
        in_specs=[SMEM] * 4 + [ANY] * 3,
        out_specs=(VMEM, VMEM),
        scratch_shapes=[
            room,
            local,
            local,
            pltpu.VMEM((blocks + 1, width, block), jnp.bfloat16),
            pltpu.VMEM((1 + rel_count, width, width), jnp.float32),
            dma((BATCHES,)),
            dma,
            dma,
        ],
        compiler_params=pltpu.CompilerParams(vmem_limit_bytes=56 * MIB),
        cost_estimate=cost,
    )(slot_at, block_at, rel_at, total, arrived, features.reshape(blocks, block, width), grad_blocks)

    swap = [(0, 1), (1, 0)]
    own = own + lax.ppermute(other, "c", swap)
    own, total = lax.optimization_barrier((own, total))
    grad_feat = pl.pallas_call(
        feat_kernel,
        out_shape=jax.ShapeDtypeStruct((blocks, block, width), jnp.bfloat16),
        in_specs=[SMEM] * 4 + [ANY, ANY, VMEM, VMEM],
        out_specs=VMEM,
        scratch_shapes=[
            room,
            local,
            pltpu.VMEM((blocks + 1, block, width), jnp.float32),
            dma((BATCHES,)),
            dma,
        ],
        compiler_params=pltpu.CompilerParams(vmem_limit_bytes=40 * MIB),
        cost_estimate=cost,
    )(slot_at, block_at, rel_at, total, arrived, grad_blocks, root_weight, rel_weight)

    shape = (chips, half_rows // chips, width // 2)
    spread = lax.all_to_all(own.reshape(shape), CHIPS, 0, 0, tiled=True)
    spread, grad_feat = lax.optimization_barrier((spread, grad_feat))
    share = (spread.sum(axis=0) * scale).astype(jnp.bfloat16)
    own = lax.all_to_all(jnp.broadcast_to(share[None], shape), CHIPS, 0, 0, tiled=True).reshape(half.shape)
    other = lax.ppermute(own, "c", swap)
    left = jnp.where(core == 0, own, other).astype(jnp.float32)
    right = jnp.where(core == 0, other, own).astype(jnp.float32)
    grad_weights = jnp.concatenate([left, right], axis=1).reshape(1 + rel_count, width, width)
    return grad_feat.reshape(features.shape), grad_weights


def solution(mesh):
    sizes = (4, 4, 4, 2)
    fine = Mesh(mesh.devices.reshape(sizes), AXES)
    return jax.shard_map(
        shards,
        mesh=fine,
        in_specs=(
            P(AXES, None),
            P(AXES, None),
            P(),
            P(),
            P(AXES, None, None),
            P(AXES),
            P(AXES, None),
            P(AXES),
            P(AXES),
        ),
        out_specs=(P(AXES, None), P()),
        check_vma=False,
    )
```

```python
import math

import jax
import jax.numpy as jnp
from jax import lax
from jax.experimental import pallas as pl
from jax.experimental.pallas import tpu as pltpu
from jax.sharding import Mesh
from jax.sharding import PartitionSpec as P

AXES = ("z", "y", "x", "c")
CHIPS = ("z", "y", "x")
VMEM = pl.BlockSpec(memory_space=pltpu.VMEM)
ANY = pl.BlockSpec(memory_space=pl.ANY)
SMEM = pl.BlockSpec(memory_space=pltpu.SMEM)
MIB = 1024 * 1024
CAP = 2
GROUP = 8
BATCHES = 2
LANES = 128
TAG_ROWS = 16


def message_kernel(
    blocks, parts, dest_any, peer_any, rel_any, source_any, tiles_ref, grad_any, out_ref,
    dest, peers, rels, sources, count, grad, held, made, marks, tags, sems, out_sem,
):
    tile_count, block, _ = tiles_ref.shape
    part = tile_count // parts
    size = 2 * block
    pairs = ((dest_any, dest), (peer_any, peers), (rel_any, rels), (source_any, sources), (grad_any, grad))
    early = [pltpu.make_async_copy(src, dst, sems.at[parts + i]) for i, (src, dst) in enumerate(pairs)]
    for copy in early:
        copy.start()

    def fetch(i):
        rows = pl.ds(i * part, part)
        return pltpu.make_async_copy(tiles_ref.at[rows], held.at[rows], sems.at[i])

    for i in range(parts):
        fetch(i).start()

    def clear(i, carry):
        count[i] = 0
        return carry

    lax.fori_loop(0, count.shape[0], clear, 0)
    marks[...] = jnp.full(marks.shape, -1.0, jnp.float32)
    side = lax.broadcasted_iota(jnp.int32, marks.shape[1:], 1) // (LANES // CAP)
    for copy in early:
        copy.wait()

    for i in range(parts):
        fetch(i).wait()

        def step(j, carry):
            for k in range(16):
                t = i * part + j * 16 + k
                peer = peers[t]
                rank = count[peer]
                count[peer] = rank + 1
                mark = (rels[t] * blocks + sources[t]).astype(jnp.float32)
                marks[peer] = jnp.where(side == rank, mark, marks[peer])
                message = lax.dot_general(
                    held[t], grad[dest[t]], (((0,), (0,)), ((), ())), preferred_element_type=jnp.float32
                ).astype(jnp.bfloat16)
                made[t, pl.ds(0, block)] = message[:, :LANES]
                made[t, pl.ds(block, block)] = message[:, LANES:]
                rows = pl.ds(pl.multiple_of(rank * size, size), size)
                pltpu.make_async_copy(made.at[t], out_ref.at[peer, rows], out_sem).start()
            return carry

        lax.fori_loop(0, part // 16, step, 0)

    tags[...] = jnp.concatenate([marks[...], marks[...]], axis=1).astype(jnp.bfloat16)
    tag_copy = pltpu.make_async_copy(tags, out_ref.at[:, pl.ds(CAP * size, TAG_ROWS)], sems.at[0])
    tag_copy.start()
    pltpu.make_async_copy(made, out_ref.at[pl.ds(0, tile_count), pl.ds(0, size)], out_sem).wait()
    tag_copy.wait()


def make_messages(tile_dest, peer_list, tile_rel, tile_source, tiles, grad_blocks, dev_count):
    tile_count, block, _ = tiles.shape
    blocks, _, width = grad_blocks.shape
    parts = 8
    numbers = pltpu.SMEM((tile_count,), jnp.int32)

    def kernel(*refs):
        message_kernel(blocks, parts, *refs)

    return pl.pallas_call(
        kernel,
        out_shape=jax.ShapeDtypeStruct((dev_count, CAP * 2 * block + TAG_ROWS, LANES), jnp.bfloat16),
        in_specs=[ANY] * 6,
        out_specs=ANY,
        scratch_shapes=[
            numbers,
            numbers,
            numbers,
            numbers,
            pltpu.SMEM((dev_count,), jnp.int32),
            pltpu.VMEM(grad_blocks.shape, jnp.bfloat16),
            pltpu.VMEM(tiles.shape, jnp.bfloat16),
            pltpu.VMEM((tile_count, 2 * block, LANES), jnp.bfloat16),
            pltpu.VMEM((dev_count, TAG_ROWS // 2, LANES), jnp.float32),
            pltpu.VMEM((dev_count, TAG_ROWS, LANES), jnp.bfloat16),
            pltpu.SemaphoreType.DMA((parts + 5,)),
            pltpu.SemaphoreType.DMA,
        ],
        compiler_params=pltpu.CompilerParams(vmem_limit_bytes=58 * MIB),
        cost_estimate=pl.CostEstimate(
            flops=2 * tile_count * block * block * width,
            bytes_accessed=tile_count * block * (block + width) * 2,
            transcendentals=0,
        ),
    )(tile_dest, peer_list, tile_rel, tile_source, tiles, grad_blocks)


def make_plan(marks, blocks, rel_count):
    senders = marks.shape[0]
    places = plan_places(senders * CAP, rel_count)
    square = (senders, senders)
    row, lane = lax.broadcasted_iota(jnp.int32, square, 0), lax.broadcasted_iota(jnp.int32, square, 1)
    below = (lane < row).astype(jnp.float32)
    ahead = (row < lane).astype(jnp.float32)
    sender = lax.broadcasted_iota(jnp.int32, (senders, 1), 0).astype(jnp.float32)
    batch = jnp.floor(sender * (BATCHES / senders))
    kind_lane = lane.astype(jnp.float32)
    tag = [marks[:, 0:1], marks[:, LANES // CAP : LANES // CAP + 1]]
    rel = [jnp.floor(t * (1.0 / blocks)) for t in tag]
    block_of = [t - r * blocks for t, r in zip(tag, rel)]
    used = [jnp.where((kind_lane == batch * rel_count + r) & (t >= 0), 1.0, 0.0) for t, r in zip(tag, rel)]
    totals = [jnp.sum(u, axis=0, keepdims=True) for u in used]
    before = [jnp.dot(below, u, preferred_element_type=jnp.float32) for u in used]
    before[1] = before[1] + totals[0]
    groups = jnp.floor((totals[0] + totals[1] + (GROUP - 1)) * (1.0 / GROUP))
    first = jnp.dot(jnp.broadcast_to(groups, (8, senders)), ahead, preferred_element_type=jnp.float32)[0:1]
    place = [jnp.sum(u * (b + first * GROUP), axis=1, keepdims=True) for u, b in zip(used, before)]
    place = [jnp.where(t >= 0, p, -1.0) for t, p in zip(tag, place)]
    at_int = lax.broadcasted_iota(jnp.int32, (senders, places), 1)
    at, at_group = at_int.astype(jnp.float32), (at_int // GROUP * GROUP).astype(jnp.float32)
    here = [jnp.where(p == at, 1.0, 0.0) for p in place]
    leads = [jnp.where(p == at_group, 1.0, 0.0) for p in place]

    def gather(hits, values):
        return jnp.sum(hits[0] * values[0] + hits[1] * values[1], axis=0, keepdims=True)

    name = [sender * CAP, sender * CAP + 1]
    message = jnp.where(gather(here, [1.0, 1.0]) > 0, gather(here, name), gather(leads, name))
    source = gather(here, [b - blocks for b in block_of]) + blocks
    relation = gather(leads, rel)
    kind_row = kind_lane[0:1]
    ends = [
        jnp.sum(jnp.where(kind_row < rel_count * (i + 1), groups, 0.0), axis=1, keepdims=True) for i in range(BATCHES)
    ]
    rows = [message, source, relation] + [jnp.broadcast_to(e, (1, places)) for e in ends]
    rows.append(jnp.zeros((8 - len(rows), places), jnp.float32))
    return jnp.concatenate(rows, axis=0).astype(jnp.int32)


def plan_places(slots, rel_count):
    return -(-(-(-slots // GROUP) + rel_count * BATCHES) * GROUP // LANES) * LANES


def arrivals(arrived_ref, held, sems):
    part = held.shape[0] // BATCHES

    def copy(i):
        rows = pl.ds(i * part, part)
        return pltpu.make_async_copy(arrived_ref.at[rows, pl.ds(0, held.shape[1])], held.at[rows], sems.at[i])

    return copy


def take(held, message, block):
    top = pl.multiple_of((message % CAP) * (2 * block), 2 * block)
    sender = message // CAP
    return jnp.concatenate([held[sender, pl.ds(top, block)], held[sender, pl.ds(top + block, block)]], axis=1)


def walk_groups(plan_ref, copy, use):
    def single(g, carry):
        use(g)
        return carry

    def batch(i, first):
        copy(i).wait()
        end = plan_ref[3 + i, 0]
        middle = first + (end - first) // 2 * 2

        def two(j, carry):
            use(first + 2 * j)
            use(first + 2 * j + 1)
            return carry

        lax.fori_loop(0, (end - first) // 2, two, 0)
        lax.fori_loop(middle, end, single, 0)
        return end

    lax.fori_loop(0, BATCHES, batch, 0)


def weight_kernel(
    arrived_ref, feat_any, grad_any, core_ref, own_ref, other_ref, plan_ref,
    held, feat, grad, turned, acc, tags, plan, sems, feat_sem, grad_sem, tag_sem,
):
    kinds, width, _ = acc.shape
    blocks, block, _ = feat.shape
    half = width // 2
    tag_copy = pltpu.make_async_copy(arrived_ref.at[:, pl.ds(held.shape[1], TAG_ROWS)], tags, tag_sem)
    feat_copy = pltpu.make_async_copy(feat_any, feat, feat_sem)
    grad_copy = pltpu.make_async_copy(grad_any, grad, grad_sem)
    tag_copy.start()
    feat_copy.start()
    grad_copy.start()
    copy = arrivals(arrived_ref, held, sems)
    for i in range(BATCHES):
        copy(i).start()
    acc[...] = jnp.zeros_like(acc)
    turned[blocks] = jnp.zeros(turned.shape[1:], turned.dtype)
    tag_copy.wait()
    plan_ref[...] = make_plan(jnp.max(tags[...].astype(jnp.float32), axis=1), blocks, kinds - 1)
    plan_copy = pltpu.make_async_copy(plan_ref, plan, tag_sem)
    plan_copy.start()
    feat_copy.wait()

    def turn(b, carry):
        for k in range(4):
            turned[b * 4 + k] = feat[b * 4 + k].T
        return carry

    lax.fori_loop(0, blocks // 4, turn, 0)
    grad_copy.wait()

    def root(g, carry):
        left = jnp.concatenate([turned[g * GROUP + k] for k in range(GROUP)], axis=1)
        right = grad[pl.ds(g * GROUP, GROUP)].reshape(GROUP * block, width)
        acc[0] += jnp.dot(left, right, preferred_element_type=jnp.float32)
        return carry

    lax.fori_loop(0, blocks // GROUP, root, 0)
    plan_copy.wait()

    def use(g):
        left = jnp.concatenate([turned[plan[1, g * GROUP + k]] for k in range(GROUP)], axis=1)
        right = jnp.concatenate([take(held, plan[0, g * GROUP + k], block) for k in range(GROUP)], axis=0)
        acc[1 + plan[2, g * GROUP]] += jnp.dot(left, right, preferred_element_type=jnp.float32)

    walk_groups(plan, copy, use)

    def split(first, second):
        for ref, lanes in ((first, pl.ds(0, half)), (second, pl.ds(half, half))):
            for r in range(kinds):
                ref[pl.ds(r * width, width)] = acc[r, :, lanes]

    @pl.when(core_ref[0] == 0)
    def _():
        split(own_ref, other_ref)

    @pl.when(core_ref[0] != 0)
    def _():
        split(other_ref, own_ref)


def feat_kernel(plan_ref, arrived_ref, grad_any, root_ref, weight_ref, out_ref, held, grad, acc, sems, grad_sem):
    blocks, block, width = out_ref.shape
    copy = arrivals(arrived_ref, held, sems)
    grad_copy = pltpu.make_async_copy(grad_any, grad, grad_sem)
    grad_copy.start()
    for i in range(BATCHES):
        copy(i).start()
    acc[blocks] = jnp.zeros(acc.shape[1:], jnp.float32)
    across = (((1,), (1,)), ((), ()))
    grad_copy.wait()

    def base(g, carry):
        rows = grad[pl.ds(g * GROUP, GROUP)].reshape(GROUP * block, width)
        part = lax.dot_general(rows, root_ref[...], across, preferred_element_type=jnp.float32)
        acc[pl.ds(g * GROUP, GROUP)] = part.reshape(GROUP, block, width)
        return carry

    lax.fori_loop(0, blocks // GROUP, base, 0)

    def use(g):
        rows = jnp.concatenate([take(held, plan_ref[0, g * GROUP + k], block) for k in range(GROUP)], axis=0)
        part = lax.dot_general(rows, weight_ref[plan_ref[2, g * GROUP]], across, preferred_element_type=jnp.float32)
        for k in range(GROUP):
            acc[plan_ref[1, g * GROUP + k]] += part[k * block : (k + 1) * block]

    walk_groups(plan_ref, copy, use)
    out_ref[...] = acc[pl.ds(0, blocks)].astype(jnp.bfloat16)


def shards(features, out_grad, rel_weight, root_weight, tiles, tile_dest, tile_peer, tile_source, tile_rel):
    dev_count = lax.axis_size(AXES)
    chips = lax.axis_size(CHIPS)
    core = lax.axis_index("c")
    block = tiles.shape[1]
    width = features.shape[1]
    rel_count = rel_weight.shape[0]
    blocks = features.shape[0] // block
    slots = dev_count * CAP
    scale = 1.0 / math.sqrt(features.shape[0] * dev_count)
    grad_blocks = out_grad.reshape(blocks, block, width)

    outgoing = make_messages(tile_dest, tile_peer[:, 0], tile_rel, tile_source, tiles, grad_blocks, dev_count)
    arrived = lax.all_to_all(outgoing, AXES, split_axis=0, concat_axis=0, tiled=True)

    room = pltpu.VMEM((dev_count, CAP * 2 * block, LANES), jnp.bfloat16)
    local = pltpu.VMEM(grad_blocks.shape, jnp.bfloat16)
    dma = pltpu.SemaphoreType.DMA
    cost = pl.CostEstimate(
        flops=slots * block * width * width, bytes_accessed=slots * block * width * 2, transcendentals=0
    )
    half_rows = (1 + rel_count) * width
    half = jax.ShapeDtypeStruct((half_rows, width // 2), jnp.float32)
    plan_type = jax.ShapeDtypeStruct((8, plan_places(slots, rel_count)), jnp.int32)
    own, other, plan = pl.pallas_call(
        weight_kernel,
        out_shape=(half, half, plan_type),
        in_specs=[ANY] * 3 + [SMEM],
        out_specs=(VMEM, VMEM, VMEM),
        scratch_shapes=[
            room,
            local,
            local,
            pltpu.VMEM((blocks + 1, width, block), jnp.bfloat16),
            pltpu.VMEM((1 + rel_count, width, width), jnp.float32),
            pltpu.VMEM((dev_count, TAG_ROWS, LANES), jnp.bfloat16),
            pltpu.SMEM(plan_type.shape, jnp.int32),
            dma((BATCHES,)),
            dma,
            dma,
            dma,
        ],
        compiler_params=pltpu.CompilerParams(vmem_limit_bytes=36 * MIB),
        cost_estimate=cost,
    )(arrived, features.reshape(blocks, block, width), grad_blocks, core[None].astype(jnp.int32))

    swap = [(0, 1), (1, 0)]
    own = own + lax.ppermute(other, "c", swap)
    own, plan = lax.optimization_barrier((own, plan))
    grad_feat = pl.pallas_call(
        feat_kernel,
        out_shape=jax.ShapeDtypeStruct((blocks, block, width), jnp.bfloat16),
        in_specs=[SMEM, ANY, ANY, VMEM, VMEM],
        out_specs=VMEM,
        scratch_shapes=[
            room,
            local,
            pltpu.VMEM((blocks + 1, block, width), jnp.float32),
            dma((BATCHES,)),
            dma,
        ],
        compiler_params=pltpu.CompilerParams(vmem_limit_bytes=32 * MIB),
        cost_estimate=cost,
    )(plan, arrived, grad_blocks, root_weight, rel_weight)

    shape = (chips, half_rows // chips, width // 2)
    spread = lax.all_to_all(own.reshape(shape), CHIPS, 0, 0, tiled=True)
    spread, grad_feat = lax.optimization_barrier((spread, grad_feat))
    share = (spread.sum(axis=0) * scale).astype(jnp.bfloat16)
    own = lax.all_to_all(jnp.broadcast_to(share[None], shape), CHIPS, 0, 0, tiled=True).reshape(half.shape)
    other = lax.ppermute(own, "c", swap)
    left = jnp.where(core == 0, own, other).astype(jnp.float32)
    right = jnp.where(core == 0, other, own).astype(jnp.float32)
    grad_weights = jnp.concatenate([left, right], axis=1).reshape(1 + rel_count, width, width)
    return grad_feat.reshape(features.shape), grad_weights


def solution(mesh):
    sizes = (4, 4, 4, 2)
    fine = Mesh(mesh.devices.reshape(sizes), AXES)
    return jax.shard_map(
        shards,
        mesh=fine,
        in_specs=(
            P(AXES, None),
            P(AXES, None),
            P(),
            P(),
            P(AXES, None, None),
            P(AXES),
            P(AXES, None),
            P(AXES),
            P(AXES),
        ),
        out_specs=(P(AXES, None), P()),
        check_vma=False,
    )
```

```python
import math

import jax
import jax.numpy as jnp
from jax import lax
from jax.experimental import pallas as pl
from jax.experimental.pallas import tpu as pltpu
from jax.sharding import Mesh
from jax.sharding import PartitionSpec as P

AXES = ("z", "y", "x", "c")
CHIPS = ("z", "y", "x")
VMEM = pl.BlockSpec(memory_space=pltpu.VMEM)
ANY = pl.BlockSpec(memory_space=pl.ANY)
SMEM = pl.BlockSpec(memory_space=pltpu.SMEM)
MIB = 1024 * 1024
CAP = 2
GROUP = 8
BATCHES = 2
LANES = 128
TAG_ROWS = 16


def message_kernel(
    blocks, parts, dest_any, peer_any, rel_any, source_any, tiles_ref, grad_any, out_ref,
    dest, peers, rels, sources, count, grad, held, made, marks, tags, sems, out_sem,
):
    tile_count, block, _ = tiles_ref.shape
    part = tile_count // parts
    size = 2 * block
    pairs = ((dest_any, dest), (peer_any, peers), (rel_any, rels), (source_any, sources), (grad_any, grad))
    early = [pltpu.make_async_copy(src, dst, sems.at[parts + i]) for i, (src, dst) in enumerate(pairs)]
    for copy in early:
        copy.start()

    def fetch(i):
        rows = pl.ds(i * part, part)
        return pltpu.make_async_copy(tiles_ref.at[rows], held.at[rows], sems.at[i])

    for i in range(parts):
        fetch(i).start()

    def clear(i, carry):
        count[i] = 0
        return carry

    lax.fori_loop(0, count.shape[0], clear, 0)
    marks[...] = jnp.full(marks.shape, -1.0, jnp.float32)
    side = lax.broadcasted_iota(jnp.int32, marks.shape[1:], 1) // (LANES // CAP)
    for copy in early:
        copy.wait()

    for i in range(parts):
        fetch(i).wait()

        def step(j, carry):
            for k in range(16):
                t = i * part + j * 16 + k
                peer = peers[t]
                rank = count[peer]
                count[peer] = rank + 1
                mark = (rels[t] * blocks + sources[t]).astype(jnp.float32)
                marks[peer] = jnp.where(side == rank, mark, marks[peer])
                message = lax.dot_general(
                    held[t], grad[dest[t]], (((0,), (0,)), ((), ())), preferred_element_type=jnp.float32
                ).astype(jnp.bfloat16)
                made[t, pl.ds(0, block)] = message[:, :LANES]
                made[t, pl.ds(block, block)] = message[:, LANES:]
                rows = pl.ds(pl.multiple_of(rank * size, size), size)
                pltpu.make_async_copy(made.at[t], out_ref.at[peer, rows], out_sem).start()
            return carry

        lax.fori_loop(0, part // 16, step, 0)

    tags[...] = jnp.concatenate([marks[...], marks[...]], axis=1).astype(jnp.bfloat16)
    tag_copy = pltpu.make_async_copy(tags, out_ref.at[:, pl.ds(CAP * size, TAG_ROWS)], sems.at[0])
    tag_copy.start()
    pltpu.make_async_copy(made, out_ref.at[pl.ds(0, tile_count), pl.ds(0, size)], out_sem).wait()
    tag_copy.wait()


def make_messages(tile_dest, peer_list, tile_rel, tile_source, tiles, grad_blocks, dev_count):
    tile_count, block, _ = tiles.shape
    blocks, _, width = grad_blocks.shape
    parts = 8
    numbers = pltpu.SMEM((tile_count,), jnp.int32)

    def kernel(*refs):
        message_kernel(blocks, parts, *refs)

    return pl.pallas_call(
        kernel,
        out_shape=jax.ShapeDtypeStruct((dev_count, CAP * 2 * block + TAG_ROWS, LANES), jnp.bfloat16),
        in_specs=[ANY] * 6,
        out_specs=ANY,
        scratch_shapes=[
            numbers,
            numbers,
            numbers,
            numbers,
            pltpu.SMEM((dev_count,), jnp.int32),
            pltpu.VMEM(grad_blocks.shape, jnp.bfloat16),
            pltpu.VMEM(tiles.shape, jnp.bfloat16),
            pltpu.VMEM((tile_count, 2 * block, LANES), jnp.bfloat16),
            pltpu.VMEM((dev_count, TAG_ROWS // 2, LANES), jnp.float32),
            pltpu.VMEM((dev_count, TAG_ROWS, LANES), jnp.bfloat16),
            pltpu.SemaphoreType.DMA((parts + 5,)),
            pltpu.SemaphoreType.DMA,
        ],
        compiler_params=pltpu.CompilerParams(vmem_limit_bytes=58 * MIB),
        cost_estimate=pl.CostEstimate(
            flops=2 * tile_count * block * block * width,
            bytes_accessed=tile_count * block * (block + width) * 2,
            transcendentals=0,
        ),
    )(tile_dest, peer_list, tile_rel, tile_source, tiles, grad_blocks)


def make_plan(marks, blocks, rel_count):
    senders = marks.shape[0]
    places = plan_places(senders * CAP, rel_count)
    square = (senders, senders)
    row, lane = lax.broadcasted_iota(jnp.int32, square, 0), lax.broadcasted_iota(jnp.int32, square, 1)
    below = (lane < row).astype(jnp.float32)
    ahead = (row < lane).astype(jnp.float32)
    sender = lax.broadcasted_iota(jnp.int32, (senders, 1), 0).astype(jnp.float32)
    batch = jnp.floor(sender * (BATCHES / senders))
    kind_lane = lane.astype(jnp.float32)
    tag = [marks[:, 0:1], marks[:, LANES // CAP : LANES // CAP + 1]]
    rel = [jnp.floor(t * (1.0 / blocks)) for t in tag]
    block_of = [t - r * blocks for t, r in zip(tag, rel)]
    used = [jnp.where((kind_lane == batch * rel_count + r) & (t >= 0), 1.0, 0.0) for t, r in zip(tag, rel)]
    totals = [jnp.sum(u, axis=0, keepdims=True) for u in used]
    before = [jnp.dot(below, u, preferred_element_type=jnp.float32) for u in used]
    before[1] = before[1] + totals[0]
    groups = jnp.floor((totals[0] + totals[1] + (GROUP - 1)) * (1.0 / GROUP))
    first = jnp.dot(jnp.broadcast_to(groups, (8, senders)), ahead, preferred_element_type=jnp.float32)[0:1]
    place = [jnp.sum(u * (b + first * GROUP), axis=1, keepdims=True) for u, b in zip(used, before)]
    place = [jnp.where(t >= 0, p, -1.0) for t, p in zip(tag, place)]
    at_int = lax.broadcasted_iota(jnp.int32, (senders, places), 1)
    at, at_group = at_int.astype(jnp.float32), (at_int // GROUP * GROUP).astype(jnp.float32)
    here = [jnp.where(p == at, 1.0, 0.0) for p in place]
    leads = [jnp.where(p == at_group, 1.0, 0.0) for p in place]

    def gather(hits, values):
        return jnp.sum(hits[0] * values[0] + hits[1] * values[1], axis=0, keepdims=True)

    name = [sender * CAP, sender * CAP + 1]
    message = jnp.where(gather(here, [1.0, 1.0]) > 0, gather(here, name), gather(leads, name))
    source = gather(here, [b - blocks for b in block_of]) + blocks
    relation = gather(leads, rel)
    kind_row = kind_lane[0:1]
    ends = [
        jnp.sum(jnp.where(kind_row < rel_count * (i + 1), groups, 0.0), axis=1, keepdims=True) for i in range(BATCHES)
    ]
    rows = [message, source, relation] + [jnp.broadcast_to(e, (1, places)) for e in ends]
    rows.append(jnp.zeros((8 - len(rows), places), jnp.float32))
    return jnp.concatenate(rows, axis=0).astype(jnp.int32)


def plan_places(slots, rel_count):
    return -(-(-(-slots // GROUP) + rel_count * BATCHES) * GROUP // LANES) * LANES


def arrivals(arrived_ref, held, sems):
    part = held.shape[0] // BATCHES

    def copy(i):
        rows = pl.ds(i * part, part)
        return pltpu.make_async_copy(arrived_ref.at[rows, pl.ds(0, held.shape[1])], held.at[rows], sems.at[i])

    return copy


def take(held, message, block):
    top = pl.multiple_of((message % CAP) * (2 * block), 2 * block)
    sender = message // CAP
    return jnp.concatenate([held[sender, pl.ds(top, block)], held[sender, pl.ds(top + block, block)]], axis=1)


def walk_groups(plan_ref, copy, use):
    def single(g, carry):
        use(g)
        return carry

    def batch(i, first):
        copy(i).wait()
        end = plan_ref[3 + i, 0]
        middle = first + (end - first) // 2 * 2

        def two(j, carry):
            use(first + 2 * j)
            use(first + 2 * j + 1)
            return carry

        lax.fori_loop(0, (end - first) // 2, two, 0)
        lax.fori_loop(middle, end, single, 0)
        return end

    lax.fori_loop(0, BATCHES, batch, 0)


def weight_kernel(
    arrived_ref, feat_any, grad_any, core_ref, own_ref, other_ref, plan_ref,
    held, feat, grad, turned, acc, tags, plan, sems, feat_sem, grad_sem, tag_sem,
):
    kinds, width, _ = acc.shape
    blocks, block, _ = feat.shape
    half = width // 2
    tag_copy = pltpu.make_async_copy(arrived_ref.at[:, pl.ds(held.shape[1], TAG_ROWS)], tags, tag_sem)
    feat_copy = pltpu.make_async_copy(feat_any, feat, feat_sem)
    grad_copy = pltpu.make_async_copy(grad_any, grad, grad_sem)
    tag_copy.start()
    feat_copy.start()
    grad_copy.start()
    copy = arrivals(arrived_ref, held, sems)
    for i in range(BATCHES):
        copy(i).start()
    acc[...] = jnp.zeros_like(acc)
    turned[blocks] = jnp.zeros(turned.shape[1:], turned.dtype)
    tag_copy.wait()
    plan_ref[...] = make_plan(jnp.max(tags[...].astype(jnp.float32), axis=1), blocks, kinds - 1)
    plan_copy = pltpu.make_async_copy(plan_ref, plan, tag_sem)
    plan_copy.start()
    feat_copy.wait()

    def turn(b, carry):
        for k in range(4):
            turned[b * 4 + k] = feat[b * 4 + k].T
        return carry

    lax.fori_loop(0, blocks // 4, turn, 0)
    grad_copy.wait()

    def root(g, carry):
        left = jnp.concatenate([turned[g * GROUP + k] for k in range(GROUP)], axis=1)
        right = grad[pl.ds(g * GROUP, GROUP)].reshape(GROUP * block, width)
        acc[0] += jnp.dot(left, right, preferred_element_type=jnp.float32)
        return carry

    lax.fori_loop(0, blocks // GROUP, root, 0)
    plan_copy.wait()

    def use(g):
        left = jnp.concatenate([turned[plan[1, g * GROUP + k]] for k in range(GROUP)], axis=1)
        right = jnp.concatenate([take(held, plan[0, g * GROUP + k], block) for k in range(GROUP)], axis=0)
        acc[1 + plan[2, g * GROUP]] += jnp.dot(left, right, preferred_element_type=jnp.float32)

    walk_groups(plan, copy, use)

    def split(first, second):
        for ref, lanes in ((first, pl.ds(0, half)), (second, pl.ds(half, half))):
            for r in range(kinds):
                ref[pl.ds(r * width, width)] = acc[r, :, lanes]

    @pl.when(core_ref[0] == 0)
    def _():
        split(own_ref, other_ref)

    @pl.when(core_ref[0] != 0)
    def _():
        split(other_ref, own_ref)


def feat_kernel(plan_ref, arrived_ref, grad_any, root_ref, weight_ref, out_ref, held, grad, acc, sems, grad_sem):
    blocks, block, width = out_ref.shape
    copy = arrivals(arrived_ref, held, sems)
    grad_copy = pltpu.make_async_copy(grad_any, grad, grad_sem)
    grad_copy.start()
    for i in range(BATCHES):
        copy(i).start()
    acc[blocks] = jnp.zeros(acc.shape[1:], jnp.float32)
    across = (((1,), (1,)), ((), ()))
    grad_copy.wait()

    def base(g, carry):
        rows = grad[pl.ds(g * GROUP, GROUP)].reshape(GROUP * block, width)
        part = lax.dot_general(rows, root_ref[...], across, preferred_element_type=jnp.float32)
        acc[pl.ds(g * GROUP, GROUP)] = part.reshape(GROUP, block, width)
        return carry

    lax.fori_loop(0, blocks // GROUP, base, 0)

    def use(g):
        rows = jnp.concatenate([take(held, plan_ref[0, g * GROUP + k], block) for k in range(GROUP)], axis=0)
        part = lax.dot_general(rows, weight_ref[plan_ref[2, g * GROUP]], across, preferred_element_type=jnp.float32)
        for k in range(GROUP):
            acc[plan_ref[1, g * GROUP + k]] += part[k * block : (k + 1) * block]

    walk_groups(plan_ref, copy, use)
    out_ref[...] = acc[pl.ds(0, blocks)].astype(jnp.bfloat16)


def shards(features, out_grad, rel_weight, root_weight, tiles, tile_dest, tile_peer, tile_source, tile_rel):
    dev_count = lax.axis_size(AXES)
    chips = lax.axis_size(CHIPS)
    core = lax.axis_index("c")
    block = tiles.shape[1]
    width = features.shape[1]
    rel_count = rel_weight.shape[0]
    blocks = features.shape[0] // block
    slots = dev_count * CAP
    scale = 1.0 / math.sqrt(features.shape[0] * dev_count)
    grad_blocks = out_grad.reshape(blocks, block, width)

    outgoing = make_messages(tile_dest, tile_peer[:, 0], tile_rel, tile_source, tiles, grad_blocks, dev_count)
    outgoing, core = lax.optimization_barrier((outgoing, core[None].astype(jnp.int32)))
    arrived = lax.all_to_all(outgoing, AXES, split_axis=0, concat_axis=0, tiled=True)

    room = pltpu.VMEM((dev_count, CAP * 2 * block, LANES), jnp.bfloat16)
    local = pltpu.VMEM(grad_blocks.shape, jnp.bfloat16)
    dma = pltpu.SemaphoreType.DMA
    cost = pl.CostEstimate(
        flops=slots * block * width * width, bytes_accessed=slots * block * width * 2, transcendentals=0
    )
    half_rows = (1 + rel_count) * width
    half = jax.ShapeDtypeStruct((half_rows, width // 2), jnp.float32)
    plan_type = jax.ShapeDtypeStruct((8, plan_places(slots, rel_count)), jnp.int32)
    own, other, plan = pl.pallas_call(
        weight_kernel,
        out_shape=(half, half, plan_type),
        in_specs=[ANY] * 3 + [SMEM],
        out_specs=(VMEM, VMEM, VMEM),
        scratch_shapes=[
            room,
            local,
            local,
            pltpu.VMEM((blocks + 1, width, block), jnp.bfloat16),
            pltpu.VMEM((1 + rel_count, width, width), jnp.float32),
            pltpu.VMEM((dev_count, TAG_ROWS, LANES), jnp.bfloat16),
            pltpu.SMEM(plan_type.shape, jnp.int32),
            dma((BATCHES,)),
            dma,
            dma,
            dma,
        ],
        compiler_params=pltpu.CompilerParams(vmem_limit_bytes=57 * MIB),
        cost_estimate=cost,
    )(arrived, features.reshape(blocks, block, width), grad_blocks, core)

    swap = [(0, 1), (1, 0)]
    own = own + lax.ppermute(other, "c", swap)
    own, plan = lax.optimization_barrier((own, plan))
    grad_feat = pl.pallas_call(
        feat_kernel,
        out_shape=jax.ShapeDtypeStruct((blocks, block, width), jnp.bfloat16),
        in_specs=[SMEM, ANY, ANY, VMEM, VMEM],
        out_specs=VMEM,
        scratch_shapes=[
            room,
            local,
            pltpu.VMEM((blocks + 1, block, width), jnp.float32),
            dma((BATCHES,)),
            dma,
        ],
        compiler_params=pltpu.CompilerParams(vmem_limit_bytes=57 * MIB),
        cost_estimate=cost,
    )(plan, arrived, grad_blocks, root_weight, rel_weight)

    shape = (chips, half_rows // chips, width // 2)
    spread = lax.all_to_all(own.reshape(shape), CHIPS, 0, 0, tiled=True)
    spread, grad_feat = lax.optimization_barrier((spread, grad_feat))
    share = (spread.sum(axis=0) * scale).astype(jnp.bfloat16)
    own = lax.all_to_all(jnp.broadcast_to(share[None], shape), CHIPS, 0, 0, tiled=True).reshape(half.shape)
    other = lax.ppermute(own, "c", swap)
    core = core[0]
    left = jnp.where(core == 0, own, other).astype(jnp.float32)
    right = jnp.where(core == 0, other, own).astype(jnp.float32)
    grad_weights = jnp.concatenate([left, right], axis=1).reshape(1 + rel_count, width, width)
    return grad_feat.reshape(features.shape), grad_weights


def solution(mesh):
    sizes = (4, 4, 4, 2)
    fine = Mesh(mesh.devices.reshape(sizes), AXES)
    return jax.shard_map(
        shards,
        mesh=fine,
        in_specs=(
            P(AXES, None),
            P(AXES, None),
            P(),
            P(),
            P(AXES, None, None),
            P(AXES),
            P(AXES, None),
            P(AXES),
            P(AXES),
        ),
        out_specs=(P(AXES, None), P()),
        check_vma=False,
    )
```

```python
import math

import jax
import jax.numpy as jnp
from jax import lax
from jax.experimental import pallas as pl
from jax.experimental.pallas import tpu as pltpu
from jax.sharding import Mesh
from jax.sharding import PartitionSpec as P

AXES = ("z", "y", "x", "c")
CHIPS = ("z", "y", "x")
VMEM = pl.BlockSpec(memory_space=pltpu.VMEM)
HBM = pl.BlockSpec(memory_space=pltpu.HBM)
SMEM = pl.BlockSpec(memory_space=pltpu.SMEM)
MIB = 1024 * 1024
CAP = 2
GROUP = 8
BATCHES = 2
LANES = 128
TAG_ROWS = 16


def message_kernel(
    blocks, parts, dest_any, peer_any, rel_any, source_any, tiles_ref, grad_any, out_ref,
    dest, peers, rels, sources, count, grad, held, made, marks, tags, sems, out_sem,
):
    tile_count, block, _ = tiles_ref.shape
    part = tile_count // parts
    size = 2 * block
    pairs = ((dest_any, dest), (peer_any, peers), (rel_any, rels), (source_any, sources), (grad_any, grad))
    early = [pltpu.make_async_copy(src, dst, sems.at[parts + i]) for i, (src, dst) in enumerate(pairs)]
    for copy in early:
        copy.start()

    def fetch(i):
        rows = pl.ds(i * part, part)
        return pltpu.make_async_copy(tiles_ref.at[rows], held.at[rows], sems.at[i])

    for i in range(parts):
        fetch(i).start()

    def clear(i, carry):
        count[i] = 0
        return carry

    lax.fori_loop(0, count.shape[0], clear, 0)
    marks[...] = jnp.full(marks.shape, -1.0, jnp.float32)
    side = lax.broadcasted_iota(jnp.int32, marks.shape[1:], 1) // (LANES // CAP)
    for copy in early:
        copy.wait()

    for i in range(parts):
        fetch(i).wait()

        def step(j, carry):
            for k in range(16):
                t = i * part + j * 16 + k
                peer = peers[t]
                rank = count[peer]
                count[peer] = rank + 1
                mark = (rels[t] * blocks + sources[t]).astype(jnp.float32)
                marks[peer] = jnp.where(side == rank, mark, marks[peer])
                message = lax.dot_general(
                    held[t], grad[dest[t]], (((0,), (0,)), ((), ())), preferred_element_type=jnp.float32
                ).astype(jnp.bfloat16)
                made[t, pl.ds(0, block)] = message[:, :LANES]
                made[t, pl.ds(block, block)] = message[:, LANES:]
                rows = pl.ds(pl.multiple_of(rank * size, size), size)
                pltpu.make_async_copy(made.at[t], out_ref.at[peer, rows], out_sem).start()
            return carry

        lax.fori_loop(0, part // 16, step, 0)

    tags[...] = jnp.concatenate([marks[...], marks[...]], axis=1).astype(jnp.bfloat16)
    tag_copy = pltpu.make_async_copy(tags, out_ref.at[:, pl.ds(CAP * size, TAG_ROWS)], sems.at[0])
    tag_copy.start()
    pltpu.make_async_copy(made, out_ref.at[pl.ds(0, tile_count), pl.ds(0, size)], out_sem).wait()
    tag_copy.wait()


def make_messages(tile_dest, peer_list, tile_rel, tile_source, tiles, grad_blocks, dev_count):
    tile_count, block, _ = tiles.shape
    blocks, _, width = grad_blocks.shape
    parts = 8
    numbers = pltpu.SMEM((tile_count,), jnp.int32)

    def kernel(*refs):
        message_kernel(blocks, parts, *refs)

    return pl.pallas_call(
        kernel,
        out_shape=jax.ShapeDtypeStruct((dev_count, CAP * 2 * block + TAG_ROWS, LANES), jnp.bfloat16),
        in_specs=[HBM] * 6,
        out_specs=HBM,
        scratch_shapes=[
            numbers,
            numbers,
            numbers,
            numbers,
            pltpu.SMEM((dev_count,), jnp.int32),
            pltpu.VMEM(grad_blocks.shape, jnp.bfloat16),
            pltpu.VMEM(tiles.shape, jnp.bfloat16),
            pltpu.VMEM((tile_count, 2 * block, LANES), jnp.bfloat16),
            pltpu.VMEM((dev_count, TAG_ROWS // 2, LANES), jnp.float32),
            pltpu.VMEM((dev_count, TAG_ROWS, LANES), jnp.bfloat16),
            pltpu.SemaphoreType.DMA((parts + 5,)),
            pltpu.SemaphoreType.DMA,
        ],
        compiler_params=pltpu.CompilerParams(vmem_limit_bytes=58 * MIB),
        cost_estimate=pl.CostEstimate(
            flops=2 * tile_count * block * block * width,
            bytes_accessed=tile_count * block * (block + width) * 2,
            transcendentals=0,
        ),
    )(tile_dest, peer_list, tile_rel, tile_source, tiles, grad_blocks)


def make_plan(marks, blocks, rel_count):
    senders = marks.shape[0]
    places = plan_places(senders * CAP, rel_count)
    square = (senders, senders)
    row, lane = lax.broadcasted_iota(jnp.int32, square, 0), lax.broadcasted_iota(jnp.int32, square, 1)
    below = (lane < row).astype(jnp.float32)
    ahead = (row < lane).astype(jnp.float32)
    sender = lax.broadcasted_iota(jnp.int32, (senders, 1), 0).astype(jnp.float32)
    batch = jnp.floor(sender * (BATCHES / senders))
    kind_lane = lane.astype(jnp.float32)
    tag = [marks[:, 0:1], marks[:, LANES // CAP : LANES // CAP + 1]]
    rel = [jnp.floor(t * (1.0 / blocks)) for t in tag]
    block_of = [t - r * blocks for t, r in zip(tag, rel)]
    used = [jnp.where((kind_lane == batch * rel_count + r) & (t >= 0), 1.0, 0.0) for t, r in zip(tag, rel)]
    totals = [jnp.sum(u, axis=0, keepdims=True) for u in used]
    before = [jnp.dot(below, u, preferred_element_type=jnp.float32) for u in used]
    before[1] = before[1] + totals[0]
    groups = jnp.floor((totals[0] + totals[1] + (GROUP - 1)) * (1.0 / GROUP))
    first = jnp.dot(jnp.broadcast_to(groups, (8, senders)), ahead, preferred_element_type=jnp.float32)[0:1]
    place = [jnp.sum(u * (b + first * GROUP), axis=1, keepdims=True) for u, b in zip(used, before)]
    place = [jnp.where(t >= 0, p, -1.0) for t, p in zip(tag, place)]
    at_int = lax.broadcasted_iota(jnp.int32, (senders, places), 1)
    at, at_group = at_int.astype(jnp.float32), (at_int // GROUP * GROUP).astype(jnp.float32)
    here = [jnp.where(p == at, 1.0, 0.0) for p in place]
    leads = [jnp.where(p == at_group, 1.0, 0.0) for p in place]

    def gather(hits, values):
        return jnp.sum(hits[0] * values[0] + hits[1] * values[1], axis=0, keepdims=True)

    name = [sender * CAP, sender * CAP + 1]
    message = jnp.where(gather(here, [1.0, 1.0]) > 0, gather(here, name), gather(leads, name))
    source = gather(here, [b - blocks for b in block_of]) + blocks
    relation = gather(leads, rel)
    kind_row = kind_lane[0:1]
    ends = [
        jnp.sum(jnp.where(kind_row < rel_count * (i + 1), groups, 0.0), axis=1, keepdims=True) for i in range(BATCHES)
    ]
    rows = [message, source, relation] + [jnp.broadcast_to(e, (1, places)) for e in ends]
    rows.append(jnp.zeros((8 - len(rows), places), jnp.float32))
    return jnp.concatenate(rows, axis=0).astype(jnp.int32)


def plan_places(slots, rel_count):
    return -(-(-(-slots // GROUP) + rel_count * BATCHES) * GROUP // LANES) * LANES


def arrivals(arrived_ref, held, sems):
    part = held.shape[0] // BATCHES

    def copy(i):
        rows = pl.ds(i * part, part)
        return pltpu.make_async_copy(arrived_ref.at[rows, pl.ds(0, held.shape[1])], held.at[rows], sems.at[i])

    return copy


def take(held, message, block):
    top = pl.multiple_of((message % CAP) * (2 * block), 2 * block)
    sender = message // CAP
    return jnp.concatenate([held[sender, pl.ds(top, block)], held[sender, pl.ds(top + block, block)]], axis=1)


def walk_groups(first, end, use):
    def single(g, carry):
        use(g)
        return carry

    def two(j, carry):
        use(first + 2 * j)
        use(first + 2 * j + 1)
        return carry

    pairs = (end - first) // 2
    lax.fori_loop(0, pairs, two, 0)
    lax.fori_loop(first + 2 * pairs, end, single, 0)


def weight_kernel(
    arrived_ref, feat_any, grad_any, core_ref, own_ref, other_ref, plan_ref,
    held, feat, grad, turned, acc, tags, plan, sems, feat_sem, grad_sem, tag_sem,
):
    kinds, width, _ = acc.shape
    blocks, block, _ = feat.shape
    half = width // 2
    tag_copy = pltpu.make_async_copy(arrived_ref.at[:, pl.ds(held.shape[1], TAG_ROWS)], tags, tag_sem)
    feat_copy = pltpu.make_async_copy(feat_any, feat, feat_sem)
    grad_copy = pltpu.make_async_copy(grad_any, grad, grad_sem)
    copy = arrivals(arrived_ref, held, sems)
    tag_copy.start()
    feat_copy.start()
    grad_copy.start()
    copy(0).start()
    acc[...] = jnp.zeros_like(acc)
    turned[blocks] = jnp.zeros(turned.shape[1:], turned.dtype)
    tag_copy.wait()
    plan_ref[...] = make_plan(jnp.max(tags[...].astype(jnp.float32), axis=1), blocks, kinds - 1)
    plan_copy = pltpu.make_async_copy(plan_ref, plan, tag_sem)
    plan_copy.start()
    feat_copy.wait()
    for i in range(1, BATCHES):
        copy(i).start()

    def turn(b, carry):
        for k in range(4):
            turned[b * 4 + k] = feat[b * 4 + k].T
        return carry

    lax.fori_loop(0, blocks // 4, turn, 0)
    grad_copy.wait()

    def root(g, carry):
        left = jnp.concatenate([turned[g * GROUP + k] for k in range(GROUP)], axis=1)
        right = grad[pl.ds(g * GROUP, GROUP)].reshape(GROUP * block, width)
        acc[0] += jnp.dot(left, right, preferred_element_type=jnp.float32)
        return carry

    lax.fori_loop(0, blocks // GROUP, root, 0)
    plan_copy.wait()

    def use(g):
        left = jnp.concatenate([turned[plan[1, g * GROUP + k]] for k in range(GROUP)], axis=1)
        right = jnp.concatenate([take(held, plan[0, g * GROUP + k], block) for k in range(GROUP)], axis=0)
        acc[1 + plan[2, g * GROUP]] += jnp.dot(left, right, preferred_element_type=jnp.float32)

    def batch(i, first):
        copy(i).wait()
        end = plan[3 + i, 0]
        walk_groups(first, end, use)
        return end

    lax.fori_loop(0, BATCHES, batch, 0)

    def split(first, second):
        for ref, lanes in ((first, pl.ds(0, half)), (second, pl.ds(half, half))):
            for r in range(kinds):
                ref[pl.ds(r * width, width)] = acc[r, :, lanes]

    @pl.when(core_ref[0] == 0)
    def _():
        split(own_ref, other_ref)

    @pl.when(core_ref[0] != 0)
    def _():
        split(other_ref, own_ref)


def feat_kernel(batch, plan_ref, arrived_ref, base_any, root_ref, weight_ref, out_any, held, acc, sem, base_sem, *grad):
    blocks, block, width = out_any.shape
    senders = held.shape[0]
    part = pl.ds(batch * senders, senders)
    copy = pltpu.make_async_copy(arrived_ref.at[part, pl.ds(0, held.shape[1])], held, sem)
    inside = acc.at[pl.ds(0, blocks)]
    base_copy = pltpu.make_async_copy(base_any, inside if batch else grad[0], base_sem)
    base_copy.start()
    copy.start()
    acc[blocks] = jnp.zeros(acc.shape[1:], jnp.float32)
    across = (((1,), (1,)), ((), ()))
    base_copy.wait()

    def base(g, carry):
        rows = grad[0][pl.ds(g * GROUP, GROUP)].reshape(GROUP * block, width)
        part = lax.dot_general(rows, root_ref[...], across, preferred_element_type=jnp.float32)
        acc[pl.ds(g * GROUP, GROUP)] = part.reshape(GROUP, block, width)
        return carry

    if batch == 0:
        lax.fori_loop(0, blocks // GROUP, base, 0)
    copy.wait()

    def use(g):
        rows = jnp.concatenate(
            [take(held, plan_ref[0, g * GROUP + k] - batch * senders * CAP, block) for k in range(GROUP)], axis=0
        )
        part = lax.dot_general(rows, weight_ref[plan_ref[2, g * GROUP]], across, preferred_element_type=jnp.float32)
        for k in range(GROUP):
            acc[plan_ref[1, g * GROUP + k]] += part[k * block : (k + 1) * block]

    walk_groups(plan_ref[2 + batch, 0] if batch else 0, plan_ref[3 + batch, 0], use)
    if batch + 1 < BATCHES:
        out_copy = pltpu.make_async_copy(inside, out_any, base_sem)
        out_copy.start()
        out_copy.wait()
    else:
        out_any[...] = acc[pl.ds(0, blocks)].astype(jnp.bfloat16)


def add_batch(batch, plan, arrived, base, root_weight, rel_weight):
    blocks, block, width = base.shape
    senders = arrived.shape[0] // BATCHES
    dma = pltpu.SemaphoreType.DMA
    last = batch + 1 == BATCHES

    def kernel(*refs):
        feat_kernel(batch, *refs)

    return pl.pallas_call(
        kernel,
        out_shape=jax.ShapeDtypeStruct(base.shape, jnp.bfloat16 if last else jnp.float32),
        in_specs=[SMEM, HBM, HBM, VMEM, VMEM],
        out_specs=VMEM if last else HBM,
        scratch_shapes=[
            pltpu.VMEM((senders, CAP * 2 * block, LANES), jnp.bfloat16),
            pltpu.VMEM((blocks + 1, block, width), jnp.float32),
            dma,
            dma,
        ]
        + ([] if batch else [pltpu.VMEM(base.shape, base.dtype)]),
        compiler_params=pltpu.CompilerParams(vmem_limit_bytes=56 * MIB),
        cost_estimate=pl.CostEstimate(
            flops=senders * CAP * block * width * width * 2,
            bytes_accessed=senders * CAP * block * width * 2,
            transcendentals=0,
        ),
    )(plan, arrived, base, root_weight, rel_weight)


def shards(features, out_grad, rel_weight, root_weight, tiles, tile_dest, tile_peer, tile_source, tile_rel):
    dev_count = lax.axis_size(AXES)
    chips = lax.axis_size(CHIPS)
    core = lax.axis_index("c")
    block = tiles.shape[1]
    width = features.shape[1]
    rel_count = rel_weight.shape[0]
    blocks = features.shape[0] // block
    slots = dev_count * CAP
    scale = 1.0 / math.sqrt(features.shape[0] * dev_count)
    grad_blocks = out_grad.reshape(blocks, block, width)

    outgoing = make_messages(tile_dest, tile_peer[:, 0], tile_rel, tile_source, tiles, grad_blocks, dev_count)
    outgoing, core = lax.optimization_barrier((outgoing, core[None].astype(jnp.int32)))
    arrived = lax.all_to_all(outgoing, AXES, split_axis=0, concat_axis=0, tiled=True)

    room = pltpu.VMEM((dev_count, CAP * 2 * block, LANES), jnp.bfloat16)
    local = pltpu.VMEM(grad_blocks.shape, jnp.bfloat16)
    dma = pltpu.SemaphoreType.DMA
    cost = pl.CostEstimate(
        flops=slots * block * width * width, bytes_accessed=slots * block * width * 2, transcendentals=0
    )
    half_rows = (1 + rel_count) * width
    half = jax.ShapeDtypeStruct((half_rows, width // 2), jnp.float32)
    plan_type = jax.ShapeDtypeStruct((8, plan_places(slots, rel_count)), jnp.int32)
    own, other, plan = pl.pallas_call(
        weight_kernel,
        out_shape=(half, half, plan_type),
        in_specs=[HBM] * 3 + [SMEM],
        out_specs=(VMEM, VMEM, VMEM),
        scratch_shapes=[
            room,
            local,
            local,
            pltpu.VMEM((blocks + 1, width, block), jnp.bfloat16),
            pltpu.VMEM((1 + rel_count, width, width), jnp.float32),
            pltpu.VMEM((dev_count, TAG_ROWS, LANES), jnp.bfloat16),
            pltpu.SMEM(plan_type.shape, jnp.int32),
            dma((BATCHES,)),
            dma,
            dma,
            dma,
        ],
        compiler_params=pltpu.CompilerParams(vmem_limit_bytes=36 * MIB),
        cost_estimate=cost,
    )(arrived, features.reshape(blocks, block, width), grad_blocks, core)

    swap = [(0, 1), (1, 0)]
    own = own + lax.ppermute(other, "c", swap)
    own, plan = lax.optimization_barrier((own, plan))
    partial = add_batch(0, plan, arrived, grad_blocks, root_weight, rel_weight)
    shape = (chips, half_rows // chips, width // 2)
    spread = lax.all_to_all(own.reshape(shape), CHIPS, 0, 0, tiled=True)
    spread, partial, plan = lax.optimization_barrier((spread, partial, plan))
    share = (spread.sum(axis=0) * scale).astype(jnp.bfloat16)
    own = lax.all_to_all(jnp.broadcast_to(share[None], shape), CHIPS, 0, 0, tiled=True).reshape(half.shape)
    grad_feat = add_batch(1, plan, arrived, partial, root_weight, rel_weight)
    own, grad_feat = lax.optimization_barrier((own, grad_feat))
    other = lax.ppermute(own, "c", swap)
    core = core[0]
    left = jnp.where(core == 0, own, other).astype(jnp.float32)
    right = jnp.where(core == 0, other, own).astype(jnp.float32)
    grad_weights = jnp.concatenate([left, right], axis=1).reshape(1 + rel_count, width, width)
    return grad_feat.reshape(features.shape), grad_weights


def solution(mesh):
    sizes = (4, 4, 4, 2)
    fine = Mesh(mesh.devices.reshape(sizes), AXES)
    return jax.shard_map(
        shards,
        mesh=fine,
        in_specs=(
            P(AXES, None),
            P(AXES, None),
            P(),
            P(),
            P(AXES, None, None),
            P(AXES),
            P(AXES, None),
            P(AXES),
            P(AXES),
        ),
        out_specs=(P(AXES, None), P()),
        check_vma=False,
    )
```

```python
import math

import jax
import jax.numpy as jnp
from jax import lax
from jax.experimental import pallas as pl
from jax.experimental.pallas import tpu as pltpu
from jax.sharding import Mesh
from jax.sharding import PartitionSpec as P

AXES = ("z", "y", "x", "c")
CHIPS = ("z", "y", "x")
VMEM = pl.BlockSpec(memory_space=pltpu.VMEM)
HBM = pl.BlockSpec(memory_space=pltpu.HBM)
SMEM = pl.BlockSpec(memory_space=pltpu.SMEM)
MIB = 1024 * 1024
CAP = 2
GROUP = 8
BATCHES = 2
LANES = 128
TAG_ROWS = 16


def message_kernel(
    blocks, parts, dest_any, peer_any, rel_any, source_any, tiles_ref, grad_any, out_ref,
    dest, peers, rels, sources, count, grad, held, made, marks, tags, sems, out_sem,
):
    tile_count, block, _ = tiles_ref.shape
    part = tile_count // parts
    size = 2 * block
    pairs = ((dest_any, dest), (peer_any, peers), (rel_any, rels), (source_any, sources), (grad_any, grad))
    early = [pltpu.make_async_copy(src, dst, sems.at[parts + i]) for i, (src, dst) in enumerate(pairs)]
    for copy in early:
        copy.start()

    def fetch(i):
        rows = pl.ds(i * part, part)
        return pltpu.make_async_copy(tiles_ref.at[rows], held.at[rows], sems.at[i])

    for i in range(parts):
        fetch(i).start()

    def clear(i, carry):
        count[i] = 0
        return carry

    lax.fori_loop(0, count.shape[0], clear, 0)
    marks[...] = jnp.full(marks.shape, -1.0, jnp.float32)
    side = lax.broadcasted_iota(jnp.int32, marks.shape[1:], 1) // (LANES // CAP)
    for copy in early:
        copy.wait()

    for i in range(parts):
        fetch(i).wait()

        def step(j, carry):
            for k in range(16):
                t = i * part + j * 16 + k
                peer = peers[t]
                rank = count[peer]
                count[peer] = rank + 1
                mark = (rels[t] * blocks + sources[t]).astype(jnp.float32)
                marks[peer] = jnp.where(side == rank, mark, marks[peer])
                message = lax.dot_general(
                    held[t], grad[dest[t]], (((0,), (0,)), ((), ())), preferred_element_type=jnp.float32
                ).astype(jnp.bfloat16)
                made[t, pl.ds(0, block)] = message[:, :LANES]
                made[t, pl.ds(block, block)] = message[:, LANES:]
                rows = pl.ds(pl.multiple_of(rank * size, size), size)
                pltpu.make_async_copy(made.at[t], out_ref.at[peer, rows], out_sem).start()
            return carry

        lax.fori_loop(0, part // 16, step, 0)

    tags[...] = jnp.concatenate([marks[...], marks[...]], axis=1).astype(jnp.bfloat16)
    tag_copy = pltpu.make_async_copy(tags, out_ref.at[:, pl.ds(CAP * size, TAG_ROWS)], sems.at[0])
    tag_copy.start()
    pltpu.make_async_copy(made, out_ref.at[pl.ds(0, tile_count), pl.ds(0, size)], out_sem).wait()
    tag_copy.wait()


def make_messages(tile_dest, peer_list, tile_rel, tile_source, tiles, grad_blocks, dev_count):
    tile_count, block, _ = tiles.shape
    blocks, _, width = grad_blocks.shape
    parts = 8
    numbers = pltpu.SMEM((tile_count,), jnp.int32)

    def kernel(*refs):
        message_kernel(blocks, parts, *refs)

    return pl.pallas_call(
        kernel,
        out_shape=jax.ShapeDtypeStruct((dev_count, CAP * 2 * block + TAG_ROWS, LANES), jnp.bfloat16),
        in_specs=[HBM] * 6,
        out_specs=HBM,
        scratch_shapes=[
            numbers,
            numbers,
            numbers,
            numbers,
            pltpu.SMEM((dev_count,), jnp.int32),
            pltpu.VMEM(grad_blocks.shape, jnp.bfloat16),
            pltpu.VMEM(tiles.shape, jnp.bfloat16),
            pltpu.VMEM((tile_count, 2 * block, LANES), jnp.bfloat16),
            pltpu.VMEM((dev_count, TAG_ROWS // 2, LANES), jnp.float32),
            pltpu.VMEM((dev_count, TAG_ROWS, LANES), jnp.bfloat16),
            pltpu.SemaphoreType.DMA((parts + 5,)),
            pltpu.SemaphoreType.DMA,
        ],
        compiler_params=pltpu.CompilerParams(vmem_limit_bytes=58 * MIB),
        cost_estimate=pl.CostEstimate(
            flops=2 * tile_count * block * block * width,
            bytes_accessed=tile_count * block * (block + width) * 2,
            transcendentals=0,
        ),
    )(tile_dest, peer_list, tile_rel, tile_source, tiles, grad_blocks)


def make_plan(marks, blocks, rel_count):
    senders = marks.shape[0]
    places = plan_places(senders * CAP, rel_count)
    square = (senders, senders)
    row, lane = lax.broadcasted_iota(jnp.int32, square, 0), lax.broadcasted_iota(jnp.int32, square, 1)
    below = (lane < row).astype(jnp.float32)
    ahead = (row < lane).astype(jnp.float32)
    sender = lax.broadcasted_iota(jnp.int32, (senders, 1), 0).astype(jnp.float32)
    batch = jnp.floor(sender * (BATCHES / senders))
    kind_lane = lane.astype(jnp.float32)
    tag = [marks[:, 0:1], marks[:, LANES // CAP : LANES // CAP + 1]]
    rel = [jnp.floor(t * (1.0 / blocks)) for t in tag]
    block_of = [t - r * blocks for t, r in zip(tag, rel)]
    used = [jnp.where((kind_lane == batch * rel_count + r) & (t >= 0), 1.0, 0.0) for t, r in zip(tag, rel)]
    totals = [jnp.sum(u, axis=0, keepdims=True) for u in used]
    before = [jnp.dot(below, u, preferred_element_type=jnp.float32) for u in used]
    before[1] = before[1] + totals[0]
    groups = jnp.floor((totals[0] + totals[1] + (GROUP - 1)) * (1.0 / GROUP))
    first = jnp.dot(jnp.broadcast_to(groups, (8, senders)), ahead, preferred_element_type=jnp.float32)[0:1]
    place = [jnp.sum(u * (b + first * GROUP), axis=1, keepdims=True) for u, b in zip(used, before)]
    place = [jnp.where(t >= 0, p, -1.0) for t, p in zip(tag, place)]
    at_int = lax.broadcasted_iota(jnp.int32, (senders, places), 1)
    at, at_group = at_int.astype(jnp.float32), (at_int // GROUP * GROUP).astype(jnp.float32)
    here = [jnp.where(p == at, 1.0, 0.0) for p in place]
    leads = [jnp.where(p == at_group, 1.0, 0.0) for p in place]

    def gather(hits, values):
        return jnp.sum(hits[0] * values[0] + hits[1] * values[1], axis=0, keepdims=True)

    name = [sender * CAP, sender * CAP + 1]
    message = jnp.where(gather(here, [1.0, 1.0]) > 0, gather(here, name), gather(leads, name))
    source = gather(here, [b - blocks for b in block_of]) + blocks
    relation = gather(leads, rel)
    kind_row = kind_lane[0:1]
    ends = [
        jnp.sum(jnp.where(kind_row < rel_count * (i + 1), groups, 0.0), axis=1, keepdims=True) for i in range(BATCHES)
    ]
    rows = [message, source, relation] + [jnp.broadcast_to(e, (1, places)) for e in ends]
    rows.append(jnp.zeros((8 - len(rows), places), jnp.float32))
    return jnp.concatenate(rows, axis=0).astype(jnp.int32)


def plan_places(slots, rel_count):
    return -(-(-(-slots // GROUP) + rel_count * BATCHES) * GROUP // LANES) * LANES


def take(held, message, block):
    top = pl.multiple_of((message % CAP) * (2 * block), 2 * block)
    sender = message // CAP
    return jnp.concatenate([held[sender, pl.ds(top, block)], held[sender, pl.ds(top + block, block)]], axis=1)


def walk_groups(first, end, use):
    def single(g, carry):
        use(g)
        return carry

    def two(j, carry):
        use(first + 2 * j)
        use(first + 2 * j + 1)
        return carry

    pairs = (end - first) // 2
    lax.fori_loop(0, pairs, two, 0)
    lax.fori_loop(first + 2 * pairs, end, single, 0)


def weight_kernel(
    arrived_ref, feat, grad, core_ref, own_ref, other_ref, plan_ref, turned, acc, plan, plan_sem
):
    kinds, width, _ = acc.shape
    blocks, block, _ = feat.shape
    half = width // 2
    tags = arrived_ref[:, pl.ds(CAP * 2 * block, TAG_ROWS)].astype(jnp.float32)
    plan_ref[...] = make_plan(jnp.max(tags, axis=1), blocks, kinds - 1)
    plan_copy = pltpu.make_async_copy(plan_ref, plan, plan_sem)
    plan_copy.start()
    acc[...] = jnp.zeros_like(acc)
    turned[blocks] = jnp.zeros(turned.shape[1:], turned.dtype)

    def turn(b, carry):
        for k in range(4):
            turned[b * 4 + k] = feat[b * 4 + k].T
        return carry

    lax.fori_loop(0, blocks // 4, turn, 0)

    def root(g, carry):
        left = jnp.concatenate([turned[g * GROUP + k] for k in range(GROUP)], axis=1)
        right = grad[pl.ds(g * GROUP, GROUP)].reshape(GROUP * block, width)
        acc[0] += jnp.dot(left, right, preferred_element_type=jnp.float32)
        return carry

    lax.fori_loop(0, blocks // GROUP, root, 0)
    plan_copy.wait()

    def use(g):
        left = jnp.concatenate([turned[plan[1, g * GROUP + k]] for k in range(GROUP)], axis=1)
        right = jnp.concatenate([take(arrived_ref, plan[0, g * GROUP + k], block) for k in range(GROUP)], axis=0)
        acc[1 + plan[2, g * GROUP]] += jnp.dot(left, right, preferred_element_type=jnp.float32)

    walk_groups(0, plan[2 + BATCHES, 0], use)

    def split(first, second):
        for ref, lanes in ((first, pl.ds(0, half)), (second, pl.ds(half, half))):
            for r in range(kinds):
                ref[pl.ds(r * width, width)] = acc[r, :, lanes]

    @pl.when(core_ref[0] == 0)
    def _():
        split(own_ref, other_ref)

    @pl.when(core_ref[0] != 0)
    def _():
        split(other_ref, own_ref)


def feat_kernel(batch, plan_ref, arrived_ref, base_any, root_ref, weight_ref, out_any, held, acc, sem, base_sem, *grad):
    blocks, block, width = out_any.shape
    senders = held.shape[0]
    part = pl.ds(batch * senders, senders)
    copy = pltpu.make_async_copy(arrived_ref.at[part, pl.ds(0, held.shape[1])], held, sem)
    inside = acc.at[pl.ds(0, blocks)]
    base_copy = pltpu.make_async_copy(base_any, inside if batch else grad[0], base_sem)
    base_copy.start()
    copy.start()
    acc[blocks] = jnp.zeros(acc.shape[1:], jnp.float32)
    across = (((1,), (1,)), ((), ()))
    base_copy.wait()

    def base(g, carry):
        rows = grad[0][pl.ds(g * GROUP, GROUP)].reshape(GROUP * block, width)
        part = lax.dot_general(rows, root_ref[...], across, preferred_element_type=jnp.float32)
        acc[pl.ds(g * GROUP, GROUP)] = part.reshape(GROUP, block, width)
        return carry

    if batch == 0:
        lax.fori_loop(0, blocks // GROUP, base, 0)
    copy.wait()

    def use(g):
        rows = jnp.concatenate(
            [take(held, plan_ref[0, g * GROUP + k] - batch * senders * CAP, block) for k in range(GROUP)], axis=0
        )
        part = lax.dot_general(rows, weight_ref[plan_ref[2, g * GROUP]], across, preferred_element_type=jnp.float32)
        for k in range(GROUP):
            acc[plan_ref[1, g * GROUP + k]] += part[k * block : (k + 1) * block]

    walk_groups(plan_ref[2 + batch, 0] if batch else 0, plan_ref[3 + batch, 0], use)
    if batch + 1 < BATCHES:
        out_copy = pltpu.make_async_copy(inside, out_any, base_sem)
        out_copy.start()
        out_copy.wait()
    else:
        out_any[...] = acc[pl.ds(0, blocks)].astype(jnp.bfloat16)


def add_batch(batch, plan, arrived, base, root_weight, rel_weight):
    blocks, block, width = base.shape
    senders = arrived.shape[0] // BATCHES
    dma = pltpu.SemaphoreType.DMA
    last = batch + 1 == BATCHES

    def kernel(*refs):
        feat_kernel(batch, *refs)

    return pl.pallas_call(
        kernel,
        out_shape=jax.ShapeDtypeStruct(base.shape, jnp.bfloat16 if last else jnp.float32),
        in_specs=[SMEM, HBM, HBM, VMEM, VMEM],
        out_specs=VMEM if last else HBM,
        scratch_shapes=[
            pltpu.VMEM((senders, CAP * 2 * block, LANES), jnp.bfloat16),
            pltpu.VMEM((blocks + 1, block, width), jnp.float32),
            dma,
            dma,
        ]
        + ([] if batch else [pltpu.VMEM(base.shape, base.dtype)]),
        compiler_params=pltpu.CompilerParams(vmem_limit_bytes=56 * MIB),
        cost_estimate=pl.CostEstimate(
            flops=senders * CAP * block * width * width * 2,
            bytes_accessed=senders * CAP * block * width * 2,
            transcendentals=0,
        ),
    )(plan, arrived, base, root_weight, rel_weight)


def shards(features, out_grad, rel_weight, root_weight, tiles, tile_dest, tile_peer, tile_source, tile_rel):
    dev_count = lax.axis_size(AXES)
    chips = lax.axis_size(CHIPS)
    core = lax.axis_index("c")
    block = tiles.shape[1]
    width = features.shape[1]
    rel_count = rel_weight.shape[0]
    blocks = features.shape[0] // block
    slots = dev_count * CAP
    scale = 1.0 / math.sqrt(features.shape[0] * dev_count)
    grad_blocks = out_grad.reshape(blocks, block, width)

    outgoing = make_messages(tile_dest, tile_peer[:, 0], tile_rel, tile_source, tiles, grad_blocks, dev_count)
    outgoing, core = lax.optimization_barrier((outgoing, core[None].astype(jnp.int32)))
    arrived = lax.all_to_all(outgoing, AXES, split_axis=0, concat_axis=0, tiled=True)

    dma = pltpu.SemaphoreType.DMA
    cost = pl.CostEstimate(
        flops=slots * block * width * width, bytes_accessed=slots * block * width * 2, transcendentals=0
    )
    half_rows = (1 + rel_count) * width
    half = jax.ShapeDtypeStruct((half_rows, width // 2), jnp.float32)
    plan_type = jax.ShapeDtypeStruct((8, plan_places(slots, rel_count)), jnp.int32)
    own, other, plan = pl.pallas_call(
        weight_kernel,
        out_shape=(half, half, plan_type),
        in_specs=[VMEM] * 3 + [SMEM],
        out_specs=(VMEM, VMEM, VMEM),
        scratch_shapes=[
            pltpu.VMEM((blocks + 1, width, block), jnp.bfloat16),
            pltpu.VMEM((1 + rel_count, width, width), jnp.float32),
            pltpu.SMEM(plan_type.shape, jnp.int32),
            dma,
        ],
        compiler_params=pltpu.CompilerParams(vmem_limit_bytes=16 * MIB),
        cost_estimate=cost,
    )(arrived, features.reshape(blocks, block, width), grad_blocks, core)

    swap = [(0, 1), (1, 0)]
    own = own + lax.ppermute(other, "c", swap)
    own, plan = lax.optimization_barrier((own, plan))
    partial = add_batch(0, plan, arrived, grad_blocks, root_weight, rel_weight)
    shape = (chips, half_rows // chips, width // 2)
    spread = lax.all_to_all(own.reshape(shape), CHIPS, 0, 0, tiled=True)
    spread, partial, plan = lax.optimization_barrier((spread, partial, plan))
    share = (spread.sum(axis=0) * scale).astype(jnp.bfloat16)
    own = lax.all_to_all(jnp.broadcast_to(share[None], shape), CHIPS, 0, 0, tiled=True).reshape(half.shape)
    grad_feat = add_batch(1, plan, arrived, partial, root_weight, rel_weight)
    own, grad_feat = lax.optimization_barrier((own, grad_feat))
    other = lax.ppermute(own, "c", swap)
    core = core[0]
    left = jnp.where(core == 0, own, other).astype(jnp.float32)
    right = jnp.where(core == 0, other, own).astype(jnp.float32)
    grad_weights = jnp.concatenate([left, right], axis=1).reshape(1 + rel_count, width, width)
    return grad_feat.reshape(features.shape), grad_weights


def solution(mesh):
    sizes = (4, 4, 4, 2)
    fine = Mesh(mesh.devices.reshape(sizes), AXES)
    return jax.shard_map(
        shards,
        mesh=fine,
        in_specs=(
            P(AXES, None),
            P(AXES, None),
            P(),
            P(),
            P(AXES, None, None),
            P(AXES),
            P(AXES, None),
            P(AXES),
            P(AXES),
        ),
        out_specs=(P(AXES, None), P()),
        check_vma=False,
    )
```

```python
import functools
import math

import jax
import jax.numpy as jnp
from jax import lax
from jax.experimental import pallas as pl
from jax.experimental.pallas import tpu as pltpu
from jax.sharding import Mesh
from jax.sharding import PartitionSpec as P

AXES = ("z", "y", "x", "c")
CHIPS = ("z", "y", "x")
VMEM = pl.BlockSpec(memory_space=pltpu.VMEM)
HBM = pl.BlockSpec(memory_space=pltpu.HBM)
SMEM = pl.BlockSpec(memory_space=pltpu.SMEM)
MIB = 1024 * 1024
CAP = 2
GROUP = 8
BATCHES = 2
LANES = 128
TAG_ROWS = 16


def message_kernel(
    blocks, parts, dest_any, peer_any, rel_any, source_any, tiles_ref, grad_any, out_ref,
    dest, peers, rels, sources, count, grad, held, made, marks, tags, sems, out_sem,
):
    tile_count, block, _ = tiles_ref.shape
    part = tile_count // parts
    size = 2 * block
    pairs = ((dest_any, dest), (peer_any, peers), (rel_any, rels), (source_any, sources), (grad_any, grad))
    early = [pltpu.make_async_copy(src, dst, sems.at[parts + i]) for i, (src, dst) in enumerate(pairs)]
    for copy in early:
        copy.start()

    def fetch(i):
        rows = pl.ds(i * part, part)
        return pltpu.make_async_copy(tiles_ref.at[rows], held.at[rows], sems.at[i])

    for i in range(parts):
        fetch(i).start()

    def clear(i, carry):
        count[i] = 0
        return carry

    lax.fori_loop(0, count.shape[0], clear, 0)
    marks[...] = jnp.full(marks.shape, -1.0, jnp.float32)
    side = lax.broadcasted_iota(jnp.int32, marks.shape[1:], 1) // (LANES // CAP)
    for copy in early:
        copy.wait()

    for i in range(parts):
        fetch(i).wait()

        def step(j, carry):
            for k in range(16):
                t = i * part + j * 16 + k
                peer = peers[t]
                rank = count[peer]
                count[peer] = rank + 1
                mark = (rels[t] * blocks + sources[t]).astype(jnp.float32)
                marks[peer] = jnp.where(side == rank, mark, marks[peer])
                message = lax.dot_general(
                    held[t], grad[dest[t]], (((0,), (0,)), ((), ())), preferred_element_type=jnp.float32
                ).astype(jnp.bfloat16)
                made[t, pl.ds(0, block)] = message[:, :LANES]
                made[t, pl.ds(block, block)] = message[:, LANES:]
                rows = pl.ds(pl.multiple_of(rank * size, size), size)
                pltpu.make_async_copy(made.at[t], out_ref.at[peer, rows], out_sem).start()
            return carry

        lax.fori_loop(0, part // 16, step, 0)

    tags[...] = jnp.concatenate([marks[...], marks[...]], axis=1).astype(jnp.bfloat16)
    tag_copy = pltpu.make_async_copy(tags, out_ref.at[:, pl.ds(CAP * size, TAG_ROWS)], sems.at[0])
    tag_copy.start()
    pltpu.make_async_copy(made, out_ref.at[pl.ds(0, tile_count), pl.ds(0, size)], out_sem).wait()
    tag_copy.wait()


def make_messages(tile_dest, peer_list, tile_rel, tile_source, tiles, grad_blocks, dev_count):
    tile_count, block, _ = tiles.shape
    blocks, _, width = grad_blocks.shape
    parts = 8
    numbers = pltpu.SMEM((tile_count,), jnp.int32)

    def kernel(*refs):
        message_kernel(blocks, parts, *refs)

    return pl.pallas_call(
        kernel,
        out_shape=jax.ShapeDtypeStruct((dev_count, CAP * 2 * block + TAG_ROWS, LANES), jnp.bfloat16),
        in_specs=[HBM] * 6,
        out_specs=HBM,
        scratch_shapes=[
            numbers,
            numbers,
            numbers,
            numbers,
            pltpu.SMEM((dev_count,), jnp.int32),
            pltpu.VMEM(grad_blocks.shape, jnp.bfloat16),
            pltpu.VMEM(tiles.shape, jnp.bfloat16),
            pltpu.VMEM((tile_count, 2 * block, LANES), jnp.bfloat16),
            pltpu.VMEM((dev_count, TAG_ROWS // 2, LANES), jnp.float32),
            pltpu.VMEM((dev_count, TAG_ROWS, LANES), jnp.bfloat16),
            pltpu.SemaphoreType.DMA((parts + 5,)),
            pltpu.SemaphoreType.DMA,
        ],
        compiler_params=pltpu.CompilerParams(vmem_limit_bytes=58 * MIB),
        cost_estimate=pl.CostEstimate(
            flops=2 * tile_count * block * block * width,
            bytes_accessed=tile_count * block * (block + width) * 2,
            transcendentals=0,
        ),
    )(tile_dest, peer_list, tile_rel, tile_source, tiles, grad_blocks)


def make_plan(marks, blocks, rel_count):
    senders = marks.shape[0]
    places = plan_places(senders * CAP, rel_count)
    square = (senders, senders)
    row, lane = lax.broadcasted_iota(jnp.int32, square, 0), lax.broadcasted_iota(jnp.int32, square, 1)
    below = (lane < row).astype(jnp.float32)
    ahead = (row < lane).astype(jnp.float32)
    sender = lax.broadcasted_iota(jnp.int32, (senders, 1), 0).astype(jnp.float32)
    batch = jnp.floor(sender * (BATCHES / senders))
    kind_lane = lane.astype(jnp.float32)
    tag = [marks[:, 0:1], marks[:, LANES // CAP : LANES // CAP + 1]]
    rel = [jnp.floor(t * (1.0 / blocks)) for t in tag]
    block_of = [t - r * blocks for t, r in zip(tag, rel)]
    used = [jnp.where((kind_lane == batch * rel_count + r) & (t >= 0), 1.0, 0.0) for t, r in zip(tag, rel)]
    totals = [jnp.sum(u, axis=0, keepdims=True) for u in used]
    before = [jnp.dot(below, u, preferred_element_type=jnp.float32) for u in used]
    before[1] = before[1] + totals[0]
    groups = jnp.floor((totals[0] + totals[1] + (GROUP - 1)) * (1.0 / GROUP))
    first = jnp.dot(jnp.broadcast_to(groups, (8, senders)), ahead, preferred_element_type=jnp.float32)[0:1]
    place = [jnp.sum(u * (b + first * GROUP), axis=1, keepdims=True) for u, b in zip(used, before)]
    place = [jnp.where(t >= 0, p, -1.0) for t, p in zip(tag, place)]
    at_int = lax.broadcasted_iota(jnp.int32, (senders, places), 1)
    at, at_group = at_int.astype(jnp.float32), (at_int // GROUP * GROUP).astype(jnp.float32)
    here = [jnp.where(p == at, 1.0, 0.0) for p in place]
    leads = [jnp.where(p == at_group, 1.0, 0.0) for p in place]

    def gather(hits, values):
        return jnp.sum(hits[0] * values[0] + hits[1] * values[1], axis=0, keepdims=True)

    name = [sender * CAP, sender * CAP + 1]
    message = jnp.where(gather(here, [1.0, 1.0]) > 0, gather(here, name), gather(leads, name))
    source = gather(here, [b - blocks for b in block_of]) + blocks
    relation = gather(leads, rel)
    kind_row = kind_lane[0:1]
    ends = [
        jnp.sum(jnp.where(kind_row < rel_count * (i + 1), groups, 0.0), axis=1, keepdims=True) for i in range(BATCHES)
    ]
    rows = [message, source, relation] + [jnp.broadcast_to(e, (1, places)) for e in ends]
    rows.append(jnp.zeros((8 - len(rows), places), jnp.float32))
    return jnp.concatenate(rows, axis=0).astype(jnp.int32)


def plan_places(slots, rel_count):
    return -(-(-(-slots // GROUP) + rel_count * BATCHES) * GROUP // LANES) * LANES


def take(held, message, block):
    top = pl.multiple_of(lax.shift_left(message & (CAP - 1), (2 * block).bit_length() - 1), 2 * block)
    sender = lax.shift_right_logical(message, CAP.bit_length() - 1)
    return jnp.concatenate([held[sender, pl.ds(top, block)], held[sender, pl.ds(top + block, block)]], axis=1)


def walk_groups(first, end, use):
    def single(g, carry):
        use(g)
        return carry

    def two(j, carry):
        use(first + 2 * j)
        use(first + 2 * j + 1)
        return carry

    pairs = lax.shift_right_logical(end - first, 1)
    lax.fori_loop(0, pairs, two, 0)
    lax.fori_loop(first + 2 * pairs, end, single, 0)


def weight_kernel(
    arrived_ref, feat, grad, core_ref, own_ref, other_ref, plan_ref, turned, acc, plan, plan_sem
):
    kinds, width, _ = acc.shape
    blocks, block, _ = feat.shape
    half = width // 2
    tags = arrived_ref[:, pl.ds(CAP * 2 * block, TAG_ROWS)].astype(jnp.float32)
    plan_ref[...] = make_plan(jnp.max(tags, axis=1), blocks, kinds - 1)
    plan_copy = pltpu.make_async_copy(plan_ref, plan, plan_sem)
    plan_copy.start()
    acc[...] = jnp.zeros_like(acc)
    turned[blocks] = jnp.zeros(turned.shape[1:], turned.dtype)

    def turn(b, carry):
        for k in range(4):
            turned[b * 4 + k] = feat[b * 4 + k].T
        return carry

    lax.fori_loop(0, blocks // 4, turn, 0)

    def root(g, carry):
        left = jnp.concatenate([turned[g * GROUP + k] for k in range(GROUP)], axis=1)
        right = grad[pl.ds(g * GROUP, GROUP)].reshape(GROUP * block, width)
        acc[0] += jnp.dot(left, right, preferred_element_type=jnp.float32)
        return carry

    lax.fori_loop(0, blocks // GROUP, root, 0)
    plan_copy.wait()

    def use(g):
        left = jnp.concatenate([turned[plan[1, g * GROUP + k]] for k in range(GROUP)], axis=1)
        right = jnp.concatenate([take(arrived_ref, plan[0, g * GROUP + k], block) for k in range(GROUP)], axis=0)
        acc[1 + plan[2, g * GROUP]] += jnp.dot(left, right, preferred_element_type=jnp.float32)

    walk_groups(0, plan[2 + BATCHES, 0], use)

    def split(first, second):
        for ref, lanes in ((first, pl.ds(0, half)), (second, pl.ds(half, half))):
            for r in range(kinds):
                ref[pl.ds(r * width, width)] = acc[r, :, lanes]

    @pl.when(core_ref[0] == 0)
    def _():
        split(own_ref, other_ref)

    @pl.when(core_ref[0] != 0)
    def _():
        split(other_ref, own_ref)


def feat_kernel(batch, plan_ref, arrived_ref, base_any, root_ref, weight_ref, out_any, held, acc, sem, base_sem, *grad):
    blocks, block, width = out_any.shape
    senders = held.shape[0]
    part = pl.ds(batch * senders, senders)
    copy = pltpu.make_async_copy(arrived_ref.at[part, pl.ds(0, held.shape[1])], held, sem)
    inside = acc.at[pl.ds(0, blocks)]
    base_copy = pltpu.make_async_copy(base_any, inside if batch else grad[0], base_sem)
    base_copy.start()
    copy.start()
    acc[blocks] = jnp.zeros(acc.shape[1:], jnp.float32)
    across = (((1,), (1,)), ((), ()))
    base_copy.wait()

    def base(g, carry):
        rows = grad[0][pl.ds(g * GROUP, GROUP)].reshape(GROUP * block, width)
        part = lax.dot_general(rows, root_ref[...], across, preferred_element_type=jnp.float32)
        acc[pl.ds(g * GROUP, GROUP)] = part.reshape(GROUP, block, width)
        return carry

    if batch == 0:
        lax.fori_loop(0, blocks // GROUP, base, 0)
    copy.wait()

    def use(g):
        rows = jnp.concatenate(
            [take(held, plan_ref[0, g * GROUP + k] - batch * senders * CAP, block) for k in range(GROUP)], axis=0
        )
        part = lax.dot_general(rows, weight_ref[plan_ref[2, g * GROUP]], across, preferred_element_type=jnp.float32)
        for k in range(GROUP):
            acc[plan_ref[1, g * GROUP + k]] += part[k * block : (k + 1) * block]

    walk_groups(plan_ref[2 + batch, 0] if batch else 0, plan_ref[3 + batch, 0], use)
    if batch + 1 < BATCHES:
        out_copy = pltpu.make_async_copy(inside, out_any, base_sem)
        out_copy.start()
        out_copy.wait()
    else:
        out_any[...] = acc[pl.ds(0, blocks)].astype(jnp.bfloat16)


def add_batch(batch, plan, arrived, base, root_weight, rel_weight):
    blocks, block, width = base.shape
    senders = arrived.shape[0] // BATCHES
    dma = pltpu.SemaphoreType.DMA
    last = batch + 1 == BATCHES

    def kernel(*refs):
        feat_kernel(batch, *refs)

    return pl.pallas_call(
        kernel,
        out_shape=jax.ShapeDtypeStruct(base.shape, jnp.bfloat16 if last else jnp.float32),
        in_specs=[SMEM, HBM, HBM, VMEM, VMEM],
        out_specs=VMEM if last else HBM,
        scratch_shapes=[
            pltpu.VMEM((senders, CAP * 2 * block, LANES), jnp.bfloat16),
            pltpu.VMEM((blocks + 1, block, width), jnp.float32),
            dma,
            dma,
        ]
        + ([] if batch else [pltpu.VMEM(base.shape, base.dtype)]),
        compiler_params=pltpu.CompilerParams(vmem_limit_bytes=56 * MIB),
        cost_estimate=pl.CostEstimate(
            flops=senders * CAP * block * width * width * 2,
            bytes_accessed=senders * CAP * block * width * 2,
            transcendentals=0,
        ),
    )(plan, arrived, base, root_weight, rel_weight)


def share_kernel(scale, spread_ref, share_ref):
    share = (jnp.sum(spread_ref[...], axis=0) * scale).astype(jnp.bfloat16)
    for i in range(share_ref.shape[0]):
        share_ref[i] = share


def shards(features, out_grad, rel_weight, root_weight, tiles, tile_dest, tile_peer, tile_source, tile_rel):
    dev_count = lax.axis_size(AXES)
    chips = lax.axis_size(CHIPS)
    core = lax.axis_index("c")
    block = tiles.shape[1]
    width = features.shape[1]
    rel_count = rel_weight.shape[0]
    blocks = features.shape[0] // block
    slots = dev_count * CAP
    scale = 1.0 / math.sqrt(features.shape[0] * dev_count)
    grad_blocks = out_grad.reshape(blocks, block, width)

    outgoing = make_messages(tile_dest, tile_peer[:, 0], tile_rel, tile_source, tiles, grad_blocks, dev_count)
    outgoing, core = lax.optimization_barrier((outgoing, core[None].astype(jnp.int32)))
    arrived = lax.all_to_all(outgoing, AXES, split_axis=0, concat_axis=0, tiled=True)

    dma = pltpu.SemaphoreType.DMA
    cost = pl.CostEstimate(
        flops=slots * block * width * width, bytes_accessed=slots * block * width * 2, transcendentals=0
    )
    half_rows = (1 + rel_count) * width
    half = jax.ShapeDtypeStruct((half_rows, width // 2), jnp.float32)
    plan_type = jax.ShapeDtypeStruct((8, plan_places(slots, rel_count)), jnp.int32)
    own, other, plan = pl.pallas_call(
        weight_kernel,
        out_shape=(half, half, plan_type),
        in_specs=[VMEM] * 3 + [SMEM],
        out_specs=(VMEM, VMEM, VMEM),
        scratch_shapes=[
            pltpu.VMEM((blocks + 1, width, block), jnp.bfloat16),
            pltpu.VMEM((1 + rel_count, width, width), jnp.float32),
            pltpu.SMEM(plan_type.shape, jnp.int32),
            dma,
        ],
        compiler_params=pltpu.CompilerParams(vmem_limit_bytes=16 * MIB),
        cost_estimate=cost,
    )(arrived, features.reshape(blocks, block, width), grad_blocks, core)

    swap = [(0, 1), (1, 0)]
    own = own + lax.ppermute(other, "c", swap)
    own, plan = lax.optimization_barrier((own, plan))
    partial = add_batch(0, plan, arrived, grad_blocks, root_weight, rel_weight)
    shape = (chips, half_rows // chips, width // 2)
    spread = lax.all_to_all(own.reshape(shape), CHIPS, 0, 0, tiled=True)
    spread, partial, plan = lax.optimization_barrier((spread, partial, plan))
    share = pl.pallas_call(
        functools.partial(share_kernel, scale),
        out_shape=jax.ShapeDtypeStruct(shape, jnp.bfloat16),
        in_specs=[VMEM],
        out_specs=VMEM,
        compiler_params=pltpu.CompilerParams(vmem_limit_bytes=8 * MIB),
    )(spread)
    own = lax.all_to_all(share, CHIPS, 0, 0, tiled=True).reshape(half.shape)
    grad_feat = add_batch(1, plan, arrived, partial, root_weight, rel_weight)
    own, grad_feat = lax.optimization_barrier((own, grad_feat))
    other = lax.ppermute(own, "c", swap)
    core = core[0]
    left = jnp.where(core == 0, own, other).astype(jnp.float32)
    right = jnp.where(core == 0, other, own).astype(jnp.float32)
    grad_weights = jnp.concatenate([left, right], axis=1).reshape(1 + rel_count, width, width)
    return grad_feat.reshape(features.shape), grad_weights


def solution(mesh):
    sizes = (4, 4, 4, 2)
    fine = Mesh(mesh.devices.reshape(sizes), AXES)
    return jax.shard_map(
        shards,
        mesh=fine,
        in_specs=(
            P(AXES, None),
            P(AXES, None),
            P(),
            P(),
            P(AXES, None, None),
            P(AXES),
            P(AXES, None),
            P(AXES),
            P(AXES),
        ),
        out_specs=(P(AXES, None), P()),
        check_vma=False,
    )
```

```python
import functools
import math

import jax
import jax.numpy as jnp
from jax import lax
from jax.experimental import pallas as pl
from jax.experimental.pallas import tpu as pltpu
from jax.sharding import Mesh
from jax.sharding import PartitionSpec as P

AXES = ("z", "y", "x", "c")
CHIPS = ("z", "y", "x")
VMEM = pl.BlockSpec(memory_space=pltpu.VMEM)
HBM = pl.BlockSpec(memory_space=pltpu.HBM)
SMEM = pl.BlockSpec(memory_space=pltpu.SMEM)
MIB = 1024 * 1024
CAP = 2
GROUP = 8
BATCHES = 2
LANES = 128
TAG_ROWS = 16


def message_kernel(
    blocks, parts, dest_any, peer_any, rel_any, source_any, tiles_ref, grad_any, out_ref,
    dest, peers, rels, sources, count, grad, held, made, marks, tags, sems, out_sem,
):
    tile_count, block, _ = tiles_ref.shape
    part = tile_count // parts
    size = 2 * block
    pairs = ((dest_any, dest), (peer_any, peers), (rel_any, rels), (source_any, sources), (grad_any, grad))
    early = [pltpu.make_async_copy(src, dst, sems.at[parts + i]) for i, (src, dst) in enumerate(pairs)]
    for copy in early:
        copy.start()

    def fetch(i):
        rows = pl.ds(i * part, part)
        return pltpu.make_async_copy(tiles_ref.at[rows], held.at[rows], sems.at[i])

    for i in range(parts):
        fetch(i).start()

    def clear(i, carry):
        count[i] = 0
        return carry

    lax.fori_loop(0, count.shape[0], clear, 0)
    marks[...] = jnp.full(marks.shape, -1.0, jnp.float32)
    side = lax.broadcasted_iota(jnp.int32, marks.shape[1:], 1) // (LANES // CAP)
    for copy in early:
        copy.wait()

    for i in range(parts):
        fetch(i).wait()

        def step(j, carry):
            for k in range(16):
                t = i * part + j * 16 + k
                peer = peers[t]
                rank = count[peer]
                count[peer] = rank + 1
                mark = (rels[t] * blocks + sources[t]).astype(jnp.float32)
                marks[peer] = jnp.where(side == rank, mark, marks[peer])
                message = lax.dot_general(
                    held[t], grad[dest[t]], (((0,), (0,)), ((), ())), preferred_element_type=jnp.float32
                ).astype(jnp.bfloat16)
                made[t, pl.ds(0, block)] = message[:, :LANES]
                made[t, pl.ds(block, block)] = message[:, LANES:]
                rows = pl.ds(pl.multiple_of(rank * size, size), size)
                pltpu.make_async_copy(made.at[t], out_ref.at[peer, rows], out_sem).start()
            return carry

        lax.fori_loop(0, part // 16, step, 0)

    tags[...] = jnp.concatenate([marks[...], marks[...]], axis=1).astype(jnp.bfloat16)
    tag_copy = pltpu.make_async_copy(tags, out_ref.at[:, pl.ds(CAP * size, TAG_ROWS)], sems.at[0])
    tag_copy.start()
    pltpu.make_async_copy(made, out_ref.at[pl.ds(0, tile_count), pl.ds(0, size)], out_sem).wait()
    tag_copy.wait()


def make_messages(tile_dest, peer_list, tile_rel, tile_source, tiles, grad_blocks, dev_count):
    tile_count, block, _ = tiles.shape
    blocks, _, width = grad_blocks.shape
    parts = 8
    numbers = pltpu.SMEM((tile_count,), jnp.int32)

    def kernel(*refs):
        message_kernel(blocks, parts, *refs)

    return pl.pallas_call(
        kernel,
        out_shape=jax.ShapeDtypeStruct((dev_count, CAP * 2 * block + TAG_ROWS, LANES), jnp.bfloat16),
        in_specs=[HBM] * 6,
        out_specs=HBM,
        scratch_shapes=[
            numbers,
            numbers,
            numbers,
            numbers,
            pltpu.SMEM((dev_count,), jnp.int32),
            pltpu.VMEM(grad_blocks.shape, jnp.bfloat16),
            pltpu.VMEM(tiles.shape, jnp.bfloat16),
            pltpu.VMEM((tile_count, 2 * block, LANES), jnp.bfloat16),
            pltpu.VMEM((dev_count, TAG_ROWS // 2, LANES), jnp.float32),
            pltpu.VMEM((dev_count, TAG_ROWS, LANES), jnp.bfloat16),
            pltpu.SemaphoreType.DMA((parts + 5,)),
            pltpu.SemaphoreType.DMA,
        ],
        compiler_params=pltpu.CompilerParams(vmem_limit_bytes=58 * MIB),
        cost_estimate=pl.CostEstimate(
            flops=2 * tile_count * block * block * width,
            bytes_accessed=tile_count * block * (block + width) * 2,
            transcendentals=0,
        ),
    )(tile_dest, peer_list, tile_rel, tile_source, tiles, grad_blocks)


def make_plan(marks, blocks, rel_count):
    senders = marks.shape[0]
    places = plan_places(senders * CAP, rel_count)
    square = (senders, senders)
    row, lane = lax.broadcasted_iota(jnp.int32, square, 0), lax.broadcasted_iota(jnp.int32, square, 1)
    below = (lane < row).astype(jnp.float32)
    ahead = (row < lane).astype(jnp.float32)
    sender = lax.broadcasted_iota(jnp.int32, (senders, 1), 0).astype(jnp.float32)
    batch = jnp.floor(sender * (BATCHES / senders))
    kind_lane = lane.astype(jnp.float32)
    tag = [marks[:, 0:1], marks[:, LANES // CAP : LANES // CAP + 1]]
    rel = [jnp.floor(t * (1.0 / blocks)) for t in tag]
    block_of = [t - r * blocks for t, r in zip(tag, rel)]
    used = [jnp.where((kind_lane == batch * rel_count + r) & (t >= 0), 1.0, 0.0) for t, r in zip(tag, rel)]
    totals = [jnp.sum(u, axis=0, keepdims=True) for u in used]
    before = [jnp.dot(below, u, preferred_element_type=jnp.float32) for u in used]
    before[1] = before[1] + totals[0]
    groups = jnp.floor((totals[0] + totals[1] + (GROUP - 1)) * (1.0 / GROUP))
    first = jnp.dot(jnp.broadcast_to(groups, (8, senders)), ahead, preferred_element_type=jnp.float32)[0:1]
    place = [jnp.sum(u * (b + first * GROUP), axis=1, keepdims=True) for u, b in zip(used, before)]
    place = [jnp.where(t >= 0, p, -1.0) for t, p in zip(tag, place)]
    at_int = lax.broadcasted_iota(jnp.int32, (senders, places), 1)
    at, at_group = at_int.astype(jnp.float32), (at_int // GROUP * GROUP).astype(jnp.float32)
    here = [jnp.where(p == at, 1.0, 0.0) for p in place]
    leads = [jnp.where(p == at_group, 1.0, 0.0) for p in place]

    def gather(hits, values):
        return jnp.sum(hits[0] * values[0] + hits[1] * values[1], axis=0, keepdims=True)

    name = [sender * CAP, sender * CAP + 1]
    message = jnp.where(gather(here, [1.0, 1.0]) > 0, gather(here, name), gather(leads, name))
    source = gather(here, [b - blocks for b in block_of]) + blocks
    relation = gather(leads, rel)
    kind_row = kind_lane[0:1]
    ends = [
        jnp.sum(jnp.where(kind_row < rel_count * (i + 1), groups, 0.0), axis=1, keepdims=True) for i in range(BATCHES)
    ]
    rows = [message, source, relation] + [jnp.broadcast_to(e, (1, places)) for e in ends]
    rows.append(jnp.zeros((8 - len(rows), places), jnp.float32))
    return jnp.concatenate(rows, axis=0).astype(jnp.int32)


def plan_places(slots, rel_count):
    return -(-(-(-slots // GROUP) + rel_count * BATCHES) * GROUP // LANES) * LANES


def take(held, message, block):
    top = pl.multiple_of(lax.shift_left(message & (CAP - 1), (2 * block).bit_length() - 1), 2 * block)
    sender = lax.shift_right_logical(message, CAP.bit_length() - 1)
    return jnp.concatenate([held[sender, pl.ds(top, block)], held[sender, pl.ds(top + block, block)]], axis=1)


def walk_groups(first, end, use):
    def single(g, carry):
        use(g)
        return carry

    def two(j, carry):
        use(first + 2 * j)
        use(first + 2 * j + 1)
        return carry

    pairs = lax.shift_right_logical(end - first, 1)
    lax.fori_loop(0, pairs, two, 0)
    lax.fori_loop(first + 2 * pairs, end, single, 0)


def weight_kernel(
    arrived_ref, feat, grad, core_ref, own_ref, other_ref, plan_ref, turned, acc, plan, plan_sem
):
    kinds, width, _ = acc.shape
    blocks, block, _ = feat.shape
    half = width // 2
    tags = arrived_ref[:, pl.ds(CAP * 2 * block, TAG_ROWS)].astype(jnp.float32)
    plan_ref[...] = make_plan(jnp.max(tags, axis=1), blocks, kinds - 1)
    plan_copy = pltpu.make_async_copy(plan_ref, plan, plan_sem)
    plan_copy.start()
    acc[...] = jnp.zeros_like(acc)
    turned[blocks] = jnp.zeros(turned.shape[1:], turned.dtype)

    def turn(b, carry):
        for k in range(4):
            turned[b * 4 + k] = feat[b * 4 + k].T
        return carry

    lax.fori_loop(0, blocks // 4, turn, 0)

    def root(g, carry):
        left = jnp.concatenate([turned[g * GROUP + k] for k in range(GROUP)], axis=1)
        right = grad[pl.ds(g * GROUP, GROUP)].reshape(GROUP * block, width)
        acc[0] += jnp.dot(left, right, preferred_element_type=jnp.float32)
        return carry

    lax.fori_loop(0, blocks // GROUP, root, 0)
    plan_copy.wait()

    def use(g):
        left = jnp.concatenate([turned[plan[1, g * GROUP + k]] for k in range(GROUP)], axis=1)
        right = jnp.concatenate([take(arrived_ref, plan[0, g * GROUP + k], block) for k in range(GROUP)], axis=0)
        acc[1 + plan[2, g * GROUP]] += jnp.dot(left, right, preferred_element_type=jnp.float32)

    walk_groups(0, plan[2 + BATCHES, 0], use)

    def split(first, second):
        for ref, lanes in ((first, pl.ds(0, half)), (second, pl.ds(half, half))):
            for r in range(kinds):
                ref[pl.ds(r * width, width)] = acc[r, :, lanes]

    @pl.when(core_ref[0] == 0)
    def _():
        split(own_ref, other_ref)

    @pl.when(core_ref[0] != 0)
    def _():
        split(other_ref, own_ref)


def feat_kernel(plan_ref, arrived_ref, grad_ref, root_ref, weight_ref, out_ref, held, acc, sems):
    blocks, block, width = out_ref.shape
    senders = held.shape[0] // BATCHES

    def copy(i):
        part = pl.ds(i * senders, senders)
        return pltpu.make_async_copy(arrived_ref.at[part, pl.ds(0, held.shape[1])], held.at[part], sems.at[i])

    for i in range(BATCHES):
        copy(i).start()
    acc[blocks] = jnp.zeros(acc.shape[1:], jnp.float32)
    across = (((1,), (1,)), ((), ()))

    def base(g, carry):
        rows = grad_ref[pl.ds(g * GROUP, GROUP)].reshape(GROUP * block, width)
        part = lax.dot_general(rows, root_ref[...], across, preferred_element_type=jnp.float32)
        acc[pl.ds(g * GROUP, GROUP)] = part.reshape(GROUP, block, width)
        return carry

    lax.fori_loop(0, blocks // GROUP, base, 0)

    def use(g):
        rows = jnp.concatenate([take(held, plan_ref[0, g * GROUP + k], block) for k in range(GROUP)], axis=0)
        part = lax.dot_general(rows, weight_ref[plan_ref[2, g * GROUP]], across, preferred_element_type=jnp.float32)
        for k in range(GROUP):
            acc[plan_ref[1, g * GROUP + k]] += part[k * block : (k + 1) * block]

    def batch(i, first):
        copy(i).wait()
        end = plan_ref[3 + i, 0]
        walk_groups(first, end, use)
        return end

    lax.fori_loop(0, BATCHES, batch, 0)
    out_ref[...] = acc[pl.ds(0, blocks)].astype(jnp.bfloat16)


def share_kernel(scale, spread_ref, share_ref):
    share = (jnp.sum(spread_ref[...], axis=0) * scale).astype(jnp.bfloat16)
    for i in range(share_ref.shape[0]):
        share_ref[i] = share


def shards(features, out_grad, rel_weight, root_weight, tiles, tile_dest, tile_peer, tile_source, tile_rel):
    dev_count = lax.axis_size(AXES)
    chips = lax.axis_size(CHIPS)
    core = lax.axis_index("c")
    block = tiles.shape[1]
    width = features.shape[1]
    rel_count = rel_weight.shape[0]
    blocks = features.shape[0] // block
    slots = dev_count * CAP
    scale = 1.0 / math.sqrt(features.shape[0] * dev_count)
    grad_blocks = out_grad.reshape(blocks, block, width)

    outgoing = make_messages(tile_dest, tile_peer[:, 0], tile_rel, tile_source, tiles, grad_blocks, dev_count)
    outgoing, core = lax.optimization_barrier((outgoing, core[None].astype(jnp.int32)))
    arrived = lax.all_to_all(outgoing, AXES, split_axis=0, concat_axis=0, tiled=True)

    dma = pltpu.SemaphoreType.DMA
    cost = pl.CostEstimate(
        flops=slots * block * width * width, bytes_accessed=slots * block * width * 2, transcendentals=0
    )
    half_rows = (1 + rel_count) * width
    half = jax.ShapeDtypeStruct((half_rows, width // 2), jnp.float32)
    plan_type = jax.ShapeDtypeStruct((8, plan_places(slots, rel_count)), jnp.int32)
    own, other, plan = pl.pallas_call(
        weight_kernel,
        out_shape=(half, half, plan_type),
        in_specs=[VMEM] * 3 + [SMEM],
        out_specs=(VMEM, VMEM, VMEM),
        scratch_shapes=[
            pltpu.VMEM((blocks + 1, width, block), jnp.bfloat16),
            pltpu.VMEM((1 + rel_count, width, width), jnp.float32),
            pltpu.SMEM(plan_type.shape, jnp.int32),
            dma,
        ],
        compiler_params=pltpu.CompilerParams(vmem_limit_bytes=16 * MIB),
        cost_estimate=cost,
    )(arrived, features.reshape(blocks, block, width), grad_blocks, core)

    swap = [(0, 1), (1, 0)]
    own = own + lax.ppermute(other, "c", swap)
    own, plan = lax.optimization_barrier((own, plan))
    grad_feat = pl.pallas_call(
        feat_kernel,
        out_shape=jax.ShapeDtypeStruct(grad_blocks.shape, jnp.bfloat16),
        in_specs=[SMEM, HBM, VMEM, VMEM, VMEM],
        out_specs=VMEM,
        scratch_shapes=[
            pltpu.VMEM((dev_count, CAP * 2 * block, LANES), jnp.bfloat16),
            pltpu.VMEM((blocks + 1, block, width), jnp.float32),
            dma((BATCHES,)),
        ],
        compiler_params=pltpu.CompilerParams(vmem_limit_bytes=44 * MIB),
        cost_estimate=cost,
    )(plan, arrived, grad_blocks, root_weight, rel_weight)
    shape = (chips, half_rows // chips, width // 2)
    spread = lax.all_to_all(own.reshape(shape), CHIPS, 0, 0, tiled=True)
    spread, grad_feat = lax.optimization_barrier((spread, grad_feat))
    share = pl.pallas_call(
        functools.partial(share_kernel, scale),
        out_shape=jax.ShapeDtypeStruct(shape, jnp.bfloat16),
        in_specs=[VMEM],
        out_specs=VMEM,
        compiler_params=pltpu.CompilerParams(vmem_limit_bytes=8 * MIB),
    )(spread)
    own = lax.all_to_all(share, CHIPS, 0, 0, tiled=True).reshape(half.shape)
    other = lax.ppermute(own, "c", swap)
    core = core[0]
    left = jnp.where(core == 0, own, other).astype(jnp.float32)
    right = jnp.where(core == 0, other, own).astype(jnp.float32)
    grad_weights = jnp.concatenate([left, right], axis=1).reshape(1 + rel_count, width, width)
    return grad_feat.reshape(features.shape), grad_weights


def solution(mesh):
    sizes = (4, 4, 4, 2)
    fine = Mesh(mesh.devices.reshape(sizes), AXES)
    return jax.shard_map(
        shards,
        mesh=fine,
        in_specs=(
            P(AXES, None),
            P(AXES, None),
            P(),
            P(),
            P(AXES, None, None),
            P(AXES),
            P(AXES, None),
            P(AXES),
            P(AXES),
        ),
        out_specs=(P(AXES, None), P()),
        check_vma=False,
    )
```

```python
import functools
import math

import jax
import jax.numpy as jnp
from jax import lax
from jax.experimental import pallas as pl
from jax.experimental.pallas import tpu as pltpu
from jax.sharding import Mesh
from jax.sharding import PartitionSpec as P

AXES = ("z", "y", "x", "c")
CHIPS = ("z", "y", "x")
VMEM = pl.BlockSpec(memory_space=pltpu.VMEM)
HBM = pl.BlockSpec(memory_space=pltpu.HBM)
SMEM = pl.BlockSpec(memory_space=pltpu.SMEM)
MIB = 1024 * 1024
GROUP = 8
LANES = 128
TAG_ROWS = 16
FIELD = 16


def message_kernel(
    blocks, parts, dest_any, peer_any, rel_any, source_any, tiles_ref, grad_any, out_ref, later_ref,
    dest, peers, rels, sources, count, seconds, flag, grad, held, made, marks, tags, sems, out_sem,
):
    tile_count, block, _ = tiles_ref.shape
    part = tile_count // parts
    pairs = ((dest_any, dest), (peer_any, peers), (rel_any, rels), (source_any, sources), (grad_any, grad))
    early = [pltpu.make_async_copy(src, dst, sems.at[parts + i]) for i, (src, dst) in enumerate(pairs)]
    for copy in early:
        copy.start()

    def fetch(i):
        rows = pl.ds(i * part, part)
        return pltpu.make_async_copy(tiles_ref.at[rows], held.at[rows], sems.at[i])

    for i in range(parts):
        fetch(i).start()

    def clear(i, carry):
        count[2 * i] = 0
        count[2 * i + 1] = 0
        seconds[i] = 0
        return carry

    lax.fori_loop(0, seconds.shape[0], clear, 0)
    flag[0] = 0
    marks[...] = jnp.full(marks.shape, -1.0, jnp.float32)
    field = lax.broadcasted_iota(jnp.int32, marks.shape[1:], 1) // FIELD
    left, right = pl.ds(0, block), pl.ds(block, block)
    half = pl.ds(2 * block, block)

    def send(src, dst):
        pltpu.make_async_copy(src, dst, out_sem).start()

    def place(t, carry):
        peer = peers[t]
        rank = count[peer]
        count[peer] = rank + 1
        mark = (rels[t] * blocks + sources[t]).astype(jnp.float32)

        @pl.when(rank == 0)
        def _():
            marks[peer] = jnp.where(field == 0, mark, marks[peer])
            send(made.at[t], out_ref.at[peer, pl.ds(0, 2 * block)])

        @pl.when(rank != 0)
        def _():
            chip = lax.shift_right_logical(peer, 1)
            later = seconds[chip]
            seconds[chip] = later + 1
            core = (peer & 1).astype(jnp.float32)
            first = 2 * chip
            for side in range(2):
                old = marks[first + side]
                old = jnp.where(field == 2 + 2 * later, core, old)
                marks[first + side] = jnp.where(field == 1 + 2 * later, mark, old)

            @pl.when(later == 0)
            def _():
                send(made.at[t, left], out_ref.at[first, half])
                send(made.at[t, right], out_ref.at[first + 1, half])

            @pl.when(later != 0)
            def _():
                flag[0] = 1
                send(made.at[t, left], later_ref.at[first])
                send(made.at[t, right], later_ref.at[first + 1])

        return carry

    for copy in early:
        copy.wait()

    for i in range(parts):
        fetch(i).wait()
        for t in range(i * part, (i + 1) * part):
            message = lax.dot_general(
                held[t], grad[dest[t]], (((0,), (0,)), ((), ())), preferred_element_type=jnp.float32
            ).astype(jnp.bfloat16)
            made[t, left] = message[:, :LANES]
            made[t, right] = message[:, LANES:]
        lax.fori_loop(i * part, (i + 1) * part, place, 0)

    any_later = flag[0].astype(jnp.float32)
    all_marks = jnp.where(field[None] == 5, any_later, marks[...])
    tags[...] = jnp.concatenate([all_marks, all_marks], axis=1).astype(jnp.bfloat16)
    tag_copy = pltpu.make_async_copy(tags, out_ref.at[:, pl.ds(3 * block, TAG_ROWS)], sems.at[0])
    tag_copy.start()
    pltpu.make_async_copy(made, out_ref.at[pl.ds(0, tile_count), pl.ds(0, 2 * block)], out_sem).wait()
    tag_copy.wait()


def make_messages(tile_dest, peer_list, tile_rel, tile_source, tiles, grad_blocks, dev_count):
    tile_count, block, _ = tiles.shape
    blocks, _, width = grad_blocks.shape
    parts = 8
    numbers = pltpu.SMEM((tile_count,), jnp.int32)

    def kernel(*refs):
        message_kernel(blocks, parts, *refs)

    return pl.pallas_call(
        kernel,
        out_shape=(
            jax.ShapeDtypeStruct((dev_count, 3 * block + TAG_ROWS, LANES), jnp.bfloat16),
            jax.ShapeDtypeStruct((dev_count, block, LANES), jnp.bfloat16),
        ),
        in_specs=[HBM] * 6,
        out_specs=(HBM, HBM),
        scratch_shapes=[
            numbers,
            numbers,
            numbers,
            numbers,
            pltpu.SMEM((dev_count,), jnp.int32),
            pltpu.SMEM((dev_count // 2,), jnp.int32),
            pltpu.SMEM((1,), jnp.int32),
            pltpu.VMEM(grad_blocks.shape, jnp.bfloat16),
            pltpu.VMEM(tiles.shape, jnp.bfloat16),
            pltpu.VMEM((tile_count, 2 * block, LANES), jnp.bfloat16),
            pltpu.VMEM((dev_count, TAG_ROWS // 2, LANES), jnp.float32),
            pltpu.VMEM((dev_count, TAG_ROWS, LANES), jnp.bfloat16),
            pltpu.SemaphoreType.DMA((parts + 5,)),
            pltpu.SemaphoreType.DMA,
        ],
        compiler_params=pltpu.CompilerParams(vmem_limit_bytes=58 * MIB),
        cost_estimate=pl.CostEstimate(
            flops=2 * tile_count * block * block * width,
            bytes_accessed=tile_count * block * (block + width) * 2,
            transcendentals=0,
        ),
    )(tile_dest, peer_list, tile_rel, tile_source, tiles, grad_blocks)


def plan_places(senders, rel_count):
    return -(-(senders + (GROUP - 1) * rel_count) // LANES) * LANES


def make_plan(tag, shift, blocks, rel_count):
    senders = tag.shape[0]
    places = plan_places(senders, rel_count)
    square = (senders, senders)
    row, lane = lax.broadcasted_iota(jnp.int32, square, 0), lax.broadcasted_iota(jnp.int32, square, 1)
    below = (lane < row).astype(jnp.float32)
    ahead = (row < lane).astype(jnp.float32)
    sender = lax.broadcasted_iota(jnp.int32, (senders, 1), 0).astype(jnp.float32)
    rel = jnp.floor(tag * (1.0 / blocks))
    block_of = tag - rel * blocks + shift
    used = jnp.where((lane.astype(jnp.float32) == rel) & (tag >= 0), 1.0, 0.0)
    totals = jnp.sum(used, axis=0, keepdims=True)
    before = jnp.dot(below, used, preferred_element_type=jnp.float32)
    groups = jnp.floor((totals + (GROUP - 1)) * (1.0 / GROUP))
    first = jnp.dot(jnp.broadcast_to(groups, (8, senders)), ahead, preferred_element_type=jnp.float32)[0:1]
    place = jnp.sum(used * (before + first * GROUP), axis=1, keepdims=True)
    place = jnp.where(tag >= 0, place, -1.0)
    at = lax.broadcasted_iota(jnp.int32, (senders, places), 1)
    here = jnp.where(place == at.astype(jnp.float32), 1.0, 0.0)
    leads = jnp.where(place == (at // GROUP * GROUP).astype(jnp.float32), 1.0, 0.0)

    def gather(hits, values):
        return jnp.sum(hits * values, axis=0, keepdims=True)

    message = jnp.where(gather(here, 1.0) > 0, gather(here, sender), gather(leads, sender))
    source = gather(here, block_of - 2 * blocks) + 2 * blocks
    total = jnp.broadcast_to(jnp.sum(groups, axis=1, keepdims=True), (1, places))
    return [message, source, gather(leads, rel), total]


def make_plans(tags, core, blocks, rel_count):
    def column(i):
        return tags[:, i * FIELD : i * FIELD + 1]

    rows = make_plan(column(0), jnp.zeros_like(column(0)), blocks, rel_count)
    for i in (1, 3):
        rows += make_plan(column(i), jnp.where(column(i + 1) == core, 0.0, float(blocks)), blocks, rel_count)
    any_later = jnp.max(jnp.where(column(5) > 0, 1.0, 0.0), axis=0, keepdims=True)
    rows += [jnp.broadcast_to(any_later, rows[0].shape)] * 4
    return jnp.concatenate(rows, axis=0).astype(jnp.int32)


def walk_groups(end, use):
    def single(g, carry):
        use(g)
        return carry

    def two(j, carry):
        use(2 * j)
        use(2 * j + 1)
        return carry

    pairs = lax.shift_right_logical(end, 1)
    lax.fori_loop(0, pairs, two, 0)
    lax.fori_loop(2 * pairs, end, single, 0)


def whole(ref, sender, block):
    return jnp.concatenate([ref[sender, pl.ds(0, block)], ref[sender, pl.ds(block, block)]], axis=1)


def turn_blocks(feat, mate, turned):
    blocks = feat.shape[0]
    turned[2 * blocks] = jnp.zeros(turned.shape[1:], turned.dtype)

    def turn(b, carry):
        for k in range(4):
            turned[b * 4 + k] = feat[b * 4 + k].T
            turned[blocks + b * 4 + k] = mate[b * 4 + k].T
        return carry

    lax.fori_loop(0, blocks // 4, turn, 0)


def weight_kernel(
    arrived_ref, feat, mate, grad, core_ref, own_ref, other_ref, plan_ref, turned, acc, part, plan, plan_sem
):
    kinds, width, _ = acc.shape
    blocks, block, _ = feat.shape
    half = width // 2
    tags = jnp.max(arrived_ref[:, pl.ds(3 * block, TAG_ROWS)].astype(jnp.float32), axis=1)
    plan_ref[...] = make_plans(tags, core_ref[0].astype(jnp.float32), blocks, kinds - 1)
    plan_copy = pltpu.make_async_copy(plan_ref, plan, plan_sem)
    plan_copy.start()
    acc[...] = jnp.zeros_like(acc)
    part[...] = jnp.zeros_like(part)
    turn_blocks(feat, mate, turned)

    def root(g, carry):
        left = jnp.concatenate([turned[g * GROUP + k] for k in range(GROUP)], axis=1)
        right = grad[pl.ds(g * GROUP, GROUP)].reshape(GROUP * block, width)
        acc[0] += jnp.dot(left, right, preferred_element_type=jnp.float32)
        return carry

    lax.fori_loop(0, blocks // GROUP, root, 0)
    plan_copy.wait()

    def lefts(g, row):
        return jnp.concatenate([turned[plan[row + 1, g * GROUP + k]] for k in range(GROUP)], axis=1)

    def use(g):
        right = jnp.concatenate([whole(arrived_ref, plan[0, g * GROUP + k], block) for k in range(GROUP)], axis=0)
        acc[1 + plan[2, g * GROUP]] += jnp.dot(lefts(g, 0), right, preferred_element_type=jnp.float32)

    def use_half(g):
        right = jnp.concatenate(
            [arrived_ref[plan[4, g * GROUP + k], pl.ds(2 * block, block)] for k in range(GROUP)], axis=0
        )
        part[plan[6, g * GROUP]] += jnp.dot(lefts(g, 4), right, preferred_element_type=jnp.float32)

    walk_groups(plan[3, 0], use)
    walk_groups(plan[7, 0], use_half)

    def split(own, other):
        for r in range(kinds):
            rows = pl.ds(r * width, width)
            own_ref[rows] = acc[r, :, own] + part[r - 1] if r else acc[r, :, own]
            other_ref[rows] = acc[r, :, other]

    first, second = pl.ds(0, half), pl.ds(half, half)

    @pl.when(core_ref[0] == 0)
    def _():
        split(first, second)

    @pl.when(core_ref[0] != 0)
    def _():
        split(second, first)


def later_kernel(plan, later, feat, mate, before_ref, own_ref, turned):
    width = feat.shape[2]
    turn_blocks(feat, mate, turned)
    own_ref[...] = before_ref[...]

    def use(g):
        left = jnp.concatenate([turned[plan[9, g * GROUP + k]] for k in range(GROUP)], axis=1)
        right = jnp.concatenate([later[plan[8, g * GROUP + k]] for k in range(GROUP)], axis=0)
        rows = pl.ds(pl.multiple_of((1 + plan[10, g * GROUP]) * width, width), width)
        own_ref[rows] += jnp.dot(left, right, preferred_element_type=jnp.float32)

    walk_groups(plan[11, 0], use)


def feat_kernel(
    plan_ref, core_ref, arrived_ref, later_any, grad_ref, root_ref, weight_ref, own_any, mate_ref,
    held, halves, later, acc, sems, later_sem,
):
    blocks, block, width = mate_ref.shape
    half = width // 2
    whole_copy = pltpu.make_async_copy(arrived_ref.at[:, pl.ds(0, 2 * block)], held, sems.at[0])
    half_copy = pltpu.make_async_copy(arrived_ref.at[:, pl.ds(2 * block, block)], halves, sems.at[1])
    whole_copy.start()
    half_copy.start()
    acc[pl.ds(blocks, blocks + 1)] = jnp.zeros((blocks + 1, block, width), jnp.float32)
    across = (((1,), (1,)), ((), ()))

    def base(g, carry):
        rows = grad_ref[pl.ds(g * GROUP, GROUP)].reshape(GROUP * block, width)
        part = lax.dot_general(rows, root_ref[...], across, preferred_element_type=jnp.float32)
        acc[pl.ds(g * GROUP, GROUP)] = part.reshape(GROUP, block, width)
        return carry

    lax.fori_loop(0, blocks // GROUP, base, 0)
    whole_copy.wait()

    def add(g, row, part):
        for k in range(GROUP):
            acc[plan_ref[row + 1, g * GROUP + k]] += part[k * block : (k + 1) * block]

    def use(g):
        rows = jnp.concatenate([whole(held, plan_ref[0, g * GROUP + k], block) for k in range(GROUP)], axis=0)
        add(g, 0, lax.dot_general(rows, weight_ref[plan_ref[2, g * GROUP]], across, preferred_element_type=jnp.float32))

    def from_half(ref, row):
        lanes = pl.ds(pl.multiple_of(core_ref[0] * half, half), half)

        def use_half(g):
            rows = jnp.concatenate([ref[plan_ref[row, g * GROUP + k]] for k in range(GROUP)], axis=0)
            weight = weight_ref[plan_ref[row + 2, g * GROUP], :, lanes]
            add(g, row, lax.dot_general(rows, weight, across, preferred_element_type=jnp.float32))

        return use_half

    walk_groups(plan_ref[3, 0], use)
    half_copy.wait()
    walk_groups(plan_ref[7, 0], from_half(halves, 4))

    @pl.when(plan_ref[11, 0] > 0)
    def _():
        copy = pltpu.make_async_copy(later_any, later, later_sem)
        copy.start()
        copy.wait()
        walk_groups(plan_ref[11, 0], from_half(later, 8))

    own_copy = pltpu.make_async_copy(acc.at[pl.ds(0, blocks)], own_any, later_sem)
    own_copy.start()
    mate_ref[...] = acc[pl.ds(blocks, blocks)].astype(jnp.bfloat16)
    own_copy.wait()


def share_kernel(scale, spread_ref, share_ref):
    share = (jnp.sum(spread_ref[...], axis=0) * scale).astype(jnp.bfloat16)
    for i in range(share_ref.shape[0]):
        share_ref[i] = share


def shards(features, out_grad, rel_weight, root_weight, tiles, tile_dest, tile_peer, tile_source, tile_rel):
    dev_count = lax.axis_size(AXES)
    chips = lax.axis_size(CHIPS)
    core = lax.axis_index("c")
    block = tiles.shape[1]
    width = features.shape[1]
    rel_count = rel_weight.shape[0]
    blocks = features.shape[0] // block
    scale = 1.0 / math.sqrt(features.shape[0] * dev_count)
    swap = [(0, 1), (1, 0)]
    grad_blocks = out_grad.reshape(blocks, block, width)
    feat_blocks = features.reshape(blocks, block, width)

    mate_blocks = lax.ppermute(feat_blocks, "c", swap)
    outgoing, later = make_messages(tile_dest, tile_peer[:, 0], tile_rel, tile_source, tiles, grad_blocks, dev_count)
    outgoing, later, core, mate_blocks = lax.optimization_barrier(
        (outgoing, later, core[None].astype(jnp.int32), mate_blocks)
    )

    def exchange(array):
        return lax.all_to_all(array, AXES, split_axis=0, concat_axis=0, tiled=True)

    arrived = exchange(outgoing)

    dma = pltpu.SemaphoreType.DMA
    cost = pl.CostEstimate(
        flops=2 * dev_count * block * width * width, bytes_accessed=dev_count * block * width * 3, transcendentals=0
    )
    half_rows = (1 + rel_count) * width
    half = jax.ShapeDtypeStruct((half_rows, width // 2), jnp.float32)
    turned = pltpu.VMEM((2 * blocks + 1, width, block), jnp.bfloat16)
    plan_type = jax.ShapeDtypeStruct((16, plan_places(dev_count, rel_count)), jnp.int32)
    own, other, plan = pl.pallas_call(
        weight_kernel,
        out_shape=(half, half, plan_type),
        in_specs=[VMEM, VMEM, VMEM, VMEM, SMEM],
        out_specs=(VMEM, VMEM, VMEM),
        scratch_shapes=[
            turned,
            pltpu.VMEM((1 + rel_count, width, width), jnp.float32),
            pltpu.VMEM((rel_count, width, width // 2), jnp.float32),
            pltpu.SMEM(plan_type.shape, jnp.int32),
            dma,
        ],
        compiler_params=pltpu.CompilerParams(vmem_limit_bytes=20 * MIB),
        cost_estimate=cost,
    )(arrived, feat_blocks, mate_blocks, grad_blocks, core)

    def take_later(later, own):
        later = exchange(later)
        own = pl.pallas_call(
            later_kernel,
            out_shape=half,
            in_specs=[SMEM] + [VMEM] * 4,
            out_specs=VMEM,
            scratch_shapes=[turned],
            compiler_params=pltpu.CompilerParams(vmem_limit_bytes=24 * MIB),
        )(plan, later, feat_blocks, mate_blocks, own)
        return later, own

    later, own = lax.cond(plan[12, 0] > 0, take_later, lambda later, own: (later, own), later, own)

    own = own + lax.ppermute(other, "c", swap)
    own, plan = lax.optimization_barrier((own, plan))
    own_feat, mate_feat = pl.pallas_call(
        feat_kernel,
        out_shape=(
            jax.ShapeDtypeStruct(grad_blocks.shape, jnp.float32),
            jax.ShapeDtypeStruct(grad_blocks.shape, jnp.bfloat16),
        ),
        in_specs=[SMEM, SMEM, HBM, HBM, VMEM, VMEM, VMEM],
        out_specs=(HBM, VMEM),
        scratch_shapes=[
            pltpu.VMEM((dev_count, 2 * block, LANES), jnp.bfloat16),
            pltpu.VMEM((dev_count, block, LANES), jnp.bfloat16),
            pltpu.VMEM((dev_count, block, LANES), jnp.bfloat16),
            pltpu.VMEM((2 * blocks + 1, block, width), jnp.float32),
            dma((2,)),
            dma,
        ],
        compiler_params=pltpu.CompilerParams(vmem_limit_bytes=49 * MIB),
        cost_estimate=cost,
    )(plan, core, arrived, later, grad_blocks, root_weight, rel_weight)
    shape = (chips, half_rows // chips, width // 2)
    spread = lax.all_to_all(own.reshape(shape), CHIPS, 0, 0, tiled=True)
    spread, own_feat, mate_feat = lax.optimization_barrier((spread, own_feat, mate_feat))
    share = pl.pallas_call(
        functools.partial(share_kernel, scale),
        out_shape=jax.ShapeDtypeStruct(shape, jnp.bfloat16),
        in_specs=[VMEM],
        out_specs=VMEM,
        compiler_params=pltpu.CompilerParams(vmem_limit_bytes=8 * MIB),
    )(spread)
    own = lax.all_to_all(share, CHIPS, 0, 0, tiled=True).reshape(half.shape)
    grad_feat = (own_feat + lax.ppermute(mate_feat, "c", swap).astype(jnp.float32)).astype(jnp.bfloat16)
    own, grad_feat = lax.optimization_barrier((own, grad_feat))
    other = lax.ppermute(own, "c", swap)
    core = core[0]
    left = jnp.where(core == 0, own, other).astype(jnp.float32)
    right = jnp.where(core == 0, other, own).astype(jnp.float32)
    grad_weights = jnp.concatenate([left, right], axis=1).reshape(1 + rel_count, width, width)
    return grad_feat.reshape(features.shape), grad_weights


def solution(mesh):
    sizes = (4, 4, 4, 2)
    fine = Mesh(mesh.devices.reshape(sizes), AXES)
    return jax.shard_map(
        shards,
        mesh=fine,
        in_specs=(
            P(AXES, None),
            P(AXES, None),
            P(),
            P(),
            P(AXES, None, None),
            P(AXES),
            P(AXES, None),
            P(AXES),
            P(AXES),
        ),
        out_specs=(P(AXES, None), P()),
        check_vma=False,
    )
```

```python
import functools
import math

import jax
import jax.numpy as jnp
from jax import lax
from jax.experimental import pallas as pl
from jax.experimental.pallas import tpu as pltpu
from jax.sharding import Mesh
from jax.sharding import PartitionSpec as P

AXES = ("z", "y", "x", "c")
CHIPS = ("z", "y", "x")
VMEM = pl.BlockSpec(memory_space=pltpu.VMEM)
HBM = pl.BlockSpec(memory_space=pltpu.HBM)
SMEM = pl.BlockSpec(memory_space=pltpu.SMEM)
MIB = 1024 * 1024
GROUP = 8
LANES = 128
TAG_ROWS = 16
FIELD = 16


def message_kernel(
    blocks, parts, dest_any, peer_any, rel_any, source_any, tiles_ref, grad_any, out_ref, later_ref,
    dest, peers, rels, sources, count, seconds, flag, grad, held, made, marks, tags, sems, out_sem,
):
    tile_count, block, _ = tiles_ref.shape
    part = tile_count // parts
    pairs = ((dest_any, dest), (peer_any, peers), (rel_any, rels), (source_any, sources), (grad_any, grad))
    early = [pltpu.make_async_copy(src, dst, sems.at[parts + i]) for i, (src, dst) in enumerate(pairs)]
    for copy in early:
        copy.start()

    def fetch(i):
        rows = pl.ds(i * part, part)
        return pltpu.make_async_copy(tiles_ref.at[rows], held.at[rows], sems.at[i])

    for i in range(parts):
        fetch(i).start()

    def clear(i, carry):
        count[2 * i] = 0
        count[2 * i + 1] = 0
        seconds[i] = 0
        return carry

    lax.fori_loop(0, seconds.shape[0], clear, 0)
    flag[0] = 0
    marks[...] = jnp.full(marks.shape, -1.0, jnp.float32)
    field = lax.broadcasted_iota(jnp.int32, marks.shape[1:], 1) // FIELD
    left, right = pl.ds(0, block), pl.ds(block, block)
    half = pl.ds(2 * block, block)

    def send(src, dst):
        pltpu.make_async_copy(src, dst, out_sem).start()

    def place(t, carry):
        peer = peers[t]
        rank = count[peer]
        count[peer] = rank + 1
        mark = (rels[t] * blocks + sources[t]).astype(jnp.float32)

        @pl.when(rank == 0)
        def _():
            marks[peer] = jnp.where(field == 0, mark, marks[peer])
            send(made.at[t], out_ref.at[peer, pl.ds(0, 2 * block)])

        @pl.when(rank != 0)
        def _():
            chip = lax.shift_right_logical(peer, 1)
            later = seconds[chip]
            seconds[chip] = later + 1
            core = (peer & 1).astype(jnp.float32)
            first = 2 * chip
            for side in range(2):
                old = marks[first + side]
                old = jnp.where(field == 2 + 2 * later, core, old)
                marks[first + side] = jnp.where(field == 1 + 2 * later, mark, old)

            @pl.when(later == 0)
            def _():
                send(made.at[t, left], out_ref.at[first, half])
                send(made.at[t, right], out_ref.at[first + 1, half])

            @pl.when(later != 0)
            def _():
                flag[0] = 1
                send(made.at[t, left], later_ref.at[first])
                send(made.at[t, right], later_ref.at[first + 1])

        return carry

    for copy in early:
        copy.wait()

    for i in range(parts):
        fetch(i).wait()
        for t in range(i * part, (i + 1) * part):
            message = lax.dot_general(
                held[t], grad[dest[t]], (((0,), (0,)), ((), ())), preferred_element_type=jnp.float32
            ).astype(jnp.bfloat16)
            made[t, left] = message[:, :LANES]
            made[t, right] = message[:, LANES:]
        lax.fori_loop(i * part, (i + 1) * part, place, 0)

    any_later = flag[0].astype(jnp.float32)
    all_marks = jnp.where(field[None] == 5, any_later, marks[...])
    tags[...] = jnp.concatenate([all_marks, all_marks], axis=1).astype(jnp.bfloat16)
    tag_copy = pltpu.make_async_copy(tags, out_ref.at[:, pl.ds(3 * block, TAG_ROWS)], sems.at[0])
    tag_copy.start()
    pltpu.make_async_copy(made, out_ref.at[pl.ds(0, tile_count), pl.ds(0, 2 * block)], out_sem).wait()
    tag_copy.wait()


def make_messages(tile_dest, peer_list, tile_rel, tile_source, tiles, grad_blocks, dev_count):
    tile_count, block, _ = tiles.shape
    blocks, _, width = grad_blocks.shape
    parts = 8
    numbers = pltpu.SMEM((tile_count,), jnp.int32)

    def kernel(*refs):
        message_kernel(blocks, parts, *refs)

    return pl.pallas_call(
        kernel,
        out_shape=(
            jax.ShapeDtypeStruct((dev_count, 3 * block + TAG_ROWS, LANES), jnp.bfloat16),
            jax.ShapeDtypeStruct((dev_count, block, LANES), jnp.bfloat16),
        ),
        in_specs=[HBM] * 6,
        out_specs=(HBM, HBM),
        scratch_shapes=[
            numbers,
            numbers,
            numbers,
            numbers,
            pltpu.SMEM((dev_count,), jnp.int32),
            pltpu.SMEM((dev_count // 2,), jnp.int32),
            pltpu.SMEM((1,), jnp.int32),
            pltpu.VMEM(grad_blocks.shape, jnp.bfloat16),
            pltpu.VMEM(tiles.shape, jnp.bfloat16),
            pltpu.VMEM((tile_count, 2 * block, LANES), jnp.bfloat16),
            pltpu.VMEM((dev_count, TAG_ROWS // 2, LANES), jnp.float32),
            pltpu.VMEM((dev_count, TAG_ROWS, LANES), jnp.bfloat16),
            pltpu.SemaphoreType.DMA((parts + 5,)),
            pltpu.SemaphoreType.DMA,
        ],
        compiler_params=pltpu.CompilerParams(vmem_limit_bytes=58 * MIB),
        cost_estimate=pl.CostEstimate(
            flops=2 * tile_count * block * block * width,
            bytes_accessed=tile_count * block * (block + width) * 2,
            transcendentals=0,
        ),
    )(tile_dest, peer_list, tile_rel, tile_source, tiles, grad_blocks)


def plan_places(senders, rel_count):
    return -(-(senders + (GROUP - 1) * rel_count) // LANES) * LANES


def make_plans(tags, core, blocks, rel_count):
    senders = tags.shape[0]
    places = plan_places(senders, rel_count)
    wide = 1 << (rel_count - 1).bit_length()
    square = (senders, senders)
    row, lane = lax.broadcasted_iota(jnp.int32, square, 0), lax.broadcasted_iota(jnp.int32, square, 1)
    lane_set, lane_rel = lane // wide, (lane % wide).astype(jnp.float32)
    below = (lane < row).astype(jnp.float32).astype(jnp.bfloat16)
    ahead = ((row < lane) & (row // wide == lane_set)).astype(jnp.float32).astype(jnp.bfloat16)
    sender = row.astype(jnp.float32)
    at = lax.broadcasted_iota(jnp.int32, (senders, places), 1)
    at, lead = at.astype(jnp.float32), (at // GROUP * GROUP).astype(jnp.float32)
    down = (((0,), (0,)), ((), ()))

    def column(i):
        return tags[:, i * FIELD : i * FIELD + 1]

    tag = [column(0), column(1), column(3)]
    shift = [0.0] + [jnp.where(column(i) == core, 0.0, float(blocks)) for i in (2, 4)]
    rel = [jnp.floor(t * (1.0 / blocks)) for t in tag]
    used = [jnp.where((lane_set == q) & (lane_rel == r) & (t >= 0), 1.0, 0.0) for q, (t, r) in enumerate(zip(tag, rel))]
    every = used[0] + used[1] + used[2]
    before = jnp.dot(below, every.astype(jnp.bfloat16), preferred_element_type=jnp.float32)
    groups = jnp.floor((jnp.sum(every, axis=0, keepdims=True) + (GROUP - 1)) * (1.0 / GROUP))
    first = jnp.dot(
        jnp.broadcast_to(groups, (TAG_ROWS, senders)).astype(jnp.bfloat16), ahead, preferred_element_type=jnp.float32
    )[0:1]
    spot = before + first * GROUP
    rows = []
    for q in range(3):
        place = jnp.where(tag[q] >= 0, jnp.sum(used[q] * spot, axis=1, keepdims=True), -1.0)
        here = jnp.where(place == at, 1.0, 0.0).astype(jnp.bfloat16)
        leads = jnp.where(place == lead, 1.0, 0.0).astype(jnp.bfloat16)
        source = tag[q] - rel[q] * blocks + shift[q] - 2 * blocks
        named = jnp.where(lane == 0, 1.0, jnp.where(lane == 1, sender, jnp.where(lane == 2, source, rel[q])))
        named = named.astype(jnp.bfloat16)
        own = lax.dot_general(named, here, down, preferred_element_type=jnp.float32)
        led = lax.dot_general(named, leads, down, preferred_element_type=jnp.float32)
        total = jnp.sum(jnp.where(lane_set[0:1] == q, groups, 0.0), axis=1, keepdims=True)
        rows += [jnp.where(own[0:1] > 0, own[1:2], led[1:2]), own[2:3] + 2 * blocks, led[3:4]]
        rows.append(jnp.broadcast_to(total, (1, places)))
    any_later = jnp.max(jnp.where(column(5) > 0, 1.0, 0.0), axis=0, keepdims=True)
    rows += [jnp.broadcast_to(any_later, (1, places))] * 4
    return jnp.concatenate(rows, axis=0).astype(jnp.int32)


def walk_groups(end, use):
    def single(g, carry):
        use(g)
        return carry

    def two(j, carry):
        use(2 * j)
        use(2 * j + 1)
        return carry

    pairs = lax.shift_right_logical(end, 1)
    lax.fori_loop(0, pairs, two, 0)
    lax.fori_loop(2 * pairs, end, single, 0)


def whole(ref, sender, block):
    return jnp.concatenate([ref[sender, pl.ds(0, block)], ref[sender, pl.ds(block, block)]], axis=1)


def turn_blocks(feat, mate, turned):
    blocks = feat.shape[0]
    turned[2 * blocks] = jnp.zeros(turned.shape[1:], turned.dtype)

    def turn(b, carry):
        for k in range(4):
            turned[b * 4 + k] = feat[b * 4 + k].T
            turned[blocks + b * 4 + k] = mate[b * 4 + k].T
        return carry

    lax.fori_loop(0, blocks // 4, turn, 0)


def weight_kernel(
    arrived_ref, feat_any, mate_any, grad_any, core_ref, own_ref, other_ref, plan_ref,
    feat, mate, grad, turned, acc, part, plan, plan_sem, sems,
):
    kinds, width, _ = acc.shape
    blocks, block, _ = feat.shape
    half = width // 2
    pairs = ((feat_any, feat), (mate_any, mate), (grad_any, grad))
    copies = [pltpu.make_async_copy(src, dst, sems.at[i]) for i, (src, dst) in enumerate(pairs)]
    for copy in copies:
        copy.start()
    tags = jnp.max(arrived_ref[:, pl.ds(3 * block, TAG_ROWS)].astype(jnp.float32), axis=1)
    plan_ref[...] = make_plans(tags, core_ref[0].astype(jnp.float32), blocks, kinds - 1)
    plan_copy = pltpu.make_async_copy(plan_ref, plan, plan_sem)
    plan_copy.start()
    acc[...] = jnp.zeros_like(acc)
    part[...] = jnp.zeros_like(part)
    for copy in copies:
        copy.wait()
    turn_blocks(feat, mate, turned)

    def root(g, carry):
        left = jnp.concatenate([turned[g * GROUP + k] for k in range(GROUP)], axis=1)
        right = grad[pl.ds(g * GROUP, GROUP)].reshape(GROUP * block, width)
        acc[0] += jnp.dot(left, right, preferred_element_type=jnp.float32)
        return carry

    lax.fori_loop(0, blocks // GROUP, root, 0)
    plan_copy.wait()

    def lefts(g, row):
        return jnp.concatenate([turned[plan[row + 1, g * GROUP + k]] for k in range(GROUP)], axis=1)

    def use(g):
        right = jnp.concatenate([whole(arrived_ref, plan[0, g * GROUP + k], block) for k in range(GROUP)], axis=0)
        acc[1 + plan[2, g * GROUP]] += jnp.dot(lefts(g, 0), right, preferred_element_type=jnp.float32)

    def use_half(g):
        right = jnp.concatenate(
            [arrived_ref[plan[4, g * GROUP + k], pl.ds(2 * block, block)] for k in range(GROUP)], axis=0
        )
        part[plan[6, g * GROUP]] += jnp.dot(lefts(g, 4), right, preferred_element_type=jnp.float32)

    walk_groups(plan[3, 0], use)
    walk_groups(plan[7, 0], use_half)

    def split(own, other):
        for r in range(kinds):
            rows = pl.ds(r * width, width)
            own_ref[rows] = acc[r, :, own] + part[r - 1] if r else acc[r, :, own]
            other_ref[rows] = acc[r, :, other]

    first, second = pl.ds(0, half), pl.ds(half, half)

    @pl.when(core_ref[0] == 0)
    def _():
        split(first, second)

    @pl.when(core_ref[0] != 0)
    def _():
        split(second, first)


def later_kernel(plan, later, feat, mate, before_ref, own_ref, turned):
    width = feat.shape[2]
    turn_blocks(feat, mate, turned)
    own_ref[...] = before_ref[...]

    def use(g):
        left = jnp.concatenate([turned[plan[9, g * GROUP + k]] for k in range(GROUP)], axis=1)
        right = jnp.concatenate([later[plan[8, g * GROUP + k]] for k in range(GROUP)], axis=0)
        rows = pl.ds(pl.multiple_of((1 + plan[10, g * GROUP]) * width, width), width)
        own_ref[rows] += jnp.dot(left, right, preferred_element_type=jnp.float32)

    walk_groups(plan[11, 0], use)


def add_groups(plan_ref, row, acc, block, products):
    def use(g):
        part = products(g)
        for k in range(GROUP):
            acc[plan_ref[row + 1, g * GROUP + k]] += part[k * block : (k + 1) * block]

    walk_groups(plan_ref[row + 3, 0], use)


ACROSS = (((1,), (1,)), ((), ()))


def halves_kernel(plan_ref, core_ref, arrived_ref, later_any, weight_ref, own_any, mate_ref, halves, acc, sem, later_sem):
    blocks, block, width = mate_ref.shape
    half = width // 2
    copy = pltpu.make_async_copy(arrived_ref.at[:, pl.ds(2 * block, block)], halves, sem)
    copy.start()
    acc[...] = jnp.zeros_like(acc)
    lanes = pl.ds(pl.multiple_of(core_ref[0] * half, half), half)

    def products(row):
        def of_group(g):
            rows = jnp.concatenate([halves[plan_ref[row, g * GROUP + k]] for k in range(GROUP)], axis=0)
            weight = weight_ref[plan_ref[row + 2, g * GROUP], :, lanes]
            return lax.dot_general(rows, weight, ACROSS, preferred_element_type=jnp.float32)

        return of_group

    copy.wait()
    add_groups(plan_ref, 4, acc, block, products(4))

    @pl.when(plan_ref[11, 0] > 0)
    def _():
        more = pltpu.make_async_copy(later_any, halves, later_sem)
        more.start()
        more.wait()
        add_groups(plan_ref, 8, acc, block, products(8))

    own_copy = pltpu.make_async_copy(acc.at[pl.ds(0, blocks)], own_any, later_sem)
    own_copy.start()
    mate_ref[...] = acc[pl.ds(blocks, blocks)].astype(jnp.bfloat16)
    own_copy.wait()


def feat_kernel(
    plan_ref, arrived_ref, own_any, mate_any, grad_ref, root_ref, weight_ref, out_ref, held, mate, acc, sems
):
    blocks, block, width = out_ref.shape
    own_copy = pltpu.make_async_copy(own_any, acc.at[pl.ds(0, blocks)], sems.at[0])
    copy = pltpu.make_async_copy(arrived_ref.at[:, pl.ds(0, 2 * block)], held, sems.at[1])
    mate_copy = pltpu.make_async_copy(mate_any, mate, sems.at[2])
    own_copy.start()
    copy.start()
    mate_copy.start()
    acc[2 * blocks] = jnp.zeros(acc.shape[1:], jnp.float32)
    own_copy.wait()

    def base(g, carry):
        rows = grad_ref[pl.ds(g * GROUP, GROUP)].reshape(GROUP * block, width)
        part = lax.dot_general(rows, root_ref[...], ACROSS, preferred_element_type=jnp.float32)
        acc[pl.ds(g * GROUP, GROUP)] += part.reshape(GROUP, block, width)
        return carry

    lax.fori_loop(0, blocks // GROUP, base, 0)
    copy.wait()

    def products(g):
        rows = jnp.concatenate([whole(held, plan_ref[0, g * GROUP + k], block) for k in range(GROUP)], axis=0)
        return lax.dot_general(rows, weight_ref[plan_ref[2, g * GROUP]], ACROSS, preferred_element_type=jnp.float32)

    add_groups(plan_ref, 0, acc, block, products)
    mate_copy.wait()
    out_ref[...] = (acc[pl.ds(0, blocks)] + mate[...].astype(jnp.float32)).astype(jnp.bfloat16)


def share_kernel(scale, spread_ref, share_ref):
    share = (jnp.sum(spread_ref[...], axis=0) * scale).astype(jnp.bfloat16)
    for i in range(share_ref.shape[0]):
        share_ref[i] = share


def shards(features, out_grad, rel_weight, root_weight, tiles, tile_dest, tile_peer, tile_source, tile_rel):
    dev_count = lax.axis_size(AXES)
    chips = lax.axis_size(CHIPS)
    core = lax.axis_index("c")
    block = tiles.shape[1]
    width = features.shape[1]
    rel_count = rel_weight.shape[0]
    blocks = features.shape[0] // block
    scale = 1.0 / math.sqrt(features.shape[0] * dev_count)
    swap = [(0, 1), (1, 0)]
    grad_blocks = out_grad.reshape(blocks, block, width)
    feat_blocks = features.reshape(blocks, block, width)

    mate_blocks = lax.ppermute(feat_blocks, "c", swap)
    outgoing, later = make_messages(tile_dest, tile_peer[:, 0], tile_rel, tile_source, tiles, grad_blocks, dev_count)
    outgoing, later, core, mate_blocks = lax.optimization_barrier(
        (outgoing, later, core[None].astype(jnp.int32), mate_blocks)
    )

    def exchange(array):
        return lax.all_to_all(array, AXES, split_axis=0, concat_axis=0, tiled=True)

    arrived = exchange(outgoing)

    dma = pltpu.SemaphoreType.DMA
    cost = pl.CostEstimate(
        flops=2 * dev_count * block * width * width, bytes_accessed=dev_count * block * width * 3, transcendentals=0
    )
    half_rows = (1 + rel_count) * width
    half = jax.ShapeDtypeStruct((half_rows, width // 2), jnp.float32)
    local = pltpu.VMEM(grad_blocks.shape, jnp.bfloat16)
    turned = pltpu.VMEM((2 * blocks + 1, width, block), jnp.bfloat16)
    plan_type = jax.ShapeDtypeStruct((16, plan_places(dev_count, rel_count)), jnp.int32)
    own, other, plan = pl.pallas_call(
        weight_kernel,
        out_shape=(half, half, plan_type),
        in_specs=[VMEM, HBM, HBM, HBM, SMEM],
        out_specs=(VMEM, VMEM, VMEM),
        scratch_shapes=[
            local,
            local,
            local,
            turned,
            pltpu.VMEM((1 + rel_count, width, width), jnp.float32),
            pltpu.VMEM((rel_count, width, width // 2), jnp.float32),
            pltpu.SMEM(plan_type.shape, jnp.int32),
            dma,
            dma((3,)),
        ],
        compiler_params=pltpu.CompilerParams(vmem_limit_bytes=24 * MIB),
        cost_estimate=cost,
    )(arrived, feat_blocks, mate_blocks, grad_blocks, core)

    own = own + lax.ppermute(other, "c", swap)

    def take_later(later, own):
        later = exchange(later)
        own = pl.pallas_call(
            later_kernel,
            out_shape=half,
            in_specs=[SMEM] + [VMEM] * 4,
            out_specs=VMEM,
            scratch_shapes=[turned],
            compiler_params=pltpu.CompilerParams(vmem_limit_bytes=24 * MIB),
        )(plan, later, feat_blocks, mate_blocks, own)
        return later, own

    later, own = lax.cond(plan[12, 0] > 0, take_later, lambda later, own: (later, own), later, own)

    own, plan = lax.optimization_barrier((own, plan))
    own_part, mate_part = pl.pallas_call(
        halves_kernel,
        out_shape=(
            jax.ShapeDtypeStruct(grad_blocks.shape, jnp.float32),
            jax.ShapeDtypeStruct(grad_blocks.shape, jnp.bfloat16),
        ),
        in_specs=[SMEM, SMEM, HBM, HBM, VMEM],
        out_specs=(HBM, VMEM),
        scratch_shapes=[
            pltpu.VMEM((dev_count, block, LANES), jnp.bfloat16),
            pltpu.VMEM((2 * blocks + 1, block, width), jnp.float32),
            dma,
            dma,
        ],
        compiler_params=pltpu.CompilerParams(vmem_limit_bytes=49 * MIB),
        cost_estimate=cost,
    )(plan, core, arrived, later, rel_weight)
    shape = (chips, half_rows // chips, width // 2)
    spread = lax.all_to_all(own.reshape(shape), CHIPS, 0, 0, tiled=True)
    spread, own_part, mate_part, plan = lax.optimization_barrier((spread, own_part, mate_part, plan))
    mate_part = lax.ppermute(mate_part, "c", swap)
    share = pl.pallas_call(
        functools.partial(share_kernel, scale),
        out_shape=jax.ShapeDtypeStruct(shape, jnp.bfloat16),
        in_specs=[VMEM],
        out_specs=VMEM,
        compiler_params=pltpu.CompilerParams(vmem_limit_bytes=8 * MIB),
    )(spread)
    own = lax.all_to_all(share, CHIPS, 0, 0, tiled=True).reshape(half.shape)
    grad_feat = pl.pallas_call(
        feat_kernel,
        out_shape=jax.ShapeDtypeStruct(grad_blocks.shape, jnp.bfloat16),
        in_specs=[SMEM, HBM, HBM, HBM, VMEM, VMEM, VMEM],
        out_specs=VMEM,
        scratch_shapes=[
            pltpu.VMEM((dev_count, 2 * block, LANES), jnp.bfloat16),
            local,
            pltpu.VMEM((2 * blocks + 1, block, width), jnp.float32),
            dma((3,)),
        ],
        compiler_params=pltpu.CompilerParams(vmem_limit_bytes=49 * MIB),
        cost_estimate=cost,
    )(plan, arrived, own_part, mate_part, grad_blocks, root_weight, rel_weight)
    own, grad_feat = lax.optimization_barrier((own, grad_feat))
    other = lax.ppermute(own, "c", swap)
    core = core[0]
    left = jnp.where(core == 0, own, other).astype(jnp.float32)
    right = jnp.where(core == 0, other, own).astype(jnp.float32)
    grad_weights = jnp.concatenate([left, right], axis=1).reshape(1 + rel_count, width, width)
    return grad_feat.reshape(features.shape), grad_weights


def solution(mesh):
    sizes = (4, 4, 4, 2)
    fine = Mesh(mesh.devices.reshape(sizes), AXES)
    return jax.shard_map(
        shards,
        mesh=fine,
        in_specs=(
            P(AXES, None),
            P(AXES, None),
            P(),
            P(),
            P(AXES, None, None),
            P(AXES),
            P(AXES, None),
            P(AXES),
            P(AXES),
        ),
        out_specs=(P(AXES, None), P()),
        check_vma=False,
    )
```

```python
import functools
import math

import jax
import jax.numpy as jnp
from jax import lax
from jax.experimental import pallas as pl
from jax.experimental.pallas import tpu as pltpu
from jax.sharding import Mesh
from jax.sharding import PartitionSpec as P

AXES = ("z", "y", "x", "c")
CHIPS = ("z", "y", "x")
VMEM = pl.BlockSpec(memory_space=pltpu.VMEM)
HBM = pl.BlockSpec(memory_space=pltpu.HBM)
SMEM = pl.BlockSpec(memory_space=pltpu.SMEM)
MIB = 1024 * 1024
GROUP = 8
LANES = 128
TAG_ROWS = 16
FIELD = 16


def message_kernel(
    blocks, parts, dest_any, peer_any, rel_any, source_any, tiles_ref, grad_any, out_ref, later_ref,
    dest, peers, rels, sources, count, seconds, flag, grad, held, made, marks, tags, sems, out_sem,
):
    tile_count, block, _ = tiles_ref.shape
    part = tile_count // parts
    pairs = ((dest_any, dest), (peer_any, peers), (rel_any, rels), (source_any, sources), (grad_any, grad))
    early = [pltpu.make_async_copy(src, dst, sems.at[parts + i]) for i, (src, dst) in enumerate(pairs)]
    for copy in early:
        copy.start()

    def fetch(i):
        rows = pl.ds(i * part, part)
        return pltpu.make_async_copy(tiles_ref.at[rows], held.at[rows], sems.at[i])

    for i in range(parts):
        fetch(i).start()

    def clear(i, carry):
        count[2 * i] = 0
        count[2 * i + 1] = 0
        seconds[i] = 0
        return carry

    lax.fori_loop(0, seconds.shape[0], clear, 0)
    flag[0] = 0
    marks[...] = jnp.full(marks.shape, -1.0, jnp.float32)
    field = lax.broadcasted_iota(jnp.int32, marks.shape[1:], 1) // FIELD
    left, right = pl.ds(0, block), pl.ds(block, block)
    half = pl.ds(2 * block, block)

    def send(src, dst):
        pltpu.make_async_copy(src, dst, out_sem).start()

    def place(t, carry):
        peer = peers[t]
        rank = count[peer]
        count[peer] = rank + 1
        mark = (rels[t] * blocks + sources[t]).astype(jnp.float32)

        @pl.when(rank == 0)
        def _():
            marks[peer] = jnp.where(field == 0, mark, marks[peer])
            send(made.at[t], out_ref.at[peer, pl.ds(0, 2 * block)])

        @pl.when(rank != 0)
        def _():
            chip = lax.shift_right_logical(peer, 1)
            later = seconds[chip]
            seconds[chip] = later + 1
            core = (peer & 1).astype(jnp.float32)
            first = 2 * chip
            for side in range(2):
                old = marks[first + side]
                old = jnp.where(field == 2 + 2 * later, core, old)
                marks[first + side] = jnp.where(field == 1 + 2 * later, mark, old)

            @pl.when(later == 0)
            def _():
                send(made.at[t, left], out_ref.at[first, half])
                send(made.at[t, right], out_ref.at[first + 1, half])

            @pl.when(later != 0)
            def _():
                flag[0] = 1
                send(made.at[t, left], later_ref.at[first])
                send(made.at[t, right], later_ref.at[first + 1])

        return carry

    for copy in early:
        copy.wait()

    for i in range(parts):
        fetch(i).wait()
        for t in range(i * part, (i + 1) * part):
            message = lax.dot_general(
                held[t], grad[dest[t]], (((0,), (0,)), ((), ())), preferred_element_type=jnp.float32
            ).astype(jnp.bfloat16)
            made[t, left] = message[:, :LANES]
            made[t, right] = message[:, LANES:]
        lax.fori_loop(i * part, (i + 1) * part, place, 0)

    any_later = flag[0].astype(jnp.float32)
    all_marks = jnp.where(field[None] == 5, any_later, marks[...])
    tags[...] = jnp.concatenate([all_marks, all_marks], axis=1).astype(jnp.bfloat16)
    tag_copy = pltpu.make_async_copy(tags, out_ref.at[:, pl.ds(3 * block, TAG_ROWS)], sems.at[0])
    tag_copy.start()
    pltpu.make_async_copy(made, out_ref.at[pl.ds(0, tile_count), pl.ds(0, 2 * block)], out_sem).wait()
    tag_copy.wait()


def make_messages(tile_dest, peer_list, tile_rel, tile_source, tiles, grad_blocks, dev_count):
    tile_count, block, _ = tiles.shape
    blocks, _, width = grad_blocks.shape
    parts = 8
    numbers = pltpu.SMEM((tile_count,), jnp.int32)

    def kernel(*refs):
        message_kernel(blocks, parts, *refs)

    return pl.pallas_call(
        kernel,
        out_shape=(
            jax.ShapeDtypeStruct((dev_count, 3 * block + TAG_ROWS, LANES), jnp.bfloat16),
            jax.ShapeDtypeStruct((dev_count, block, LANES), jnp.bfloat16),
        ),
        in_specs=[HBM] * 6,
        out_specs=(HBM, HBM),
        scratch_shapes=[
            numbers,
            numbers,
            numbers,
            numbers,
            pltpu.SMEM((dev_count,), jnp.int32),
            pltpu.SMEM((dev_count // 2,), jnp.int32),
            pltpu.SMEM((1,), jnp.int32),
            pltpu.VMEM(grad_blocks.shape, jnp.bfloat16),
            pltpu.VMEM(tiles.shape, jnp.bfloat16),
            pltpu.VMEM((tile_count, 2 * block, LANES), jnp.bfloat16),
            pltpu.VMEM((dev_count, TAG_ROWS // 2, LANES), jnp.float32),
            pltpu.VMEM((dev_count, TAG_ROWS, LANES), jnp.bfloat16),
            pltpu.SemaphoreType.DMA((parts + 5,)),
            pltpu.SemaphoreType.DMA,
        ],
        compiler_params=pltpu.CompilerParams(vmem_limit_bytes=58 * MIB),
        cost_estimate=pl.CostEstimate(
            flops=2 * tile_count * block * block * width,
            bytes_accessed=tile_count * block * (block + width) * 2,
            transcendentals=0,
        ),
    )(tile_dest, peer_list, tile_rel, tile_source, tiles, grad_blocks)


def plan_places(senders, rel_count):
    return -(-(senders + (GROUP - 1) * rel_count) // LANES) * LANES


def make_plans(tags, core, blocks, rel_count):
    senders = tags.shape[0]
    places = plan_places(senders, rel_count)
    wide = 1 << (rel_count - 1).bit_length()
    square = (senders, senders)
    row, lane = lax.broadcasted_iota(jnp.int32, square, 0), lax.broadcasted_iota(jnp.int32, square, 1)
    lane_set, lane_rel = lane // wide, (lane % wide).astype(jnp.float32)
    below = (lane < row).astype(jnp.float32).astype(jnp.bfloat16)
    ahead = ((row < lane) & (row // wide == lane_set)).astype(jnp.float32).astype(jnp.bfloat16)
    at = lax.broadcasted_iota(jnp.int32, (senders, places), 1)
    at, lead = at.astype(jnp.float32), (at // GROUP * GROUP).astype(jnp.float32)

    def column(i):
        return tags[:, i * FIELD : i * FIELD + 1]

    tag = [column(0), column(1), column(3)]
    rel = [jnp.floor(t * (1.0 / blocks)) for t in tag]
    used = [jnp.where((lane_set == q) & (lane_rel == r) & (t >= 0), 1.0, 0.0) for q, (t, r) in enumerate(zip(tag, rel))]
    every = used[0] + used[1] + used[2]
    before = jnp.dot(below, every.astype(jnp.bfloat16), preferred_element_type=jnp.float32)
    groups = jnp.floor((jnp.sum(every, axis=0, keepdims=True) + (GROUP - 1)) * (1.0 / GROUP))
    first = jnp.dot(
        jnp.broadcast_to(groups, (TAG_ROWS, senders)).astype(jnp.bfloat16), ahead, preferred_element_type=jnp.float32
    )[0:1]
    spot = before + first * GROUP
    across = tags.T
    line = lax.broadcasted_iota(jnp.int32, (TAG_ROWS, senders), 0)
    name = lax.broadcasted_iota(jnp.int32, (1, senders), 1).astype(jnp.float32)
    rows = []
    for q, i in enumerate((0, 1, 3)):
        place = jnp.where(tag[q] >= 0, jnp.sum(used[q] * spot, axis=1, keepdims=True), -1.0)
        here = jnp.where(place == at, 1.0, 0.0).astype(jnp.bfloat16)
        leads = jnp.where(place == lead, 1.0, 0.0).astype(jnp.bfloat16)
        mark = across[i * FIELD : i * FIELD + 1]
        relation = jnp.floor(mark * (1.0 / blocks))
        source = mark - relation * blocks - 2 * blocks
        if q:
            owner = across[(i + 1) * FIELD : (i + 1) * FIELD + 1]
            source = source + jnp.where(owner == core, 0.0, float(blocks))
        named = jnp.where(line == 0, 1.0, jnp.where(line == 1, name, jnp.where(line == 2, source, relation)))
        named = named.astype(jnp.bfloat16)
        own = jnp.dot(named, here, preferred_element_type=jnp.float32)
        led = jnp.dot(named, leads, preferred_element_type=jnp.float32)
        total = jnp.sum(jnp.where(lane_set[0:1] == q, groups, 0.0), axis=1, keepdims=True)
        rows += [jnp.where(own[0:1] > 0, own[1:2], led[1:2]), own[2:3] + 2 * blocks, led[3:4]]
        rows.append(jnp.broadcast_to(total, (1, places)))
    any_later = jnp.max(jnp.where(column(5) > 0, 1.0, 0.0), axis=0, keepdims=True)
    rows += [jnp.broadcast_to(any_later, (1, places))] * 4
    return jnp.concatenate(rows, axis=0).astype(jnp.int32)


def walk_groups(end, use):
    def single(g, carry):
        use(g)
        return carry

    def two(j, carry):
        use(2 * j)
        use(2 * j + 1)
        return carry

    pairs = lax.shift_right_logical(end, 1)
    lax.fori_loop(0, pairs, two, 0)
    lax.fori_loop(2 * pairs, end, single, 0)


def whole(ref, sender, block):
    return jnp.concatenate([ref[sender, pl.ds(0, block)], ref[sender, pl.ds(block, block)]], axis=1)


def turn_blocks(feat, mate, turned):
    blocks = feat.shape[0]
    turned[2 * blocks] = jnp.zeros(turned.shape[1:], turned.dtype)

    def turn(b, carry):
        for k in range(4):
            turned[b * 4 + k] = feat[b * 4 + k].T
            turned[blocks + b * 4 + k] = mate[b * 4 + k].T
        return carry

    lax.fori_loop(0, blocks // 4, turn, 0)


def weight_kernel(
    arrived_ref, feat_any, mate_any, grad_any, core_ref, own_ref, other_ref, plan_ref,
    feat, mate, grad, turned, acc, part, plan, plan_sem, sems,
):
    kinds, width, _ = acc.shape
    blocks, block, _ = feat.shape
    half = width // 2
    pairs = ((feat_any, feat), (mate_any, mate), (grad_any, grad))
    copies = [pltpu.make_async_copy(src, dst, sems.at[i]) for i, (src, dst) in enumerate(pairs)]
    for copy in copies:
        copy.start()
    tags = jnp.max(arrived_ref[:, pl.ds(3 * block, TAG_ROWS)].astype(jnp.float32), axis=1)
    plan_ref[...] = make_plans(tags, core_ref[0].astype(jnp.float32), blocks, kinds - 1)
    plan_copy = pltpu.make_async_copy(plan_ref, plan, plan_sem)
    plan_copy.start()
    acc[...] = jnp.zeros_like(acc)
    part[...] = jnp.zeros_like(part)
    for copy in copies:
        copy.wait()
    turn_blocks(feat, mate, turned)

    def root(g, carry):
        left = jnp.concatenate([turned[g * GROUP + k] for k in range(GROUP)], axis=1)
        right = grad[pl.ds(g * GROUP, GROUP)].reshape(GROUP * block, width)
        acc[0] += jnp.dot(left, right, preferred_element_type=jnp.float32)
        return carry

    lax.fori_loop(0, blocks // GROUP, root, 0)
    plan_copy.wait()

    def lefts(g, row):
        return jnp.concatenate([turned[plan[row + 1, g * GROUP + k]] for k in range(GROUP)], axis=1)

    def use(g):
        right = jnp.concatenate([whole(arrived_ref, plan[0, g * GROUP + k], block) for k in range(GROUP)], axis=0)
        acc[1 + plan[2, g * GROUP]] += jnp.dot(lefts(g, 0), right, preferred_element_type=jnp.float32)

    def use_half(g):
        right = jnp.concatenate(
            [arrived_ref[plan[4, g * GROUP + k], pl.ds(2 * block, block)] for k in range(GROUP)], axis=0
        )
        part[plan[6, g * GROUP]] += jnp.dot(lefts(g, 4), right, preferred_element_type=jnp.float32)

    walk_groups(plan[3, 0], use)
    walk_groups(plan[7, 0], use_half)

    def split(own, other):
        for r in range(kinds):
            rows = pl.ds(r * width, width)
            own_ref[rows] = acc[r, :, own] + part[r - 1] if r else acc[r, :, own]
            other_ref[rows] = acc[r, :, other]

    first, second = pl.ds(0, half), pl.ds(half, half)

    @pl.when(core_ref[0] == 0)
    def _():
        split(first, second)

    @pl.when(core_ref[0] != 0)
    def _():
        split(second, first)


def later_kernel(plan, later_any, feat_any, mate_any, before_any, own_ref, later, feat, mate, turned, sems):
    width = feat.shape[2]
    pairs = ((before_any, own_ref), (feat_any, feat), (mate_any, mate), (later_any, later))
    copies = [pltpu.make_async_copy(src, dst, sems.at[i]) for i, (src, dst) in enumerate(pairs)]
    for copy in copies:
        copy.start()
    for copy in copies[:3]:
        copy.wait()

    @pl.when(plan[11, 0] > 0)
    def _():
        turn_blocks(feat, mate, turned)

    copies[3].wait()

    def use(g):
        left = jnp.concatenate([turned[plan[9, g * GROUP + k]] for k in range(GROUP)], axis=1)
        right = jnp.concatenate([later[plan[8, g * GROUP + k]] for k in range(GROUP)], axis=0)
        rows = pl.ds(pl.multiple_of((1 + plan[10, g * GROUP]) * width, width), width)
        own_ref[rows] += jnp.dot(left, right, preferred_element_type=jnp.float32)

    walk_groups(plan[11, 0], use)


def add_groups(plan_ref, row, acc, block, products):
    def use(g):
        part = products(g)
        for k in range(GROUP):
            acc[plan_ref[row + 1, g * GROUP + k]] += part[k * block : (k + 1) * block]

    walk_groups(plan_ref[row + 3, 0], use)


ACROSS = (((1,), (1,)), ((), ()))


def halves_kernel(plan_ref, core_ref, arrived_ref, later_any, weight_ref, own_any, mate_ref, halves, acc, sem, later_sem):
    blocks, block, width = mate_ref.shape
    half = width // 2
    copy = pltpu.make_async_copy(arrived_ref.at[:, pl.ds(2 * block, block)], halves, sem)
    copy.start()
    acc[...] = jnp.zeros_like(acc)
    lanes = pl.ds(pl.multiple_of(core_ref[0] * half, half), half)

    def products(row):
        def of_group(g):
            rows = jnp.concatenate([halves[plan_ref[row, g * GROUP + k]] for k in range(GROUP)], axis=0)
            weight = weight_ref[plan_ref[row + 2, g * GROUP], :, lanes]
            return lax.dot_general(rows, weight, ACROSS, preferred_element_type=jnp.float32)

        return of_group

    copy.wait()
    add_groups(plan_ref, 4, acc, block, products(4))

    @pl.when(plan_ref[11, 0] > 0)
    def _():
        more = pltpu.make_async_copy(later_any, halves, later_sem)
        more.start()
        more.wait()
        add_groups(plan_ref, 8, acc, block, products(8))

    own_copy = pltpu.make_async_copy(acc.at[pl.ds(0, blocks)], own_any, later_sem)
    own_copy.start()
    mate_ref[...] = acc[pl.ds(blocks, blocks)].astype(jnp.bfloat16)
    own_copy.wait()


def feat_kernel(
    plan_ref, arrived_ref, own_any, mate_any, grad_ref, root_ref, weight_ref, out_ref, held, mate, acc, sems
):
    blocks, block, width = out_ref.shape
    own_copy = pltpu.make_async_copy(own_any, acc.at[pl.ds(0, blocks)], sems.at[0])
    copy = pltpu.make_async_copy(arrived_ref.at[:, pl.ds(0, 2 * block)], held, sems.at[1])
    mate_copy = pltpu.make_async_copy(mate_any, mate, sems.at[2])
    own_copy.start()
    copy.start()
    mate_copy.start()
    acc[2 * blocks] = jnp.zeros(acc.shape[1:], jnp.float32)
    own_copy.wait()

    def base(g, carry):
        rows = grad_ref[pl.ds(g * GROUP, GROUP)].reshape(GROUP * block, width)
        part = lax.dot_general(rows, root_ref[...], ACROSS, preferred_element_type=jnp.float32)
        acc[pl.ds(g * GROUP, GROUP)] += part.reshape(GROUP, block, width)
        return carry

    lax.fori_loop(0, blocks // GROUP, base, 0)
    copy.wait()

    def products(g):
        rows = jnp.concatenate([whole(held, plan_ref[0, g * GROUP + k], block) for k in range(GROUP)], axis=0)
        return lax.dot_general(rows, weight_ref[plan_ref[2, g * GROUP]], ACROSS, preferred_element_type=jnp.float32)

    add_groups(plan_ref, 0, acc, block, products)
    mate_copy.wait()
    out_ref[...] = (acc[pl.ds(0, blocks)] + mate[...].astype(jnp.float32)).astype(jnp.bfloat16)


def share_kernel(scale, spread_ref, share_ref):
    share = (jnp.sum(spread_ref[...], axis=0) * scale).astype(jnp.bfloat16)
    for i in range(share_ref.shape[0]):
        share_ref[i] = share


def shards(features, out_grad, rel_weight, root_weight, tiles, tile_dest, tile_peer, tile_source, tile_rel):
    dev_count = lax.axis_size(AXES)
    chips = lax.axis_size(CHIPS)
    core = lax.axis_index("c")
    block = tiles.shape[1]
    width = features.shape[1]
    rel_count = rel_weight.shape[0]
    blocks = features.shape[0] // block
    scale = 1.0 / math.sqrt(features.shape[0] * dev_count)
    swap = [(0, 1), (1, 0)]
    grad_blocks = out_grad.reshape(blocks, block, width)
    feat_blocks = features.reshape(blocks, block, width)

    mate_blocks = lax.ppermute(feat_blocks, "c", swap)
    outgoing, later = make_messages(tile_dest, tile_peer[:, 0], tile_rel, tile_source, tiles, grad_blocks, dev_count)
    outgoing, later, core, mate_blocks = lax.optimization_barrier(
        (outgoing, later, core[None].astype(jnp.int32), mate_blocks)
    )

    def exchange(array):
        return lax.all_to_all(array, AXES, split_axis=0, concat_axis=0, tiled=True)

    arrived = exchange(outgoing)

    dma = pltpu.SemaphoreType.DMA
    cost = pl.CostEstimate(
        flops=2 * dev_count * block * width * width, bytes_accessed=dev_count * block * width * 3, transcendentals=0
    )
    half_rows = (1 + rel_count) * width
    half = jax.ShapeDtypeStruct((half_rows, width // 2), jnp.float32)
    local = pltpu.VMEM(grad_blocks.shape, jnp.bfloat16)
    turned = pltpu.VMEM((2 * blocks + 1, width, block), jnp.bfloat16)
    plan_type = jax.ShapeDtypeStruct((16, plan_places(dev_count, rel_count)), jnp.int32)
    own, other, plan = pl.pallas_call(
        weight_kernel,
        out_shape=(half, half, plan_type),
        in_specs=[VMEM, HBM, HBM, HBM, SMEM],
        out_specs=(VMEM, VMEM, VMEM),
        scratch_shapes=[
            local,
            local,
            local,
            turned,
            pltpu.VMEM((1 + rel_count, width, width), jnp.float32),
            pltpu.VMEM((rel_count, width, width // 2), jnp.float32),
            pltpu.SMEM(plan_type.shape, jnp.int32),
            dma,
            dma((3,)),
        ],
        compiler_params=pltpu.CompilerParams(vmem_limit_bytes=24 * MIB),
        cost_estimate=cost,
    )(arrived, feat_blocks, mate_blocks, grad_blocks, core)

    own = own + lax.ppermute(other, "c", swap)

    def take_later(later, own):
        later = exchange(later)
        own = pl.pallas_call(
            later_kernel,
            out_shape=half,
            in_specs=[SMEM] + [HBM] * 4,
            out_specs=VMEM,
            scratch_shapes=[pltpu.VMEM(later.shape, jnp.bfloat16), local, local, turned, dma((4,))],
            compiler_params=pltpu.CompilerParams(vmem_limit_bytes=57 * MIB),
        )(plan, later, feat_blocks, mate_blocks, own)
        return later, own

    def take_none(later, own):
        unread = pl.pallas_call(
            lambda core_ref, out_ref: None,
            out_shape=jax.ShapeDtypeStruct(later.shape, later.dtype),
            in_specs=[SMEM],
            out_specs=HBM,
        )(core)
        return unread, own

    later, own = lax.cond(plan[12, 0] > 0, take_later, take_none, later, own)

    own, plan = lax.optimization_barrier((own, plan))
    own_part, mate_part = pl.pallas_call(
        halves_kernel,
        out_shape=(
            jax.ShapeDtypeStruct(grad_blocks.shape, jnp.float32),
            jax.ShapeDtypeStruct(grad_blocks.shape, jnp.bfloat16),
        ),
        in_specs=[SMEM, SMEM, HBM, HBM, VMEM],
        out_specs=(HBM, VMEM),
        scratch_shapes=[
            pltpu.VMEM((dev_count, block, LANES), jnp.bfloat16),
            pltpu.VMEM((2 * blocks + 1, block, width), jnp.float32),
            dma,
            dma,
        ],
        compiler_params=pltpu.CompilerParams(vmem_limit_bytes=49 * MIB),
        cost_estimate=cost,
    )(plan, core, arrived, later, rel_weight)
    shape = (chips, half_rows // chips, width // 2)
    spread = lax.all_to_all(own.reshape(shape), CHIPS, 0, 0, tiled=True)
    spread, own_part, mate_part, plan = lax.optimization_barrier((spread, own_part, mate_part, plan))
    mate_part = lax.ppermute(mate_part, "c", swap)
    share = pl.pallas_call(
        functools.partial(share_kernel, scale),
        out_shape=jax.ShapeDtypeStruct(shape, jnp.bfloat16),
        in_specs=[VMEM],
        out_specs=VMEM,
        compiler_params=pltpu.CompilerParams(vmem_limit_bytes=8 * MIB),
    )(spread)
    own = lax.all_to_all(share, CHIPS, 0, 0, tiled=True).reshape(half.shape)
    grad_feat = pl.pallas_call(
        feat_kernel,
        out_shape=jax.ShapeDtypeStruct(grad_blocks.shape, jnp.bfloat16),
        in_specs=[SMEM, HBM, HBM, HBM, VMEM, VMEM, VMEM],
        out_specs=VMEM,
        scratch_shapes=[
            pltpu.VMEM((dev_count, 2 * block, LANES), jnp.bfloat16),
            local,
            pltpu.VMEM((2 * blocks + 1, block, width), jnp.float32),
            dma((3,)),
        ],
        compiler_params=pltpu.CompilerParams(vmem_limit_bytes=49 * MIB),
        cost_estimate=cost,
    )(plan, arrived, own_part, mate_part, grad_blocks, root_weight, rel_weight)
    own, grad_feat = lax.optimization_barrier((own, grad_feat))
    other = lax.ppermute(own, "c", swap)
    core = core[0]
    left = jnp.where(core == 0, own, other).astype(jnp.float32)
    right = jnp.where(core == 0, other, own).astype(jnp.float32)
    grad_weights = jnp.concatenate([left, right], axis=1).reshape(1 + rel_count, width, width)
    return grad_feat.reshape(features.shape), grad_weights


def solution(mesh):
    sizes = (4, 4, 4, 2)
    fine = Mesh(mesh.devices.reshape(sizes), AXES)
    return jax.shard_map(
        shards,
        mesh=fine,
        in_specs=(
            P(AXES, None),
            P(AXES, None),
            P(),
            P(),
            P(AXES, None, None),
            P(AXES),
            P(AXES, None),
            P(AXES),
            P(AXES),
        ),
        out_specs=(P(AXES, None), P()),
        check_vma=False,
    )
```

```python
import functools
import math

import jax
import jax.numpy as jnp
from jax import lax
from jax.experimental import pallas as pl
from jax.experimental.pallas import tpu as pltpu
from jax.sharding import Mesh
from jax.sharding import PartitionSpec as P

AXES = ("z", "y", "x", "c")
CHIPS = ("z", "y", "x")
VMEM = pl.BlockSpec(memory_space=pltpu.VMEM)
HBM = pl.BlockSpec(memory_space=pltpu.HBM)
SMEM = pl.BlockSpec(memory_space=pltpu.SMEM)
MIB = 1024 * 1024
GROUP = 8
LANES = 128
TAG_ROWS = 16
FIELD = 16


def message_kernel(
    blocks, parts, dest_any, peer_any, rel_any, source_any, tiles_ref, grad_any, out_ref, later_ref,
    dest, peers, rels, sources, count, seconds, flag, grad, held, made, marks, tags, sems, out_sem,
):
    tile_count, block, _ = tiles_ref.shape
    part = tile_count // parts
    pairs = ((dest_any, dest), (peer_any, peers), (rel_any, rels), (source_any, sources), (grad_any, grad))
    early = [pltpu.make_async_copy(src, dst, sems.at[parts + i]) for i, (src, dst) in enumerate(pairs)]
    for copy in early:
        copy.start()

    def fetch(i):
        rows = pl.ds(i * part, part)
        return pltpu.make_async_copy(tiles_ref.at[rows], held.at[rows], sems.at[i])

    for i in range(parts):
        fetch(i).start()

    def clear(i, carry):
        count[2 * i] = 0
        count[2 * i + 1] = 0
        seconds[i] = 0
        return carry

    lax.fori_loop(0, seconds.shape[0], clear, 0)
    flag[0] = 0
    marks[...] = jnp.full(marks.shape, -1.0, jnp.float32)
    field = lax.broadcasted_iota(jnp.int32, marks.shape[1:], 1) // FIELD
    left, right = pl.ds(0, block), pl.ds(block, block)
    half = pl.ds(2 * block, block)

    def send(src, dst):
        pltpu.make_async_copy(src, dst, out_sem).start()

    def place(t, carry):
        peer = peers[t]
        rank = count[peer]
        count[peer] = rank + 1
        mark = (rels[t] * blocks + sources[t]).astype(jnp.float32)

        @pl.when(rank == 0)
        def _():
            marks[peer] = jnp.where(field == 0, mark, marks[peer])
            send(made.at[t], out_ref.at[peer, pl.ds(0, 2 * block)])

        @pl.when(rank != 0)
        def _():
            chip = lax.shift_right_logical(peer, 1)
            later = seconds[chip]
            seconds[chip] = later + 1
            core = (peer & 1).astype(jnp.float32)
            first = 2 * chip
            for side in range(2):
                old = marks[first + side]
                old = jnp.where(field == 2 + 2 * later, core, old)
                marks[first + side] = jnp.where(field == 1 + 2 * later, mark, old)

            @pl.when(later == 0)
            def _():
                send(made.at[t, left], out_ref.at[first, half])
                send(made.at[t, right], out_ref.at[first + 1, half])

            @pl.when(later != 0)
            def _():
                flag[0] = 1
                send(made.at[t, left], later_ref.at[first])
                send(made.at[t, right], later_ref.at[first + 1])

        return carry

    for copy in early:
        copy.wait()

    for i in range(parts):
        fetch(i).wait()
        for t in range(i * part, (i + 1) * part):
            message = lax.dot_general(
                held[t], grad[dest[t]], (((0,), (0,)), ((), ())), preferred_element_type=jnp.float32
            ).astype(jnp.bfloat16)
            made[t, left] = message[:, :LANES]
            made[t, right] = message[:, LANES:]
        lax.fori_loop(i * part, (i + 1) * part, place, 0)

    any_later = flag[0].astype(jnp.float32)
    all_marks = jnp.where(field[None] == 5, any_later, marks[...])
    tags[...] = jnp.concatenate([all_marks, all_marks], axis=1).astype(jnp.bfloat16)
    tag_copy = pltpu.make_async_copy(tags, out_ref.at[:, pl.ds(3 * block, TAG_ROWS)], sems.at[0])
    tag_copy.start()
    pltpu.make_async_copy(made, out_ref.at[pl.ds(0, tile_count), pl.ds(0, 2 * block)], out_sem).wait()
    tag_copy.wait()


def make_messages(tile_dest, peer_list, tile_rel, tile_source, tiles, grad_blocks, dev_count):
    tile_count, block, _ = tiles.shape
    blocks, _, width = grad_blocks.shape
    parts = 8
    numbers = pltpu.SMEM((tile_count,), jnp.int32)

    def kernel(*refs):
        message_kernel(blocks, parts, *refs)

    return pl.pallas_call(
        kernel,
        out_shape=(
            jax.ShapeDtypeStruct((dev_count, 3 * block + TAG_ROWS, LANES), jnp.bfloat16),
            jax.ShapeDtypeStruct((dev_count, block, LANES), jnp.bfloat16),
        ),
        in_specs=[HBM] * 6,
        out_specs=(HBM, HBM),
        scratch_shapes=[
            numbers,
            numbers,
            numbers,
            numbers,
            pltpu.SMEM((dev_count,), jnp.int32),
            pltpu.SMEM((dev_count // 2,), jnp.int32),
            pltpu.SMEM((1,), jnp.int32),
            pltpu.VMEM(grad_blocks.shape, jnp.bfloat16),
            pltpu.VMEM(tiles.shape, jnp.bfloat16),
            pltpu.VMEM((tile_count, 2 * block, LANES), jnp.bfloat16),
            pltpu.VMEM((dev_count, TAG_ROWS // 2, LANES), jnp.float32),
            pltpu.VMEM((dev_count, TAG_ROWS, LANES), jnp.bfloat16),
            pltpu.SemaphoreType.DMA((parts + 5,)),
            pltpu.SemaphoreType.DMA,
        ],
        compiler_params=pltpu.CompilerParams(vmem_limit_bytes=58 * MIB),
        cost_estimate=pl.CostEstimate(
            flops=2 * tile_count * block * block * width,
            bytes_accessed=tile_count * block * (block + width) * 2,
            transcendentals=0,
        ),
    )(tile_dest, peer_list, tile_rel, tile_source, tiles, grad_blocks)


def plan_places(senders, rel_count):
    return -(-(senders + (GROUP - 1) * rel_count) // LANES) * LANES


def make_plans(tags, core, blocks, rel_count):
    senders = tags.shape[0]
    places = plan_places(senders, rel_count)
    wide = 1 << (rel_count - 1).bit_length()
    square = (senders, senders)
    row, lane = lax.broadcasted_iota(jnp.int32, square, 0), lax.broadcasted_iota(jnp.int32, square, 1)
    lane_set, lane_rel = lane // wide, (lane % wide).astype(jnp.float32)
    below = (lane < row).astype(jnp.float32).astype(jnp.bfloat16)
    ahead = ((row < lane) & (row // wide == lane_set)).astype(jnp.float32).astype(jnp.bfloat16)
    at = lax.broadcasted_iota(jnp.int32, (senders, places), 1)
    at, lead = at.astype(jnp.float32), (at // GROUP * GROUP).astype(jnp.float32)

    def column(i):
        return tags[:, i * FIELD : i * FIELD + 1]

    tag = [column(0), column(1), column(3)]
    rel = [jnp.floor(t * (1.0 / blocks)) for t in tag]
    used = [jnp.where((lane_set == q) & (lane_rel == r) & (t >= 0), 1.0, 0.0) for q, (t, r) in enumerate(zip(tag, rel))]
    every = used[0] + used[1] + used[2]
    before = jnp.dot(below, every.astype(jnp.bfloat16), preferred_element_type=jnp.float32)
    groups = jnp.floor((jnp.sum(every, axis=0, keepdims=True) + (GROUP - 1)) * (1.0 / GROUP))
    first = jnp.dot(
        jnp.broadcast_to(groups, (TAG_ROWS, senders)).astype(jnp.bfloat16), ahead, preferred_element_type=jnp.float32
    )[0:1]
    spot = before + first * GROUP
    across = tags.T
    line = lax.broadcasted_iota(jnp.int32, (TAG_ROWS, senders), 0)
    name = lax.broadcasted_iota(jnp.int32, (1, senders), 1).astype(jnp.float32)
    rows = []
    for q, i in enumerate((0, 1, 3)):
        place = jnp.where(tag[q] >= 0, jnp.sum(used[q] * spot, axis=1, keepdims=True), -1.0)
        here = jnp.where(place == at, 1.0, 0.0).astype(jnp.bfloat16)
        leads = jnp.where(place == lead, 1.0, 0.0).astype(jnp.bfloat16)
        mark = across[i * FIELD : i * FIELD + 1]
        relation = jnp.floor(mark * (1.0 / blocks))
        source = mark - relation * blocks - 2 * blocks
        if q:
            owner = across[(i + 1) * FIELD : (i + 1) * FIELD + 1]
            source = source + jnp.where(owner == core, 0.0, float(blocks))
        named = jnp.where(line == 0, 1.0, jnp.where(line == 1, name, jnp.where(line == 2, source, relation)))
        named = named.astype(jnp.bfloat16)
        own = jnp.dot(named, here, preferred_element_type=jnp.float32)
        led = jnp.dot(named, leads, preferred_element_type=jnp.float32)
        total = jnp.sum(jnp.where(lane_set[0:1] == q, groups, 0.0), axis=1, keepdims=True)
        rows += [jnp.where(own[0:1] > 0, own[1:2], led[1:2]), own[2:3] + 2 * blocks, led[3:4]]
        rows.append(jnp.broadcast_to(total, (1, places)))
    rows += [jnp.zeros((1, places), jnp.float32)] * 4
    return jnp.concatenate(rows, axis=0).astype(jnp.int32)


def walk_groups(end, use):
    def single(g, carry):
        use(g)
        return carry

    def two(j, carry):
        use(2 * j)
        use(2 * j + 1)
        return carry

    pairs = lax.shift_right_logical(end, 1)
    lax.fori_loop(0, pairs, two, 0)
    lax.fori_loop(2 * pairs, end, single, 0)


def whole(ref, sender, block):
    return jnp.concatenate([ref[sender, pl.ds(0, block)], ref[sender, pl.ds(block, block)]], axis=1)


def turn_blocks(feat, mate, turned):
    blocks = feat.shape[0]
    turned[2 * blocks] = jnp.zeros(turned.shape[1:], turned.dtype)

    def turn(b, carry):
        for k in range(4):
            turned[b * 4 + k] = feat[b * 4 + k].T
            turned[blocks + b * 4 + k] = mate[b * 4 + k].T
        return carry

    lax.fori_loop(0, blocks // 4, turn, 0)


def weight_kernel(
    arrived_ref, feat_any, mate_any, grad_any, core_ref, own_ref, other_ref, plan_ref,
    held, halves, tags, feat, mate, grad, turned, acc, part, plan, plan_sem, sems,
):
    kinds, width, _ = acc.shape
    blocks, block, _ = feat.shape
    half = width // 2
    pairs = (
        (arrived_ref.at[:, pl.ds(3 * block, TAG_ROWS)], tags),
        (feat_any, feat),
        (mate_any, mate),
        (grad_any, grad),
        (arrived_ref.at[:, pl.ds(0, 2 * block)], held),
        (arrived_ref.at[:, pl.ds(2 * block, block)], halves),
    )
    copies = [pltpu.make_async_copy(src, dst, sems.at[i]) for i, (src, dst) in enumerate(pairs)]
    for copy in copies[:5]:
        copy.start()
    acc[...] = jnp.zeros_like(acc)
    part[...] = jnp.zeros_like(part)
    copies[0].wait()
    plan_ref[...] = make_plans(
        jnp.max(tags[...].astype(jnp.float32), axis=1), core_ref[0].astype(jnp.float32), blocks, kinds - 1
    )
    plan_copy = pltpu.make_async_copy(plan_ref, plan, plan_sem)
    plan_copy.start()
    copies[1].wait()
    copies[2].wait()
    copies[5].start()
    turn_blocks(feat, mate, turned)
    copies[3].wait()

    def root(g, carry):
        left = jnp.concatenate([turned[g * GROUP + k] for k in range(GROUP)], axis=1)
        right = grad[pl.ds(g * GROUP, GROUP)].reshape(GROUP * block, width)
        acc[0] += jnp.dot(left, right, preferred_element_type=jnp.float32)
        return carry

    lax.fori_loop(0, blocks // GROUP, root, 0)
    plan_copy.wait()

    def lefts(g, row):
        return jnp.concatenate([turned[plan[row + 1, g * GROUP + k]] for k in range(GROUP)], axis=1)

    def use(g):
        right = jnp.concatenate([whole(held, plan[0, g * GROUP + k], block) for k in range(GROUP)], axis=0)
        acc[1 + plan[2, g * GROUP]] += jnp.dot(lefts(g, 0), right, preferred_element_type=jnp.float32)

    def use_half(g):
        right = jnp.concatenate([halves[plan[4, g * GROUP + k]] for k in range(GROUP)], axis=0)
        part[plan[6, g * GROUP]] += jnp.dot(lefts(g, 4), right, preferred_element_type=jnp.float32)

    copies[4].wait()
    walk_groups(plan[3, 0], use)
    copies[5].wait()
    walk_groups(plan[7, 0], use_half)

    def split(own, other):
        for r in range(kinds):
            rows = pl.ds(r * width, width)
            own_ref[rows] = acc[r, :, own] + part[r - 1] if r else acc[r, :, own]
            other_ref[rows] = acc[r, :, other]

    first, second = pl.ds(0, half), pl.ds(half, half)

    @pl.when(core_ref[0] == 0)
    def _():
        split(first, second)

    @pl.when(core_ref[0] != 0)
    def _():
        split(second, first)


def later_kernel(plan, later_any, feat_any, mate_any, before_any, own_ref, later, feat, mate, turned, sems):
    width = feat.shape[2]
    pairs = ((before_any, own_ref), (feat_any, feat), (mate_any, mate), (later_any, later))
    copies = [pltpu.make_async_copy(src, dst, sems.at[i]) for i, (src, dst) in enumerate(pairs)]
    for copy in copies:
        copy.start()
    for copy in copies[:3]:
        copy.wait()

    @pl.when(plan[11, 0] > 0)
    def _():
        turn_blocks(feat, mate, turned)

    copies[3].wait()

    def use(g):
        left = jnp.concatenate([turned[plan[9, g * GROUP + k]] for k in range(GROUP)], axis=1)
        right = jnp.concatenate([later[plan[8, g * GROUP + k]] for k in range(GROUP)], axis=0)
        rows = pl.ds(pl.multiple_of((1 + plan[10, g * GROUP]) * width, width), width)
        own_ref[rows] += jnp.dot(left, right, preferred_element_type=jnp.float32)

    walk_groups(plan[11, 0], use)


def add_groups(plan_ref, row, acc, block, products):
    def use(g):
        part = products(g)
        for k in range(GROUP):
            acc[plan_ref[row + 1, g * GROUP + k]] += part[k * block : (k + 1) * block]

    walk_groups(plan_ref[row + 3, 0], use)


ACROSS = (((1,), (1,)), ((), ()))


def halves_kernel(
    plan_ref, core_ref, arrived_ref, later_any, grad_ref, root_ref, weight_ref, own_any, mate_ref,
    halves, acc, sem, later_sem,
):
    blocks, block, width = mate_ref.shape
    half = width // 2
    copy = pltpu.make_async_copy(arrived_ref.at[:, pl.ds(2 * block, block)], halves, sem)
    copy.start()
    acc[pl.ds(blocks, blocks + 1)] = jnp.zeros((blocks + 1, block, width), jnp.float32)
    lanes = pl.ds(pl.multiple_of(core_ref[0] * half, half), half)

    def products(row):
        def of_group(g):
            rows = jnp.concatenate([halves[plan_ref[row, g * GROUP + k]] for k in range(GROUP)], axis=0)
            weight = weight_ref[plan_ref[row + 2, g * GROUP], :, lanes]
            return lax.dot_general(rows, weight, ACROSS, preferred_element_type=jnp.float32)

        return of_group

    def base(g, carry):
        rows = grad_ref[pl.ds(g * GROUP, GROUP)].reshape(GROUP * block, width)
        part = lax.dot_general(rows, root_ref[...], ACROSS, preferred_element_type=jnp.float32)
        acc[pl.ds(g * GROUP, GROUP)] = part.reshape(GROUP, block, width)
        return carry

    lax.fori_loop(0, blocks // GROUP, base, 0)
    copy.wait()
    add_groups(plan_ref, 4, acc, block, products(4))

    @pl.when(plan_ref[11, 0] > 0)
    def _():
        more = pltpu.make_async_copy(later_any, halves, later_sem)
        more.start()
        more.wait()
        add_groups(plan_ref, 8, acc, block, products(8))

    own_copy = pltpu.make_async_copy(acc.at[pl.ds(0, blocks)], own_any, later_sem)
    own_copy.start()
    mate_ref[...] = acc[pl.ds(blocks, blocks)].astype(jnp.bfloat16)
    own_copy.wait()


def feat_kernel(
    plan_ref, arrived_ref, own_any, mate_any, weight_ref, out_ref, held, mate, acc, sems
):
    blocks, block, width = out_ref.shape
    own_copy = pltpu.make_async_copy(own_any, acc.at[pl.ds(0, blocks)], sems.at[0])
    copy = pltpu.make_async_copy(arrived_ref.at[:, pl.ds(0, 2 * block)], held, sems.at[1])
    mate_copy = pltpu.make_async_copy(mate_any, mate, sems.at[2])
    own_copy.start()
    copy.start()
    mate_copy.start()
    acc[2 * blocks] = jnp.zeros(acc.shape[1:], jnp.float32)
    own_copy.wait()
    copy.wait()

    def products(g):
        rows = jnp.concatenate([whole(held, plan_ref[0, g * GROUP + k], block) for k in range(GROUP)], axis=0)
        return lax.dot_general(rows, weight_ref[plan_ref[2, g * GROUP]], ACROSS, preferred_element_type=jnp.float32)

    add_groups(plan_ref, 0, acc, block, products)
    mate_copy.wait()
    out_ref[...] = (acc[pl.ds(0, blocks)] + mate[...].astype(jnp.float32)).astype(jnp.bfloat16)


def share_kernel(scale, spread_ref, share_ref):
    share = (jnp.sum(spread_ref[...], axis=0) * scale).astype(jnp.bfloat16)
    for i in range(share_ref.shape[0]):
        share_ref[i] = share


def shards(features, out_grad, rel_weight, root_weight, tiles, tile_dest, tile_peer, tile_source, tile_rel):
    dev_count = lax.axis_size(AXES)
    chips = lax.axis_size(CHIPS)
    core = lax.axis_index("c")
    block = tiles.shape[1]
    width = features.shape[1]
    rel_count = rel_weight.shape[0]
    blocks = features.shape[0] // block
    scale = 1.0 / math.sqrt(features.shape[0] * dev_count)
    swap = [(0, 1), (1, 0)]
    grad_blocks = out_grad.reshape(blocks, block, width)
    feat_blocks = features.reshape(blocks, block, width)

    mate_blocks = lax.ppermute(feat_blocks, "c", swap)
    outgoing, later = make_messages(tile_dest, tile_peer[:, 0], tile_rel, tile_source, tiles, grad_blocks, dev_count)
    outgoing, later, core, mate_blocks = lax.optimization_barrier(
        (outgoing, later, core[None].astype(jnp.int32), mate_blocks)
    )

    def exchange(array):
        return lax.all_to_all(array, AXES, split_axis=0, concat_axis=0, tiled=True)

    arrived = exchange(outgoing)

    dma = pltpu.SemaphoreType.DMA
    cost = pl.CostEstimate(
        flops=2 * dev_count * block * width * width, bytes_accessed=dev_count * block * width * 3, transcendentals=0
    )
    half_rows = (1 + rel_count) * width
    half = jax.ShapeDtypeStruct((half_rows, width // 2), jnp.float32)
    local = pltpu.VMEM(grad_blocks.shape, jnp.bfloat16)
    turned = pltpu.VMEM((2 * blocks + 1, width, block), jnp.bfloat16)
    plan_type = jax.ShapeDtypeStruct((16, plan_places(dev_count, rel_count)), jnp.int32)
    def weights(arrived):
        own, other, plan = pl.pallas_call(
            weight_kernel,
            out_shape=(half, half, plan_type),
            in_specs=[HBM, HBM, HBM, HBM, SMEM],
            out_specs=(VMEM, VMEM, VMEM),
            scratch_shapes=[
                pltpu.VMEM((dev_count, 2 * block, LANES), jnp.bfloat16),
                pltpu.VMEM((dev_count, block, LANES), jnp.bfloat16),
                pltpu.VMEM((dev_count, TAG_ROWS, LANES), jnp.bfloat16),
                local,
                local,
                local,
                turned,
                pltpu.VMEM((1 + rel_count, width, width), jnp.float32),
                pltpu.VMEM((rel_count, width, width // 2), jnp.float32),
                pltpu.SMEM(plan_type.shape, jnp.int32),
                dma,
                dma((6,)),
            ],
            compiler_params=pltpu.CompilerParams(vmem_limit_bytes=50 * MIB),
            cost_estimate=cost,
        )(arrived, feat_blocks, mate_blocks, grad_blocks, core)
        return own + lax.ppermute(other, "c", swap), plan

    def take_later(arrived, later):
        later = exchange(later)
        own, plan = weights(arrived)
        later, own, plan = lax.optimization_barrier((later, own, plan))
        own = pl.pallas_call(
            later_kernel,
            out_shape=half,
            in_specs=[SMEM] + [HBM] * 4,
            out_specs=VMEM,
            scratch_shapes=[pltpu.VMEM(later.shape, jnp.bfloat16), local, local, turned, dma((4,))],
            compiler_params=pltpu.CompilerParams(vmem_limit_bytes=57 * MIB),
        )(plan, later, feat_blocks, mate_blocks, own)
        return later, own, plan

    def take_none(arrived, later):
        own, plan = weights(arrived)
        unread = pl.pallas_call(
            lambda core_ref, out_ref: None,
            out_shape=jax.ShapeDtypeStruct(later.shape, later.dtype),
            in_specs=[SMEM],
            out_specs=HBM,
        )(core)
        return unread, own, plan

    any_later = jnp.max(arrived[:, 3 * block, 5 * FIELD]) > 0
    later, own, plan = lax.cond(any_later, take_later, take_none, arrived, later)
    own, plan = lax.optimization_barrier((own, plan))
    own_part, mate_part = pl.pallas_call(
        halves_kernel,
        out_shape=(
            jax.ShapeDtypeStruct(grad_blocks.shape, jnp.float32),
            jax.ShapeDtypeStruct(grad_blocks.shape, jnp.bfloat16),
        ),
        in_specs=[SMEM, SMEM, HBM, HBM, VMEM, VMEM, VMEM],
        out_specs=(HBM, VMEM),
        scratch_shapes=[
            pltpu.VMEM((dev_count, block, LANES), jnp.bfloat16),
            pltpu.VMEM((2 * blocks + 1, block, width), jnp.float32),
            dma,
            dma,
        ],
        compiler_params=pltpu.CompilerParams(vmem_limit_bytes=49 * MIB),
        cost_estimate=cost,
    )(plan, core, arrived, later, grad_blocks, root_weight, rel_weight)
    shape = (chips, half_rows // chips, width // 2)
    spread = lax.all_to_all(own.reshape(shape), CHIPS, 0, 0, tiled=True)
    spread, own_part, mate_part, plan = lax.optimization_barrier((spread, own_part, mate_part, plan))
    mate_part = lax.ppermute(mate_part, "c", swap)
    share = pl.pallas_call(
        functools.partial(share_kernel, scale),
        out_shape=jax.ShapeDtypeStruct(shape, jnp.bfloat16),
        in_specs=[VMEM],
        out_specs=VMEM,
        compiler_params=pltpu.CompilerParams(vmem_limit_bytes=8 * MIB),
    )(spread)
    own = lax.all_to_all(share, CHIPS, 0, 0, tiled=True).reshape(half.shape)
    grad_feat = pl.pallas_call(
        feat_kernel,
        out_shape=jax.ShapeDtypeStruct(grad_blocks.shape, jnp.bfloat16),
        in_specs=[SMEM, HBM, HBM, HBM, VMEM],
        out_specs=VMEM,
        scratch_shapes=[
            pltpu.VMEM((dev_count, 2 * block, LANES), jnp.bfloat16),
            local,
            pltpu.VMEM((2 * blocks + 1, block, width), jnp.float32),
            dma((3,)),
        ],
        compiler_params=pltpu.CompilerParams(vmem_limit_bytes=49 * MIB),
        cost_estimate=cost,
    )(plan, arrived, own_part, mate_part, rel_weight)
    own, grad_feat = lax.optimization_barrier((own, grad_feat))
    other = lax.ppermute(own, "c", swap)
    core = core[0]
    left = jnp.where(core == 0, own, other).astype(jnp.float32)
    right = jnp.where(core == 0, other, own).astype(jnp.float32)
    grad_weights = jnp.concatenate([left, right], axis=1).reshape(1 + rel_count, width, width)
    return grad_feat.reshape(features.shape), grad_weights


def solution(mesh):
    sizes = (4, 4, 4, 2)
    fine = Mesh(mesh.devices.reshape(sizes), AXES)
    return jax.shard_map(
        shards,
        mesh=fine,
        in_specs=(
            P(AXES, None),
            P(AXES, None),
            P(),
            P(),
            P(AXES, None, None),
            P(AXES),
            P(AXES, None),
            P(AXES),
            P(AXES),
        ),
        out_specs=(P(AXES, None), P()),
        check_vma=False,
    )
```

```python
import functools
import math

import jax
import jax.numpy as jnp
from jax import lax
from jax.experimental import pallas as pl
from jax.experimental.pallas import tpu as pltpu
from jax.sharding import Mesh
from jax.sharding import PartitionSpec as P

AXES = ("z", "y", "x", "c")
CHIPS = ("z", "y", "x")
VMEM = pl.BlockSpec(memory_space=pltpu.VMEM)
HBM = pl.BlockSpec(memory_space=pltpu.HBM)
SMEM = pl.BlockSpec(memory_space=pltpu.SMEM)
MIB = 1024 * 1024
GROUP = 8
LANES = 128
TAG_ROWS = 16
FIELD = 16


def message_kernel(
    blocks, parts, dest_any, peer_any, rel_any, source_any, tiles_ref, grad_any, out_ref, later_ref,
    dest, peers, rels, sources, count, seconds, flag, grad, held, made, marks, tags, sems, out_sem,
):
    tile_count, block, _ = tiles_ref.shape
    part = tile_count // parts
    pairs = ((dest_any, dest), (peer_any, peers), (rel_any, rels), (source_any, sources), (grad_any, grad))
    early = [pltpu.make_async_copy(src, dst, sems.at[parts + i]) for i, (src, dst) in enumerate(pairs)]
    for copy in early:
        copy.start()

    def fetch(i):
        rows = pl.ds(i * part, part)
        return pltpu.make_async_copy(tiles_ref.at[rows], held.at[rows], sems.at[i])

    for i in range(parts):
        fetch(i).start()

    def clear(i, carry):
        count[2 * i] = 0
        count[2 * i + 1] = 0
        seconds[i] = 0
        return carry

    lax.fori_loop(0, seconds.shape[0], clear, 0)
    flag[0] = 0
    marks[...] = jnp.full(marks.shape, -1.0, jnp.float32)
    field = lax.broadcasted_iota(jnp.int32, marks.shape[1:], 1) // FIELD
    left, right = pl.ds(0, block), pl.ds(block, block)
    half = pl.ds(2 * block, block)

    def send(src, dst):
        pltpu.make_async_copy(src, dst, out_sem).start()

    def place(t, carry):
        peer = peers[t]
        rank = count[peer]
        count[peer] = rank + 1
        mark = (rels[t] * blocks + sources[t]).astype(jnp.float32)

        @pl.when(rank == 0)
        def _():
            marks[peer] = jnp.where(field == 0, mark, marks[peer])
            send(made.at[t], out_ref.at[peer, pl.ds(0, 2 * block)])

        @pl.when(rank != 0)
        def _():
            chip = lax.shift_right_logical(peer, 1)
            later = seconds[chip]
            seconds[chip] = later + 1
            core = (peer & 1).astype(jnp.float32)
            first = 2 * chip
            for side in range(2):
                old = marks[first + side]
                old = jnp.where(field == 2 + 2 * later, core, old)
                marks[first + side] = jnp.where(field == 1 + 2 * later, mark, old)

            @pl.when(later == 0)
            def _():
                send(made.at[t, left], out_ref.at[first, half])
                send(made.at[t, right], out_ref.at[first + 1, half])

            @pl.when(later != 0)
            def _():
                flag[0] = 1
                send(made.at[t, left], later_ref.at[first])
                send(made.at[t, right], later_ref.at[first + 1])

        return carry

    for copy in early:
        copy.wait()

    for i in range(parts):
        fetch(i).wait()
        for t in range(i * part, (i + 1) * part):
            message = lax.dot_general(
                held[t], grad[dest[t]], (((0,), (0,)), ((), ())), preferred_element_type=jnp.float32
            ).astype(jnp.bfloat16)
            made[t, left] = message[:, :LANES]
            made[t, right] = message[:, LANES:]
        lax.fori_loop(i * part, (i + 1) * part, place, 0)

    any_later = flag[0].astype(jnp.float32)
    all_marks = jnp.where(field[None] == 5, any_later, marks[...])
    tags[...] = jnp.concatenate([all_marks, all_marks], axis=1).astype(jnp.bfloat16)
    tag_copy = pltpu.make_async_copy(tags, out_ref.at[:, pl.ds(3 * block, TAG_ROWS)], sems.at[0])
    tag_copy.start()
    pltpu.make_async_copy(made, out_ref.at[pl.ds(0, tile_count), pl.ds(0, 2 * block)], out_sem).wait()
    tag_copy.wait()


def make_messages(tile_dest, peer_list, tile_rel, tile_source, tiles, grad_blocks, dev_count):
    tile_count, block, _ = tiles.shape
    blocks, _, width = grad_blocks.shape
    parts = 8
    numbers = pltpu.SMEM((tile_count,), jnp.int32)

    def kernel(*refs):
        message_kernel(blocks, parts, *refs)

    return pl.pallas_call(
        kernel,
        out_shape=(
            jax.ShapeDtypeStruct((dev_count, 3 * block + TAG_ROWS, LANES), jnp.bfloat16),
            jax.ShapeDtypeStruct((dev_count, block, LANES), jnp.bfloat16),
        ),
        in_specs=[HBM] * 6,
        out_specs=(HBM, HBM),
        scratch_shapes=[
            numbers,
            numbers,
            numbers,
            numbers,
            pltpu.SMEM((dev_count,), jnp.int32),
            pltpu.SMEM((dev_count // 2,), jnp.int32),
            pltpu.SMEM((1,), jnp.int32),
            pltpu.VMEM(grad_blocks.shape, jnp.bfloat16),
            pltpu.VMEM(tiles.shape, jnp.bfloat16),
            pltpu.VMEM((tile_count, 2 * block, LANES), jnp.bfloat16),
            pltpu.VMEM((dev_count, TAG_ROWS // 2, LANES), jnp.float32),
            pltpu.VMEM((dev_count, TAG_ROWS, LANES), jnp.bfloat16),
            pltpu.SemaphoreType.DMA((parts + 5,)),
            pltpu.SemaphoreType.DMA,
        ],
        compiler_params=pltpu.CompilerParams(vmem_limit_bytes=58 * MIB),
        cost_estimate=pl.CostEstimate(
            flops=2 * tile_count * block * block * width,
            bytes_accessed=tile_count * block * (block + width) * 2,
            transcendentals=0,
        ),
    )(tile_dest, peer_list, tile_rel, tile_source, tiles, grad_blocks)


def plan_places(senders, rel_count):
    return -(-(senders + (GROUP - 1) * rel_count) // LANES) * LANES


def make_plans(tags, core, blocks, rel_count):
    senders = tags.shape[0]
    places = plan_places(senders, rel_count)
    wide = 1 << (rel_count - 1).bit_length()
    square = (senders, senders)
    row, lane = lax.broadcasted_iota(jnp.int32, square, 0), lax.broadcasted_iota(jnp.int32, square, 1)
    lane_set, lane_rel = lane // wide, (lane % wide).astype(jnp.float32)
    below = (lane < row).astype(jnp.float32).astype(jnp.bfloat16)
    ahead = ((row < lane) & (row // wide == lane_set)).astype(jnp.float32).astype(jnp.bfloat16)
    at = lax.broadcasted_iota(jnp.int32, (senders, places), 1)
    at, lead = at.astype(jnp.float32), (at // GROUP * GROUP).astype(jnp.float32)

    def column(i):
        return tags[:, i * FIELD : i * FIELD + 1]

    tag = [column(0), column(1), column(3)]
    rel = [jnp.floor(t * (1.0 / blocks)) for t in tag]
    used = [jnp.where((lane_set == q) & (lane_rel == r) & (t >= 0), 1.0, 0.0) for q, (t, r) in enumerate(zip(tag, rel))]
    every = used[0] + used[1] + used[2]
    before = jnp.dot(below, every.astype(jnp.bfloat16), preferred_element_type=jnp.float32)
    groups = jnp.floor((jnp.sum(every, axis=0, keepdims=True) + (GROUP - 1)) * (1.0 / GROUP))
    first = jnp.dot(
        jnp.broadcast_to(groups, (TAG_ROWS, senders)).astype(jnp.bfloat16), ahead, preferred_element_type=jnp.float32
    )[0:1]
    spot = before + first * GROUP
    across = tags.T
    line = lax.broadcasted_iota(jnp.int32, (TAG_ROWS, senders), 0)
    name = lax.broadcasted_iota(jnp.int32, (1, senders), 1).astype(jnp.float32)
    rows = []
    for q, i in enumerate((0, 1, 3)):
        place = jnp.where(tag[q] >= 0, jnp.sum(used[q] * spot, axis=1, keepdims=True), -1.0)
        here = jnp.where(place == at, 1.0, 0.0).astype(jnp.bfloat16)
        leads = jnp.where(place == lead, 1.0, 0.0).astype(jnp.bfloat16)
        mark = across[i * FIELD : i * FIELD + 1]
        relation = jnp.floor(mark * (1.0 / blocks))
        source = mark - relation * blocks - 2 * blocks
        if q:
            owner = across[(i + 1) * FIELD : (i + 1) * FIELD + 1]
            source = source + jnp.where(owner == core, 0.0, float(blocks))
        named = jnp.where(line == 0, 1.0, jnp.where(line == 1, name, jnp.where(line == 2, source, relation)))
        named = named.astype(jnp.bfloat16)
        own = jnp.dot(named, here, preferred_element_type=jnp.float32)
        led = jnp.dot(named, leads, preferred_element_type=jnp.float32)
        total = jnp.sum(jnp.where(lane_set[0:1] == q, groups, 0.0), axis=1, keepdims=True)
        rows += [jnp.where(own[0:1] > 0, own[1:2], led[1:2]), own[2:3] + 2 * blocks, led[3:4]]
        rows.append(jnp.broadcast_to(total, (1, places)))
    rows += [jnp.zeros((1, places), jnp.float32)] * 4
    return jnp.concatenate(rows, axis=0).astype(jnp.int32)


def walk_groups(end, use):
    def single(g, carry):
        use(g)
        return carry

    def two(j, carry):
        use(2 * j)
        use(2 * j + 1)
        return carry

    pairs = lax.shift_right_logical(end, 1)
    lax.fori_loop(0, pairs, two, 0)
    lax.fori_loop(2 * pairs, end, single, 0)


def whole(ref, sender, block):
    return jnp.concatenate([ref[sender, pl.ds(0, block)], ref[sender, pl.ds(block, block)]], axis=1)


def later_flag_kernel(arrived_ref, flag_ref, tags, sem):
    first = arrived_ref.shape[1] - TAG_ROWS
    copy = pltpu.make_async_copy(arrived_ref.at[:, pl.ds(first, TAG_ROWS)], tags, sem)
    copy.start()
    copy.wait()
    most = jnp.max(tags[...].astype(jnp.float32), axis=0)
    field = lax.broadcasted_iota(jnp.int32, most.shape, 1) // FIELD
    flag_ref[0] = (jnp.max(jnp.where(field == 5, most, -1.0)) > 0).astype(jnp.int32)


def turn_blocks(feat, mate, turned):
    blocks = feat.shape[0]
    turned[2 * blocks] = jnp.zeros(turned.shape[1:], turned.dtype)

    def turn(b, carry):
        for k in range(4):
            turned[b * 4 + k] = feat[b * 4 + k].T
            turned[blocks + b * 4 + k] = mate[b * 4 + k].T
        return carry

    lax.fori_loop(0, blocks // 4, turn, 0)


def weight_kernel(
    arrived_ref, feat_any, mate_any, grad_any, core_ref, own_ref, other_ref, plan_ref,
    held, halves, tags, feat, mate, grad, turned, acc, part, plan, plan_sem, sems,
):
    kinds, width, _ = acc.shape
    blocks, block, _ = feat.shape
    half = width // 2
    pairs = (
        (arrived_ref.at[:, pl.ds(3 * block, TAG_ROWS)], tags),
        (feat_any, feat),
        (mate_any, mate),
        (grad_any, grad),
        (arrived_ref.at[:, pl.ds(0, 2 * block)], held),
        (arrived_ref.at[:, pl.ds(2 * block, block)], halves),
    )
    copies = [pltpu.make_async_copy(src, dst, sems.at[i]) for i, (src, dst) in enumerate(pairs)]
    for copy in copies[:5]:
        copy.start()
    acc[...] = jnp.zeros_like(acc)
    part[...] = jnp.zeros_like(part)
    copies[0].wait()
    plan_ref[...] = make_plans(
        jnp.max(tags[...].astype(jnp.float32), axis=1), core_ref[0].astype(jnp.float32), blocks, kinds - 1
    )
    plan_copy = pltpu.make_async_copy(plan_ref, plan, plan_sem)
    plan_copy.start()
    copies[1].wait()
    copies[2].wait()
    copies[5].start()
    turn_blocks(feat, mate, turned)
    copies[3].wait()

    def root(g, carry):
        left = jnp.concatenate([turned[g * GROUP + k] for k in range(GROUP)], axis=1)
        right = grad[pl.ds(g * GROUP, GROUP)].reshape(GROUP * block, width)
        acc[0] += jnp.dot(left, right, preferred_element_type=jnp.float32)
        return carry

    lax.fori_loop(0, blocks // GROUP, root, 0)
    plan_copy.wait()

    def lefts(g, row):
        return jnp.concatenate([turned[plan[row + 1, g * GROUP + k]] for k in range(GROUP)], axis=1)

    def use(g):
        right = jnp.concatenate([whole(held, plan[0, g * GROUP + k], block) for k in range(GROUP)], axis=0)
        acc[1 + plan[2, g * GROUP]] += jnp.dot(lefts(g, 0), right, preferred_element_type=jnp.float32)

    def use_half(g):
        right = jnp.concatenate([halves[plan[4, g * GROUP + k]] for k in range(GROUP)], axis=0)
        part[plan[6, g * GROUP]] += jnp.dot(lefts(g, 4), right, preferred_element_type=jnp.float32)

    copies[4].wait()
    walk_groups(plan[3, 0], use)
    copies[5].wait()
    walk_groups(plan[7, 0], use_half)

    def split(own, other):
        for r in range(kinds):
            rows = pl.ds(r * width, width)
            own_ref[rows] = acc[r, :, own] + part[r - 1] if r else acc[r, :, own]
            other_ref[rows] = acc[r, :, other]

    first, second = pl.ds(0, half), pl.ds(half, half)

    @pl.when(core_ref[0] == 0)
    def _():
        split(first, second)

    @pl.when(core_ref[0] != 0)
    def _():
        split(second, first)


def later_kernel(plan, later_any, feat_any, mate_any, before_any, own_ref, later, feat, mate, turned, sems):
    width = feat.shape[2]
    pairs = ((before_any, own_ref), (feat_any, feat), (mate_any, mate), (later_any, later))
    copies = [pltpu.make_async_copy(src, dst, sems.at[i]) for i, (src, dst) in enumerate(pairs)]
    for copy in copies:
        copy.start()
    for copy in copies[:3]:
        copy.wait()

    @pl.when(plan[11, 0] > 0)
    def _():
        turn_blocks(feat, mate, turned)

    copies[3].wait()

    def use(g):
        left = jnp.concatenate([turned[plan[9, g * GROUP + k]] for k in range(GROUP)], axis=1)
        right = jnp.concatenate([later[plan[8, g * GROUP + k]] for k in range(GROUP)], axis=0)
        rows = pl.ds(pl.multiple_of((1 + plan[10, g * GROUP]) * width, width), width)
        own_ref[rows] += jnp.dot(left, right, preferred_element_type=jnp.float32)

    walk_groups(plan[11, 0], use)


def add_groups(plan_ref, row, acc, block, products):
    def use(g):
        part = products(g)
        for k in range(GROUP):
            acc[plan_ref[row + 1, g * GROUP + k]] += part[k * block : (k + 1) * block]

    walk_groups(plan_ref[row + 3, 0], use)


ACROSS = (((1,), (1,)), ((), ()))


def halves_kernel(
    plan_ref, core_ref, arrived_ref, grad_ref, root_ref, weight_ref, own_any, mate_ref, halves, acc, sem
):
    blocks, block, width = mate_ref.shape
    copy = pltpu.make_async_copy(arrived_ref.at[:, pl.ds(2 * block, block)], halves, sem)
    copy.start()
    acc[pl.ds(blocks, blocks + 1)] = jnp.zeros((blocks + 1, block, width), jnp.float32)

    def base(g, carry):
        rows = grad_ref[pl.ds(g * GROUP, GROUP)].reshape(GROUP * block, width)
        part = lax.dot_general(rows, root_ref[...], ACROSS, preferred_element_type=jnp.float32)
        acc[pl.ds(g * GROUP, GROUP)] = part.reshape(GROUP, block, width)
        return carry

    lax.fori_loop(0, blocks // GROUP, base, 0)
    copy.wait()
    add_groups(plan_ref, 4, acc, block, half_products(plan_ref, core_ref, weight_ref, halves, 4))
    own_copy = pltpu.make_async_copy(acc.at[pl.ds(0, blocks)], own_any, sem)
    own_copy.start()
    mate_ref[...] = acc[pl.ds(blocks, blocks)].astype(jnp.bfloat16)
    own_copy.wait()


def half_products(plan_ref, core_ref, weight_ref, halves, row):
    width = weight_ref.shape[1]
    half = width // 2
    lanes = pl.ds(pl.multiple_of(core_ref[0] * half, half), half)

    def products(g):
        rows = jnp.concatenate([halves[plan_ref[row, g * GROUP + k]] for k in range(GROUP)], axis=0)
        weight = weight_ref[plan_ref[row + 2, g * GROUP], :, lanes]
        return lax.dot_general(rows, weight, ACROSS, preferred_element_type=jnp.float32)

    return products


def early_kernel(plan_ref, core_ref, arrived_ref, grad_ref, root_ref, weight_ref, out_any, held, halves, acc, sems):
    blocks, block, width = grad_ref.shape
    copy = pltpu.make_async_copy(arrived_ref.at[:, pl.ds(0, 2 * block)], held, sems.at[0])
    half_copy = pltpu.make_async_copy(arrived_ref.at[:, pl.ds(2 * block, block)], halves, sems.at[1])
    copy.start()
    half_copy.start()
    acc[pl.ds(blocks, blocks + 1)] = jnp.zeros((blocks + 1, block, width), jnp.float32)

    def base(g, carry):
        rows = grad_ref[pl.ds(g * GROUP, GROUP)].reshape(GROUP * block, width)
        part = lax.dot_general(rows, root_ref[...], ACROSS, preferred_element_type=jnp.float32)
        acc[pl.ds(g * GROUP, GROUP)] = part.reshape(GROUP, block, width)
        return carry

    lax.fori_loop(0, blocks // GROUP, base, 0)

    def products(g):
        rows = jnp.concatenate([whole(held, plan_ref[0, g * GROUP + k], block) for k in range(GROUP)], axis=0)
        return lax.dot_general(rows, weight_ref[plan_ref[2, g * GROUP]], ACROSS, preferred_element_type=jnp.float32)

    copy.wait()
    add_groups(plan_ref, 0, acc, block, products)
    half_copy.wait()
    add_groups(plan_ref, 4, acc, block, half_products(plan_ref, core_ref, weight_ref, halves, 4))
    out_copy = pltpu.make_async_copy(acc.at[pl.ds(0, 2 * blocks)], out_any, sems.at[0])
    out_copy.start()
    out_copy.wait()


def late_kernel(plan_ref, core_ref, early_any, later_any, weight_ref, own_any, mate_ref, halves, acc, sems):
    blocks, block, width = mate_ref.shape
    early_copy = pltpu.make_async_copy(early_any, acc.at[pl.ds(0, 2 * blocks)], sems.at[0])
    later_copy = pltpu.make_async_copy(later_any, halves, sems.at[1])
    early_copy.start()
    later_copy.start()
    acc[2 * blocks] = jnp.zeros(acc.shape[1:], jnp.float32)
    early_copy.wait()
    later_copy.wait()
    add_groups(plan_ref, 8, acc, block, half_products(plan_ref, core_ref, weight_ref, halves, 8))
    own_copy = pltpu.make_async_copy(acc.at[pl.ds(0, blocks)], own_any, sems.at[0])
    own_copy.start()
    mate_ref[...] = acc[pl.ds(blocks, blocks)].astype(jnp.bfloat16)
    own_copy.wait()


def feat_kernel(
    plan_ref, arrived_ref, own_any, mate_any, weight_ref, out_ref, held, mate, acc, sems
):
    blocks, block, width = out_ref.shape
    own_copy = pltpu.make_async_copy(own_any, acc.at[pl.ds(0, blocks)], sems.at[0])
    copy = pltpu.make_async_copy(arrived_ref.at[:, pl.ds(0, 2 * block)], held, sems.at[1])
    mate_copy = pltpu.make_async_copy(mate_any, mate, sems.at[2])
    own_copy.start()
    copy.start()
    mate_copy.start()
    acc[2 * blocks] = jnp.zeros(acc.shape[1:], jnp.float32)
    own_copy.wait()
    copy.wait()

    def products(g):
        rows = jnp.concatenate([whole(held, plan_ref[0, g * GROUP + k], block) for k in range(GROUP)], axis=0)
        return lax.dot_general(rows, weight_ref[plan_ref[2, g * GROUP]], ACROSS, preferred_element_type=jnp.float32)

    add_groups(plan_ref, 0, acc, block, products)
    mate_copy.wait()
    out_ref[...] = (acc[pl.ds(0, blocks)] + mate[...].astype(jnp.float32)).astype(jnp.bfloat16)


def share_kernel(scale, spread_ref, share_ref):
    share = (jnp.sum(spread_ref[...], axis=0) * scale).astype(jnp.bfloat16)
    for i in range(share_ref.shape[0]):
        share_ref[i] = share


def shards(features, out_grad, rel_weight, root_weight, tiles, tile_dest, tile_peer, tile_source, tile_rel):
    dev_count = lax.axis_size(AXES)
    chips = lax.axis_size(CHIPS)
    core = lax.axis_index("c")
    block = tiles.shape[1]
    width = features.shape[1]
    rel_count = rel_weight.shape[0]
    blocks = features.shape[0] // block
    scale = 1.0 / math.sqrt(features.shape[0] * dev_count)
    swap = [(0, 1), (1, 0)]
    grad_blocks = out_grad.reshape(blocks, block, width)
    feat_blocks = features.reshape(blocks, block, width)

    mate_blocks = lax.ppermute(feat_blocks, "c", swap)
    outgoing, later = make_messages(tile_dest, tile_peer[:, 0], tile_rel, tile_source, tiles, grad_blocks, dev_count)
    outgoing, later, core, mate_blocks = lax.optimization_barrier(
        (outgoing, later, core[None].astype(jnp.int32), mate_blocks)
    )

    def exchange(array):
        return lax.all_to_all(array, AXES, split_axis=0, concat_axis=0, tiled=True)

    arrived = exchange(outgoing)

    dma = pltpu.SemaphoreType.DMA
    cost = pl.CostEstimate(
        flops=2 * dev_count * block * width * width, bytes_accessed=dev_count * block * width * 3, transcendentals=0
    )
    half_rows = (1 + rel_count) * width
    half = jax.ShapeDtypeStruct((half_rows, width // 2), jnp.float32)
    local = pltpu.VMEM(grad_blocks.shape, jnp.bfloat16)
    turned = pltpu.VMEM((2 * blocks + 1, width, block), jnp.bfloat16)
    plan_type = jax.ShapeDtypeStruct((16, plan_places(dev_count, rel_count)), jnp.int32)
    def weights(arrived):
        own, other, plan = pl.pallas_call(
            weight_kernel,
            out_shape=(half, half, plan_type),
            in_specs=[HBM, HBM, HBM, HBM, SMEM],
            out_specs=(VMEM, VMEM, VMEM),
            scratch_shapes=[
                pltpu.VMEM((dev_count, 2 * block, LANES), jnp.bfloat16),
                pltpu.VMEM((dev_count, block, LANES), jnp.bfloat16),
                pltpu.VMEM((dev_count, TAG_ROWS, LANES), jnp.bfloat16),
                local,
                local,
                local,
                turned,
                pltpu.VMEM((1 + rel_count, width, width), jnp.float32),
                pltpu.VMEM((rel_count, width, width // 2), jnp.float32),
                pltpu.SMEM(plan_type.shape, jnp.int32),
                dma,
                dma((6,)),
            ],
            compiler_params=pltpu.CompilerParams(vmem_limit_bytes=50 * MIB),
            cost_estimate=cost,
        )(arrived, feat_blocks, mate_blocks, grad_blocks, core)
        return own + lax.ppermute(other, "c", swap), plan

    own_type = jax.ShapeDtypeStruct(grad_blocks.shape, jnp.float32)
    mate_type = jax.ShapeDtypeStruct(grad_blocks.shape, jnp.bfloat16)
    held = pltpu.VMEM((dev_count, 2 * block, LANES), jnp.bfloat16)
    halves = pltpu.VMEM((dev_count, block, LANES), jnp.bfloat16)
    sums = pltpu.VMEM((2 * blocks + 1, block, width), jnp.float32)
    roomy = pltpu.CompilerParams(vmem_limit_bytes=49 * MIB)

    def finish(own, plan, first_sums, last_sums):
        own, plan = lax.optimization_barrier((own, plan))
        own_part, mate_part = first_sums(plan)
        shape = (chips, half_rows // chips, width // 2)
        spread = lax.all_to_all(own.reshape(shape), CHIPS, 0, 0, tiled=True)
        spread, own_part, mate_part, plan = lax.optimization_barrier((spread, own_part, mate_part, plan))
        mate_part = lax.ppermute(mate_part, "c", swap)
        share = pl.pallas_call(
            functools.partial(share_kernel, scale),
            out_shape=jax.ShapeDtypeStruct(shape, jnp.bfloat16),
            in_specs=[VMEM],
            out_specs=VMEM,
            compiler_params=pltpu.CompilerParams(vmem_limit_bytes=8 * MIB),
        )(spread)
        own = lax.all_to_all(share, CHIPS, 0, 0, tiled=True).reshape(half.shape)
        grad_feat = last_sums(plan, own_part, mate_part)
        own, grad_feat = lax.optimization_barrier((own, grad_feat))
        other = lax.ppermute(own, "c", swap)
        left = jnp.where(core[0] == 0, own, other).astype(jnp.float32)
        right = jnp.where(core[0] == 0, other, own).astype(jnp.float32)
        grad_weights = jnp.concatenate([left, right], axis=1).reshape(1 + rel_count, width, width)
        return grad_feat.reshape(features.shape), grad_weights

    def take_later(arrived, later):
        later = exchange(later)
        own, plan = weights(arrived)
        early = pl.pallas_call(
            early_kernel,
            out_shape=jax.ShapeDtypeStruct((2 * blocks, block, width), jnp.float32),
            in_specs=[SMEM, SMEM, HBM, VMEM, VMEM, VMEM],
            out_specs=HBM,
            scratch_shapes=[held, halves, sums, dma((2,))],
            compiler_params=roomy,
            cost_estimate=cost,
        )(plan, core, arrived, grad_blocks, root_weight, rel_weight)
        later, own, plan, early = lax.optimization_barrier((later, own, plan, early))
        own = pl.pallas_call(
            later_kernel,
            out_shape=half,
            in_specs=[SMEM] + [HBM] * 4,
            out_specs=VMEM,
            scratch_shapes=[halves, local, local, turned, dma((4,))],
            compiler_params=pltpu.CompilerParams(vmem_limit_bytes=57 * MIB),
        )(plan, later, feat_blocks, mate_blocks, own)

        def first_sums(plan):
            return pl.pallas_call(
                late_kernel,
                out_shape=(own_type, mate_type),
                in_specs=[SMEM, SMEM, HBM, HBM, VMEM],
                out_specs=(HBM, VMEM),
                scratch_shapes=[halves, sums, dma((2,))],
                compiler_params=roomy,
                cost_estimate=cost,
            )(plan, core, early, later, rel_weight)

        def last_sums(plan, own_part, mate_part):
            return (own_part + mate_part.astype(jnp.float32)).astype(jnp.bfloat16)

        return finish(own, plan, first_sums, last_sums)

    def take_none(arrived, later):
        own, plan = weights(arrived)

        def first_sums(plan):
            return pl.pallas_call(
                halves_kernel,
                out_shape=(own_type, mate_type),
                in_specs=[SMEM, SMEM, HBM, VMEM, VMEM, VMEM],
                out_specs=(HBM, VMEM),
                scratch_shapes=[halves, sums, dma],
                compiler_params=roomy,
                cost_estimate=cost,
            )(plan, core, arrived, grad_blocks, root_weight, rel_weight)

        def last_sums(plan, own_part, mate_part):
            return pl.pallas_call(
                feat_kernel,
                out_shape=mate_type,
                in_specs=[SMEM, HBM, HBM, HBM, VMEM],
                out_specs=VMEM,
                scratch_shapes=[held, local, sums, dma((3,))],
                compiler_params=roomy,
                cost_estimate=cost,
            )(plan, arrived, own_part, mate_part, rel_weight)

        return finish(own, plan, first_sums, last_sums)

    any_later = pl.pallas_call(
        later_flag_kernel,
        out_shape=jax.ShapeDtypeStruct((1,), jnp.int32),
        in_specs=[HBM],
        out_specs=SMEM,
        scratch_shapes=[pltpu.VMEM((dev_count, TAG_ROWS, LANES), jnp.bfloat16), dma],
        compiler_params=pltpu.CompilerParams(vmem_limit_bytes=58 * MIB),
    )(arrived)
    return lax.cond(any_later[0] > 0, take_later, take_none, arrived, later)


def solution(mesh):
    sizes = (4, 4, 4, 2)
    fine = Mesh(mesh.devices.reshape(sizes), AXES)
    return jax.shard_map(
        shards,
        mesh=fine,
        in_specs=(
            P(AXES, None),
            P(AXES, None),
            P(),
            P(),
            P(AXES, None, None),
            P(AXES),
            P(AXES, None),
            P(AXES),
            P(AXES),
        ),
        out_specs=(P(AXES, None), P()),
        check_vma=False,
    )
```

```python
import functools
import math

import jax
import jax.numpy as jnp
from jax import lax
from jax.experimental import pallas as pl
from jax.experimental.pallas import tpu as pltpu
from jax.sharding import Mesh
from jax.sharding import PartitionSpec as P

AXES = ("z", "y", "x", "c")
CHIPS = ("z", "y", "x")
VMEM = pl.BlockSpec(memory_space=pltpu.VMEM)
HBM = pl.BlockSpec(memory_space=pltpu.HBM)
SMEM = pl.BlockSpec(memory_space=pltpu.SMEM)
MIB = 1024 * 1024
GROUP = 8
LANES = 128
TAG_ROWS = 16
FIELD = 16


def message_kernel(
    blocks, parts, dest_any, peer_any, rel_any, source_any, tiles_ref, grad_any, out_ref, later_ref,
    dest, peers, rels, sources, ranks, count, seconds, flag, grad, held, made, marks, tags, sems, out_sem,
):
    tile_count, block, _ = tiles_ref.shape
    part = tile_count // parts
    pairs = ((dest_any, dest), (peer_any, peers), (rel_any, rels), (source_any, sources), (grad_any, grad))
    early = [pltpu.make_async_copy(src, dst, sems.at[parts + i]) for i, (src, dst) in enumerate(pairs)]
    for copy in early:
        copy.start()

    def fetch(i):
        rows = pl.ds(i * part, part)
        return pltpu.make_async_copy(tiles_ref.at[rows], held.at[rows], sems.at[i])

    for i in range(parts):
        fetch(i).start()

    def clear(i, carry):
        count[2 * i] = 0
        count[2 * i + 1] = 0
        seconds[i] = 0
        return carry

    lax.fori_loop(0, seconds.shape[0], clear, 0)
    flag[0] = 0
    marks[...] = jnp.full(marks.shape, -1.0, jnp.float32)
    field = lax.broadcasted_iota(jnp.int32, marks.shape[1:], 1) // FIELD
    left, right = pl.ds(0, block), pl.ds(block, block)
    half = pl.ds(2 * block, block)

    def send(src, dst):
        pltpu.make_async_copy(src, dst, out_sem).start()

    def rank_one(t, carry):
        peer = peers[t]
        chip = lax.shift_right_logical(peer, 1)
        mark = (rels[t] * blocks + sources[t]).astype(jnp.float32)
        second = count[peer]
        count[peer] = second + 1
        ranks[t] = 0

        @pl.when(second == 0)
        def _():
            marks[peer] = jnp.where(field == 0, mark, marks[peer])

        @pl.when(second != 0)
        def _():
            later = seconds[chip]
            seconds[chip] = later + 1
            ranks[t] = 1 + later
            flag[0] = flag[0] | later
            core = (peer & 1).astype(jnp.float32)
            for side in range(2):
                old = marks[2 * chip + side]
                old = jnp.where(field == 2 + 2 * later, core, old)
                marks[2 * chip + side] = jnp.where(field == 1 + 2 * later, mark, old)

        return carry

    for copy in early[:4]:
        copy.wait()
    lax.fori_loop(0, tile_count, rank_one, 0)
    any_later = flag[0].astype(jnp.float32)
    all_marks = jnp.where(field[None] == 5, any_later, marks[...])
    tags[...] = jnp.concatenate([all_marks, all_marks], axis=1).astype(jnp.bfloat16)
    tag_copy = pltpu.make_async_copy(tags, out_ref.at[:, pl.ds(3 * block, TAG_ROWS)], sems.at[parts])
    tag_copy.start()
    early[4].wait()

    def place(t, carry):
        peer = peers[t]
        rank = ranks[t]

        @pl.when(rank == 0)
        def _():
            send(made.at[t], out_ref.at[peer, pl.ds(0, 2 * block)])

        @pl.when(rank != 0)
        def _():
            first = lax.shift_left(lax.shift_right_logical(peer, 1), 1)

            @pl.when(rank == 1)
            def _():
                send(made.at[t, left], out_ref.at[first, half])
                send(made.at[t, right], out_ref.at[first + 1, half])

            @pl.when(rank != 1)
            def _():
                send(made.at[t, left], later_ref.at[first])
                send(made.at[t, right], later_ref.at[first + 1])

        return carry

    for i in range(parts):
        fetch(i).wait()
        for t in range(i * part, (i + 1) * part):
            message = lax.dot_general(
                held[t], grad[dest[t]], (((0,), (0,)), ((), ())), preferred_element_type=jnp.float32
            ).astype(jnp.bfloat16)
            made[t, left] = message[:, :LANES]
            made[t, right] = message[:, LANES:]
        lax.fori_loop(i * part, (i + 1) * part, place, 0)

    pltpu.make_async_copy(made, out_ref.at[pl.ds(0, tile_count), pl.ds(0, 2 * block)], out_sem).wait()
    tag_copy.wait()


def make_messages(tile_dest, peer_list, tile_rel, tile_source, tiles, grad_blocks, dev_count):
    tile_count, block, _ = tiles.shape
    blocks, _, width = grad_blocks.shape
    parts = 8
    numbers = pltpu.SMEM((tile_count,), jnp.int32)

    def kernel(*refs):
        message_kernel(blocks, parts, *refs)

    return pl.pallas_call(
        kernel,
        out_shape=(
            jax.ShapeDtypeStruct((dev_count, 3 * block + TAG_ROWS, LANES), jnp.bfloat16),
            jax.ShapeDtypeStruct((dev_count, block, LANES), jnp.bfloat16),
        ),
        in_specs=[HBM] * 6,
        out_specs=(HBM, HBM),
        scratch_shapes=[
            numbers,
            numbers,
            numbers,
            numbers,
            numbers,
            pltpu.SMEM((dev_count,), jnp.int32),
            pltpu.SMEM((dev_count // 2,), jnp.int32),
            pltpu.SMEM((1,), jnp.int32),
            pltpu.VMEM(grad_blocks.shape, jnp.bfloat16),
            pltpu.VMEM(tiles.shape, jnp.bfloat16),
            pltpu.VMEM((tile_count, 2 * block, LANES), jnp.bfloat16),
            pltpu.VMEM((dev_count, TAG_ROWS // 2, LANES), jnp.float32),
            pltpu.VMEM((dev_count, TAG_ROWS, LANES), jnp.bfloat16),
            pltpu.SemaphoreType.DMA((parts + 5,)),
            pltpu.SemaphoreType.DMA,
        ],
        compiler_params=pltpu.CompilerParams(vmem_limit_bytes=58 * MIB),
        cost_estimate=pl.CostEstimate(
            flops=2 * tile_count * block * block * width,
            bytes_accessed=tile_count * block * (block + width) * 2,
            transcendentals=0,
        ),
    )(tile_dest, peer_list, tile_rel, tile_source, tiles, grad_blocks)


def plan_places(senders, rel_count):
    return -(-(senders + (GROUP - 1) * rel_count) // LANES) * LANES


def make_plans(tags, core, blocks, rel_count):
    senders = tags.shape[0]
    places = plan_places(senders, rel_count)
    wide = 1 << (rel_count - 1).bit_length()
    square = (senders, senders)
    row, lane = lax.broadcasted_iota(jnp.int32, square, 0), lax.broadcasted_iota(jnp.int32, square, 1)
    lane_set, lane_rel = lane // wide, (lane % wide).astype(jnp.float32)
    below = (lane < row).astype(jnp.float32).astype(jnp.bfloat16)
    ahead = ((row < lane) & (row // wide == lane_set)).astype(jnp.float32).astype(jnp.bfloat16)
    at = lax.broadcasted_iota(jnp.int32, (senders, places), 1)
    at, lead = at.astype(jnp.float32), (at // GROUP * GROUP).astype(jnp.float32)

    def column(i):
        return tags[:, i * FIELD : i * FIELD + 1]

    tag = [column(0), column(1), column(3)]
    rel = [jnp.floor(t * (1.0 / blocks)) for t in tag]
    used = [jnp.where((lane_set == q) & (lane_rel == r) & (t >= 0), 1.0, 0.0) for q, (t, r) in enumerate(zip(tag, rel))]
    every = used[0] + used[1] + used[2]
    before = jnp.dot(below, every.astype(jnp.bfloat16), preferred_element_type=jnp.float32)
    groups = jnp.floor((jnp.sum(every, axis=0, keepdims=True) + (GROUP - 1)) * (1.0 / GROUP))
    first = jnp.dot(
        jnp.broadcast_to(groups, (TAG_ROWS, senders)).astype(jnp.bfloat16), ahead, preferred_element_type=jnp.float32
    )[0:1]
    spot = before + first * GROUP
    across = tags.T
    line = lax.broadcasted_iota(jnp.int32, (TAG_ROWS, senders), 0)
    name = lax.broadcasted_iota(jnp.int32, (1, senders), 1).astype(jnp.float32)
    rows = []
    for q, i in enumerate((0, 1, 3)):
        place = jnp.where(tag[q] >= 0, jnp.sum(used[q] * spot, axis=1, keepdims=True), -1.0)
        here = jnp.where(place == at, 1.0, 0.0).astype(jnp.bfloat16)
        leads = jnp.where(place == lead, 1.0, 0.0).astype(jnp.bfloat16)
        mark = across[i * FIELD : i * FIELD + 1]
        relation = jnp.floor(mark * (1.0 / blocks))
        source = mark - relation * blocks - 2 * blocks
        if q:
            owner = across[(i + 1) * FIELD : (i + 1) * FIELD + 1]
            source = source + jnp.where(owner == core, 0.0, float(blocks))
        named = jnp.where(line == 0, 1.0, jnp.where(line == 1, name, jnp.where(line == 2, source, relation)))
        named = named.astype(jnp.bfloat16)
        own = jnp.dot(named, here, preferred_element_type=jnp.float32)
        led = jnp.dot(named, leads, preferred_element_type=jnp.float32)
        total = jnp.sum(jnp.where(lane_set[0:1] == q, groups, 0.0), axis=1, keepdims=True)
        rows += [jnp.where(own[0:1] > 0, own[1:2], led[1:2]), own[2:3] + 2 * blocks, led[3:4]]
        rows.append(jnp.broadcast_to(total, (1, places)))
    rows += [jnp.zeros((1, places), jnp.float32)] * 4
    return jnp.concatenate(rows, axis=0).astype(jnp.int32)


def walk_groups(end, use):
    def single(g, carry):
        use(g)
        return carry

    def two(j, carry):
        use(2 * j)
        use(2 * j + 1)
        return carry

    pairs = lax.shift_right_logical(end, 1)
    lax.fori_loop(0, pairs, two, 0)
    lax.fori_loop(2 * pairs, end, single, 0)


def whole(ref, sender, block):
    return jnp.concatenate([ref[sender, pl.ds(0, block)], ref[sender, pl.ds(block, block)]], axis=1)


def later_flag_kernel(arrived_ref, flag_ref, tags, sem):
    first = arrived_ref.shape[1] - TAG_ROWS
    copy = pltpu.make_async_copy(arrived_ref.at[:, pl.ds(first, TAG_ROWS)], tags, sem)
    copy.start()
    copy.wait()
    most = jnp.max(tags[...].astype(jnp.float32), axis=0)
    field = lax.broadcasted_iota(jnp.int32, most.shape, 1) // FIELD
    flag_ref[0] = (jnp.max(jnp.where(field == 5, most, -1.0)) > 0).astype(jnp.int32)


def turn_blocks(feat, mate, turned):
    blocks = feat.shape[0]
    turned[2 * blocks] = jnp.zeros(turned.shape[1:], turned.dtype)

    def turn(b, carry):
        for k in range(4):
            turned[b * 4 + k] = feat[b * 4 + k].T
            turned[blocks + b * 4 + k] = mate[b * 4 + k].T
        return carry

    lax.fori_loop(0, blocks // 4, turn, 0)


def weight_kernel(
    arrived_ref, feat_any, mate_any, grad_any, core_ref, own_ref, other_ref, plan_ref,
    held, halves, tags, feat, mate, grad, turned, acc, part, plan, plan_sem, sems,
):
    kinds, width, _ = acc.shape
    blocks, block, _ = feat.shape
    half = width // 2
    pairs = (
        (arrived_ref.at[:, pl.ds(3 * block, TAG_ROWS)], tags),
        (feat_any, feat),
        (mate_any, mate),
        (grad_any, grad),
        (arrived_ref.at[:, pl.ds(0, 2 * block)], held),
        (arrived_ref.at[:, pl.ds(2 * block, block)], halves),
    )
    copies = [pltpu.make_async_copy(src, dst, sems.at[i]) for i, (src, dst) in enumerate(pairs)]
    for copy in copies[:5]:
        copy.start()
    acc[...] = jnp.zeros_like(acc)
    part[...] = jnp.zeros_like(part)
    copies[0].wait()
    plan_ref[...] = make_plans(
        jnp.max(tags[...].astype(jnp.float32), axis=1), core_ref[0].astype(jnp.float32), blocks, kinds - 1
    )
    plan_copy = pltpu.make_async_copy(plan_ref, plan, plan_sem)
    plan_copy.start()
    copies[1].wait()
    copies[2].wait()
    copies[5].start()
    turn_blocks(feat, mate, turned)
    copies[3].wait()

    def root(g, carry):
        left = jnp.concatenate([turned[g * GROUP + k] for k in range(GROUP)], axis=1)
        right = grad[pl.ds(g * GROUP, GROUP)].reshape(GROUP * block, width)
        acc[0] += jnp.dot(left, right, preferred_element_type=jnp.float32)
        return carry

    lax.fori_loop(0, blocks // GROUP, root, 0)
    plan_copy.wait()

    def lefts(g, row):
        return jnp.concatenate([turned[plan[row + 1, g * GROUP + k]] for k in range(GROUP)], axis=1)

    def use(g):
        right = jnp.concatenate([whole(held, plan[0, g * GROUP + k], block) for k in range(GROUP)], axis=0)
        acc[1 + plan[2, g * GROUP]] += jnp.dot(lefts(g, 0), right, preferred_element_type=jnp.float32)

    def use_half(g):
        right = jnp.concatenate([halves[plan[4, g * GROUP + k]] for k in range(GROUP)], axis=0)
        part[plan[6, g * GROUP]] += jnp.dot(lefts(g, 4), right, preferred_element_type=jnp.float32)

    copies[4].wait()
    walk_groups(plan[3, 0], use)
    copies[5].wait()
    walk_groups(plan[7, 0], use_half)

    def split(own, other):
        for r in range(kinds):
            rows = pl.ds(r * width, width)
            own_ref[rows] = acc[r, :, own] + part[r - 1] if r else acc[r, :, own]
            other_ref[rows] = acc[r, :, other]

    first, second = pl.ds(0, half), pl.ds(half, half)

    @pl.when(core_ref[0] == 0)
    def _():
        split(first, second)

    @pl.when(core_ref[0] != 0)
    def _():
        split(second, first)


def later_kernel(plan, later_any, feat_any, mate_any, before_any, own_ref, later, feat, mate, turned, sems):
    width = feat.shape[2]
    pairs = ((before_any, own_ref), (feat_any, feat), (mate_any, mate), (later_any, later))
    copies = [pltpu.make_async_copy(src, dst, sems.at[i]) for i, (src, dst) in enumerate(pairs)]
    for copy in copies:
        copy.start()
    for copy in copies[:3]:
        copy.wait()

    @pl.when(plan[11, 0] > 0)
    def _():
        turn_blocks(feat, mate, turned)

    copies[3].wait()

    def use(g):
        left = jnp.concatenate([turned[plan[9, g * GROUP + k]] for k in range(GROUP)], axis=1)
        right = jnp.concatenate([later[plan[8, g * GROUP + k]] for k in range(GROUP)], axis=0)
        rows = pl.ds(pl.multiple_of((1 + plan[10, g * GROUP]) * width, width), width)
        own_ref[rows] += jnp.dot(left, right, preferred_element_type=jnp.float32)

    walk_groups(plan[11, 0], use)


def add_groups(plan_ref, row, acc, block, products):
    def use(g):
        part = products(g)
        for k in range(GROUP):
            acc[plan_ref[row + 1, g * GROUP + k]] += part[k * block : (k + 1) * block]

    walk_groups(plan_ref[row + 3, 0], use)


ACROSS = (((1,), (1,)), ((), ()))


def halves_kernel(
    plan_ref, core_ref, arrived_ref, grad_ref, root_ref, weight_ref, own_any, mate_ref, halves, acc, sem
):
    blocks, block, width = mate_ref.shape
    copy = pltpu.make_async_copy(arrived_ref.at[:, pl.ds(2 * block, block)], halves, sem)
    copy.start()
    acc[pl.ds(blocks, blocks + 1)] = jnp.zeros((blocks + 1, block, width), jnp.float32)

    def base(g, carry):
        rows = grad_ref[pl.ds(g * GROUP, GROUP)].reshape(GROUP * block, width)
        part = lax.dot_general(rows, root_ref[...], ACROSS, preferred_element_type=jnp.float32)
        acc[pl.ds(g * GROUP, GROUP)] = part.reshape(GROUP, block, width)
        return carry

    lax.fori_loop(0, blocks // GROUP, base, 0)
    copy.wait()
    add_groups(plan_ref, 4, acc, block, half_products(plan_ref, core_ref, weight_ref, halves, 4))
    own_copy = pltpu.make_async_copy(acc.at[pl.ds(0, blocks)], own_any, sem)
    own_copy.start()
    mate_ref[...] = acc[pl.ds(blocks, blocks)].astype(jnp.bfloat16)
    own_copy.wait()


def half_products(plan_ref, core_ref, weight_ref, halves, row):
    width = weight_ref.shape[1]
    half = width // 2
    lanes = pl.ds(pl.multiple_of(core_ref[0] * half, half), half)

    def products(g):
        rows = jnp.concatenate([halves[plan_ref[row, g * GROUP + k]] for k in range(GROUP)], axis=0)
        weight = weight_ref[plan_ref[row + 2, g * GROUP], :, lanes]
        return lax.dot_general(rows, weight, ACROSS, preferred_element_type=jnp.float32)

    return products


def early_kernel(plan_ref, core_ref, arrived_ref, grad_ref, root_ref, weight_ref, out_any, held, halves, acc, sems):
    blocks, block, width = grad_ref.shape
    copy = pltpu.make_async_copy(arrived_ref.at[:, pl.ds(0, 2 * block)], held, sems.at[0])
    half_copy = pltpu.make_async_copy(arrived_ref.at[:, pl.ds(2 * block, block)], halves, sems.at[1])
    copy.start()
    half_copy.start()
    acc[pl.ds(blocks, blocks + 1)] = jnp.zeros((blocks + 1, block, width), jnp.float32)

    def base(g, carry):
        rows = grad_ref[pl.ds(g * GROUP, GROUP)].reshape(GROUP * block, width)
        part = lax.dot_general(rows, root_ref[...], ACROSS, preferred_element_type=jnp.float32)
        acc[pl.ds(g * GROUP, GROUP)] = part.reshape(GROUP, block, width)
        return carry

    lax.fori_loop(0, blocks // GROUP, base, 0)

    def products(g):
        rows = jnp.concatenate([whole(held, plan_ref[0, g * GROUP + k], block) for k in range(GROUP)], axis=0)
        return lax.dot_general(rows, weight_ref[plan_ref[2, g * GROUP]], ACROSS, preferred_element_type=jnp.float32)

    copy.wait()
    add_groups(plan_ref, 0, acc, block, products)
    half_copy.wait()
    add_groups(plan_ref, 4, acc, block, half_products(plan_ref, core_ref, weight_ref, halves, 4))
    out_copy = pltpu.make_async_copy(acc.at[pl.ds(0, 2 * blocks)], out_any, sems.at[0])
    out_copy.start()
    out_copy.wait()


def late_kernel(plan_ref, core_ref, early_any, later_any, weight_ref, own_any, mate_ref, halves, acc, sems):
    blocks, block, width = mate_ref.shape
    early_copy = pltpu.make_async_copy(early_any, acc.at[pl.ds(0, 2 * blocks)], sems.at[0])
    later_copy = pltpu.make_async_copy(later_any, halves, sems.at[1])
    early_copy.start()
    later_copy.start()
    acc[2 * blocks] = jnp.zeros(acc.shape[1:], jnp.float32)
    early_copy.wait()
    later_copy.wait()
    add_groups(plan_ref, 8, acc, block, half_products(plan_ref, core_ref, weight_ref, halves, 8))
    own_copy = pltpu.make_async_copy(acc.at[pl.ds(0, blocks)], own_any, sems.at[0])
    own_copy.start()
    mate_ref[...] = acc[pl.ds(blocks, blocks)].astype(jnp.bfloat16)
    own_copy.wait()


def feat_kernel(
    plan_ref, arrived_ref, own_any, mate_any, weight_ref, out_ref, held, mate, acc, sems
):
    blocks, block, width = out_ref.shape
    own_copy = pltpu.make_async_copy(own_any, acc.at[pl.ds(0, blocks)], sems.at[0])
    copy = pltpu.make_async_copy(arrived_ref.at[:, pl.ds(0, 2 * block)], held, sems.at[1])
    mate_copy = pltpu.make_async_copy(mate_any, mate, sems.at[2])
    own_copy.start()
    copy.start()
    mate_copy.start()
    acc[2 * blocks] = jnp.zeros(acc.shape[1:], jnp.float32)
    own_copy.wait()
    copy.wait()

    def products(g):
        rows = jnp.concatenate([whole(held, plan_ref[0, g * GROUP + k], block) for k in range(GROUP)], axis=0)
        return lax.dot_general(rows, weight_ref[plan_ref[2, g * GROUP]], ACROSS, preferred_element_type=jnp.float32)

    add_groups(plan_ref, 0, acc, block, products)
    mate_copy.wait()
    out_ref[...] = (acc[pl.ds(0, blocks)] + mate[...].astype(jnp.float32)).astype(jnp.bfloat16)


def share_kernel(scale, spread_ref, share_ref):
    share = (jnp.sum(spread_ref[...], axis=0) * scale).astype(jnp.bfloat16)
    for i in range(share_ref.shape[0]):
        share_ref[i] = share


def shards(features, out_grad, rel_weight, root_weight, tiles, tile_dest, tile_peer, tile_source, tile_rel):
    dev_count = lax.axis_size(AXES)
    chips = lax.axis_size(CHIPS)
    core = lax.axis_index("c")
    block = tiles.shape[1]
    width = features.shape[1]
    rel_count = rel_weight.shape[0]
    blocks = features.shape[0] // block
    scale = 1.0 / math.sqrt(features.shape[0] * dev_count)
    swap = [(0, 1), (1, 0)]
    grad_blocks = out_grad.reshape(blocks, block, width)
    feat_blocks = features.reshape(blocks, block, width)

    mate_blocks = lax.ppermute(feat_blocks, "c", swap)
    outgoing, later = make_messages(tile_dest, tile_peer[:, 0], tile_rel, tile_source, tiles, grad_blocks, dev_count)
    outgoing, later, core, mate_blocks = lax.optimization_barrier(
        (outgoing, later, core[None].astype(jnp.int32), mate_blocks)
    )

    def exchange(array):
        return lax.all_to_all(array, AXES, split_axis=0, concat_axis=0, tiled=True)

    arrived = exchange(outgoing)

    dma = pltpu.SemaphoreType.DMA
    cost = pl.CostEstimate(
        flops=2 * dev_count * block * width * width, bytes_accessed=dev_count * block * width * 3, transcendentals=0
    )
    half_rows = (1 + rel_count) * width
    half = jax.ShapeDtypeStruct((half_rows, width // 2), jnp.float32)
    local = pltpu.VMEM(grad_blocks.shape, jnp.bfloat16)
    turned = pltpu.VMEM((2 * blocks + 1, width, block), jnp.bfloat16)
    plan_type = jax.ShapeDtypeStruct((16, plan_places(dev_count, rel_count)), jnp.int32)
    def weights(arrived):
        own, other, plan = pl.pallas_call(
            weight_kernel,
            out_shape=(half, half, plan_type),
            in_specs=[HBM, HBM, HBM, HBM, SMEM],
            out_specs=(VMEM, VMEM, VMEM),
            scratch_shapes=[
                pltpu.VMEM((dev_count, 2 * block, LANES), jnp.bfloat16),
                pltpu.VMEM((dev_count, block, LANES), jnp.bfloat16),
                pltpu.VMEM((dev_count, TAG_ROWS, LANES), jnp.bfloat16),
                local,
                local,
                local,
                turned,
                pltpu.VMEM((1 + rel_count, width, width), jnp.float32),
                pltpu.VMEM((rel_count, width, width // 2), jnp.float32),
                pltpu.SMEM(plan_type.shape, jnp.int32),
                dma,
                dma((6,)),
            ],
            compiler_params=pltpu.CompilerParams(vmem_limit_bytes=50 * MIB),
            cost_estimate=cost,
        )(arrived, feat_blocks, mate_blocks, grad_blocks, core)
        return own + lax.ppermute(other, "c", swap), plan

    own_type = jax.ShapeDtypeStruct(grad_blocks.shape, jnp.float32)
    mate_type = jax.ShapeDtypeStruct(grad_blocks.shape, jnp.bfloat16)
    held = pltpu.VMEM((dev_count, 2 * block, LANES), jnp.bfloat16)
    halves = pltpu.VMEM((dev_count, block, LANES), jnp.bfloat16)
    sums = pltpu.VMEM((2 * blocks + 1, block, width), jnp.float32)
    roomy = pltpu.CompilerParams(vmem_limit_bytes=49 * MIB)

    def finish(own, plan, first_sums, last_sums):
        own, plan = lax.optimization_barrier((own, plan))
        own_part, mate_part = first_sums(plan)
        shape = (chips, half_rows // chips, width // 2)
        spread = lax.all_to_all(own.reshape(shape), CHIPS, 0, 0, tiled=True)
        spread, own_part, mate_part, plan = lax.optimization_barrier((spread, own_part, mate_part, plan))
        mate_part = lax.ppermute(mate_part, "c", swap)
        share = pl.pallas_call(
            functools.partial(share_kernel, scale),
            out_shape=jax.ShapeDtypeStruct(shape, jnp.bfloat16),
            in_specs=[VMEM],
            out_specs=VMEM,
            compiler_params=pltpu.CompilerParams(vmem_limit_bytes=8 * MIB),
        )(spread)
        own = lax.all_to_all(share, CHIPS, 0, 0, tiled=True).reshape(half.shape)
        grad_feat = last_sums(plan, own_part, mate_part)
        own, grad_feat = lax.optimization_barrier((own, grad_feat))
        other = lax.ppermute(own, "c", swap)
        left = jnp.where(core[0] == 0, own, other).astype(jnp.float32)
        right = jnp.where(core[0] == 0, other, own).astype(jnp.float32)
        grad_weights = jnp.concatenate([left, right], axis=1).reshape(1 + rel_count, width, width)
        return grad_feat.reshape(features.shape), grad_weights

    def take_later(arrived, later):
        later = exchange(later)
        own, plan = weights(arrived)
        early = pl.pallas_call(
            early_kernel,
            out_shape=jax.ShapeDtypeStruct((2 * blocks, block, width), jnp.float32),
            in_specs=[SMEM, SMEM, HBM, VMEM, VMEM, VMEM],
            out_specs=HBM,
            scratch_shapes=[held, halves, sums, dma((2,))],
            compiler_params=roomy,
            cost_estimate=cost,
        )(plan, core, arrived, grad_blocks, root_weight, rel_weight)
        later, own, plan, early = lax.optimization_barrier((later, own, plan, early))
        own = pl.pallas_call(
            later_kernel,
            out_shape=half,
            in_specs=[SMEM] + [HBM] * 4,
            out_specs=VMEM,
            scratch_shapes=[halves, local, local, turned, dma((4,))],
            compiler_params=pltpu.CompilerParams(vmem_limit_bytes=57 * MIB),
        )(plan, later, feat_blocks, mate_blocks, own)

        def first_sums(plan):
            return pl.pallas_call(
                late_kernel,
                out_shape=(own_type, mate_type),
                in_specs=[SMEM, SMEM, HBM, HBM, VMEM],
                out_specs=(HBM, VMEM),
                scratch_shapes=[halves, sums, dma((2,))],
                compiler_params=roomy,
                cost_estimate=cost,
            )(plan, core, early, later, rel_weight)

        def last_sums(plan, own_part, mate_part):
            return (own_part + mate_part.astype(jnp.float32)).astype(jnp.bfloat16)

        return finish(own, plan, first_sums, last_sums)

    def take_none(arrived, later):
        own, plan = weights(arrived)

        def first_sums(plan):
            return pl.pallas_call(
                halves_kernel,
                out_shape=(own_type, mate_type),
                in_specs=[SMEM, SMEM, HBM, VMEM, VMEM, VMEM],
                out_specs=(HBM, VMEM),
                scratch_shapes=[halves, sums, dma],
                compiler_params=roomy,
                cost_estimate=cost,
            )(plan, core, arrived, grad_blocks, root_weight, rel_weight)

        def last_sums(plan, own_part, mate_part):
            return pl.pallas_call(
                feat_kernel,
                out_shape=mate_type,
                in_specs=[SMEM, HBM, HBM, HBM, VMEM],
                out_specs=VMEM,
                scratch_shapes=[held, local, sums, dma((3,))],
                compiler_params=roomy,
                cost_estimate=cost,
            )(plan, arrived, own_part, mate_part, rel_weight)

        return finish(own, plan, first_sums, last_sums)

    any_later = pl.pallas_call(
        later_flag_kernel,
        out_shape=jax.ShapeDtypeStruct((1,), jnp.int32),
        in_specs=[HBM],
        out_specs=SMEM,
        scratch_shapes=[pltpu.VMEM((dev_count, TAG_ROWS, LANES), jnp.bfloat16), dma],
        compiler_params=pltpu.CompilerParams(vmem_limit_bytes=58 * MIB),
    )(arrived)
    return lax.cond(any_later[0] > 0, take_later, take_none, arrived, later)


def solution(mesh):
    sizes = (4, 4, 4, 2)
    fine = Mesh(mesh.devices.reshape(sizes), AXES)
    return jax.shard_map(
        shards,
        mesh=fine,
        in_specs=(
            P(AXES, None),
            P(AXES, None),
            P(),
            P(),
            P(AXES, None, None),
            P(AXES),
            P(AXES, None),
            P(AXES),
            P(AXES),
        ),
        out_specs=(P(AXES, None), P()),
        check_vma=False,
    )
```

```python
import functools
import math

import jax
import jax.numpy as jnp
from jax import lax
from jax.experimental import pallas as pl
from jax.experimental.pallas import tpu as pltpu
from jax.sharding import Mesh
from jax.sharding import PartitionSpec as P

AXES = ("z", "y", "x", "c")
CHIPS = ("z", "y", "x")
VMEM = pl.BlockSpec(memory_space=pltpu.VMEM)
HBM = pl.BlockSpec(memory_space=pltpu.HBM)
SMEM = pl.BlockSpec(memory_space=pltpu.SMEM)
MIB = 1024 * 1024
GROUP = 8
LANES = 128
TAG_ROWS = 16
FIELD = 16


def message_kernel(
    blocks, parts, dest_any, peer_any, rel_any, source_any, tiles_ref, grad_any, out_ref, later_ref,
    dest, peers, rels, sources, count, seconds, flag, grad, held, made, marks, tags, sems, out_sem,
):
    tile_count, block, _ = tiles_ref.shape
    part = tile_count // parts
    pairs = ((dest_any, dest), (peer_any, peers), (rel_any, rels), (source_any, sources), (grad_any, grad))
    early = [pltpu.make_async_copy(src, dst, sems.at[parts + i]) for i, (src, dst) in enumerate(pairs)]
    for copy in early:
        copy.start()

    def fetch(i):
        rows = pl.ds(i * part, part)
        return pltpu.make_async_copy(tiles_ref.at[rows], held.at[rows], sems.at[i])

    for i in range(parts):
        fetch(i).start()

    def clear(i, carry):
        count[2 * i] = 0
        count[2 * i + 1] = 0
        seconds[i] = 0
        return carry

    lax.fori_loop(0, seconds.shape[0], clear, 0)
    flag[0] = 0
    marks[...] = jnp.full(marks.shape, -1.0, jnp.float32)
    field = lax.broadcasted_iota(jnp.int32, marks.shape[1:], 1) // FIELD
    left, right = pl.ds(0, block), pl.ds(block, block)
    half = pl.ds(2 * block, block)

    def send(src, dst):
        pltpu.make_async_copy(src, dst, out_sem).start()

    def place(t, carry):
        peer = peers[t]
        rank = count[peer]
        count[peer] = rank + 1
        mark = (rels[t] * blocks + sources[t]).astype(jnp.float32)

        @pl.when(rank == 0)
        def _():
            marks[peer] = jnp.where(field == 0, mark, marks[peer])
            send(made.at[t], out_ref.at[peer, pl.ds(0, 2 * block)])

        @pl.when(rank != 0)
        def _():
            chip = lax.shift_right_logical(peer, 1)
            later = seconds[chip]
            seconds[chip] = later + 1
            core = (peer & 1).astype(jnp.float32)
            first = 2 * chip
            for side in range(2):
                old = marks[first + side]
                old = jnp.where(field == 2 + 2 * later, core, old)
                marks[first + side] = jnp.where(field == 1 + 2 * later, mark, old)

            @pl.when(later == 0)
            def _():
                send(made.at[t, left], out_ref.at[first, half])
                send(made.at[t, right], out_ref.at[first + 1, half])

            @pl.when(later != 0)
            def _():
                flag[0] = 1
                send(made.at[t, left], later_ref.at[first])
                send(made.at[t, right], later_ref.at[first + 1])

        return carry

    for copy in early:
        copy.wait()

    for i in range(parts):
        fetch(i).wait()
        for t in range(i * part, (i + 1) * part):
            message = lax.dot_general(
                held[t], grad[dest[t]], (((0,), (0,)), ((), ())), preferred_element_type=jnp.float32
            ).astype(jnp.bfloat16)
            made[t, left] = message[:, :LANES]
            made[t, right] = message[:, LANES:]
        for t in range(i * part, (i + 1) * part):
            place(t, 0)

    any_later = flag[0].astype(jnp.float32)
    all_marks = jnp.where(field[None] == 5, any_later, marks[...])
    tags[...] = jnp.concatenate([all_marks, all_marks], axis=1).astype(jnp.bfloat16)
    tag_copy = pltpu.make_async_copy(tags, out_ref.at[:, pl.ds(3 * block, TAG_ROWS)], sems.at[0])
    tag_copy.start()
    pltpu.make_async_copy(made, out_ref.at[pl.ds(0, tile_count), pl.ds(0, 2 * block)], out_sem).wait()
    tag_copy.wait()


def make_messages(tile_dest, peer_list, tile_rel, tile_source, tiles, grad_blocks, dev_count):
    tile_count, block, _ = tiles.shape
    blocks, _, width = grad_blocks.shape
    parts = 8
    numbers = pltpu.SMEM((tile_count,), jnp.int32)

    def kernel(*refs):
        message_kernel(blocks, parts, *refs)

    return pl.pallas_call(
        kernel,
        out_shape=(
            jax.ShapeDtypeStruct((dev_count, 3 * block + TAG_ROWS, LANES), jnp.bfloat16),
            jax.ShapeDtypeStruct((dev_count, block, LANES), jnp.bfloat16),
        ),
        in_specs=[HBM] * 6,
        out_specs=(HBM, HBM),
        scratch_shapes=[
            numbers,
            numbers,
            numbers,
            numbers,
            pltpu.SMEM((dev_count,), jnp.int32),
            pltpu.SMEM((dev_count // 2,), jnp.int32),
            pltpu.SMEM((1,), jnp.int32),
            pltpu.VMEM(grad_blocks.shape, jnp.bfloat16),
            pltpu.VMEM(tiles.shape, jnp.bfloat16),
            pltpu.VMEM((tile_count, 2 * block, LANES), jnp.bfloat16),
            pltpu.VMEM((dev_count, TAG_ROWS // 2, LANES), jnp.float32),
            pltpu.VMEM((dev_count, TAG_ROWS, LANES), jnp.bfloat16),
            pltpu.SemaphoreType.DMA((parts + 5,)),
            pltpu.SemaphoreType.DMA,
        ],
        compiler_params=pltpu.CompilerParams(vmem_limit_bytes=58 * MIB),
        cost_estimate=pl.CostEstimate(
            flops=2 * tile_count * block * block * width,
            bytes_accessed=tile_count * block * (block + width) * 2,
            transcendentals=0,
        ),
    )(tile_dest, peer_list, tile_rel, tile_source, tiles, grad_blocks)


def plan_places(senders, rel_count):
    return -(-(senders + (GROUP - 1) * rel_count) // LANES) * LANES


def make_plans(tags, core, blocks, rel_count):
    senders = tags.shape[0]
    places = plan_places(senders, rel_count)
    wide = 1 << (rel_count - 1).bit_length()
    square = (senders, senders)
    row, lane = lax.broadcasted_iota(jnp.int32, square, 0), lax.broadcasted_iota(jnp.int32, square, 1)
    lane_set, lane_rel = lane // wide, (lane % wide).astype(jnp.float32)
    below = (lane < row).astype(jnp.float32).astype(jnp.bfloat16)
    ahead = ((row < lane) & (row // wide == lane_set)).astype(jnp.float32).astype(jnp.bfloat16)
    at = lax.broadcasted_iota(jnp.int32, (senders, places), 1)
    at, lead = at.astype(jnp.float32), (at // GROUP * GROUP).astype(jnp.float32)

    def column(i):
        return tags[:, i * FIELD : i * FIELD + 1]

    tag = [column(0), column(1), column(3)]
    rel = [jnp.floor(t * (1.0 / blocks)) for t in tag]
    used = [jnp.where((lane_set == q) & (lane_rel == r) & (t >= 0), 1.0, 0.0) for q, (t, r) in enumerate(zip(tag, rel))]
    every = used[0] + used[1] + used[2]
    before = jnp.dot(below, every.astype(jnp.bfloat16), preferred_element_type=jnp.float32)
    groups = jnp.floor((jnp.sum(every, axis=0, keepdims=True) + (GROUP - 1)) * (1.0 / GROUP))
    first = jnp.dot(
        jnp.broadcast_to(groups, (TAG_ROWS, senders)).astype(jnp.bfloat16), ahead, preferred_element_type=jnp.float32
    )[0:1]
    spot = before + first * GROUP
    across = tags.T
    line = lax.broadcasted_iota(jnp.int32, (TAG_ROWS, senders), 0)
    name = lax.broadcasted_iota(jnp.int32, (1, senders), 1).astype(jnp.float32)
    rows = []
    for q, i in enumerate((0, 1, 3)):
        place = jnp.where(tag[q] >= 0, jnp.sum(used[q] * spot, axis=1, keepdims=True), -1.0)
        here = jnp.where(place == at, 1.0, 0.0).astype(jnp.bfloat16)
        leads = jnp.where(place == lead, 1.0, 0.0).astype(jnp.bfloat16)
        mark = across[i * FIELD : i * FIELD + 1]
        relation = jnp.floor(mark * (1.0 / blocks))
        source = mark - relation * blocks - 2 * blocks
        if q:
            owner = across[(i + 1) * FIELD : (i + 1) * FIELD + 1]
            source = source + jnp.where(owner == core, 0.0, float(blocks))
        named = jnp.where(line == 0, 1.0, jnp.where(line == 1, name, jnp.where(line == 2, source, relation)))
        named = named.astype(jnp.bfloat16)
        own = jnp.dot(named, here, preferred_element_type=jnp.float32)
        led = jnp.dot(named, leads, preferred_element_type=jnp.float32)
        total = jnp.sum(jnp.where(lane_set[0:1] == q, groups, 0.0), axis=1, keepdims=True)
        rows += [jnp.where(own[0:1] > 0, own[1:2], led[1:2]), own[2:3] + 2 * blocks, led[3:4]]
        rows.append(jnp.broadcast_to(total, (1, places)))
    rows += [jnp.zeros((1, places), jnp.float32)] * 4
    return jnp.concatenate(rows, axis=0).astype(jnp.int32)


def walk_groups(end, use):
    def single(g, carry):
        use(g)
        return carry

    def two(j, carry):
        use(2 * j)
        use(2 * j + 1)
        return carry

    pairs = lax.shift_right_logical(end, 1)
    lax.fori_loop(0, pairs, two, 0)
    lax.fori_loop(2 * pairs, end, single, 0)


def whole(ref, sender, block):
    return jnp.concatenate([ref[sender, pl.ds(0, block)], ref[sender, pl.ds(block, block)]], axis=1)


def later_flag_kernel(arrived_ref, flag_ref, tags, sem):
    first = arrived_ref.shape[1] - TAG_ROWS
    copy = pltpu.make_async_copy(arrived_ref.at[:, pl.ds(first, TAG_ROWS)], tags, sem)
    copy.start()
    copy.wait()
    most = jnp.max(tags[...].astype(jnp.float32), axis=0)
    field = lax.broadcasted_iota(jnp.int32, most.shape, 1) // FIELD
    flag_ref[0] = (jnp.max(jnp.where(field == 5, most, -1.0)) > 0).astype(jnp.int32)


def turn_blocks(feat, mate, turned):
    blocks = feat.shape[0]
    turned[2 * blocks] = jnp.zeros(turned.shape[1:], turned.dtype)

    def turn(b, carry):
        for k in range(4):
            turned[b * 4 + k] = feat[b * 4 + k].T
            turned[blocks + b * 4 + k] = mate[b * 4 + k].T
        return carry

    lax.fori_loop(0, blocks // 4, turn, 0)


def weight_kernel(
    arrived_ref, feat_any, mate_any, grad_any, core_ref, own_ref, other_ref, plan_ref,
    held, halves, tags, feat, mate, grad, turned, acc, part, plan, plan_sem, sems,
):
    kinds, width, _ = acc.shape
    blocks, block, _ = feat.shape
    half = width // 2
    pairs = (
        (arrived_ref.at[:, pl.ds(3 * block, TAG_ROWS)], tags),
        (feat_any, feat),
        (mate_any, mate),
        (grad_any, grad),
        (arrived_ref.at[:, pl.ds(0, 2 * block)], held),
        (arrived_ref.at[:, pl.ds(2 * block, block)], halves),
    )
    copies = [pltpu.make_async_copy(src, dst, sems.at[i]) for i, (src, dst) in enumerate(pairs)]
    for copy in copies[:5]:
        copy.start()
    acc[...] = jnp.zeros_like(acc)
    part[...] = jnp.zeros_like(part)
    copies[0].wait()
    plan_ref[...] = make_plans(
        jnp.max(tags[...].astype(jnp.float32), axis=1), core_ref[0].astype(jnp.float32), blocks, kinds - 1
    )
    plan_copy = pltpu.make_async_copy(plan_ref, plan, plan_sem)
    plan_copy.start()
    copies[1].wait()
    copies[2].wait()
    copies[5].start()
    turn_blocks(feat, mate, turned)
    copies[3].wait()

    def root(g, carry):
        left = jnp.concatenate([turned[g * GROUP + k] for k in range(GROUP)], axis=1)
        right = grad[pl.ds(g * GROUP, GROUP)].reshape(GROUP * block, width)
        acc[0] += jnp.dot(left, right, preferred_element_type=jnp.float32)
        return carry

    lax.fori_loop(0, blocks // GROUP, root, 0)
    plan_copy.wait()

    def lefts(g, row):
        return jnp.concatenate([turned[plan[row + 1, g * GROUP + k]] for k in range(GROUP)], axis=1)

    def use(g):
        right = jnp.concatenate([whole(held, plan[0, g * GROUP + k], block) for k in range(GROUP)], axis=0)
        acc[1 + plan[2, g * GROUP]] += jnp.dot(lefts(g, 0), right, preferred_element_type=jnp.float32)

    def use_half(g):
        right = jnp.concatenate([halves[plan[4, g * GROUP + k]] for k in range(GROUP)], axis=0)
        part[plan[6, g * GROUP]] += jnp.dot(lefts(g, 4), right, preferred_element_type=jnp.float32)

    copies[4].wait()
    walk_groups(plan[3, 0], use)
    copies[5].wait()
    walk_groups(plan[7, 0], use_half)

    def split(own, other):
        for r in range(kinds):
            rows = pl.ds(r * width, width)
            own_ref[rows] = acc[r, :, own] + part[r - 1] if r else acc[r, :, own]
            other_ref[rows] = acc[r, :, other]

    first, second = pl.ds(0, half), pl.ds(half, half)

    @pl.when(core_ref[0] == 0)
    def _():
        split(first, second)

    @pl.when(core_ref[0] != 0)
    def _():
        split(second, first)


def later_kernel(plan, later_any, feat_any, mate_any, before_any, own_ref, later, feat, mate, turned, sems):
    width = feat.shape[2]
    pairs = ((before_any, own_ref), (feat_any, feat), (mate_any, mate), (later_any, later))
    copies = [pltpu.make_async_copy(src, dst, sems.at[i]) for i, (src, dst) in enumerate(pairs)]
    for copy in copies:
        copy.start()
    for copy in copies[:3]:
        copy.wait()

    @pl.when(plan[11, 0] > 0)
    def _():
        turn_blocks(feat, mate, turned)

    copies[3].wait()

    def use(g):
        left = jnp.concatenate([turned[plan[9, g * GROUP + k]] for k in range(GROUP)], axis=1)
        right = jnp.concatenate([later[plan[8, g * GROUP + k]] for k in range(GROUP)], axis=0)
        rows = pl.ds(pl.multiple_of((1 + plan[10, g * GROUP]) * width, width), width)
        own_ref[rows] += jnp.dot(left, right, preferred_element_type=jnp.float32)

    walk_groups(plan[11, 0], use)


def add_groups(plan_ref, row, acc, block, products):
    def use(g):
        part = products(g)
        for k in range(GROUP):
            acc[plan_ref[row + 1, g * GROUP + k]] += part[k * block : (k + 1) * block]

    walk_groups(plan_ref[row + 3, 0], use)


ACROSS = (((1,), (1,)), ((), ()))


def halves_kernel(
    plan_ref, core_ref, arrived_ref, grad_ref, root_ref, weight_ref, own_any, mate_ref, halves, acc, sem
):
    blocks, block, width = mate_ref.shape
    copy = pltpu.make_async_copy(arrived_ref.at[:, pl.ds(2 * block, block)], halves, sem)
    copy.start()
    acc[pl.ds(blocks, blocks + 1)] = jnp.zeros((blocks + 1, block, width), jnp.float32)

    def base(g, carry):
        rows = grad_ref[pl.ds(g * GROUP, GROUP)].reshape(GROUP * block, width)
        part = lax.dot_general(rows, root_ref[...], ACROSS, preferred_element_type=jnp.float32)
        acc[pl.ds(g * GROUP, GROUP)] = part.reshape(GROUP, block, width)
        return carry

    lax.fori_loop(0, blocks // GROUP, base, 0)
    copy.wait()
    add_groups(plan_ref, 4, acc, block, half_products(plan_ref, core_ref, weight_ref, halves, 4))
    own_copy = pltpu.make_async_copy(acc.at[pl.ds(0, blocks)], own_any, sem)
    own_copy.start()
    mate_ref[...] = acc[pl.ds(blocks, blocks)].astype(jnp.bfloat16)
    own_copy.wait()


def half_products(plan_ref, core_ref, weight_ref, halves, row):
    width = weight_ref.shape[1]
    half = width // 2
    lanes = pl.ds(pl.multiple_of(core_ref[0] * half, half), half)

    def products(g):
        rows = jnp.concatenate([halves[plan_ref[row, g * GROUP + k]] for k in range(GROUP)], axis=0)
        weight = weight_ref[plan_ref[row + 2, g * GROUP], :, lanes]
        return lax.dot_general(rows, weight, ACROSS, preferred_element_type=jnp.float32)

    return products


def early_kernel(plan_ref, core_ref, arrived_ref, grad_ref, root_ref, weight_ref, out_any, held, halves, acc, sems):
    blocks, block, width = grad_ref.shape
    copy = pltpu.make_async_copy(arrived_ref.at[:, pl.ds(0, 2 * block)], held, sems.at[0])
    half_copy = pltpu.make_async_copy(arrived_ref.at[:, pl.ds(2 * block, block)], halves, sems.at[1])
    copy.start()
    half_copy.start()
    acc[pl.ds(blocks, blocks + 1)] = jnp.zeros((blocks + 1, block, width), jnp.float32)

    def base(g, carry):
        rows = grad_ref[pl.ds(g * GROUP, GROUP)].reshape(GROUP * block, width)
        part = lax.dot_general(rows, root_ref[...], ACROSS, preferred_element_type=jnp.float32)
        acc[pl.ds(g * GROUP, GROUP)] = part.reshape(GROUP, block, width)
        return carry

    lax.fori_loop(0, blocks // GROUP, base, 0)

    def products(g):
        rows = jnp.concatenate([whole(held, plan_ref[0, g * GROUP + k], block) for k in range(GROUP)], axis=0)
        return lax.dot_general(rows, weight_ref[plan_ref[2, g * GROUP]], ACROSS, preferred_element_type=jnp.float32)

    copy.wait()
    add_groups(plan_ref, 0, acc, block, products)
    half_copy.wait()
    add_groups(plan_ref, 4, acc, block, half_products(plan_ref, core_ref, weight_ref, halves, 4))
    out_copy = pltpu.make_async_copy(acc.at[pl.ds(0, 2 * blocks)], out_any, sems.at[0])
    out_copy.start()
    out_copy.wait()


def late_kernel(plan_ref, core_ref, early_any, later_any, weight_ref, own_any, mate_ref, halves, acc, sems):
    blocks, block, width = mate_ref.shape
    early_copy = pltpu.make_async_copy(early_any, acc.at[pl.ds(0, 2 * blocks)], sems.at[0])
    later_copy = pltpu.make_async_copy(later_any, halves, sems.at[1])
    early_copy.start()
    later_copy.start()
    acc[2 * blocks] = jnp.zeros(acc.shape[1:], jnp.float32)
    early_copy.wait()
    later_copy.wait()
    add_groups(plan_ref, 8, acc, block, half_products(plan_ref, core_ref, weight_ref, halves, 8))
    own_copy = pltpu.make_async_copy(acc.at[pl.ds(0, blocks)], own_any, sems.at[0])
    own_copy.start()
    mate_ref[...] = acc[pl.ds(blocks, blocks)].astype(jnp.bfloat16)
    own_copy.wait()


def feat_kernel(
    plan_ref, arrived_ref, own_any, mate_any, weight_ref, out_ref, held, mate, acc, sems
):
    blocks, block, width = out_ref.shape
    own_copy = pltpu.make_async_copy(own_any, acc.at[pl.ds(0, blocks)], sems.at[0])
    copy = pltpu.make_async_copy(arrived_ref.at[:, pl.ds(0, 2 * block)], held, sems.at[1])
    mate_copy = pltpu.make_async_copy(mate_any, mate, sems.at[2])
    own_copy.start()
    copy.start()
    mate_copy.start()
    acc[2 * blocks] = jnp.zeros(acc.shape[1:], jnp.float32)
    own_copy.wait()
    copy.wait()

    def products(g):
        rows = jnp.concatenate([whole(held, plan_ref[0, g * GROUP + k], block) for k in range(GROUP)], axis=0)
        return lax.dot_general(rows, weight_ref[plan_ref[2, g * GROUP]], ACROSS, preferred_element_type=jnp.float32)

    add_groups(plan_ref, 0, acc, block, products)
    mate_copy.wait()
    out_ref[...] = (acc[pl.ds(0, blocks)] + mate[...].astype(jnp.float32)).astype(jnp.bfloat16)


def share_kernel(scale, spread_ref, share_ref):
    share = (jnp.sum(spread_ref[...], axis=0) * scale).astype(jnp.bfloat16)
    for i in range(share_ref.shape[0]):
        share_ref[i] = share


def join_kernel(core_ref, own_ref, other_ref, out_ref):
    kinds, width, _ = out_ref.shape
    half = width // 2

    def join(first, second):
        for r in range(kinds):
            rows = pl.ds(r * width, width)
            out_ref[r, :, pl.ds(0, half)] = first[rows].astype(jnp.float32)
            out_ref[r, :, pl.ds(half, half)] = second[rows].astype(jnp.float32)

    @pl.when(core_ref[0] == 0)
    def _():
        join(own_ref, other_ref)

    @pl.when(core_ref[0] != 0)
    def _():
        join(other_ref, own_ref)


def shards(features, out_grad, rel_weight, root_weight, tiles, tile_dest, tile_peer, tile_source, tile_rel):
    dev_count = lax.axis_size(AXES)
    chips = lax.axis_size(CHIPS)
    core = lax.axis_index("c")
    block = tiles.shape[1]
    width = features.shape[1]
    rel_count = rel_weight.shape[0]
    blocks = features.shape[0] // block
    scale = 1.0 / math.sqrt(features.shape[0] * dev_count)
    swap = [(0, 1), (1, 0)]
    grad_blocks = out_grad.reshape(blocks, block, width)
    feat_blocks = features.reshape(blocks, block, width)

    mate_blocks = lax.ppermute(feat_blocks, "c", swap)
    outgoing, later = make_messages(tile_dest, tile_peer[:, 0], tile_rel, tile_source, tiles, grad_blocks, dev_count)
    outgoing, later, core, mate_blocks = lax.optimization_barrier(
        (outgoing, later, core[None].astype(jnp.int32), mate_blocks)
    )

    def exchange(array):
        return lax.all_to_all(array, AXES, split_axis=0, concat_axis=0, tiled=True)

    arrived = exchange(outgoing)

    dma = pltpu.SemaphoreType.DMA
    cost = pl.CostEstimate(
        flops=2 * dev_count * block * width * width, bytes_accessed=dev_count * block * width * 3, transcendentals=0
    )
    half_rows = (1 + rel_count) * width
    half = jax.ShapeDtypeStruct((half_rows, width // 2), jnp.float32)
    local = pltpu.VMEM(grad_blocks.shape, jnp.bfloat16)
    turned = pltpu.VMEM((2 * blocks + 1, width, block), jnp.bfloat16)
    plan_type = jax.ShapeDtypeStruct((16, plan_places(dev_count, rel_count)), jnp.int32)
    def weights(arrived):
        own, other, plan = pl.pallas_call(
            weight_kernel,
            out_shape=(half, half, plan_type),
            in_specs=[HBM, HBM, HBM, HBM, SMEM],
            out_specs=(VMEM, VMEM, VMEM),
            scratch_shapes=[
                pltpu.VMEM((dev_count, 2 * block, LANES), jnp.bfloat16),
                pltpu.VMEM((dev_count, block, LANES), jnp.bfloat16),
                pltpu.VMEM((dev_count, TAG_ROWS, LANES), jnp.bfloat16),
                local,
                local,
                local,
                turned,
                pltpu.VMEM((1 + rel_count, width, width), jnp.float32),
                pltpu.VMEM((rel_count, width, width // 2), jnp.float32),
                pltpu.SMEM(plan_type.shape, jnp.int32),
                dma,
                dma((6,)),
            ],
            compiler_params=pltpu.CompilerParams(vmem_limit_bytes=50 * MIB),
            cost_estimate=cost,
        )(arrived, feat_blocks, mate_blocks, grad_blocks, core)
        return own + lax.ppermute(other, "c", swap), plan

    own_type = jax.ShapeDtypeStruct(grad_blocks.shape, jnp.float32)
    mate_type = jax.ShapeDtypeStruct(grad_blocks.shape, jnp.bfloat16)
    held = pltpu.VMEM((dev_count, 2 * block, LANES), jnp.bfloat16)
    halves = pltpu.VMEM((dev_count, block, LANES), jnp.bfloat16)
    sums = pltpu.VMEM((2 * blocks + 1, block, width), jnp.float32)
    roomy = pltpu.CompilerParams(vmem_limit_bytes=49 * MIB)

    def finish(own, plan, first_sums, last_sums):
        own, plan = lax.optimization_barrier((own, plan))
        own_part, mate_part = first_sums(plan)
        shape = (chips, half_rows // chips, width // 2)
        spread = lax.all_to_all(own.reshape(shape), CHIPS, 0, 0, tiled=True)
        spread, own_part, mate_part, plan = lax.optimization_barrier((spread, own_part, mate_part, plan))
        mate_part = lax.ppermute(mate_part, "c", swap)
        share = pl.pallas_call(
            functools.partial(share_kernel, scale),
            out_shape=jax.ShapeDtypeStruct(shape, jnp.bfloat16),
            in_specs=[VMEM],
            out_specs=VMEM,
            compiler_params=pltpu.CompilerParams(vmem_limit_bytes=8 * MIB),
        )(spread)
        own = lax.all_to_all(share, CHIPS, 0, 0, tiled=True).reshape(half.shape)
        grad_feat = last_sums(plan, own_part, mate_part)
        own, grad_feat = lax.optimization_barrier((own, grad_feat))
        other = lax.ppermute(own, "c", swap)
        grad_weights = pl.pallas_call(
            join_kernel,
            out_shape=jax.ShapeDtypeStruct((1 + rel_count, width, width), jnp.float32),
            in_specs=[SMEM, VMEM, VMEM],
            out_specs=VMEM,
            compiler_params=pltpu.CompilerParams(vmem_limit_bytes=16 * MIB),
        )(core, own, other)
        return grad_feat.reshape(features.shape), grad_weights

    def take_later(arrived, later):
        later = exchange(later)
        own, plan = weights(arrived)
        early = pl.pallas_call(
            early_kernel,
            out_shape=jax.ShapeDtypeStruct((2 * blocks, block, width), jnp.float32),
            in_specs=[SMEM, SMEM, HBM, VMEM, VMEM, VMEM],
            out_specs=HBM,
            scratch_shapes=[held, halves, sums, dma((2,))],
            compiler_params=roomy,
            cost_estimate=cost,
        )(plan, core, arrived, grad_blocks, root_weight, rel_weight)
        later, own, plan, early = lax.optimization_barrier((later, own, plan, early))
        own = pl.pallas_call(
            later_kernel,
            out_shape=half,
            in_specs=[SMEM] + [HBM] * 4,
            out_specs=VMEM,
            scratch_shapes=[halves, local, local, turned, dma((4,))],
            compiler_params=pltpu.CompilerParams(vmem_limit_bytes=57 * MIB),
        )(plan, later, feat_blocks, mate_blocks, own)

        def first_sums(plan):
            return pl.pallas_call(
                late_kernel,
                out_shape=(own_type, mate_type),
                in_specs=[SMEM, SMEM, HBM, HBM, VMEM],
                out_specs=(HBM, VMEM),
                scratch_shapes=[halves, sums, dma((2,))],
                compiler_params=roomy,
                cost_estimate=cost,
            )(plan, core, early, later, rel_weight)

        def last_sums(plan, own_part, mate_part):
            return (own_part + mate_part.astype(jnp.float32)).astype(jnp.bfloat16)

        return finish(own, plan, first_sums, last_sums)

    def take_none(arrived, later):
        own, plan = weights(arrived)

        def first_sums(plan):
            return pl.pallas_call(
                halves_kernel,
                out_shape=(own_type, mate_type),
                in_specs=[SMEM, SMEM, HBM, VMEM, VMEM, VMEM],
                out_specs=(HBM, VMEM),
                scratch_shapes=[halves, sums, dma],
                compiler_params=roomy,
                cost_estimate=cost,
            )(plan, core, arrived, grad_blocks, root_weight, rel_weight)

        def last_sums(plan, own_part, mate_part):
            return pl.pallas_call(
                feat_kernel,
                out_shape=mate_type,
                in_specs=[SMEM, HBM, HBM, HBM, VMEM],
                out_specs=VMEM,
                scratch_shapes=[held, local, sums, dma((3,))],
                compiler_params=roomy,
                cost_estimate=cost,
            )(plan, arrived, own_part, mate_part, rel_weight)

        return finish(own, plan, first_sums, last_sums)

    any_later = pl.pallas_call(
        later_flag_kernel,
        out_shape=jax.ShapeDtypeStruct((1,), jnp.int32),
        in_specs=[HBM],
        out_specs=SMEM,
        scratch_shapes=[pltpu.VMEM((dev_count, TAG_ROWS, LANES), jnp.bfloat16), dma],
        compiler_params=pltpu.CompilerParams(vmem_limit_bytes=58 * MIB),
    )(arrived)
    return lax.cond(any_later[0] > 0, take_later, take_none, arrived, later)


def solution(mesh):
    sizes = (4, 4, 4, 2)
    fine = Mesh(mesh.devices.reshape(sizes), AXES)
    return jax.shard_map(
        shards,
        mesh=fine,
        in_specs=(
            P(AXES, None),
            P(AXES, None),
            P(),
            P(),
            P(AXES, None, None),
            P(AXES),
            P(AXES, None),
            P(AXES),
            P(AXES),
        ),
        out_specs=(P(AXES, None), P()),
        check_vma=False,
    )
```

```python
import functools
import math

import jax
import jax.numpy as jnp
from jax import lax
from jax.experimental import pallas as pl
from jax.experimental.pallas import tpu as pltpu
from jax.sharding import Mesh
from jax.sharding import PartitionSpec as P

AXES = ("z", "y", "x", "c")
CHIPS = ("z", "y", "x")
VMEM = pl.BlockSpec(memory_space=pltpu.VMEM)
HBM = pl.BlockSpec(memory_space=pltpu.HBM)
SMEM = pl.BlockSpec(memory_space=pltpu.SMEM)
MIB = 1024 * 1024
GROUP = 8
LANES = 128
TAG_ROWS = 16
FIELD = 16


def message_kernel(
    blocks, parts, dest_any, peer_any, rel_any, source_any, tiles_ref, grad_any, out_ref, later_ref,
    dest, peers, rels, sources, count, seconds, flag, grad, held, made, marks, tags, sems, out_sem,
):
    tile_count, block, _ = tiles_ref.shape
    part = tile_count // parts
    pairs = ((dest_any, dest), (peer_any, peers), (rel_any, rels), (source_any, sources), (grad_any, grad))
    early = [pltpu.make_async_copy(src, dst, sems.at[parts + i]) for i, (src, dst) in enumerate(pairs)]
    for copy in early:
        copy.start()

    def fetch(i):
        rows = pl.ds(i * part, part)
        return pltpu.make_async_copy(tiles_ref.at[rows], held.at[rows], sems.at[i])

    for i in range(parts):
        fetch(i).start()

    def clear(i, carry):
        count[2 * i] = 0
        count[2 * i + 1] = 0
        seconds[i] = 0
        return carry

    lax.fori_loop(0, seconds.shape[0], clear, 0)
    flag[0] = 0
    marks[...] = jnp.full(marks.shape, -1.0, jnp.float32)
    field = lax.broadcasted_iota(jnp.int32, marks.shape[1:], 1) // FIELD
    left, right = pl.ds(0, block), pl.ds(block, block)
    half = pl.ds(2 * block, block)

    def send(src, dst):
        pltpu.make_async_copy(src, dst, out_sem).start()

    def place(t, carry):
        peer = peers[t]
        rank = count[peer]
        count[peer] = rank + 1
        mark = (rels[t] * blocks + sources[t]).astype(jnp.float32)

        @pl.when(rank == 0)
        def _():
            marks[peer] = jnp.where(field == 0, mark, marks[peer])
            send(made.at[t], out_ref.at[peer, pl.ds(0, 2 * block)])

        @pl.when(rank != 0)
        def _():
            chip = lax.shift_right_logical(peer, 1)
            later = seconds[chip]
            seconds[chip] = later + 1
            core = (peer & 1).astype(jnp.float32)
            first = 2 * chip
            for side in range(2):
                old = marks[first + side]
                old = jnp.where(field == 2 + 2 * later, core, old)
                marks[first + side] = jnp.where(field == 1 + 2 * later, mark, old)

            @pl.when(later == 0)
            def _():
                send(made.at[t, left], out_ref.at[first, half])
                send(made.at[t, right], out_ref.at[first + 1, half])

            @pl.when(later != 0)
            def _():
                flag[0] = 1
                send(made.at[t, left], later_ref.at[first])
                send(made.at[t, right], later_ref.at[first + 1])

        return carry

    for copy in early:
        copy.wait()

    for i in range(parts):
        fetch(i).wait()
        for t in range(i * part, (i + 1) * part):
            message = lax.dot_general(
                held[t], grad[dest[t]], (((0,), (0,)), ((), ())), preferred_element_type=jnp.float32
            ).astype(jnp.bfloat16)
            made[t, left] = message[:, :LANES]
            made[t, right] = message[:, LANES:]
        for t in range(i * part, (i + 1) * part):
            place(t, 0)

    any_later = flag[0].astype(jnp.float32)
    all_marks = jnp.where(field[None] == 5, any_later, marks[...])
    tags[...] = jnp.concatenate([all_marks, all_marks], axis=1).astype(jnp.bfloat16)
    tag_copy = pltpu.make_async_copy(tags, out_ref.at[:, pl.ds(3 * block, TAG_ROWS)], sems.at[0])
    tag_copy.start()
    pltpu.make_async_copy(made, out_ref.at[pl.ds(0, tile_count), pl.ds(0, 2 * block)], out_sem).wait()
    tag_copy.wait()


def make_messages(tile_dest, peer_list, tile_rel, tile_source, tiles, grad_blocks, dev_count):
    tile_count, block, _ = tiles.shape
    blocks, _, width = grad_blocks.shape
    parts = 8
    numbers = pltpu.SMEM((tile_count,), jnp.int32)

    def kernel(*refs):
        message_kernel(blocks, parts, *refs)

    return pl.pallas_call(
        kernel,
        out_shape=(
            jax.ShapeDtypeStruct((dev_count, 3 * block + TAG_ROWS, LANES), jnp.bfloat16),
            jax.ShapeDtypeStruct((dev_count, block, LANES), jnp.bfloat16),
        ),
        in_specs=[HBM] * 6,
        out_specs=(HBM, HBM),
        scratch_shapes=[
            numbers,
            numbers,
            numbers,
            numbers,
            pltpu.SMEM((dev_count,), jnp.int32),
            pltpu.SMEM((dev_count // 2,), jnp.int32),
            pltpu.SMEM((1,), jnp.int32),
            pltpu.VMEM(grad_blocks.shape, jnp.bfloat16),
            pltpu.VMEM(tiles.shape, jnp.bfloat16),
            pltpu.VMEM((tile_count, 2 * block, LANES), jnp.bfloat16),
            pltpu.VMEM((dev_count, TAG_ROWS // 2, LANES), jnp.float32),
            pltpu.VMEM((dev_count, TAG_ROWS, LANES), jnp.bfloat16),
            pltpu.SemaphoreType.DMA((parts + 5,)),
            pltpu.SemaphoreType.DMA,
        ],
        compiler_params=pltpu.CompilerParams(vmem_limit_bytes=58 * MIB),
        cost_estimate=pl.CostEstimate(
            flops=2 * tile_count * block * block * width,
            bytes_accessed=tile_count * block * (block + width) * 2,
            transcendentals=0,
        ),
    )(tile_dest, peer_list, tile_rel, tile_source, tiles, grad_blocks)


def plan_places(senders, rel_count):
    return -(-(senders + (GROUP - 1) * rel_count) // LANES) * LANES


def make_plans(tags, core, blocks, rel_count):
    senders = tags.shape[0]
    places = plan_places(senders, rel_count)
    wide = 1 << (rel_count - 1).bit_length()
    square = (senders, senders)
    row, lane = lax.broadcasted_iota(jnp.int32, square, 0), lax.broadcasted_iota(jnp.int32, square, 1)
    lane_set, lane_rel = lane // wide, (lane % wide).astype(jnp.float32)
    below = (lane < row).astype(jnp.float32).astype(jnp.bfloat16)
    ahead = ((row < lane) & (row // wide == lane_set)).astype(jnp.float32).astype(jnp.bfloat16)
    at = lax.broadcasted_iota(jnp.int32, (senders, places), 1)
    at, lead = at.astype(jnp.float32), (at // GROUP * GROUP).astype(jnp.float32)

    def column(i):
        return tags[:, i * FIELD : i * FIELD + 1]

    tag = [column(0), column(1), column(3)]
    rel = [jnp.floor(t * (1.0 / blocks)) for t in tag]
    used = [jnp.where((lane_set == q) & (lane_rel == r) & (t >= 0), 1.0, 0.0) for q, (t, r) in enumerate(zip(tag, rel))]
    every = used[0] + used[1] + used[2]
    before = jnp.dot(below, every.astype(jnp.bfloat16), preferred_element_type=jnp.float32)
    groups = jnp.floor((jnp.sum(every, axis=0, keepdims=True) + (GROUP - 1)) * (1.0 / GROUP))
    first = jnp.dot(
        jnp.broadcast_to(groups, (TAG_ROWS, senders)).astype(jnp.bfloat16), ahead, preferred_element_type=jnp.float32
    )[0:1]
    spot = before + first * GROUP
    across = tags.T
    line = lax.broadcasted_iota(jnp.int32, (TAG_ROWS, senders), 0)
    name = lax.broadcasted_iota(jnp.int32, (1, senders), 1).astype(jnp.float32)
    rows = []
    for q, i in enumerate((0, 1, 3)):
        place = jnp.where(tag[q] >= 0, jnp.sum(used[q] * spot, axis=1, keepdims=True), -1.0)
        here = jnp.where(place == at, 1.0, 0.0).astype(jnp.bfloat16)
        leads = jnp.where(place == lead, 1.0, 0.0).astype(jnp.bfloat16)
        mark = across[i * FIELD : i * FIELD + 1]
        relation = jnp.floor(mark * (1.0 / blocks))
        source = mark - relation * blocks - 2 * blocks
        if q:
            owner = across[(i + 1) * FIELD : (i + 1) * FIELD + 1]
            source = source + jnp.where(owner == core, 0.0, float(blocks))
        named = jnp.where(line == 0, 1.0, jnp.where(line == 1, name, jnp.where(line == 2, source, relation)))
        named = named.astype(jnp.bfloat16)
        own = jnp.dot(named, here, preferred_element_type=jnp.float32)
        led = jnp.dot(named, leads, preferred_element_type=jnp.float32)
        total = jnp.sum(jnp.where(lane_set[0:1] == q, groups, 0.0), axis=1, keepdims=True)
        rows += [jnp.where(own[0:1] > 0, own[1:2], led[1:2]), own[2:3] + 2 * blocks, led[3:4]]
        rows.append(jnp.broadcast_to(total, (1, places)))
    rows += [jnp.zeros((1, places), jnp.float32)] * 4
    return jnp.concatenate(rows, axis=0).astype(jnp.int32)


def walk_groups(end, use):
    def single(g, carry):
        use(g)
        return carry

    def four(j, carry):
        for k in range(4):
            use(4 * j + k)
        return carry

    fours = lax.shift_right_logical(end, 2)
    lax.fori_loop(0, fours, four, 0)
    lax.fori_loop(4 * fours, end, single, 0)


def whole(ref, sender, block):
    return jnp.concatenate([ref[sender, pl.ds(0, block)], ref[sender, pl.ds(block, block)]], axis=1)


def later_flag_kernel(arrived_ref, flag_ref, tags, sem):
    first = arrived_ref.shape[1] - TAG_ROWS
    copy = pltpu.make_async_copy(arrived_ref.at[:, pl.ds(first, TAG_ROWS)], tags, sem)
    copy.start()
    copy.wait()
    most = jnp.max(tags[...].astype(jnp.float32), axis=0)
    field = lax.broadcasted_iota(jnp.int32, most.shape, 1) // FIELD
    flag_ref[0] = (jnp.max(jnp.where(field == 5, most, -1.0)) > 0).astype(jnp.int32)


def turn_blocks(feat, mate, turned):
    blocks = feat.shape[0]
    turned[2 * blocks] = jnp.zeros(turned.shape[1:], turned.dtype)

    def turn(b, carry):
        for k in range(4):
            turned[b * 4 + k] = feat[b * 4 + k].T
            turned[blocks + b * 4 + k] = mate[b * 4 + k].T
        return carry

    lax.fori_loop(0, blocks // 4, turn, 0)


def weight_kernel(
    arrived_ref, feat_any, mate_any, grad_any, core_ref, own_ref, other_ref, plan_ref,
    held, halves, tags, feat, mate, grad, turned, acc, part, plan, plan_sem, sems,
):
    kinds, width, _ = acc.shape
    blocks, block, _ = feat.shape
    half = width // 2
    pairs = (
        (arrived_ref.at[:, pl.ds(3 * block, TAG_ROWS)], tags),
        (feat_any, feat),
        (mate_any, mate),
        (grad_any, grad),
        (arrived_ref.at[:, pl.ds(0, 2 * block)], held),
        (arrived_ref.at[:, pl.ds(2 * block, block)], halves),
    )
    copies = [pltpu.make_async_copy(src, dst, sems.at[i]) for i, (src, dst) in enumerate(pairs)]
    for copy in copies[:5]:
        copy.start()
    acc[...] = jnp.zeros_like(acc)
    part[...] = jnp.zeros_like(part)
    copies[0].wait()
    plan_ref[...] = make_plans(
        jnp.max(tags[...].astype(jnp.float32), axis=1), core_ref[0].astype(jnp.float32), blocks, kinds - 1
    )
    plan_copy = pltpu.make_async_copy(plan_ref, plan, plan_sem)
    plan_copy.start()
    copies[1].wait()
    copies[2].wait()
    copies[5].start()
    turn_blocks(feat, mate, turned)
    copies[3].wait()

    def root(g, carry):
        left = jnp.concatenate([turned[g * GROUP + k] for k in range(GROUP)], axis=1)
        right = grad[pl.ds(g * GROUP, GROUP)].reshape(GROUP * block, width)
        acc[0] += jnp.dot(left, right, preferred_element_type=jnp.float32)
        return carry

    lax.fori_loop(0, blocks // GROUP, root, 0)
    plan_copy.wait()

    def lefts(g, row):
        return jnp.concatenate([turned[plan[row + 1, g * GROUP + k]] for k in range(GROUP)], axis=1)

    def use(g):
        right = jnp.concatenate([whole(held, plan[0, g * GROUP + k], block) for k in range(GROUP)], axis=0)
        acc[1 + plan[2, g * GROUP]] += jnp.dot(lefts(g, 0), right, preferred_element_type=jnp.float32)

    def use_half(g):
        right = jnp.concatenate([halves[plan[4, g * GROUP + k]] for k in range(GROUP)], axis=0)
        part[plan[6, g * GROUP]] += jnp.dot(lefts(g, 4), right, preferred_element_type=jnp.float32)

    copies[4].wait()
    walk_groups(plan[3, 0], use)
    copies[5].wait()
    walk_groups(plan[7, 0], use_half)

    def split(own, other):
        for r in range(kinds):
            rows = pl.ds(r * width, width)
            own_ref[rows] = acc[r, :, own] + part[r - 1] if r else acc[r, :, own]
            other_ref[rows] = acc[r, :, other]

    first, second = pl.ds(0, half), pl.ds(half, half)

    @pl.when(core_ref[0] == 0)
    def _():
        split(first, second)

    @pl.when(core_ref[0] != 0)
    def _():
        split(second, first)


def later_kernel(plan, later_any, feat_any, mate_any, before_any, own_ref, later, feat, mate, turned, sems):
    width = feat.shape[2]
    pairs = ((before_any, own_ref), (feat_any, feat), (mate_any, mate), (later_any, later))
    copies = [pltpu.make_async_copy(src, dst, sems.at[i]) for i, (src, dst) in enumerate(pairs)]
    for copy in copies:
        copy.start()
    for copy in copies[:3]:
        copy.wait()

    @pl.when(plan[11, 0] > 0)
    def _():
        turn_blocks(feat, mate, turned)

    copies[3].wait()

    def use(g):
        left = jnp.concatenate([turned[plan[9, g * GROUP + k]] for k in range(GROUP)], axis=1)
        right = jnp.concatenate([later[plan[8, g * GROUP + k]] for k in range(GROUP)], axis=0)
        rows = pl.ds(pl.multiple_of((1 + plan[10, g * GROUP]) * width, width), width)
        own_ref[rows] += jnp.dot(left, right, preferred_element_type=jnp.float32)

    walk_groups(plan[11, 0], use)


def add_groups(plan_ref, row, acc, block, products):
    def use(g):
        part = products(g)
        for k in range(GROUP):
            acc[plan_ref[row + 1, g * GROUP + k]] += part[k * block : (k + 1) * block]

    walk_groups(plan_ref[row + 3, 0], use)


ACROSS = (((1,), (1,)), ((), ()))


def halves_kernel(
    plan_ref, core_ref, arrived_ref, grad_ref, root_ref, weight_ref, own_any, mate_ref, halves, acc, sem
):
    blocks, block, width = mate_ref.shape
    copy = pltpu.make_async_copy(arrived_ref.at[:, pl.ds(2 * block, block)], halves, sem)
    copy.start()
    acc[pl.ds(blocks, blocks + 1)] = jnp.zeros((blocks + 1, block, width), jnp.float32)

    def base(g, carry):
        rows = grad_ref[pl.ds(g * GROUP, GROUP)].reshape(GROUP * block, width)
        part = lax.dot_general(rows, root_ref[...], ACROSS, preferred_element_type=jnp.float32)
        acc[pl.ds(g * GROUP, GROUP)] = part.reshape(GROUP, block, width)
        return carry

    lax.fori_loop(0, blocks // GROUP, base, 0)
    copy.wait()
    add_groups(plan_ref, 4, acc, block, half_products(plan_ref, core_ref, weight_ref, halves, 4))
    own_copy = pltpu.make_async_copy(acc.at[pl.ds(0, blocks)], own_any, sem)
    own_copy.start()
    mate_ref[...] = acc[pl.ds(blocks, blocks)].astype(jnp.bfloat16)
    own_copy.wait()


def half_products(plan_ref, core_ref, weight_ref, halves, row):
    width = weight_ref.shape[1]
    half = width // 2
    lanes = pl.ds(pl.multiple_of(core_ref[0] * half, half), half)

    def products(g):
        rows = jnp.concatenate([halves[plan_ref[row, g * GROUP + k]] for k in range(GROUP)], axis=0)
        weight = weight_ref[plan_ref[row + 2, g * GROUP], :, lanes]
        return lax.dot_general(rows, weight, ACROSS, preferred_element_type=jnp.float32)

    return products


def early_kernel(plan_ref, core_ref, arrived_ref, grad_ref, root_ref, weight_ref, out_any, held, halves, acc, sems):
    blocks, block, width = grad_ref.shape
    copy = pltpu.make_async_copy(arrived_ref.at[:, pl.ds(0, 2 * block)], held, sems.at[0])
    half_copy = pltpu.make_async_copy(arrived_ref.at[:, pl.ds(2 * block, block)], halves, sems.at[1])
    copy.start()
    half_copy.start()
    acc[pl.ds(blocks, blocks + 1)] = jnp.zeros((blocks + 1, block, width), jnp.float32)

    def base(g, carry):
        rows = grad_ref[pl.ds(g * GROUP, GROUP)].reshape(GROUP * block, width)
        part = lax.dot_general(rows, root_ref[...], ACROSS, preferred_element_type=jnp.float32)
        acc[pl.ds(g * GROUP, GROUP)] = part.reshape(GROUP, block, width)
        return carry

    lax.fori_loop(0, blocks // GROUP, base, 0)

    def products(g):
        rows = jnp.concatenate([whole(held, plan_ref[0, g * GROUP + k], block) for k in range(GROUP)], axis=0)
        return lax.dot_general(rows, weight_ref[plan_ref[2, g * GROUP]], ACROSS, preferred_element_type=jnp.float32)

    copy.wait()
    add_groups(plan_ref, 0, acc, block, products)
    half_copy.wait()
    add_groups(plan_ref, 4, acc, block, half_products(plan_ref, core_ref, weight_ref, halves, 4))
    out_copy = pltpu.make_async_copy(acc.at[pl.ds(0, 2 * blocks)], out_any, sems.at[0])
    out_copy.start()
    out_copy.wait()


def late_kernel(plan_ref, core_ref, early_any, later_any, weight_ref, own_any, mate_ref, halves, acc, sems):
    blocks, block, width = mate_ref.shape
    early_copy = pltpu.make_async_copy(early_any, acc.at[pl.ds(0, 2 * blocks)], sems.at[0])
    later_copy = pltpu.make_async_copy(later_any, halves, sems.at[1])
    early_copy.start()
    later_copy.start()
    acc[2 * blocks] = jnp.zeros(acc.shape[1:], jnp.float32)
    early_copy.wait()
    later_copy.wait()
    add_groups(plan_ref, 8, acc, block, half_products(plan_ref, core_ref, weight_ref, halves, 8))
    own_copy = pltpu.make_async_copy(acc.at[pl.ds(0, blocks)], own_any, sems.at[0])
    own_copy.start()
    mate_ref[...] = acc[pl.ds(blocks, blocks)].astype(jnp.bfloat16)
    own_copy.wait()


def feat_kernel(
    plan_ref, arrived_ref, own_any, mate_any, weight_ref, out_ref, held, mate, acc, sems
):
    blocks, block, width = out_ref.shape
    own_copy = pltpu.make_async_copy(own_any, acc.at[pl.ds(0, blocks)], sems.at[0])
    copy = pltpu.make_async_copy(arrived_ref.at[:, pl.ds(0, 2 * block)], held, sems.at[1])
    mate_copy = pltpu.make_async_copy(mate_any, mate, sems.at[2])
    own_copy.start()
    copy.start()
    mate_copy.start()
    acc[2 * blocks] = jnp.zeros(acc.shape[1:], jnp.float32)
    own_copy.wait()
    copy.wait()

    def products(g):
        rows = jnp.concatenate([whole(held, plan_ref[0, g * GROUP + k], block) for k in range(GROUP)], axis=0)
        return lax.dot_general(rows, weight_ref[plan_ref[2, g * GROUP]], ACROSS, preferred_element_type=jnp.float32)

    add_groups(plan_ref, 0, acc, block, products)
    mate_copy.wait()
    out_ref[...] = (acc[pl.ds(0, blocks)] + mate[...].astype(jnp.float32)).astype(jnp.bfloat16)


def share_kernel(scale, spread_ref, share_ref):
    share = (jnp.sum(spread_ref[...], axis=0) * scale).astype(jnp.bfloat16)
    for i in range(share_ref.shape[0]):
        share_ref[i] = share


def join_kernel(core_ref, own_ref, other_ref, out_ref):
    kinds, width, _ = out_ref.shape
    half = width // 2

    def join(first, second):
        for r in range(kinds):
            rows = pl.ds(r * width, width)
            out_ref[r, :, pl.ds(0, half)] = first[rows].astype(jnp.float32)
            out_ref[r, :, pl.ds(half, half)] = second[rows].astype(jnp.float32)

    @pl.when(core_ref[0] == 0)
    def _():
        join(own_ref, other_ref)

    @pl.when(core_ref[0] != 0)
    def _():
        join(other_ref, own_ref)


def shards(features, out_grad, rel_weight, root_weight, tiles, tile_dest, tile_peer, tile_source, tile_rel):
    dev_count = lax.axis_size(AXES)
    chips = lax.axis_size(CHIPS)
    core = lax.axis_index("c")
    block = tiles.shape[1]
    width = features.shape[1]
    rel_count = rel_weight.shape[0]
    blocks = features.shape[0] // block
    scale = 1.0 / math.sqrt(features.shape[0] * dev_count)
    swap = [(0, 1), (1, 0)]
    grad_blocks = out_grad.reshape(blocks, block, width)
    feat_blocks = features.reshape(blocks, block, width)

    mate_blocks = lax.ppermute(feat_blocks, "c", swap)
    outgoing, later = make_messages(tile_dest, tile_peer[:, 0], tile_rel, tile_source, tiles, grad_blocks, dev_count)
    outgoing, later, core, mate_blocks = lax.optimization_barrier(
        (outgoing, later, core[None].astype(jnp.int32), mate_blocks)
    )

    def exchange(array):
        return lax.all_to_all(array, AXES, split_axis=0, concat_axis=0, tiled=True)

    arrived = exchange(outgoing)

    dma = pltpu.SemaphoreType.DMA
    cost = pl.CostEstimate(
        flops=2 * dev_count * block * width * width, bytes_accessed=dev_count * block * width * 3, transcendentals=0
    )
    half_rows = (1 + rel_count) * width
    half = jax.ShapeDtypeStruct((half_rows, width // 2), jnp.float32)
    local = pltpu.VMEM(grad_blocks.shape, jnp.bfloat16)
    turned = pltpu.VMEM((2 * blocks + 1, width, block), jnp.bfloat16)
    plan_type = jax.ShapeDtypeStruct((16, plan_places(dev_count, rel_count)), jnp.int32)
    def weights(arrived):
        own, other, plan = pl.pallas_call(
            weight_kernel,
            out_shape=(half, half, plan_type),
            in_specs=[HBM, HBM, HBM, HBM, SMEM],
            out_specs=(VMEM, VMEM, VMEM),
            scratch_shapes=[
                pltpu.VMEM((dev_count, 2 * block, LANES), jnp.bfloat16),
                pltpu.VMEM((dev_count, block, LANES), jnp.bfloat16),
                pltpu.VMEM((dev_count, TAG_ROWS, LANES), jnp.bfloat16),
                local,
                local,
                local,
                turned,
                pltpu.VMEM((1 + rel_count, width, width), jnp.float32),
                pltpu.VMEM((rel_count, width, width // 2), jnp.float32),
                pltpu.SMEM(plan_type.shape, jnp.int32),
                dma,
                dma((6,)),
            ],
            compiler_params=pltpu.CompilerParams(vmem_limit_bytes=50 * MIB),
            cost_estimate=cost,
        )(arrived, feat_blocks, mate_blocks, grad_blocks, core)
        return own + lax.ppermute(other, "c", swap), plan

    own_type = jax.ShapeDtypeStruct(grad_blocks.shape, jnp.float32)
    mate_type = jax.ShapeDtypeStruct(grad_blocks.shape, jnp.bfloat16)
    held = pltpu.VMEM((dev_count, 2 * block, LANES), jnp.bfloat16)
    halves = pltpu.VMEM((dev_count, block, LANES), jnp.bfloat16)
    sums = pltpu.VMEM((2 * blocks + 1, block, width), jnp.float32)
    roomy = pltpu.CompilerParams(vmem_limit_bytes=49 * MIB)

    def finish(own, plan, first_sums, last_sums):
        own, plan = lax.optimization_barrier((own, plan))
        own_part, mate_part = first_sums(plan)
        shape = (chips, half_rows // chips, width // 2)
        spread = lax.all_to_all(own.reshape(shape), CHIPS, 0, 0, tiled=True)
        spread, own_part, mate_part, plan = lax.optimization_barrier((spread, own_part, mate_part, plan))
        mate_part = lax.ppermute(mate_part, "c", swap)
        share = pl.pallas_call(
            functools.partial(share_kernel, scale),
            out_shape=jax.ShapeDtypeStruct(shape, jnp.bfloat16),
            in_specs=[VMEM],
            out_specs=VMEM,
            compiler_params=pltpu.CompilerParams(vmem_limit_bytes=8 * MIB),
        )(spread)
        own = lax.all_to_all(share, CHIPS, 0, 0, tiled=True).reshape(half.shape)
        grad_feat = last_sums(plan, own_part, mate_part)
        own, grad_feat = lax.optimization_barrier((own, grad_feat))
        other = lax.ppermute(own, "c", swap)
        grad_weights = pl.pallas_call(
            join_kernel,
            out_shape=jax.ShapeDtypeStruct((1 + rel_count, width, width), jnp.float32),
            in_specs=[SMEM, VMEM, VMEM],
            out_specs=VMEM,
            compiler_params=pltpu.CompilerParams(vmem_limit_bytes=16 * MIB),
        )(core, own, other)
        return grad_feat.reshape(features.shape), grad_weights

    def take_later(arrived, later):
        later = exchange(later)
        own, plan = weights(arrived)
        early = pl.pallas_call(
            early_kernel,
            out_shape=jax.ShapeDtypeStruct((2 * blocks, block, width), jnp.float32),
            in_specs=[SMEM, SMEM, HBM, VMEM, VMEM, VMEM],
            out_specs=HBM,
            scratch_shapes=[held, halves, sums, dma((2,))],
            compiler_params=roomy,
            cost_estimate=cost,
        )(plan, core, arrived, grad_blocks, root_weight, rel_weight)
        later, own, plan, early = lax.optimization_barrier((later, own, plan, early))
        own = pl.pallas_call(
            later_kernel,
            out_shape=half,
            in_specs=[SMEM] + [HBM] * 4,
            out_specs=VMEM,
            scratch_shapes=[halves, local, local, turned, dma((4,))],
            compiler_params=pltpu.CompilerParams(vmem_limit_bytes=57 * MIB),
        )(plan, later, feat_blocks, mate_blocks, own)

        def first_sums(plan):
            return pl.pallas_call(
                late_kernel,
                out_shape=(own_type, mate_type),
                in_specs=[SMEM, SMEM, HBM, HBM, VMEM],
                out_specs=(HBM, VMEM),
                scratch_shapes=[halves, sums, dma((2,))],
                compiler_params=roomy,
                cost_estimate=cost,
            )(plan, core, early, later, rel_weight)

        def last_sums(plan, own_part, mate_part):
            return (own_part + mate_part.astype(jnp.float32)).astype(jnp.bfloat16)

        return finish(own, plan, first_sums, last_sums)

    def take_none(arrived, later):
        own, plan = weights(arrived)

        def first_sums(plan):
            return pl.pallas_call(
                halves_kernel,
                out_shape=(own_type, mate_type),
                in_specs=[SMEM, SMEM, HBM, VMEM, VMEM, VMEM],
                out_specs=(HBM, VMEM),
                scratch_shapes=[halves, sums, dma],
                compiler_params=roomy,
                cost_estimate=cost,
            )(plan, core, arrived, grad_blocks, root_weight, rel_weight)

        def last_sums(plan, own_part, mate_part):
            return pl.pallas_call(
                feat_kernel,
                out_shape=mate_type,
                in_specs=[SMEM, HBM, HBM, HBM, VMEM],
                out_specs=VMEM,
                scratch_shapes=[held, local, sums, dma((3,))],
                compiler_params=roomy,
                cost_estimate=cost,
            )(plan, arrived, own_part, mate_part, rel_weight)

        return finish(own, plan, first_sums, last_sums)

    any_later = pl.pallas_call(
        later_flag_kernel,
        out_shape=jax.ShapeDtypeStruct((1,), jnp.int32),
        in_specs=[HBM],
        out_specs=SMEM,
        scratch_shapes=[pltpu.VMEM((dev_count, TAG_ROWS, LANES), jnp.bfloat16), dma],
        compiler_params=pltpu.CompilerParams(vmem_limit_bytes=58 * MIB),
    )(arrived)
    return lax.cond(any_later[0] > 0, take_later, take_none, arrived, later)


def solution(mesh):
    sizes = (4, 4, 4, 2)
    fine = Mesh(mesh.devices.reshape(sizes), AXES)
    return jax.shard_map(
        shards,
        mesh=fine,
        in_specs=(
            P(AXES, None),
            P(AXES, None),
            P(),
            P(),
            P(AXES, None, None),
            P(AXES),
            P(AXES, None),
            P(AXES),
            P(AXES),
        ),
        out_specs=(P(AXES, None), P()),
        check_vma=False,
    )
```

```python
import functools
import math

import jax
import jax.numpy as jnp
from jax import lax
from jax.experimental import pallas as pl
from jax.experimental.pallas import tpu as pltpu
from jax.sharding import Mesh
from jax.sharding import PartitionSpec as P

AXES = ("z", "y", "x", "c")
CHIPS = ("z", "y", "x")
VMEM = pl.BlockSpec(memory_space=pltpu.VMEM)
HBM = pl.BlockSpec(memory_space=pltpu.HBM)
SMEM = pl.BlockSpec(memory_space=pltpu.SMEM)
MIB = 1024 * 1024
GROUP = 8
LANES = 128
TAG_ROWS = 16
FIELD = 16


def message_kernel(
    blocks, parts, dest_any, peer_any, rel_any, source_any, tiles_ref, grad_any, out_ref, later_ref,
    dest, peers, rels, sources, count, seconds, flag, grad, held, made, marks, tags, sems, out_sem,
):
    tile_count, block, _ = tiles_ref.shape
    part = tile_count // parts
    pairs = ((dest_any, dest), (peer_any, peers), (rel_any, rels), (source_any, sources), (grad_any, grad))
    early = [pltpu.make_async_copy(src, dst, sems.at[parts + i]) for i, (src, dst) in enumerate(pairs)]
    for copy in early:
        copy.start()

    def fetch(i):
        rows = pl.ds(i * part, part)
        return pltpu.make_async_copy(tiles_ref.at[rows], held.at[rows], sems.at[i])

    for i in range(parts):
        fetch(i).start()

    def clear(i, carry):
        count[2 * i] = 0
        count[2 * i + 1] = 0
        seconds[i] = 0
        return carry

    lax.fori_loop(0, seconds.shape[0], clear, 0)
    flag[0] = 0
    marks[...] = jnp.full(marks.shape, -1.0, jnp.float32)
    field = lax.broadcasted_iota(jnp.int32, marks.shape[1:], 1) // FIELD
    left, right = pl.ds(0, block), pl.ds(block, block)
    half = pl.ds(2 * block, block)

    def send(src, dst):
        pltpu.make_async_copy(src, dst, out_sem).start()

    def place(t, carry):
        peer = peers[t]
        rank = count[peer]
        count[peer] = rank + 1
        mark = (rels[t] * blocks + sources[t]).astype(jnp.float32)

        @pl.when(rank == 0)
        def _():
            marks[peer] = jnp.where(field == 0, mark, marks[peer])
            send(made.at[t], out_ref.at[peer, pl.ds(0, 2 * block)])

        @pl.when(rank != 0)
        def _():
            chip = lax.shift_right_logical(peer, 1)
            later = seconds[chip]
            seconds[chip] = later + 1
            core = (peer & 1).astype(jnp.float32)
            first = 2 * chip
            for side in range(2):
                old = marks[first + side]
                old = jnp.where(field == 2 + 2 * later, core, old)
                marks[first + side] = jnp.where(field == 1 + 2 * later, mark, old)

            @pl.when(later == 0)
            def _():
                send(made.at[t, left], out_ref.at[first, half])
                send(made.at[t, right], out_ref.at[first + 1, half])

            @pl.when(later != 0)
            def _():
                flag[0] = 1
                send(made.at[t, left], later_ref.at[first])
                send(made.at[t, right], later_ref.at[first + 1])

        return carry

    for copy in early:
        copy.wait()

    for i in range(parts):
        fetch(i).wait()
        for t in range(i * part, (i + 1) * part):
            message = lax.dot_general(
                held[t], grad[dest[t]], (((0,), (0,)), ((), ())), preferred_element_type=jnp.float32
            ).astype(jnp.bfloat16)
            made[t, left] = message[:, :LANES]
            made[t, right] = message[:, LANES:]
        for t in range(i * part, (i + 1) * part):
            place(t, 0)

    any_later = flag[0].astype(jnp.float32)
    all_marks = jnp.where(field[None] == 5, any_later, marks[...])
    tags[...] = jnp.concatenate([all_marks, all_marks], axis=1).astype(jnp.bfloat16)
    tag_copy = pltpu.make_async_copy(tags, out_ref.at[:, pl.ds(3 * block, TAG_ROWS)], sems.at[0])
    tag_copy.start()
    pltpu.make_async_copy(made, out_ref.at[pl.ds(0, tile_count), pl.ds(0, 2 * block)], out_sem).wait()
    tag_copy.wait()


def make_messages(tile_dest, peer_list, tile_rel, tile_source, tiles, grad_blocks, dev_count):
    tile_count, block, _ = tiles.shape
    blocks, _, width = grad_blocks.shape
    parts = 8
    numbers = pltpu.SMEM((tile_count,), jnp.int32)

    def kernel(*refs):
        message_kernel(blocks, parts, *refs)

    return pl.pallas_call(
        kernel,
        out_shape=(
            jax.ShapeDtypeStruct((dev_count, 3 * block + TAG_ROWS, LANES), jnp.bfloat16),
            jax.ShapeDtypeStruct((dev_count, block, LANES), jnp.bfloat16),
        ),
        in_specs=[HBM] * 6,
        out_specs=(HBM, HBM),
        scratch_shapes=[
            numbers,
            numbers,
            numbers,
            numbers,
            pltpu.SMEM((dev_count,), jnp.int32),
            pltpu.SMEM((dev_count // 2,), jnp.int32),
            pltpu.SMEM((1,), jnp.int32),
            pltpu.VMEM(grad_blocks.shape, jnp.bfloat16),
            pltpu.VMEM(tiles.shape, jnp.bfloat16),
            pltpu.VMEM((tile_count, 2 * block, LANES), jnp.bfloat16),
            pltpu.VMEM((dev_count, TAG_ROWS // 2, LANES), jnp.float32),
            pltpu.VMEM((dev_count, TAG_ROWS, LANES), jnp.bfloat16),
            pltpu.SemaphoreType.DMA((parts + 5,)),
            pltpu.SemaphoreType.DMA,
        ],
        compiler_params=pltpu.CompilerParams(vmem_limit_bytes=58 * MIB),
        cost_estimate=pl.CostEstimate(
            flops=2 * tile_count * block * block * width,
            bytes_accessed=tile_count * block * (block + width) * 2,
            transcendentals=0,
        ),
    )(tile_dest, peer_list, tile_rel, tile_source, tiles, grad_blocks)


def plan_places(senders, rel_count):
    return -(-(senders + (GROUP - 1) * rel_count) // LANES) * LANES


def make_plans(tags, core, blocks, rel_count):
    senders = tags.shape[0]
    places = plan_places(senders, rel_count)
    wide = 1 << (rel_count - 1).bit_length()
    square = (senders, senders)
    row, lane = lax.broadcasted_iota(jnp.int32, square, 0), lax.broadcasted_iota(jnp.int32, square, 1)
    lane_set, lane_rel = lane // wide, (lane % wide).astype(jnp.float32)
    below = (lane < row).astype(jnp.float32).astype(jnp.bfloat16)
    ahead = ((row < lane) & (row // wide == lane_set)).astype(jnp.float32).astype(jnp.bfloat16)
    at = lax.broadcasted_iota(jnp.int32, (senders, places), 1)
    at, lead = at.astype(jnp.float32), (at // GROUP * GROUP).astype(jnp.float32)

    def column(i):
        return tags[:, i * FIELD : i * FIELD + 1]

    tag = [column(0), column(1), column(3)]
    rel = [jnp.floor(t * (1.0 / blocks)) for t in tag]
    used = [jnp.where((lane_set == q) & (lane_rel == r) & (t >= 0), 1.0, 0.0) for q, (t, r) in enumerate(zip(tag, rel))]
    every = used[0] + used[1] + used[2]
    before = jnp.dot(below, every.astype(jnp.bfloat16), preferred_element_type=jnp.float32)
    groups = jnp.floor((jnp.sum(every, axis=0, keepdims=True) + (GROUP - 1)) * (1.0 / GROUP))
    first = jnp.dot(
        jnp.broadcast_to(groups, (TAG_ROWS, senders)).astype(jnp.bfloat16), ahead, preferred_element_type=jnp.float32
    )[0:1]
    spot = before + first * GROUP
    across = tags.T
    line = lax.broadcasted_iota(jnp.int32, (TAG_ROWS, senders), 0)
    name = lax.broadcasted_iota(jnp.int32, (1, senders), 1).astype(jnp.float32)
    rows = []
    for q, i in enumerate((0, 1, 3)):
        place = jnp.where(tag[q] >= 0, jnp.sum(used[q] * spot, axis=1, keepdims=True), -1.0)
        here = jnp.where(place == at, 1.0, 0.0).astype(jnp.bfloat16)
        leads = jnp.where(place == lead, 1.0, 0.0).astype(jnp.bfloat16)
        mark = across[i * FIELD : i * FIELD + 1]
        relation = jnp.floor(mark * (1.0 / blocks))
        source = mark - relation * blocks - 2 * blocks
        if q:
            owner = across[(i + 1) * FIELD : (i + 1) * FIELD + 1]
            source = source + jnp.where(owner == core, 0.0, float(blocks))
        named = jnp.where(line == 0, 1.0, jnp.where(line == 1, name, jnp.where(line == 2, source, relation)))
        named = named.astype(jnp.bfloat16)
        own = jnp.dot(named, here, preferred_element_type=jnp.float32)
        led = jnp.dot(named, leads, preferred_element_type=jnp.float32)
        total = jnp.sum(jnp.where(lane_set[0:1] == q, groups, 0.0), axis=1, keepdims=True)
        rows += [jnp.where(own[0:1] > 0, own[1:2], led[1:2]), own[2:3] + 2 * blocks, led[3:4]]
        rows.append(jnp.broadcast_to(total, (1, places)))
    rows += [jnp.zeros((1, places), jnp.float32)] * 4
    return jnp.concatenate(rows, axis=0).astype(jnp.int32)


def walk_groups(end, use):
    def single(g, carry):
        use(g)
        return carry

    def four(j, carry):
        for k in range(4):
            use(4 * j + k)
        return carry

    def two(j, carry):
        for k in range(2):
            use(2 * j + k)
        return carry

    fours, twos = lax.shift_right_logical(end, 2), lax.shift_right_logical(end, 1)
    lax.fori_loop(0, fours, four, 0)
    lax.fori_loop(2 * fours, twos, two, 0)
    lax.fori_loop(2 * twos, end, single, 0)


def whole(ref, sender, block):
    return jnp.concatenate([ref[sender, pl.ds(0, block)], ref[sender, pl.ds(block, block)]], axis=1)


def later_flag_kernel(arrived_ref, flag_ref, tags, sem):
    first = arrived_ref.shape[1] - TAG_ROWS
    copy = pltpu.make_async_copy(arrived_ref.at[:, pl.ds(first, TAG_ROWS)], tags, sem)
    copy.start()
    copy.wait()
    most = jnp.max(tags[...].astype(jnp.float32), axis=0)
    field = lax.broadcasted_iota(jnp.int32, most.shape, 1) // FIELD
    flag_ref[0] = (jnp.max(jnp.where(field == 5, most, -1.0)) > 0).astype(jnp.int32)


def turn_blocks(feat, mate, turned):
    blocks = feat.shape[0]
    turned[2 * blocks] = jnp.zeros(turned.shape[1:], turned.dtype)

    def turn(b, carry):
        for k in range(4):
            turned[b * 4 + k] = feat[b * 4 + k].T
            turned[blocks + b * 4 + k] = mate[b * 4 + k].T
        return carry

    lax.fori_loop(0, blocks // 4, turn, 0)


def weight_kernel(
    arrived_ref, feat_any, mate_any, grad_any, core_ref, own_ref, other_ref, plan_ref,
    held, halves, tags, feat, mate, grad, turned, acc, part, plan, plan_sem, sems,
):
    kinds, width, _ = acc.shape
    blocks, block, _ = feat.shape
    half = width // 2
    pairs = (
        (arrived_ref.at[:, pl.ds(3 * block, TAG_ROWS)], tags),
        (feat_any, feat),
        (mate_any, mate),
        (grad_any, grad),
        (arrived_ref.at[:, pl.ds(0, 2 * block)], held),
        (arrived_ref.at[:, pl.ds(2 * block, block)], halves),
    )
    copies = [pltpu.make_async_copy(src, dst, sems.at[i]) for i, (src, dst) in enumerate(pairs)]
    for copy in copies[:5]:
        copy.start()
    acc[...] = jnp.zeros_like(acc)
    part[...] = jnp.zeros_like(part)
    copies[0].wait()
    plan_ref[...] = make_plans(
        jnp.max(tags[...].astype(jnp.float32), axis=1), core_ref[0].astype(jnp.float32), blocks, kinds - 1
    )
    plan_copy = pltpu.make_async_copy(plan_ref, plan, plan_sem)
    plan_copy.start()
    copies[1].wait()
    copies[2].wait()
    copies[5].start()
    turn_blocks(feat, mate, turned)
    copies[3].wait()

    def root(g, carry):
        left = jnp.concatenate([turned[g * GROUP + k] for k in range(GROUP)], axis=1)
        right = grad[pl.ds(g * GROUP, GROUP)].reshape(GROUP * block, width)
        acc[0] += jnp.dot(left, right, preferred_element_type=jnp.float32)
        return carry

    lax.fori_loop(0, blocks // GROUP, root, 0)
    plan_copy.wait()

    def lefts(g, row):
        return jnp.concatenate([turned[plan[row + 1, g * GROUP + k]] for k in range(GROUP)], axis=1)

    def use(g):
        right = jnp.concatenate([whole(held, plan[0, g * GROUP + k], block) for k in range(GROUP)], axis=0)
        acc[1 + plan[2, g * GROUP]] += jnp.dot(lefts(g, 0), right, preferred_element_type=jnp.float32)

    def use_half(g):
        right = jnp.concatenate([halves[plan[4, g * GROUP + k]] for k in range(GROUP)], axis=0)
        part[plan[6, g * GROUP]] += jnp.dot(lefts(g, 4), right, preferred_element_type=jnp.float32)

    copies[4].wait()
    walk_groups(plan[3, 0], use)
    copies[5].wait()
    walk_groups(plan[7, 0], use_half)

    def split(own, other):
        for r in range(kinds):
            rows = pl.ds(r * width, width)
            own_ref[rows] = acc[r, :, own] + part[r - 1] if r else acc[r, :, own]
            other_ref[rows] = acc[r, :, other]

    first, second = pl.ds(0, half), pl.ds(half, half)

    @pl.when(core_ref[0] == 0)
    def _():
        split(first, second)

    @pl.when(core_ref[0] != 0)
    def _():
        split(second, first)


def later_kernel(plan, later_any, feat_any, mate_any, before_any, own_ref, later, feat, mate, turned, sems):
    width = feat.shape[2]
    pairs = ((before_any, own_ref), (feat_any, feat), (mate_any, mate), (later_any, later))
    copies = [pltpu.make_async_copy(src, dst, sems.at[i]) for i, (src, dst) in enumerate(pairs)]
    for copy in copies:
        copy.start()
    for copy in copies[:3]:
        copy.wait()

    @pl.when(plan[11, 0] > 0)
    def _():
        turn_blocks(feat, mate, turned)

    copies[3].wait()

    def use(g):
        left = jnp.concatenate([turned[plan[9, g * GROUP + k]] for k in range(GROUP)], axis=1)
        right = jnp.concatenate([later[plan[8, g * GROUP + k]] for k in range(GROUP)], axis=0)
        rows = pl.ds(pl.multiple_of((1 + plan[10, g * GROUP]) * width, width), width)
        own_ref[rows] += jnp.dot(left, right, preferred_element_type=jnp.float32)

    walk_groups(plan[11, 0], use)


def add_groups(plan_ref, row, acc, block, products):
    def use(g):
        part = products(g)
        for k in range(GROUP):
            acc[plan_ref[row + 1, g * GROUP + k]] += part[k * block : (k + 1) * block]

    walk_groups(plan_ref[row + 3, 0], use)


ACROSS = (((1,), (1,)), ((), ()))


def halves_kernel(
    plan_ref, core_ref, arrived_ref, grad_ref, root_ref, weight_ref, own_any, mate_ref, halves, acc, sem
):
    blocks, block, width = mate_ref.shape
    copy = pltpu.make_async_copy(arrived_ref.at[:, pl.ds(2 * block, block)], halves, sem)
    copy.start()
    acc[pl.ds(blocks, blocks + 1)] = jnp.zeros((blocks + 1, block, width), jnp.float32)

    def base(g, carry):
        rows = grad_ref[pl.ds(g * GROUP, GROUP)].reshape(GROUP * block, width)
        part = lax.dot_general(rows, root_ref[...], ACROSS, preferred_element_type=jnp.float32)
        acc[pl.ds(g * GROUP, GROUP)] = part.reshape(GROUP, block, width)
        return carry

    lax.fori_loop(0, blocks // GROUP, base, 0)
    copy.wait()
    add_groups(plan_ref, 4, acc, block, half_products(plan_ref, core_ref, weight_ref, halves, 4))
    own_copy = pltpu.make_async_copy(acc.at[pl.ds(0, blocks)], own_any, sem)
    own_copy.start()
    mate_ref[...] = acc[pl.ds(blocks, blocks)].astype(jnp.bfloat16)
    own_copy.wait()


def half_products(plan_ref, core_ref, weight_ref, halves, row):
    width = weight_ref.shape[1]
    half = width // 2
    lanes = pl.ds(pl.multiple_of(core_ref[0] * half, half), half)

    def products(g):
        rows = jnp.concatenate([halves[plan_ref[row, g * GROUP + k]] for k in range(GROUP)], axis=0)
        weight = weight_ref[plan_ref[row + 2, g * GROUP], :, lanes]
        return lax.dot_general(rows, weight, ACROSS, preferred_element_type=jnp.float32)

    return products


def early_kernel(plan_ref, core_ref, arrived_ref, grad_ref, root_ref, weight_ref, out_any, held, halves, acc, sems):
    blocks, block, width = grad_ref.shape
    copy = pltpu.make_async_copy(arrived_ref.at[:, pl.ds(0, 2 * block)], held, sems.at[0])
    half_copy = pltpu.make_async_copy(arrived_ref.at[:, pl.ds(2 * block, block)], halves, sems.at[1])
    copy.start()
    half_copy.start()
    acc[pl.ds(blocks, blocks + 1)] = jnp.zeros((blocks + 1, block, width), jnp.float32)

    def base(g, carry):
        rows = grad_ref[pl.ds(g * GROUP, GROUP)].reshape(GROUP * block, width)
        part = lax.dot_general(rows, root_ref[...], ACROSS, preferred_element_type=jnp.float32)
        acc[pl.ds(g * GROUP, GROUP)] = part.reshape(GROUP, block, width)
        return carry

    lax.fori_loop(0, blocks // GROUP, base, 0)

    def products(g):
        rows = jnp.concatenate([whole(held, plan_ref[0, g * GROUP + k], block) for k in range(GROUP)], axis=0)
        return lax.dot_general(rows, weight_ref[plan_ref[2, g * GROUP]], ACROSS, preferred_element_type=jnp.float32)

    copy.wait()
    add_groups(plan_ref, 0, acc, block, products)
    half_copy.wait()
    add_groups(plan_ref, 4, acc, block, half_products(plan_ref, core_ref, weight_ref, halves, 4))
    out_copy = pltpu.make_async_copy(acc.at[pl.ds(0, 2 * blocks)], out_any, sems.at[0])
    out_copy.start()
    out_copy.wait()


def late_kernel(plan_ref, core_ref, early_any, later_any, weight_ref, own_any, mate_ref, halves, acc, sems):
    blocks, block, width = mate_ref.shape
    early_copy = pltpu.make_async_copy(early_any, acc.at[pl.ds(0, 2 * blocks)], sems.at[0])
    later_copy = pltpu.make_async_copy(later_any, halves, sems.at[1])
    early_copy.start()
    later_copy.start()
    acc[2 * blocks] = jnp.zeros(acc.shape[1:], jnp.float32)
    early_copy.wait()
    later_copy.wait()
    add_groups(plan_ref, 8, acc, block, half_products(plan_ref, core_ref, weight_ref, halves, 8))
    own_copy = pltpu.make_async_copy(acc.at[pl.ds(0, blocks)], own_any, sems.at[0])
    own_copy.start()
    mate_ref[...] = acc[pl.ds(blocks, blocks)].astype(jnp.bfloat16)
    own_copy.wait()


def feat_kernel(
    plan_ref, arrived_ref, own_any, mate_any, weight_ref, out_ref, held, mate, acc, sems
):
    blocks, block, width = out_ref.shape
    own_copy = pltpu.make_async_copy(own_any, acc.at[pl.ds(0, blocks)], sems.at[0])
    copy = pltpu.make_async_copy(arrived_ref.at[:, pl.ds(0, 2 * block)], held, sems.at[1])
    mate_copy = pltpu.make_async_copy(mate_any, mate, sems.at[2])
    own_copy.start()
    copy.start()
    mate_copy.start()
    acc[2 * blocks] = jnp.zeros(acc.shape[1:], jnp.float32)
    own_copy.wait()
    copy.wait()

    def products(g):
        rows = jnp.concatenate([whole(held, plan_ref[0, g * GROUP + k], block) for k in range(GROUP)], axis=0)
        return lax.dot_general(rows, weight_ref[plan_ref[2, g * GROUP]], ACROSS, preferred_element_type=jnp.float32)

    add_groups(plan_ref, 0, acc, block, products)
    mate_copy.wait()
    out_ref[...] = (acc[pl.ds(0, blocks)] + mate[...].astype(jnp.float32)).astype(jnp.bfloat16)


def share_kernel(scale, spread_ref, share_ref):
    share = (jnp.sum(spread_ref[...], axis=0) * scale).astype(jnp.bfloat16)
    for i in range(share_ref.shape[0]):
        share_ref[i] = share


def join_kernel(core_ref, own_ref, other_ref, out_ref):
    kinds, width, _ = out_ref.shape
    half = width // 2

    def join(first, second):
        for r in range(kinds):
            rows = pl.ds(r * width, width)
            out_ref[r, :, pl.ds(0, half)] = first[rows].astype(jnp.float32)
            out_ref[r, :, pl.ds(half, half)] = second[rows].astype(jnp.float32)

    @pl.when(core_ref[0] == 0)
    def _():
        join(own_ref, other_ref)

    @pl.when(core_ref[0] != 0)
    def _():
        join(other_ref, own_ref)


def shards(features, out_grad, rel_weight, root_weight, tiles, tile_dest, tile_peer, tile_source, tile_rel):
    dev_count = lax.axis_size(AXES)
    chips = lax.axis_size(CHIPS)
    core = lax.axis_index("c")
    block = tiles.shape[1]
    width = features.shape[1]
    rel_count = rel_weight.shape[0]
    blocks = features.shape[0] // block
    scale = 1.0 / math.sqrt(features.shape[0] * dev_count)
    swap = [(0, 1), (1, 0)]
    grad_blocks = out_grad.reshape(blocks, block, width)
    feat_blocks = features.reshape(blocks, block, width)

    mate_blocks = lax.ppermute(feat_blocks, "c", swap)
    outgoing, later = make_messages(tile_dest, tile_peer[:, 0], tile_rel, tile_source, tiles, grad_blocks, dev_count)
    outgoing, later, core, mate_blocks = lax.optimization_barrier(
        (outgoing, later, core[None].astype(jnp.int32), mate_blocks)
    )

    def exchange(array):
        return lax.all_to_all(array, AXES, split_axis=0, concat_axis=0, tiled=True)

    arrived = exchange(outgoing)

    dma = pltpu.SemaphoreType.DMA
    cost = pl.CostEstimate(
        flops=2 * dev_count * block * width * width, bytes_accessed=dev_count * block * width * 3, transcendentals=0
    )
    half_rows = (1 + rel_count) * width
    half = jax.ShapeDtypeStruct((half_rows, width // 2), jnp.float32)
    local = pltpu.VMEM(grad_blocks.shape, jnp.bfloat16)
    turned = pltpu.VMEM((2 * blocks + 1, width, block), jnp.bfloat16)
    plan_type = jax.ShapeDtypeStruct((16, plan_places(dev_count, rel_count)), jnp.int32)
    def weights(arrived):
        own, other, plan = pl.pallas_call(
            weight_kernel,
            out_shape=(half, half, plan_type),
            in_specs=[HBM, HBM, HBM, HBM, SMEM],
            out_specs=(VMEM, VMEM, VMEM),
            scratch_shapes=[
                pltpu.VMEM((dev_count, 2 * block, LANES), jnp.bfloat16),
                pltpu.VMEM((dev_count, block, LANES), jnp.bfloat16),
                pltpu.VMEM((dev_count, TAG_ROWS, LANES), jnp.bfloat16),
                local,
                local,
                local,
                turned,
                pltpu.VMEM((1 + rel_count, width, width), jnp.float32),
                pltpu.VMEM((rel_count, width, width // 2), jnp.float32),
                pltpu.SMEM(plan_type.shape, jnp.int32),
                dma,
                dma((6,)),
            ],
            compiler_params=pltpu.CompilerParams(vmem_limit_bytes=50 * MIB),
            cost_estimate=cost,
        )(arrived, feat_blocks, mate_blocks, grad_blocks, core)
        return own + lax.ppermute(other, "c", swap), plan

    own_type = jax.ShapeDtypeStruct(grad_blocks.shape, jnp.float32)
    mate_type = jax.ShapeDtypeStruct(grad_blocks.shape, jnp.bfloat16)
    held = pltpu.VMEM((dev_count, 2 * block, LANES), jnp.bfloat16)
    halves = pltpu.VMEM((dev_count, block, LANES), jnp.bfloat16)
    sums = pltpu.VMEM((2 * blocks + 1, block, width), jnp.float32)
    roomy = pltpu.CompilerParams(vmem_limit_bytes=49 * MIB)

    def finish(own, plan, first_sums, last_sums):
        own, plan = lax.optimization_barrier((own, plan))
        own_part, mate_part = first_sums(plan)
        shape = (chips, half_rows // chips, width // 2)
        spread = lax.all_to_all(own.reshape(shape), CHIPS, 0, 0, tiled=True)
        spread, own_part, mate_part, plan = lax.optimization_barrier((spread, own_part, mate_part, plan))
        mate_part = lax.ppermute(mate_part, "c", swap)
        share = pl.pallas_call(
            functools.partial(share_kernel, scale),
            out_shape=jax.ShapeDtypeStruct(shape, jnp.bfloat16),
            in_specs=[VMEM],
            out_specs=VMEM,
            compiler_params=pltpu.CompilerParams(vmem_limit_bytes=8 * MIB),
        )(spread)
        own = lax.all_to_all(share, CHIPS, 0, 0, tiled=True).reshape(half.shape)
        grad_feat = last_sums(plan, own_part, mate_part)
        own, grad_feat = lax.optimization_barrier((own, grad_feat))
        other = lax.ppermute(own, "c", swap)
        grad_weights = pl.pallas_call(
            join_kernel,
            out_shape=jax.ShapeDtypeStruct((1 + rel_count, width, width), jnp.float32),
            in_specs=[SMEM, VMEM, VMEM],
            out_specs=VMEM,
            compiler_params=pltpu.CompilerParams(vmem_limit_bytes=16 * MIB),
        )(core, own, other)
        return grad_feat.reshape(features.shape), grad_weights

    def take_later(arrived, later):
        later = exchange(later)
        own, plan = weights(arrived)
        early = pl.pallas_call(
            early_kernel,
            out_shape=jax.ShapeDtypeStruct((2 * blocks, block, width), jnp.float32),
            in_specs=[SMEM, SMEM, HBM, VMEM, VMEM, VMEM],
            out_specs=HBM,
            scratch_shapes=[held, halves, sums, dma((2,))],
            compiler_params=roomy,
            cost_estimate=cost,
        )(plan, core, arrived, grad_blocks, root_weight, rel_weight)
        later, own, plan, early = lax.optimization_barrier((later, own, plan, early))
        own = pl.pallas_call(
            later_kernel,
            out_shape=half,
            in_specs=[SMEM] + [HBM] * 4,
            out_specs=VMEM,
            scratch_shapes=[halves, local, local, turned, dma((4,))],
            compiler_params=pltpu.CompilerParams(vmem_limit_bytes=57 * MIB),
        )(plan, later, feat_blocks, mate_blocks, own)

        def first_sums(plan):
            return pl.pallas_call(
                late_kernel,
                out_shape=(own_type, mate_type),
                in_specs=[SMEM, SMEM, HBM, HBM, VMEM],
                out_specs=(HBM, VMEM),
                scratch_shapes=[halves, sums, dma((2,))],
                compiler_params=roomy,
                cost_estimate=cost,
            )(plan, core, early, later, rel_weight)

        def last_sums(plan, own_part, mate_part):
            return (own_part + mate_part.astype(jnp.float32)).astype(jnp.bfloat16)

        return finish(own, plan, first_sums, last_sums)

    def take_none(arrived, later):
        own, plan = weights(arrived)

        def first_sums(plan):
            return pl.pallas_call(
                halves_kernel,
                out_shape=(own_type, mate_type),
                in_specs=[SMEM, SMEM, HBM, VMEM, VMEM, VMEM],
                out_specs=(HBM, VMEM),
                scratch_shapes=[halves, sums, dma],
                compiler_params=roomy,
                cost_estimate=cost,
            )(plan, core, arrived, grad_blocks, root_weight, rel_weight)

        def last_sums(plan, own_part, mate_part):
            return pl.pallas_call(
                feat_kernel,
                out_shape=mate_type,
                in_specs=[SMEM, HBM, HBM, HBM, VMEM],
                out_specs=VMEM,
                scratch_shapes=[held, local, sums, dma((3,))],
                compiler_params=roomy,
                cost_estimate=cost,
            )(plan, arrived, own_part, mate_part, rel_weight)

        return finish(own, plan, first_sums, last_sums)

    any_later = pl.pallas_call(
        later_flag_kernel,
        out_shape=jax.ShapeDtypeStruct((1,), jnp.int32),
        in_specs=[HBM],
        out_specs=SMEM,
        scratch_shapes=[pltpu.VMEM((dev_count, TAG_ROWS, LANES), jnp.bfloat16), dma],
        compiler_params=pltpu.CompilerParams(vmem_limit_bytes=58 * MIB),
    )(arrived)
    return lax.cond(any_later[0] > 0, take_later, take_none, arrived, later)


def solution(mesh):
    sizes = (4, 4, 4, 2)
    fine = Mesh(mesh.devices.reshape(sizes), AXES)
    return jax.shard_map(
        shards,
        mesh=fine,
        in_specs=(
            P(AXES, None),
            P(AXES, None),
            P(),
            P(),
            P(AXES, None, None),
            P(AXES),
            P(AXES, None),
            P(AXES),
            P(AXES),
        ),
        out_specs=(P(AXES, None), P()),
        check_vma=False,
    )
```
